32 devices in a mesh: seq: 8 (over z, y), batch: 4 (over x, core).
Axes of the slice: x: 2, y: 2, z: 4, core: 2. Of those that a mesh axis runs over, the one named last changes fastest.
Arguments:
- layer_input: bfloat16 [8, 4096, 1024], P('batch', 'seq'), may hold values from -6 to 6
- skip_input: bfloat16 [8, 4096, 1024], P('batch', 'seq'), may hold values from -6 to 6
- time_embed: bfloat16 [8, 1024], P('batch'), may hold values from -6 to 6
- lengths: int32 [8], P('batch'), may hold values from 273 to 4096, as said below
- cond_drop: int32 [8], P('batch'), may hold values 0 or 1
- cotangent: bfloat16 [8, 4096, 1024], P('batch', 'seq'), may hold values from -6 to 6
- skip_weight: bfloat16 [2048, 1024], P('seq'), may hold values from -0.125 to 0.125
- adaln_weight: bfloat16 [1024, 6144], P('seq'), may hold values from -0.1875 to 0.1875
- adaln_bias: bfloat16 [6144], P('seq'), may hold values from -3 to 3
- qkv_weight: bfloat16 [1024, 3072], P('seq'), may hold values from -0.1875 to 0.1875
- out_weight: bfloat16 [1024, 1024], P('seq'), may hold values from -3 to 3
- up_weight: bfloat16 [1024, 4096], P('seq'), may hold values from -0.1875 to 0.1875
- down_weight: bfloat16 [4096, 1024], P('seq'), may hold values from -0.09375 to 0.09375
Outputs:
- layer_output: bfloat16 [8, 4096, 1024], P('batch', 'seq')
- grad_input: bfloat16 [8, 4096, 1024], P('batch', 'seq')
- grad_skip: bfloat16 [8, 4096, 1024], P('batch', 'seq')
- grad_skip_weight: float32 [2048, 1024], P('seq')
- grad_adaln_weight: float32 [1024, 6144], P('seq')
- grad_adaln_bias: float32 [6144], P('seq')
- grad_qkv_weight: float32 [1024, 3072], P('seq')
- grad_out_weight: float32 [1024, 1024], P('seq')
- grad_up_weight: float32 [1024, 4096], P('seq')
- grad_down_weight: float32 [4096, 1024], P('seq')
The draws below stay inside these ranges and needn't reach their ends.
Inputs may be any that keep to these rules, and one draw needn't show every extreme that they name: `lengths`: of the 2 utterances that one index of batch holds, one has all 4096 frames.
All inputs are finite; a program needn't handle non-finite values. No bound on the sum of `cond_drop` on one device may be relied on, other than what follows from the above.
Results may differ from the reference program's by a relative error of at most 0.019.
Values may be sent and summed in bfloat16 or wider, within the bound.
A program may use at most 480 MiB of HBM per device.

```python
import jax
import jax.numpy as jnp
from jax import lax

D = 1024
HEADS = 16
HEAD_DIM = 64
FF = 4096
UTT_DEV = 2
FRAMES = 4096
UTTS = 8


def draw_lengths(key, part):
    key = jax.random.fold_in(key, 11)
    lowest = max(1, FRAMES // 15)
    spans = jax.random.randint(jax.random.fold_in(key, 1), (UTTS,), lowest, FRAMES + 1)
    chosen = jax.random.randint(jax.random.fold_in(key, 2), (UTTS // UTT_DEV,), 0, UTT_DEV)
    slot_index = jnp.arange(UTTS, dtype=jnp.int32)
    longest = slot_index % UTT_DEV == jnp.repeat(chosen, UTT_DEV)
    return jnp.where(longest, FRAMES, spans).astype(jnp.int32)


def with_ends(entries, stream_key, smallest, top_value):
    shape = entries.shape
    index_at = [jax.random.randint(jax.random.fold_in(stream_key, axis), (), 0, shape[axis]) for axis in range(len(shape))]
    entries = entries.at[tuple(index_at)].set(smallest)
    longest = shape.index(max(shape))
    index_at[longest] = (index_at[longest] + 1) % shape[longest]
    return entries.at[tuple(index_at)].set(top_value)


def levels(own_key, extent, shards, least, high):
    factor_of, own = 1.0, jax.random.fold_in(own_key, 6)
    for dim, parts in shards:
        heights = jnp.exp(jax.random.uniform(jax.random.fold_in(own, dim), (parts,), jnp.float32, least / len(shards), high / len(shards)))
        factor_of = factor_of * jnp.repeat(heights, extent[dim] // parts).reshape([-1 if axis == dim else 1 for axis in range(len(extent))])
    return factor_of


def bell_draw(key, extent, scale, reach, pieces=(), kind=jnp.bfloat16):
    level = levels(key, extent, pieces, -0.22, 0.18) if pieces else 1.0
    entries = jax.random.normal(key, extent, jnp.float32) * scale * level
    return jnp.minimum(jnp.maximum(entries, -reach), reach).astype(kind)


def setup_inputs(seed: int = 0) -> dict:
    key_of = jax.random.split(jax.random.key(seed), 14)
    layer_input = bell_draw(key_of[0], (UTTS, FRAMES, D), 1.0, 6.0, ((0, 4), (1, 8)))
    skip_input = bell_draw(key_of[1], (UTTS, FRAMES, D), 1.0, 6.0, ((0, 4), (1, 8)))
    time_embed = bell_draw(key_of[2], (UTTS, D), 1.0, 6.0, ((0, 4),))
    lengths = draw_lengths(jax.random.fold_in(key_of[13], 71), 0)
    cond_drop = with_ends((jax.random.randint(key_of[4], (UTTS,), 0, 4) < 1).astype(jnp.int32), jax.random.fold_in(key_of[4], 1), 0, 1)
    cotangent = bell_draw(key_of[5], (UTTS, FRAMES, D), 1.0, 6.0, ((0, 4), (1, 8)))
    skip_weight = bell_draw(key_of[6], (2 * D, D), (2 * D) ** -0.5, 0.125, ((0, 8),))
    adaln_weight = bell_draw(key_of[7], (D, 6 * D), D ** -0.5, 0.1875, ((0, 8),))
    adaln_bias = bell_draw(key_of[8], (6 * D,), 0.5, 3.0, ((0, 8),))
    qkv_weight = bell_draw(key_of[9], (D, 3 * D), D ** -0.5, 0.1875, ((0, 8),))
    out_weight = bell_draw(key_of[10], (D, D), (max(1, D // 256)) ** -0.5, 3.0, ((0, 8),))
    up_weight = bell_draw(key_of[11], (D, FF), D ** -0.5, 0.1875, ((0, 8),))
    down_weight = bell_draw(key_of[12], (FF, D), FF ** -0.5, 0.09375, ((0, 8),))
    return {"layer_input": layer_input, "skip_input": skip_input, "time_embed": time_embed, "lengths": lengths, "cond_drop": cond_drop, "cotangent": cotangent, "skip_weight": skip_weight, "adaln_weight": adaln_weight, "adaln_bias": adaln_bias, "qkv_weight": qkv_weight, "out_weight": out_weight, "up_weight": up_weight, "down_weight": down_weight}


EPS = 1e-06
MASKED = -1e+30

@jax.custom_vjp
def low(v):
    return lax.optimization_barrier(v.astype(jnp.bfloat16)).astype(jnp.float32)

@jax.custom_vjp
def low_back(v):
    return v

def low_keep(v):
    return (low(v), None)

def low_pass(kept, grad):
    return (grad,)

def back_keep(v):
    return (v, None)

def back_low(kept, grad):
    return (low(grad),)
low.defvjp(low_keep, low_pass)
low_back.defvjp(back_keep, back_low)

def product(left, right):
    return jnp.dot(left, right, precision=lax.Precision.HIGHEST)

def layer_norm(stream):
    centre = stream - lax.optimization_barrier(jnp.mean(stream, axis=-1, keepdims=True))
    spread = lax.optimization_barrier(jnp.mean(centre * centre, axis=-1, keepdims=True))
    return centre * lax.rsqrt(spread + EPS)

def rotary_tables(positions):
    half_dim = HEAD_DIM // 2
    channel = jnp.arange(half_dim, dtype=jnp.float32)
    inverse = jnp.power(10000.0, -2.0 * channel / HEAD_DIM)
    angles = positions.astype(jnp.float32)[:, None] * inverse[None, :]
    angles = jnp.concatenate([angles, angles], axis=1)
    return (jnp.cos(angles), jnp.sin(angles))

def rotate_heads(field, cosine_table, sine_table):
    half_dim = field.shape[-1] // 2
    turned = jnp.concatenate([-field[..., half_dim:], field[..., :half_dim]], axis=-1)
    return field * cosine_table + turned * sine_table

def forward_layer(weights, layer_in, skip_in, time_in, length):
    skip_w, adaln_w, adaln_b, qkv_w, out_w, up_w, down_w = weights
    joined = jnp.concatenate([layer_in, skip_in], axis=-1)
    residual_in = low_back(product(joined, skip_w))
    modulation = (product(low(jax.nn.silu(time_in))[None, :], adaln_w)[0] + adaln_b).reshape(6, D)
    normed_attn = low(layer_norm(residual_in) * (1.0 + modulation[1]) + modulation[0])
    projected = low_back(product(normed_attn, qkv_w)).reshape(FRAMES, 3, HEADS, HEAD_DIM)
    positions = jnp.arange(FRAMES, dtype=jnp.int32)
    cosine_table, sine_table = rotary_tables(positions)
    cosine_table = cosine_table[:, None, :]
    sine_table = sine_table[:, None, :]
    queries = low(rotate_heads(projected[:, 0], cosine_table, sine_table) * 0.125)
    keys_rot = low(rotate_heads(projected[:, 1], cosine_table, sine_table))
    values = low(projected[:, 2])
    scores = low_back(jnp.einsum('qhd,khd->hqk', queries, keys_rot, precision=lax.Precision.HIGHEST))
    key_live = positions < length
    scores = jnp.where(key_live[None, None, :], scores, MASKED)
    probs = low(jax.nn.softmax(scores, axis=-1))
    attended = low_back(low(jnp.einsum('hqk,khd->qhd', probs, values, precision=lax.Precision.HIGHEST)))
    branch_attn = low_back(product(attended.reshape(FRAMES, D), out_w))
    residual_mid = residual_in + modulation[2] * branch_attn
    normed_ffn = low(layer_norm(residual_mid) * (1.0 + modulation[4]) + modulation[3])
    hidden_pre = low_back(product(normed_ffn, up_w))
    hidden_act = low(jax.nn.gelu(hidden_pre, approximate=True))
    branch_ffn = low_back(product(hidden_act, down_w))
    return residual_mid + modulation[5] * branch_ffn

def reference(layer_input, skip_input, time_embed, lengths, cond_drop, cotangent, skip_weight, adaln_weight, adaln_bias, qkv_weight, out_weight, up_weight, down_weight):
    positions = jnp.arange(FRAMES, dtype=jnp.int32)
    valid_mask = (positions[None, :] < lengths[:, None]).astype(jnp.float32)
    dropped = cond_drop.astype(jnp.float32)[:, None] * valid_mask
    kept_count = jnp.maximum(jnp.sum(valid_mask - dropped), 1.0)
    drop_count = jnp.maximum(jnp.sum(dropped), 1.0)
    every_count = kept_count + drop_count
    loss_weight = (valid_mask - dropped) * (every_count / (2.0 * kept_count)) + dropped * (every_count / (2.0 * drop_count))
    params = tuple((weight_arg.astype(jnp.float32) for weight_arg in (skip_weight, adaln_weight, adaln_bias, qkv_weight, out_weight, up_weight, down_weight)))
    zero_grads = jax.tree.map(jnp.zeros_like, params)

    def one_sequence(totals, scan_item):
        layer_in, skip_in, time_in, length, upstream, weight_row = scan_item

        def run_layer(weights, first_in, second_in):
            return forward_layer(weights, first_in, second_in, time_in.astype(jnp.float32), length)
        result, pullback = jax.vjp(run_layer, params, layer_in.astype(jnp.float32), skip_in.astype(jnp.float32))
        grad_weights, grad_first, grad_second = pullback(upstream.astype(jnp.float32) * weight_row[:, None])
        totals = jax.tree.map(lambda total, term: total + term, totals, grad_weights)
        return (totals, (result.astype(jnp.bfloat16), grad_first.astype(jnp.bfloat16), grad_second.astype(jnp.bfloat16)))
    totals, outputs = lax.scan(one_sequence, zero_grads, (layer_input, skip_input, time_embed, lengths, cotangent, loss_weight))
    layer_output, grad_input, grad_skip = outputs
    return (layer_output, grad_input, grad_skip, totals[0], totals[1], totals[2], totals[3], totals[4], totals[5], totals[6])
```

```python
import functools
import jax
import jax.numpy as jnp
from jax import lax
from jax.sharding import PartitionSpec as P
from jax.experimental import pallas as pl
from jax.experimental.pallas import tpu as pltpu
HEAD_DIM = 64
EPS = 1e-06
LOG2E = 1.4426950408889634
LN2 = 0.6931471805599453
MASKED = -1e30
RANGE = 100.0
BF = jnp.bfloat16
F32 = jnp.float32
VMEM_LIMIT = 60 * 2**20


def nt(left, right):
    return lax.dot_general(left, right, (((1,), (1,)), ((), ())), preferred_element_type=F32)


def nn(left, right):
    return lax.dot_general(left, right, (((1,), (0,)), ((), ())), preferred_element_type=F32)


def head_sums(product, lane):
    first = jnp.sum(jnp.where(lane < 64, product, 0.0), axis=1, keepdims=True)
    second = jnp.sum(jnp.where(lane >= 64, product, 0.0), axis=1, keepdims=True)
    return (first, second)


def lanes_of(rows):
    return lax.broadcasted_iota(jnp.int32, (rows, 128), 1)


def flash_forward_kernel(len_ref, q_ref, k_ref, v_ref, o_ref, lse_ref, ka, kb, vta, vtb, mean_ref, top_ref, *, bq, bk):
    step = pl.program_id(0)
    length = len_ref[0]
    frames = k_ref.shape[0]

    @pl.when(step == 0)
    def _():
        def build(j, carry):
            rows = pl.ds(pl.multiple_of(j * bk, bk), bk)
            lane = lanes_of(bk)
            pos = j * bk + lax.broadcasted_iota(jnp.int32, (bk, 128), 0)
            bias = jnp.where(pos < length, 0.0, MASKED)
            keys = k_ref[rows, :].astype(F32)
            ka[rows, :] = jnp.where(lane < 64, keys, jnp.where(lane == 64, bias, jnp.where(lane == 65, 1.0, 0.0))).astype(BF)
            kb[rows, :] = jnp.where(lane >= 64, keys, jnp.where(lane == 0, bias, jnp.where(lane == 1, 1.0, 0.0))).astype(BF)
            vals = v_ref[rows, :].astype(F32)
            vta[:, rows] = jnp.where(lane < 64, vals, 1.0).T.astype(BF)
            vtb[:, rows] = jnp.where(lane >= 64, vals, 1.0).T.astype(BF)
            keys = jnp.where(pos < length, keys, 0.0)
            norm_a, norm_b = head_sums(keys * keys, lane)
            total, top_a, top_b = carry
            return (
                total + jnp.sum(keys, axis=0, keepdims=True),
                jnp.maximum(top_a, jnp.max(norm_a)),
                jnp.maximum(top_b, jnp.max(norm_b)),
            )

        total, top_a, top_b = lax.fori_loop(
            0, frames // bk, build, (jnp.zeros((1, 128), F32), jnp.float32(0.0), jnp.float32(0.0))
        )
        mean_ref[0:1, :] = total / length.astype(F32)
        top_ref[0] = top_a
        top_ref[1] = top_b

    lane = lanes_of(bq)
    queries = q_ref[...].astype(F32)
    bounds = [
        jnp.sqrt(jnp.max(norm) * top_ref[head]) * 1.001
        for head, norm in enumerate(head_sums(queries * queries, lane))
    ]
    shifts = [jnp.maximum(bound - RANGE, 0.0) for bound in bounds]
    lows = [jnp.min(low) for low in head_sums(queries * mean_ref[0:1, :], lane)]
    tame = jnp.logical_and(lows[0] - shifts[0] >= -RANGE, lows[1] - shifts[1] >= -RANGE)
    qa = jnp.where(lane < 64, queries, jnp.where(lane == 64, 1.0, jnp.where(lane == 65, -shifts[0], 0.0)))
    qb = jnp.where(lane >= 64, queries, jnp.where(lane == 0, 1.0, jnp.where(lane == 1, -shifts[1], 0.0)))
    qa, qb = qa.astype(BF), qb.astype(BF)

    def body(j, carry):
        rows = pl.ds(pl.multiple_of(j * bk, bk), bk)
        out = []
        scores = [nt(ka[rows, :], qa), nt(kb[rows, :], qb)]
        for score, vt, (top, acc) in zip(scores, (vta, vtb), carry):
            new = jnp.maximum(top, jnp.max(score, axis=0, keepdims=True))
            probs = jnp.exp2(score - new).astype(BF)
            acc = acc * jnp.exp2(top - new) + nn(vt[:, rows], probs)
            out.append((new, acc))
        return tuple(out)

    live = (length + bk - 1) // bk

    def finish(shift_a, acc_a, shift_b, acc_b):
        sum_a, sum_b = acc_a[64:65], acc_b[0:1]
        both = jnp.concatenate([acc_a[:64] / sum_a, acc_b[64:] / sum_b], axis=0)
        o_ref[...] = both.T.astype(BF)
        lse_ref[...] = jnp.concatenate(
            [shift_a + jnp.log2(sum_a), shift_b + jnp.log2(sum_b), jnp.zeros((6, bq), F32)], axis=0
        )

    @pl.when(tame)
    def _():
        def plain(j, carry):
            rows = pl.ds(pl.multiple_of(j * bk, bk), bk)
            out = []
            for keys, query, vt, acc in ((ka, qa, vta, carry[0]), (kb, qb, vtb, carry[1])):
                probs = jnp.exp2(nt(keys[rows, :], query)).astype(BF)
                out.append(acc + nn(vt[:, rows], probs))
            return tuple(out)

        start = jnp.zeros((128, bq), F32)
        acc_a, acc_b = lax.fori_loop(0, live, plain, (start, start))
        rounded = [shift.astype(BF).astype(F32) for shift in shifts]
        finish(rounded[0], acc_a, rounded[1], acc_b)

    @pl.when(jnp.logical_not(tame))
    def _():
        start = (jnp.full((1, bq), MASKED, F32), jnp.zeros((128, bq), F32))
        (top_a, acc_a), (top_b, acc_b) = lax.fori_loop(0, live, body, (start, start))
        rounded = [shift.astype(BF).astype(F32) for shift in shifts]
        finish(rounded[0] + top_a, acc_a, rounded[1] + top_b, acc_b)


def attention_cost(frames, products):
    return pl.CostEstimate(
        flops=2 * products * 2 * frames * frames * 128,
        bytes_accessed=frames * 128 * 2 * 8,
        transcendentals=2 * frames * frames,
    )


def flash_forward(length, qkv, bq, bk):
    frames = qkv.shape[0]
    return pl.pallas_call(
        functools.partial(flash_forward_kernel, bq=bq, bk=bk),
        grid_spec=pltpu.PrefetchScalarGridSpec(
            num_scalar_prefetch=1,
            grid=(frames // bq,),
            in_specs=[
                pl.BlockSpec((bq, 128), lambda i, *_: (i, 0)),
                pl.BlockSpec((frames, 128), lambda i, *_: (0, 1)),
                pl.BlockSpec((frames, 128), lambda i, *_: (0, 2)),
            ],
            out_specs=[
                pl.BlockSpec((bq, 128), lambda i, *_: (i, 0)),
                pl.BlockSpec((8, bq), lambda i, *_: (0, i)),
            ],
            scratch_shapes=[
                pltpu.VMEM((frames, 128), BF),
                pltpu.VMEM((frames, 128), BF),
                pltpu.VMEM((128, frames), BF),
                pltpu.VMEM((128, frames), BF),
                pltpu.VMEM((8, 128), F32),
                pltpu.SMEM((2,), F32),
            ],
        ),
        out_shape=[
            jax.ShapeDtypeStruct((frames, 128), BF),
            jax.ShapeDtypeStruct((8, frames), F32),
        ],
        compiler_params=pltpu.CompilerParams(vmem_limit_bytes=VMEM_LIMIT),
        cost_estimate=attention_cost(frames, 2),
        name="attend_forward",
    )(length, qkv, qkv, qkv)


def turn_back(grad, cos, sin):
    lane = lanes_of(grad.shape[0])
    turned = jnp.where((lane & 63) < 32, pltpu.roll(grad, 96, 1), pltpu.roll(grad, 32, 1))
    return grad * cos - turned * sin


def three(column, lane, at):
    high = column.astype(BF).astype(F32)
    rest = column - high
    mid = rest.astype(BF).astype(F32)
    low = rest - mid
    return jnp.where(lane == at, -high, jnp.where(lane == at + 1, -mid, jnp.where(lane == at + 2, -low, 0.0)))


def flash_backward_kernel(
    len_ref, q_ref, k_ref, v_ref, o_ref, do_ref, lse_ref, cos_ref, sin_ref,
    g_ref, ka, kb, va, vb, dkt, dvt, *, bq, bk,
):
    step = pl.program_id(0)
    steps = pl.num_programs(0)
    length = len_ref[0]
    frames = k_ref.shape[0]

    @pl.when(step == 0)
    def _():
        def build(j, carry):
            rows = pl.ds(pl.multiple_of(j * bk, bk), bk)
            lane = lanes_of(bk)
            pos = j * bk + lax.broadcasted_iota(jnp.int32, (bk, 128), 0)
            bias = jnp.where(pos < length, 0.0, MASKED)
            keys = k_ref[rows, :].astype(F32)
            vals = v_ref[rows, :].astype(F32)
            ones_a = jnp.where(lane < 67, 1.0, 0.0)
            ones_b = jnp.where(lane < 3, 1.0, 0.0)
            ka[rows, :] = jnp.where(lane < 64, keys, jnp.where(lane == 67, bias, ones_a)).astype(BF)
            kb[rows, :] = jnp.where(lane >= 64, keys, jnp.where(lane == 3, bias, ones_b)).astype(BF)
            va[rows, :] = jnp.where(lane < 64, vals, ones_a).astype(BF)
            vb[rows, :] = jnp.where(lane >= 64, vals, ones_b).astype(BF)
            return carry

        lax.fori_loop(0, frames // bk, build, 0)
        dkt[...] = jnp.zeros_like(dkt)
        dvt[...] = jnp.zeros_like(dvt)

    @pl.when(step * bq >= length)
    def _():
        rows = pl.ds(pl.multiple_of(step * bq, bq), bq)
        g_ref[rows, 0:128] = jnp.zeros((bq, 128), BF)

    @pl.when(step * bq < length)
    def _():
        lane = lanes_of(bq)
        queries = q_ref[...].astype(F32)
        dout = do_ref[...].astype(F32)
        product = dout * o_ref[...].astype(F32)
        delta_a, delta_b = head_sums(product, lane)
        lse = lse_ref[...].T
        qa = jnp.where(lane < 64, queries, jnp.where(lane == 67, 1.0, three(lse[:, 0:1], lane, 64))).astype(BF)
        qb = jnp.where(lane >= 64, queries, jnp.where(lane == 3, 1.0, three(lse[:, 1:2], lane, 0))).astype(BF)
        da = jnp.where(lane < 64, dout, three(delta_a, lane, 64)).astype(BF)
        db = jnp.where(lane >= 64, dout, three(delta_b, lane, 0)).astype(BF)
        qt = queries.T.astype(BF)
        dt = dout.T.astype(BF)

        def body(j, carry):
            rows = pl.ds(pl.multiple_of(j * bk, bk), bk)
            out = []
            for head, (qh, dh, kh, vh, dq) in enumerate(((qa, da, ka, va, carry[0]), (qb, db, kb, vb, carry[1]))):
                part = slice(head * 64, head * 64 + 64)
                keys = kh[rows, :]
                probs = jnp.exp2(nt(qh, keys))
                grad = (probs * nt(dh, vh[rows, :])).astype(BF)
                dvt[part, rows] += nn(dt, probs.astype(BF))[part]
                dkt[part, rows] += nn(qt, grad)[part]
                out.append(dq + nn(grad, keys))
            return tuple(out)

        start = jnp.zeros((bq, 128), F32)
        live = (length + bk - 1) // bk
        dq_a, dq_b = lax.fori_loop(0, live, body, (start, start))
        dq = jnp.where(lane < 64, dq_a, dq_b) * 0.125
        rows = pl.ds(pl.multiple_of(step * bq, bq), bq)
        g_ref[rows, 0:128] = turn_back(dq, cos_ref[rows, :], sin_ref[rows, :]).astype(BF)

    @pl.when(step == steps - 1)
    def _():
        def finish(j, carry):
            rows = pl.ds(pl.multiple_of(j * bk, bk), bk)
            dk = dkt[:, rows].T * LN2
            g_ref[rows, 128:256] = turn_back(dk, cos_ref[rows, :], sin_ref[rows, :]).astype(BF)
            g_ref[rows, 256:384] = dvt[:, rows].T.astype(BF)
            return carry

        lax.fori_loop(0, frames // bk, finish, 0)


def flash_backward(length, qkv, out, dout, lse, cos, sin, bq, bk):
    frames = qkv.shape[0]
    part = pl.BlockSpec((bq, 128), lambda i, *_: (i, 0))
    whole = pl.BlockSpec((frames, 128), lambda i, *_: (0, 0))
    return pl.pallas_call(
        functools.partial(flash_backward_kernel, bq=bq, bk=bk),
        grid_spec=pltpu.PrefetchScalarGridSpec(
            num_scalar_prefetch=1,
            grid=(frames // bq,),
            in_specs=[
                part,
                pl.BlockSpec((frames, 128), lambda i, *_: (0, 1)),
                pl.BlockSpec((frames, 128), lambda i, *_: (0, 2)),
                part,
                part,
                pl.BlockSpec((8, bq), lambda i, *_: (0, i)),
                whole,
                whole,
            ],
            out_specs=pl.BlockSpec((frames, 384), lambda i, *_: (0, 0)),
            scratch_shapes=[pltpu.VMEM((frames, 128), BF)] * 4
            + [pltpu.VMEM((128, frames), F32)] * 2,
        ),
        out_shape=jax.ShapeDtypeStruct((frames, 384), BF),
        compiler_params=pltpu.CompilerParams(vmem_limit_bytes=VMEM_LIMIT),
        cost_estimate=attention_cost(frames, 5),
        name="attend_backward",
    )(length, qkv, qkv, qkv, out, dout, lse, cos, sin)


def project_kernel(x_ref, w_ref, cos_ref, sin_ref, out_ref):
    projected = nn(x_ref[...], w_ref[...])
    groups = out_ref.shape[0]
    rows = x_ref.shape[0]
    lane = lanes_of(rows)
    cos, sin = cos_ref[...], sin_ref[...]
    for part in range(3):
        for group in range(groups):
            at = (part * groups + group) * 128
            piece = projected[:, at : at + 128]
            if part < 2:
                turned = jnp.where(
                    (lane & 63) < 32, pltpu.roll(piece, 96, 1), pltpu.roll(piece, 32, 1)
                )
                piece = piece * cos + turned * sin
            if part == 0:
                piece = piece * (0.125 * LOG2E)
            out_ref[group, :, part * 128 : part * 128 + 128] = piece.astype(BF)


def project_heads(x, weight, cos, sin, groups, block=256):
    rows, width = x.shape
    return pl.pallas_call(
        project_kernel,
        grid=(rows // block,),
        in_specs=[
            pl.BlockSpec((block, width), lambda i: (i, 0)),
            pl.BlockSpec(weight.shape, lambda i: (0, 0)),
            pl.BlockSpec((block, 128), lambda i: (i, 0)),
            pl.BlockSpec((block, 128), lambda i: (i, 0)),
        ],
        out_specs=pl.BlockSpec((groups, block, 384), lambda i: (0, i, 0)),
        out_shape=jax.ShapeDtypeStruct((groups, rows, 384), BF),
        compiler_params=pltpu.CompilerParams(vmem_limit_bytes=VMEM_LIMIT),
        cost_estimate=pl.CostEstimate(
            flops=2 * rows * weight.size, bytes_accessed=2 * weight.size, transcendentals=0
        ),
        name="project_heads",
    )(x, weight, cos, sin)


def layer_norm(stream):
    centre = stream - jnp.mean(stream, axis=-1, keepdims=True)
    spread = jnp.mean(centre * centre, axis=-1, keepdims=True)
    inverse = lax.rsqrt(spread + EPS)
    return (centre * inverse, inverse)


def norm_back(grad_normed, normed, inverse):
    first_mean = jnp.mean(grad_normed, axis=-1, keepdims=True)
    second_mean = jnp.mean(grad_normed * normed, axis=-1, keepdims=True)
    return inverse * (grad_normed - first_mean - normed * second_mean)


def rotary_tables(positions):
    half_dim = HEAD_DIM // 2
    channel = jnp.arange(half_dim, dtype=jnp.float32)
    inverse = jnp.power(10000.0, -2.0 * channel / HEAD_DIM)
    angles = positions.astype(jnp.float32)[:, None] * inverse[None, :]
    angles = jnp.concatenate([angles, angles], axis=1)
    return (jnp.cos(angles), jnp.sin(angles))


def rotate_heads(field, cosine_table, sine_table):
    half_dim = field.shape[-1] // 2
    turned = jnp.concatenate([-field[..., half_dim:], field[..., :half_dim]], axis=-1)
    return field * cosine_table + turned * sine_table


def smooth_gelu(values):
    return jax.nn.gelu(values, approximate=True)


def cross(left, right):
    return lax.dot_general(
        left, right, (((0,), (0,)), ((), ())), preferred_element_type=jnp.float32
    )


def back_product(left, right):
    return lax.dot_general(
        left, right, (((1,), (1,)), ((), ())), preferred_element_type=jnp.float32
    )


def block_terms(query_block, dout_block, lse_block, delta_block, key_block, value_block, key_live):
    scores = jnp.einsum(
        "bqhd,bkhd->bhqk", query_block, key_block, preferred_element_type=jnp.float32
    )
    lse_heads = jnp.transpose(lse_block, (0, 2, 1))[..., None]
    probs = jnp.where(key_live[:, None, None, :], jnp.exp(scores - lse_heads), 0.0)
    grad_probs = jnp.einsum(
        "bqhd,bkhd->bhqk", dout_block, value_block, preferred_element_type=jnp.float32
    )
    delta_heads = jnp.transpose(delta_block, (0, 2, 1))[..., None]
    dscore = (probs * (grad_probs - delta_heads)).astype(jnp.bfloat16)
    return (probs.astype(jnp.bfloat16), dscore)


def exchange(pieces, axis="seq"):
    count = pieces.shape[0]
    me = lax.axis_index(axis)
    out = pieces
    for step in [count // 2] + [s for s in range(1, count) if s != count // 2]:
        piece = lax.dynamic_index_in_dim(pieces, lax.rem(me + step, count), 0, keepdims=False)
        got = lax.ppermute(piece, axis, [(i, (i + step) % count) for i in range(count)])
        out = lax.dynamic_update_index_in_dim(out, got, lax.rem(me + count - step, count), 0)
    return out


def gather_weight(weight):
    parts = lax.axis_size("batch")
    if weight.shape[0] % parts:
        return lax.all_gather(weight, "seq", axis=0, tiled=True)
    rows = weight.shape[0] // parts
    mine = lax.dynamic_slice_in_dim(weight, lax.axis_index("batch") * rows, rows, 0)
    return lax.all_gather(mine, ("seq", "batch"), axis=0, tiled=True)


def sum_weight(grad):
    parts = lax.axis_size("batch") * lax.axis_size("seq")
    low = grad.astype(jnp.bfloat16)
    if grad.shape[0] % parts:
        shard = lax.psum_scatter(low, "seq", scatter_dimension=0, tiled=True)
        return lax.psum(shard, "batch").astype(jnp.float32)
    shard = lax.psum_scatter(low, ("seq", "batch"), scatter_dimension=0, tiled=True)
    return lax.all_gather(shard, "batch", axis=0, tiled=True).astype(jnp.float32)


def paired_tables(positions):
    cos, sin = rotary_tables(positions)
    half = HEAD_DIM // 2
    signed = jnp.concatenate([-sin[:, :half], sin[:, half:]], axis=1)
    return jnp.tile(cos, (1, 2)), jnp.tile(signed, (1, 2))


def on_device(
    layer_input,
    skip_input,
    time_embed,
    lengths,
    cond_drop,
    cotangent,
    skip_weight,
    adaln_weight,
    adaln_bias,
    qkv_weight,
    out_weight,
    up_weight,
    down_weight,
):
    utt_count, frame_span, model_width = layer_input.shape
    head_count = model_width // HEAD_DIM
    row_count = utt_count * frame_span
    seq_here = lax.axis_index("seq")
    seq_count = lax.axis_size("seq")
    frame_count = frame_span * seq_count
    by_heads = head_count == 2 * seq_count and frame_count % 1024 == 0
    local_pos = seq_here * frame_span + jnp.arange(frame_span, dtype=jnp.int32)
    local_live = local_pos[None, :] < lengths[:, None]
    valid_mask = local_live.astype(jnp.float32)
    drop = cond_drop.astype(jnp.float32)
    dropped = drop[:, None] * valid_mask
    frames_live = jnp.minimum(lengths, frame_count).astype(jnp.float32)
    kept_total, drop_total = lax.psum(
        (jnp.sum((1.0 - drop) * frames_live), jnp.sum(drop * frames_live)), "batch"
    )
    kept_total = jnp.maximum(kept_total, 1.0)
    drop_total = jnp.maximum(drop_total, 1.0)
    every_count = kept_total + drop_total
    loss_weight = (valid_mask - dropped) * (every_count / (2.0 * kept_total)) + dropped * (
        every_count / (2.0 * drop_total)
    )
    silu_time = jax.nn.silu(time_embed.astype(jnp.float32)).astype(jnp.bfloat16)
    row_span = adaln_weight.shape[0]
    silu_mine = lax.dynamic_slice_in_dim(silu_time, seq_here * row_span, row_span, 1)
    mod_part = jnp.dot(silu_mine, adaln_weight, preferred_element_type=jnp.float32)
    bias_span = adaln_bias.shape[0]
    bias_here = lax.dynamic_update_slice_in_dim(
        jnp.zeros((mod_part.shape[1],), jnp.float32),
        adaln_bias.astype(jnp.float32),
        seq_here * bias_span,
        0,
    )
    modulation = lax.psum(mod_part + bias_here, "seq").reshape(utt_count, 6, model_width)
    skip_full = gather_weight(skip_weight)
    qkv_full = gather_weight(qkv_weight)
    out_full = gather_weight(out_weight)
    up_full = gather_weight(up_weight)
    down_full = gather_weight(down_weight)
    joined = jnp.concatenate([layer_input, skip_input], axis=-1).reshape(row_count, 2 * model_width)
    residual_in = jnp.dot(joined, skip_full, preferred_element_type=jnp.float32).reshape(
        utt_count, frame_span, model_width
    )
    shift_attn = modulation[:, 0][:, None, :]
    scale_attn = modulation[:, 1][:, None, :]
    gate_attn = modulation[:, 2][:, None, :]
    shift_ffn = modulation[:, 3][:, None, :]
    scale_ffn = modulation[:, 4][:, None, :]
    gate_ffn = modulation[:, 5][:, None, :]
    hat_attn, inv_attn = layer_norm(residual_in)
    normed_attn = (
        (hat_attn * (1.0 + scale_attn) + shift_attn)
        .astype(jnp.bfloat16)
        .reshape(row_count, model_width)
    )
    if by_heads:
        cos_all, sin_all = paired_tables(jnp.arange(frame_count, dtype=jnp.int32))
        cos_here = lax.dynamic_slice_in_dim(cos_all, seq_here * frame_span, frame_span, 0)
        sin_here = lax.dynamic_slice_in_dim(sin_all, seq_here * frame_span, frame_span, 0)
        packed, attended_mine, lse_mine, attended_parts = [], [], [], []
        for utt in range(utt_count):
            sent = project_heads(
                normed_attn[utt * frame_span : (utt + 1) * frame_span],
                qkv_full,
                cos_here,
                sin_here,
                seq_count,
            )
            packed.append(exchange(sent).reshape(frame_count, 384))
        for utt in range(utt_count):
            heads_out, lse = flash_forward(lengths[utt : utt + 1], packed[utt], 1024, 1024)
            attended_mine.append(heads_out)
            lse_mine.append(lse)
            back = exchange(heads_out.reshape(seq_count, frame_span, 128))
            attended_parts.append(back.transpose(1, 0, 2).reshape(frame_span, model_width))
        attended_low = jnp.concatenate(attended_parts, axis=0)
    else:
        projected = jnp.dot(normed_attn, qkv_full, preferred_element_type=jnp.float32).reshape(
            utt_count, frame_span, 3, head_count, HEAD_DIM
        )
        cosine_table, sine_table = rotary_tables(local_pos)
        cosine_table = cosine_table[None, :, None, :]
        sine_table = sine_table[None, :, None, :]
        queries = (rotate_heads(projected[:, :, 0], cosine_table, sine_table) * 0.125).astype(
            jnp.bfloat16
        )
        keys_rot = rotate_heads(projected[:, :, 1], cosine_table, sine_table).astype(jnp.bfloat16)
        values = projected[:, :, 2].astype(jnp.bfloat16)
        start_top = jnp.full((utt_count, head_count, frame_span), MASKED, jnp.float32)
        top_score = start_top
        key_piece = lax.all_gather(keys_rot, "seq", axis=1, tiled=True)
        value_piece = lax.all_gather(values, "seq", axis=1, tiled=True)
        piece_len = key_piece.shape[1]
        piece_live = jnp.arange(piece_len, dtype=jnp.int32)[None, :] < lengths[:, None]
        scores = jnp.einsum("bqhd,bkhd->bhqk", queries, key_piece, preferred_element_type=jnp.float32)
        scores = jnp.where(piece_live[:, None, None, :], scores, MASKED)
        new_top = jnp.maximum(top_score, jnp.max(scores, axis=-1))
        expo = jnp.where(piece_live[:, None, None, :], jnp.exp(scores - new_top[..., None]), 0.0)
        denom = jnp.sum(expo, axis=-1)
        partial_out = jnp.einsum(
            "bhqk,bkhd->bqhd",
            expo.astype(jnp.bfloat16),
            value_piece,
            preferred_element_type=jnp.float32,
        )
        accum = partial_out
        accum, top_score, denom = (accum, new_top, denom)
        attended_full = accum / jnp.transpose(denom, (0, 2, 1))[..., None]
        lse_rows = jnp.transpose(top_score + jnp.log(denom), (0, 2, 1))
        attended_low = attended_full.astype(jnp.bfloat16).reshape(row_count, model_width)
    branch_attn = jnp.dot(attended_low, out_full, preferred_element_type=jnp.float32).reshape(
        utt_count, frame_span, model_width
    )
    residual_mid = residual_in + gate_attn * branch_attn
    hat_ffn, inv_ffn = layer_norm(residual_mid)
    normed_ffn = (
        (hat_ffn * (1.0 + scale_ffn) + shift_ffn)
        .astype(jnp.bfloat16)
        .reshape(row_count, model_width)
    )
    hidden_pre = jnp.dot(normed_ffn, up_full, preferred_element_type=jnp.float32)
    hidden_act = smooth_gelu(hidden_pre).astype(jnp.bfloat16)
    branch_ffn = jnp.dot(hidden_act, down_full, preferred_element_type=jnp.float32).reshape(
        utt_count, frame_span, model_width
    )
    layer_output = (residual_mid + gate_ffn * branch_ffn).astype(jnp.bfloat16)
    qkv_back, out_back, up_back, down_back = qkv_full, out_full, up_full, down_full
    skip_back = skip_full
    upstream = cotangent.astype(jnp.float32) * loss_weight[..., None]
    grad_branch_ffn = (upstream * gate_ffn).astype(jnp.bfloat16).reshape(row_count, model_width)
    grad_gate_ffn = jnp.sum(upstream * branch_ffn, axis=1)
    grad_down = cross(hidden_act, grad_branch_ffn)
    grad_hidden_act = back_product(grad_branch_ffn, down_back)
    gelu_value, gelu_pull = jax.vjp(smooth_gelu, hidden_pre)
    grad_hidden_pre = gelu_pull(grad_hidden_act)[0].astype(jnp.bfloat16)
    grad_up = cross(normed_ffn, grad_hidden_pre)
    grad_normed_ffn = back_product(grad_hidden_pre, up_back).reshape(
        utt_count, frame_span, model_width
    )
    grad_shift_ffn = jnp.sum(grad_normed_ffn, axis=1)
    grad_scale_ffn = jnp.sum(grad_normed_ffn * hat_ffn, axis=1)
    grad_mid = upstream + norm_back(grad_normed_ffn * (1.0 + scale_ffn), hat_ffn, inv_ffn)
    grad_branch_attn = (grad_mid * gate_attn).astype(jnp.bfloat16).reshape(row_count, model_width)
    grad_gate_attn = jnp.sum(grad_mid * branch_attn, axis=1)
    grad_out = cross(attended_low, grad_branch_attn)
    grad_attended_flat = back_product(grad_branch_attn, out_back).astype(jnp.bfloat16)
    if by_heads:
        grad_parts = []
        for utt in range(utt_count):
            sent = grad_attended_flat[utt * frame_span : (utt + 1) * frame_span]
            sent = sent.reshape(frame_span, seq_count, 128).transpose(1, 0, 2)
            dout = exchange(sent).reshape(frame_count, 128)
            grads = flash_backward(
                lengths[utt : utt + 1],
                packed[utt],
                attended_mine[utt],
                dout,
                lse_mine[utt],
                cos_all,
                sin_all,
                1024,
                1024,
            )
            back = exchange(grads.reshape(seq_count, frame_span, 384))
            back = back.reshape(seq_count, frame_span, 3, 128).transpose(1, 2, 0, 3)
            grad_parts.append(back.reshape(frame_span, 3 * model_width))
        grad_projected = jnp.concatenate(grad_parts, axis=0)
    else:
        grad_attended = grad_attended_flat.reshape(
            utt_count, frame_span, head_count, HEAD_DIM
        )
        delta_rows = jnp.sum(grad_attended.astype(jnp.float32) * attended_full, axis=-1)
        lse_all, delta_all = (
            lax.all_gather(lse_rows, "seq", axis=1, tiled=True),
            lax.all_gather(delta_rows, "seq", axis=1, tiled=True),
        )
        key_piece = lax.all_gather(keys_rot, "seq", axis=1, tiled=True)
        value_piece = lax.all_gather(values, "seq", axis=1, tiled=True)
        piece_len = key_piece.shape[1]
        piece_live = jnp.arange(piece_len, dtype=jnp.int32)[None, :] < lengths[:, None]
        probs_low, dscore = block_terms(
            queries, grad_attended, lse_rows, delta_rows, key_piece, value_piece, piece_live
        )
        grad_queries = jnp.einsum(
            "bhqk,bkhd->bqhd", dscore, key_piece, preferred_element_type=jnp.float32
        )
        query_piece = lax.all_gather(queries, "seq", axis=1, tiled=True)
        dout_piece = lax.all_gather(grad_attended, "seq", axis=1, tiled=True)
        probs_low, dscore = block_terms(
            query_piece, dout_piece, lse_all, delta_all, keys_rot, values, local_live
        )
        grad_k = jnp.einsum("bhqk,bqhd->bkhd", dscore, query_piece, preferred_element_type=jnp.float32)
        grad_v = jnp.einsum(
            "bhqk,bqhd->bkhd", probs_low, dout_piece, preferred_element_type=jnp.float32
        )
        grad_q_pre = rotate_heads(grad_queries * 0.125, cosine_table, -sine_table)
        grad_k_pre = rotate_heads(grad_k, cosine_table, -sine_table)
        grad_projected = (
            jnp.stack([grad_q_pre, grad_k_pre, grad_v], axis=2)
            .reshape(row_count, 3 * model_width)
            .astype(jnp.bfloat16)
        )
    grad_qkv = cross(normed_attn, grad_projected)
    grad_normed_attn = back_product(grad_projected, qkv_back).reshape(
        utt_count, frame_span, model_width
    )
    grad_shift_attn = jnp.sum(grad_normed_attn, axis=1)
    grad_scale_attn = jnp.sum(grad_normed_attn * hat_attn, axis=1)
    grad_stream = grad_mid + norm_back(grad_normed_attn * (1.0 + scale_attn), hat_attn, inv_attn)
    grad_stream_low = grad_stream.astype(jnp.bfloat16).reshape(row_count, model_width)
    grad_skip_w = cross(joined, grad_stream_low)
    grad_joined = back_product(grad_stream_low, skip_back)
    grad_input = (
        grad_joined[:, :model_width]
        .reshape(utt_count, frame_span, model_width)
        .astype(jnp.bfloat16)
    )
    grad_skip = (
        grad_joined[:, model_width:]
        .reshape(utt_count, frame_span, model_width)
        .astype(jnp.bfloat16)
    )
    grad_modulation = jnp.stack(
        [
            grad_shift_attn,
            grad_scale_attn,
            grad_gate_attn,
            grad_shift_ffn,
            grad_scale_ffn,
            grad_gate_ffn,
        ],
        axis=1,
    ).reshape(utt_count, 6 * model_width)
    mod_total = lax.psum(grad_modulation, "seq")
    mod_every, silu_every = (
        lax.all_gather(mod_total.astype(jnp.bfloat16), "batch", axis=0, tiled=True).astype(
            mod_total.dtype
        ),
        lax.all_gather(
            silu_time.astype(jnp.float32).astype(jnp.bfloat16), "batch", axis=0, tiled=True
        ).astype(jnp.float32),
    )
    silu_rows = lax.dynamic_slice_in_dim(silu_every, seq_here * row_span, row_span, 1)
    adaln_rows = jnp.dot(silu_rows.T, mod_every, precision=lax.Precision.HIGHEST)
    bias_rows = lax.dynamic_slice_in_dim(
        jnp.sum(mod_every, axis=0), seq_here * bias_span, bias_span, 0
    )
    summed = [sum_weight(grad) for grad in (grad_skip_w, grad_qkv, grad_out, grad_up, grad_down)]
    results = (summed[0], adaln_rows, bias_rows, summed[1], summed[2], summed[3], summed[4])
    return (
        layer_output,
        grad_input,
        grad_skip,
        results[0],
        results[1],
        results[2],
        results[3],
        results[4],
        results[5],
        results[6],
    )


def solution(mesh):
    placed = (
        P("batch", "seq", None),
        P("batch", "seq", None),
        P("batch", None),
        P("batch"),
        P("batch"),
        P("batch", "seq", None),
        P("seq", None),
        P("seq", None),
        P("seq"),
        P("seq", None),
        P("seq", None),
        P("seq", None),
        P("seq", None),
    )
    return jax.shard_map(
        on_device,
        mesh=mesh,
        in_specs=placed,
        out_specs=(
            P("batch", "seq", None),
            P("batch", "seq", None),
            P("batch", "seq", None),
            P("seq", None),
            P("seq", None),
            P("seq"),
            P("seq", None),
            P("seq", None),
            P("seq", None),
            P("seq", None),
        ),
        check_vma=False,
    )
```

```python
import functools
import jax
import jax.numpy as jnp
from jax import lax
from jax.sharding import PartitionSpec as P
from jax.experimental import pallas as pl
from jax.experimental.pallas import tpu as pltpu
HEAD_DIM = 64
EPS = 1e-06
LOG2E = 1.4426950408889634
LN2 = 0.6931471805599453
MASKED = -1e30
RANGE = 100.0
BF = jnp.bfloat16
F32 = jnp.float32
VMEM_LIMIT = 60 * 2**20


def nt(left, right):
    return lax.dot_general(left, right, (((1,), (1,)), ((), ())), preferred_element_type=F32)


def nn(left, right):
    return lax.dot_general(left, right, (((1,), (0,)), ((), ())), preferred_element_type=F32)


def head_sums(product, lane):
    first = jnp.sum(jnp.where(lane < 64, product, 0.0), axis=1, keepdims=True)
    second = jnp.sum(jnp.where(lane >= 64, product, 0.0), axis=1, keepdims=True)
    return (first, second)


def lanes_of(rows):
    return lax.broadcasted_iota(jnp.int32, (rows, 128), 1)


def flash_forward_kernel(len_ref, q_ref, k_ref, v_ref, o_ref, lse_ref, ka, kb, vta, vtb, mean_ref, top_ref, *, bq, bk):
    step = pl.program_id(0)
    length = len_ref[0]
    frames = k_ref.shape[0]

    @pl.when(step == 0)
    def _():
        def build(j, carry):
            rows = pl.ds(pl.multiple_of(j * bk, bk), bk)
            lane = lanes_of(bk)
            pos = j * bk + lax.broadcasted_iota(jnp.int32, (bk, 128), 0)
            bias = jnp.where(pos < length, 0.0, MASKED)
            keys = k_ref[rows, :].astype(F32)
            ka[rows, :] = jnp.where(lane < 64, keys, jnp.where(lane == 64, bias, jnp.where(lane == 65, 1.0, 0.0))).astype(BF)
            kb[rows, :] = jnp.where(lane >= 64, keys, jnp.where(lane == 0, bias, jnp.where(lane == 1, 1.0, 0.0))).astype(BF)
            vals = v_ref[rows, :].astype(F32)
            vta[:, rows] = jnp.where(lane < 64, vals, 1.0).T.astype(BF)
            vtb[:, rows] = jnp.where(lane >= 64, vals, 1.0).T.astype(BF)
            keys = jnp.where(pos < length, keys, 0.0)
            norm_a, norm_b = head_sums(keys * keys, lane)
            total, top_a, top_b = carry
            return (
                total + jnp.sum(keys, axis=0, keepdims=True),
                jnp.maximum(top_a, jnp.max(norm_a)),
                jnp.maximum(top_b, jnp.max(norm_b)),
            )

        total, top_a, top_b = lax.fori_loop(
            0, frames // bk, build, (jnp.zeros((1, 128), F32), jnp.float32(0.0), jnp.float32(0.0))
        )
        mean_ref[0:1, :] = total / length.astype(F32)
        top_ref[0] = top_a
        top_ref[1] = top_b

    lane = lanes_of(bq)
    queries = q_ref[...].astype(F32)
    bounds = [
        jnp.sqrt(jnp.max(norm) * top_ref[head]) * 1.001
        for head, norm in enumerate(head_sums(queries * queries, lane))
    ]
    shifts = [jnp.maximum(bound - RANGE, 0.0) for bound in bounds]
    lows = [jnp.min(low) for low in head_sums(queries * mean_ref[0:1, :], lane)]
    tame = jnp.logical_and(lows[0] - shifts[0] >= -RANGE, lows[1] - shifts[1] >= -RANGE)
    qa = jnp.where(lane < 64, queries, jnp.where(lane == 64, 1.0, jnp.where(lane == 65, -shifts[0], 0.0)))
    qb = jnp.where(lane >= 64, queries, jnp.where(lane == 0, 1.0, jnp.where(lane == 1, -shifts[1], 0.0)))
    qa, qb = qa.astype(BF), qb.astype(BF)

    def body(j, carry):
        rows = pl.ds(pl.multiple_of(j * bk, bk), bk)
        out = []
        scores = [nt(ka[rows, :], qa), nt(kb[rows, :], qb)]
        for score, vt, (top, acc) in zip(scores, (vta, vtb), carry):
            new = jnp.maximum(top, jnp.max(score, axis=0, keepdims=True))
            probs = jnp.exp2(score - new).astype(BF)
            acc = acc * jnp.exp2(top - new) + nn(vt[:, rows], probs)
            out.append((new, acc))
        return tuple(out)

    live = (length + bk - 1) // bk

    def finish(shift_a, acc_a, shift_b, acc_b):
        sum_a, sum_b = acc_a[64:65], acc_b[0:1]
        both = jnp.concatenate([acc_a[:64] / sum_a, acc_b[64:] / sum_b], axis=0)
        o_ref[...] = both.T.astype(BF)
        lse_ref[...] = jnp.concatenate(
            [shift_a + jnp.log2(sum_a), shift_b + jnp.log2(sum_b), jnp.zeros((6, bq), F32)], axis=0
        )

    @pl.when(tame)
    def _():
        def plain(j, carry):
            rows = pl.ds(pl.multiple_of(j * bk, bk), bk)
            out = []
            for keys, query, vt, acc in ((ka, qa, vta, carry[0]), (kb, qb, vtb, carry[1])):
                probs = jnp.exp2(nt(keys[rows, :], query)).astype(BF)
                out.append(acc + nn(vt[:, rows], probs))
            return tuple(out)

        start = jnp.zeros((128, bq), F32)
        acc_a, acc_b = lax.fori_loop(0, live, plain, (start, start))
        rounded = [shift.astype(BF).astype(F32) for shift in shifts]
        finish(rounded[0], acc_a, rounded[1], acc_b)

    @pl.when(jnp.logical_not(tame))
    def _():
        start = (jnp.full((1, bq), MASKED, F32), jnp.zeros((128, bq), F32))
        (top_a, acc_a), (top_b, acc_b) = lax.fori_loop(0, live, body, (start, start))
        rounded = [shift.astype(BF).astype(F32) for shift in shifts]
        finish(rounded[0] + top_a, acc_a, rounded[1] + top_b, acc_b)


def attention_cost(frames, products):
    return pl.CostEstimate(
        flops=2 * products * 2 * frames * frames * 128,
        bytes_accessed=frames * 128 * 2 * 8,
        transcendentals=2 * frames * frames,
    )


def flash_forward(length, qkv, bq, bk):
    frames = qkv.shape[0]
    return pl.pallas_call(
        functools.partial(flash_forward_kernel, bq=bq, bk=bk),
        grid_spec=pltpu.PrefetchScalarGridSpec(
            num_scalar_prefetch=1,
            grid=(frames // bq,),
            in_specs=[
                pl.BlockSpec((bq, 128), lambda i, *_: (i, 0)),
                pl.BlockSpec((frames, 128), lambda i, *_: (0, 1)),
                pl.BlockSpec((frames, 128), lambda i, *_: (0, 2)),
            ],
            out_specs=[
                pl.BlockSpec((bq, 128), lambda i, *_: (i, 0)),
                pl.BlockSpec((8, bq), lambda i, *_: (0, i)),
            ],
            scratch_shapes=[
                pltpu.VMEM((frames, 128), BF),
                pltpu.VMEM((frames, 128), BF),
                pltpu.VMEM((128, frames), BF),
                pltpu.VMEM((128, frames), BF),
                pltpu.VMEM((8, 128), F32),
                pltpu.SMEM((2,), F32),
            ],
        ),
        out_shape=[
            jax.ShapeDtypeStruct((frames, 128), BF),
            jax.ShapeDtypeStruct((8, frames), F32),
        ],
        compiler_params=pltpu.CompilerParams(vmem_limit_bytes=VMEM_LIMIT),
        cost_estimate=attention_cost(frames, 2),
        name="attend_forward",
    )(length, qkv, qkv, qkv)


def turn_back(grad, cos, sin):
    lane = lanes_of(grad.shape[0])
    turned = jnp.where((lane & 63) < 32, pltpu.roll(grad, 96, 1), pltpu.roll(grad, 32, 1))
    return grad * cos - turned * sin


def three(column, lane, at):
    high = column.astype(BF).astype(F32)
    rest = column - high
    mid = rest.astype(BF).astype(F32)
    low = rest - mid
    return jnp.where(lane == at, -high, jnp.where(lane == at + 1, -mid, jnp.where(lane == at + 2, -low, 0.0)))


def flash_backward_kernel(
    len_ref, q_ref, k_ref, v_ref, o_ref, do_ref, lse_ref, cos_ref, sin_ref,
    g_ref, ka, kb, va, vb, dkt, dvt, *, bq, bk,
):
    step = pl.program_id(0)
    steps = pl.num_programs(0)
    length = len_ref[0]
    frames = k_ref.shape[0]

    @pl.when(step == 0)
    def _():
        def build(j, carry):
            rows = pl.ds(pl.multiple_of(j * bk, bk), bk)
            lane = lanes_of(bk)
            pos = j * bk + lax.broadcasted_iota(jnp.int32, (bk, 128), 0)
            bias = jnp.where(pos < length, 0.0, MASKED)
            keys = k_ref[rows, :].astype(F32)
            vals = v_ref[rows, :].astype(F32)
            ones_a = jnp.where(lane < 67, 1.0, 0.0)
            ones_b = jnp.where(lane < 3, 1.0, 0.0)
            ka[rows, :] = jnp.where(lane < 64, keys, jnp.where(lane == 67, bias, ones_a)).astype(BF)
            kb[rows, :] = jnp.where(lane >= 64, keys, jnp.where(lane == 3, bias, ones_b)).astype(BF)
            va[rows, :] = jnp.where(lane < 64, vals, ones_a).astype(BF)
            vb[rows, :] = jnp.where(lane >= 64, vals, ones_b).astype(BF)
            return carry

        lax.fori_loop(0, frames // bk, build, 0)
        dkt[...] = jnp.zeros_like(dkt)
        dvt[...] = jnp.zeros_like(dvt)

    @pl.when(step * bq >= length)
    def _():
        rows = pl.ds(pl.multiple_of(step * bq, bq), bq)
        g_ref[rows, 0:128] = jnp.zeros((bq, 128), BF)

    @pl.when(step * bq < length)
    def _():
        lane = lanes_of(bq)
        queries = q_ref[...].astype(F32)
        dout = do_ref[...].astype(F32)
        product = dout * o_ref[...].astype(F32)
        delta_a, delta_b = head_sums(product, lane)
        lse = lse_ref[...].T
        qa = jnp.where(lane < 64, queries, jnp.where(lane == 67, 1.0, three(lse[:, 0:1], lane, 64))).astype(BF)
        qb = jnp.where(lane >= 64, queries, jnp.where(lane == 3, 1.0, three(lse[:, 1:2], lane, 0))).astype(BF)
        da = jnp.where(lane < 64, dout, three(delta_a, lane, 64)).astype(BF)
        db = jnp.where(lane >= 64, dout, three(delta_b, lane, 0)).astype(BF)
        qt = queries.T.astype(BF)
        dt = dout.T.astype(BF)

        def body(j, carry):
            rows = pl.ds(pl.multiple_of(j * bk, bk), bk)
            out = []
            for head, (qh, dh, kh, vh, dq) in enumerate(((qa, da, ka, va, carry[0]), (qb, db, kb, vb, carry[1]))):
                part = slice(head * 64, head * 64 + 64)
                keys = kh[rows, :]
                probs = jnp.exp2(nt(qh, keys))
                grad = (probs * nt(dh, vh[rows, :])).astype(BF)
                dvt[part, rows] += nn(dt, probs.astype(BF))[part]
                dkt[part, rows] += nn(qt, grad)[part]
                out.append(dq + nn(grad, keys))
            return tuple(out)

        start = jnp.zeros((bq, 128), F32)
        live = (length + bk - 1) // bk
        dq_a, dq_b = lax.fori_loop(0, live, body, (start, start))
        dq = jnp.where(lane < 64, dq_a, dq_b) * 0.125
        rows = pl.ds(pl.multiple_of(step * bq, bq), bq)
        g_ref[rows, 0:128] = turn_back(dq, cos_ref[rows, :], sin_ref[rows, :]).astype(BF)

    @pl.when(step == steps - 1)
    def _():
        def finish(j, carry):
            rows = pl.ds(pl.multiple_of(j * bk, bk), bk)
            dk = dkt[:, rows].T * LN2
            g_ref[rows, 128:256] = turn_back(dk, cos_ref[rows, :], sin_ref[rows, :]).astype(BF)
            g_ref[rows, 256:384] = dvt[:, rows].T.astype(BF)
            return carry

        lax.fori_loop(0, frames // bk, finish, 0)


def flash_backward(length, qkv, out, dout, lse, cos, sin, bq, bk):
    frames = qkv.shape[0]
    part = pl.BlockSpec((bq, 128), lambda i, *_: (i, 0))
    whole = pl.BlockSpec((frames, 128), lambda i, *_: (0, 0))
    return pl.pallas_call(
        functools.partial(flash_backward_kernel, bq=bq, bk=bk),
        grid_spec=pltpu.PrefetchScalarGridSpec(
            num_scalar_prefetch=1,
            grid=(frames // bq,),
            in_specs=[
                part,
                pl.BlockSpec((frames, 128), lambda i, *_: (0, 1)),
                pl.BlockSpec((frames, 128), lambda i, *_: (0, 2)),
                part,
                part,
                pl.BlockSpec((8, bq), lambda i, *_: (0, i)),
                whole,
                whole,
            ],
            out_specs=pl.BlockSpec((frames, 384), lambda i, *_: (0, 0)),
            scratch_shapes=[pltpu.VMEM((frames, 128), BF)] * 4
            + [pltpu.VMEM((128, frames), F32)] * 2,
        ),
        out_shape=jax.ShapeDtypeStruct((frames, 384), BF),
        compiler_params=pltpu.CompilerParams(vmem_limit_bytes=VMEM_LIMIT),
        cost_estimate=attention_cost(frames, 5),
        name="attend_backward",
    )(length, qkv, qkv, qkv, out, dout, lse, cos, sin)


def layer_norm(stream):
    centre = stream - jnp.mean(stream, axis=-1, keepdims=True)
    spread = jnp.mean(centre * centre, axis=-1, keepdims=True)
    inverse = lax.rsqrt(spread + EPS)
    return (centre * inverse, inverse)


def norm_back(grad_normed, normed, inverse):
    first_mean = jnp.mean(grad_normed, axis=-1, keepdims=True)
    second_mean = jnp.mean(grad_normed * normed, axis=-1, keepdims=True)
    return inverse * (grad_normed - first_mean - normed * second_mean)


def tn(left, right):
    return lax.dot_general(left, right, (((0,), (0,)), ((), ())), preferred_element_type=F32)


GELU_C = 0.7978845608028654
GELU_A = 0.044715


def gelu_and_slope(z):
    square = z * z
    turn = jnp.tanh(GELU_C * z * (1.0 + GELU_A * square))
    half = 0.5 * (1.0 + turn)
    slope = half + 0.5 * z * (1.0 - turn * turn) * (GELU_C * (1.0 + 3.0 * GELU_A * square))
    return z * half, slope


def row_blocks(rows):
    block = min(rows, 256)
    return [(at, slice(at, at + block)) for at in range(0, rows, block)]


def ffn_forward_kernel(
    att_ref, outw_ref, res_ref, mod_ref, cot_ref, weight_ref, up_ref, down_ref,
    branch_ref, act_ref, slope_ref, gb_ref, out_ref, gate_ref, normed, acc,
):
    step = pl.program_id(0)
    rows = att_ref.shape[0]
    span = rows // mod_ref.shape[0]

    @pl.when(step == 0)
    def _():
        for at, part in row_blocks(span):
            for utt in range(mod_ref.shape[0]):
                here = slice(utt * span + part.start, utt * span + part.stop)
                mod = mod_ref[utt]
                branch = nn(att_ref[here, :], outw_ref[...])
                branch_ref[here, :] = branch
                hat, _ = layer_norm(res_ref[here, :] + mod[2:3] * branch)
                normed[here, :] = (hat * (1.0 + mod[4:5]) + mod[3:4]).astype(BF)
        acc[...] = jnp.zeros_like(acc)

    for _, part in row_blocks(rows):
        act, slope = gelu_and_slope(nn(normed[part, :], up_ref[...]))
        act = act.astype(BF)
        act_ref[part, :] = act
        slope_ref[part, :] = slope.astype(BF)
        acc[part, :] += nn(act, down_ref[...])

    @pl.when(step == pl.num_programs(0) - 1)
    def _():
        for utt in range(mod_ref.shape[0]):
            mod = mod_ref[utt]
            total = jnp.zeros((1, acc.shape[1]), F32)
            for _, part in row_blocks(span):
                here = slice(utt * span + part.start, utt * span + part.stop)
                branch = acc[here, :]
                mid = res_ref[here, :] + mod[2:3] * branch_ref[here, :]
                out_ref[here, :] = (mid + mod[5:6] * branch).astype(BF)
                upstream = cot_ref[here, :].astype(F32) * weight_ref[here, :]
                gb_ref[here, :] = (upstream * mod[5:6]).astype(BF)
                total += jnp.sum(upstream * branch, axis=0, keepdims=True)
            gate_ref[utt : utt + 1, :] = total


def ffn_backward_kernel(
    att_ref, outw_ref, res_ref, branch_ref, mod_ref, cot_ref, weight_ref, gb_ref,
    act_ref, slope_ref, up_ref, down_ref,
    gup_ref, gdown_ref, gmid_ref, gatt_ref, gout_ref, sums_ref, normed, acc, gba,
):
    step = pl.program_id(0)
    rows = att_ref.shape[0]
    utts = mod_ref.shape[0]
    span = rows // utts

    def hat_of(here, mod):
        return layer_norm(res_ref[here, :] + mod[2:3] * branch_ref[here, :])

    @pl.when(step == 0)
    def _():
        for utt in range(utts):
            mod = mod_ref[utt]
            for _, part in row_blocks(span):
                here = slice(utt * span + part.start, utt * span + part.stop)
                hat, _ = hat_of(here, mod)
                normed[here, :] = (hat * (1.0 + mod[4:5]) + mod[3:4]).astype(BF)
        acc[...] = jnp.zeros_like(acc)

    pieces = []
    for _, part in row_blocks(rows):
        grad = nt(gb_ref[part, :], down_ref[...]) * slope_ref[part, :].astype(F32)
        grad = grad.astype(BF)
        acc[part, :] += nt(grad, up_ref[...])
        pieces.append(grad)
    gdown_ref[...] = tn(act_ref[...], gb_ref[...]).astype(BF)
    gup_ref[...] = tn(normed[...], jnp.concatenate(pieces, axis=0)).astype(BF)

    @pl.when(step == pl.num_programs(0) - 1)
    def _():
        for utt in range(utts):
            mod = mod_ref[utt]
            width = acc.shape[1]
            shift = jnp.zeros((1, width), F32)
            scale = jnp.zeros((1, width), F32)
            gate = jnp.zeros((1, width), F32)
            for _, part in row_blocks(span):
                here = slice(utt * span + part.start, utt * span + part.stop)
                hat, inverse = hat_of(here, mod)
                grad = acc[here, :]
                shift += jnp.sum(grad, axis=0, keepdims=True)
                scale += jnp.sum(grad * hat, axis=0, keepdims=True)
                upstream = cot_ref[here, :].astype(F32) * weight_ref[here, :]
                mid = upstream + norm_back(grad * (1.0 + mod[4:5]), hat, inverse)
                gmid_ref[here, :] = mid
                gate += jnp.sum(mid * branch_ref[here, :], axis=0, keepdims=True)
                low = (mid * mod[2:3]).astype(BF)
                gba[here, :] = low
                gatt_ref[here, :] = nt(low, outw_ref[...]).astype(BF)
            sums_ref[utt, 0:1, :] = shift
            sums_ref[utt, 1:2, :] = scale
            sums_ref[utt, 2:3, :] = gate
        gout_ref[...] = tn(att_ref[...], gba[...]).astype(BF)


def whole_spec(shape):
    zeros = (0,) * len(shape)
    return pl.BlockSpec(shape, lambda i: zeros, pipeline_mode=pl.Buffered(1))


def ffn_forward(att, outw, res, mods, cot, weight, up, down, chunk=512):
    rows, width = res.shape
    hidden = up.shape[1]
    whole = [whole_spec(a.shape) for a in (att, outw, res, mods, cot, weight)]
    col = pl.BlockSpec((rows, chunk), lambda i: (0, i))
    utts = mods.shape[0]
    return pl.pallas_call(
        ffn_forward_kernel,
        grid=(hidden // chunk,),
        in_specs=whole
        + [
            pl.BlockSpec((width, chunk), lambda i: (0, i)),
            pl.BlockSpec((chunk, width), lambda i: (i, 0)),
        ],
        out_specs=[
            whole_spec((rows, width)),
            col,
            col,
            whole_spec((rows, width)),
            whole_spec((rows, width)),
            whole_spec((utts, width)),
        ],
        out_shape=[
            jax.ShapeDtypeStruct((rows, width), F32),
            jax.ShapeDtypeStruct((rows, hidden), BF),
            jax.ShapeDtypeStruct((rows, hidden), BF),
            jax.ShapeDtypeStruct((rows, width), BF),
            jax.ShapeDtypeStruct((rows, width), BF),
            jax.ShapeDtypeStruct((utts, width), F32),
        ],
        scratch_shapes=[pltpu.VMEM((rows, width), BF), pltpu.VMEM((rows, width), F32)],
        compiler_params=pltpu.CompilerParams(vmem_limit_bytes=VMEM_LIMIT),
        cost_estimate=pl.CostEstimate(
            flops=2 * rows * width * (width + 2 * hidden),
            bytes_accessed=60 * 2**20,
            transcendentals=rows * hidden,
        ),
        name="ffn_forward",
    )(att, outw, res, mods, cot, weight, up, down)


def ffn_backward(att, outw, res, branch, mods, cot, weight, gb, act, slope, up, down, chunk=512):
    rows, width = res.shape
    hidden = up.shape[1]
    utts = mods.shape[0]
    whole = [whole_spec(a.shape) for a in (att, outw, res, branch, mods, cot, weight, gb)]
    col = pl.BlockSpec((rows, chunk), lambda i: (0, i))
    upspec = pl.BlockSpec((width, chunk), lambda i: (0, i))
    downspec = pl.BlockSpec((chunk, width), lambda i: (i, 0))
    return pl.pallas_call(
        ffn_backward_kernel,
        grid=(hidden // chunk,),
        in_specs=whole + [col, col, upspec, downspec],
        out_specs=[
            upspec,
            downspec,
            whole_spec((rows, width)),
            whole_spec((rows, width)),
            whole_spec((width, width)),
            whole_spec((utts, 8, width)),
        ],
        out_shape=[
            jax.ShapeDtypeStruct((width, hidden), BF),
            jax.ShapeDtypeStruct((hidden, width), BF),
            jax.ShapeDtypeStruct((rows, width), F32),
            jax.ShapeDtypeStruct((rows, width), BF),
            jax.ShapeDtypeStruct((width, width), BF),
            jax.ShapeDtypeStruct((utts, 8, width), F32),
        ],
        scratch_shapes=[
            pltpu.VMEM((rows, width), BF),
            pltpu.VMEM((rows, width), F32),
            pltpu.VMEM((rows, width), BF),
        ],
        compiler_params=pltpu.CompilerParams(vmem_limit_bytes=VMEM_LIMIT),
        cost_estimate=pl.CostEstimate(
            flops=2 * rows * width * (2 * width + 4 * hidden),
            bytes_accessed=90 * 2**20,
            transcendentals=0,
        ),
        name="ffn_backward",
    )(att, outw, res, branch, mods, cot, weight, gb, act, slope, up, down)


def project_kernel(x_ref, w_ref, cos_ref, sin_ref, out_ref):
    projected = nn(x_ref[...], w_ref[...])
    groups = out_ref.shape[0]
    rows = x_ref.shape[0]
    lane = lanes_of(rows)
    cos, sin = cos_ref[...], sin_ref[...]
    for part in range(3):
        for group in range(groups):
            at = (part * groups + group) * 128
            piece = projected[:, at : at + 128]
            if part < 2:
                turned = jnp.where(
                    (lane & 63) < 32, pltpu.roll(piece, 96, 1), pltpu.roll(piece, 32, 1)
                )
                piece = piece * cos + turned * sin
            if part == 0:
                piece = piece * (0.125 * LOG2E)
            out_ref[group, :, part * 128 : part * 128 + 128] = piece.astype(BF)


def project_heads(x, weight, cos, sin, groups, block=256):
    rows, width = x.shape
    return pl.pallas_call(
        project_kernel,
        grid=(rows // block,),
        in_specs=[
            pl.BlockSpec((block, width), lambda i: (i, 0)),
            pl.BlockSpec(weight.shape, lambda i: (0, 0)),
            pl.BlockSpec((block, 128), lambda i: (i, 0)),
            pl.BlockSpec((block, 128), lambda i: (i, 0)),
        ],
        out_specs=pl.BlockSpec((groups, block, 384), lambda i: (0, i, 0)),
        out_shape=jax.ShapeDtypeStruct((groups, rows, 384), BF),
        compiler_params=pltpu.CompilerParams(vmem_limit_bytes=VMEM_LIMIT),
        cost_estimate=pl.CostEstimate(
            flops=2 * rows * weight.size, bytes_accessed=2 * weight.size, transcendentals=0
        ),
        name="project_heads",
    )(x, weight, cos, sin)


def rotary_tables(positions):
    half_dim = HEAD_DIM // 2
    channel = jnp.arange(half_dim, dtype=jnp.float32)
    inverse = jnp.power(10000.0, -2.0 * channel / HEAD_DIM)
    angles = positions.astype(jnp.float32)[:, None] * inverse[None, :]
    angles = jnp.concatenate([angles, angles], axis=1)
    return (jnp.cos(angles), jnp.sin(angles))


def rotate_heads(field, cosine_table, sine_table):
    half_dim = field.shape[-1] // 2
    turned = jnp.concatenate([-field[..., half_dim:], field[..., :half_dim]], axis=-1)
    return field * cosine_table + turned * sine_table


def smooth_gelu(values):
    return jax.nn.gelu(values, approximate=True)


def cross(left, right):
    return lax.dot_general(
        left, right, (((0,), (0,)), ((), ())), preferred_element_type=jnp.float32
    )


def back_product(left, right):
    return lax.dot_general(
        left, right, (((1,), (1,)), ((), ())), preferred_element_type=jnp.float32
    )


def block_terms(query_block, dout_block, lse_block, delta_block, key_block, value_block, key_live):
    scores = jnp.einsum(
        "bqhd,bkhd->bhqk", query_block, key_block, preferred_element_type=jnp.float32
    )
    lse_heads = jnp.transpose(lse_block, (0, 2, 1))[..., None]
    probs = jnp.where(key_live[:, None, None, :], jnp.exp(scores - lse_heads), 0.0)
    grad_probs = jnp.einsum(
        "bqhd,bkhd->bhqk", dout_block, value_block, preferred_element_type=jnp.float32
    )
    delta_heads = jnp.transpose(delta_block, (0, 2, 1))[..., None]
    dscore = (probs * (grad_probs - delta_heads)).astype(jnp.bfloat16)
    return (probs.astype(jnp.bfloat16), dscore)


def exchange(pieces):
    count, rows, width = pieces.shape
    me = lax.axis_index("seq")
    outer, inner = me // 2, me % 2
    nest = pieces.reshape(count // 2, 2, rows, width)
    far = lax.dynamic_index_in_dim(nest, 1 - inner, 1, keepdims=False)
    got = lax.ppermute(far, "seq", [(i, i ^ 1) for i in range(count)])
    nest = lax.dynamic_update_index_in_dim(nest, got, 1 - inner, 1)
    out = nest
    for flip in (3, 2, 1):
        there = jnp.bitwise_xor(outer, flip)
        piece = lax.dynamic_index_in_dim(nest, there, 0, keepdims=False)
        got = lax.ppermute(piece, "seq", [(i, i ^ (2 * flip)) for i in range(count)])
        out = lax.dynamic_update_index_in_dim(out, got, there, 0)
    return out.reshape(count, rows, width)


def batch_swap(value, flip):
    return lax.ppermute(value, "batch", [(i, i ^ flip) for i in range(4)])


def batch_bits():
    here = lax.axis_index("batch")
    return here // 2, here % 2


def in_quarters(rows):
    return lax.axis_size("batch") == 4 and rows % 4 == 0


def join_pair(bit, mine, other, axis):
    first = jnp.where(bit == 0, mine, other)
    second = jnp.where(bit == 0, other, mine)
    return jnp.stack([first, second], axis=axis)


def gather_weight(weight):
    rows, width = weight.shape
    if not in_quarters(rows):
        return lax.all_gather(weight, "seq", axis=0, tiled=True)
    span = rows // 4
    high, low = batch_bits()
    mine = lax.dynamic_slice_in_dim(weight, lax.axis_index("batch") * span, span, 0)
    held = lax.all_gather(mine, "seq", axis=0, tiled=False)
    held = join_pair(high, held, batch_swap(held, 2), 1)
    held = join_pair(low, held, batch_swap(held, 1), 2)
    return held.reshape(-1, width)


def pair_sum(value, bit, flip, axis):
    send = lax.dynamic_index_in_dim(value, 1 - bit, axis, keepdims=False)
    keep = lax.dynamic_index_in_dim(value, bit, axis, keepdims=False)
    got = batch_swap(send, flip)
    return (keep.astype(jnp.float32) + got.astype(jnp.float32)).astype(jnp.bfloat16)


def sum_weight(grad):
    rows, width = grad.shape
    low_grad = grad.astype(jnp.bfloat16)
    seq_count = lax.axis_size("seq")
    if not in_quarters(rows // seq_count):
        shard = lax.psum_scatter(low_grad, "seq", scatter_dimension=0, tiled=True)
        return lax.psum(shard, "batch").astype(jnp.float32)
    high, low = batch_bits()
    held = low_grad.reshape(seq_count, 2, 2, rows // (4 * seq_count), width)
    held = pair_sum(held, low, 1, 2)
    held = pair_sum(held, high, 2, 1)
    shard = lax.psum_scatter(held, "seq", scatter_dimension=0, tiled=False)
    return lax.all_gather(shard, "batch", axis=0, tiled=True).astype(jnp.float32)


def paired_tables(positions):
    cos, sin = rotary_tables(positions)
    half = HEAD_DIM // 2
    signed = jnp.concatenate([-sin[:, :half], sin[:, half:]], axis=1)
    return jnp.tile(cos, (1, 2)), jnp.tile(signed, (1, 2))


def on_device(
    layer_input,
    skip_input,
    time_embed,
    lengths,
    cond_drop,
    cotangent,
    skip_weight,
    adaln_weight,
    adaln_bias,
    qkv_weight,
    out_weight,
    up_weight,
    down_weight,
):
    utt_count, frame_span, model_width = layer_input.shape
    head_count = model_width // HEAD_DIM
    row_count = utt_count * frame_span
    seq_here = lax.axis_index("seq")
    seq_count = lax.axis_size("seq")
    frame_count = frame_span * seq_count
    by_heads = head_count == 2 * seq_count and frame_count % 1024 == 0
    local_pos = seq_here * frame_span + jnp.arange(frame_span, dtype=jnp.int32)
    local_live = local_pos[None, :] < lengths[:, None]
    valid_mask = local_live.astype(jnp.float32)
    drop = cond_drop.astype(jnp.float32)
    dropped = drop[:, None] * valid_mask
    frames_live = jnp.minimum(lengths, frame_count).astype(jnp.float32)
    kept_total, drop_total = lax.psum(
        (jnp.sum((1.0 - drop) * frames_live), jnp.sum(drop * frames_live)), "batch"
    )
    kept_total = jnp.maximum(kept_total, 1.0)
    drop_total = jnp.maximum(drop_total, 1.0)
    every_count = kept_total + drop_total
    loss_weight = (valid_mask - dropped) * (every_count / (2.0 * kept_total)) + dropped * (
        every_count / (2.0 * drop_total)
    )
    silu_time = jax.nn.silu(time_embed.astype(jnp.float32)).astype(jnp.bfloat16)
    row_span = adaln_weight.shape[0]
    silu_mine = lax.dynamic_slice_in_dim(silu_time, seq_here * row_span, row_span, 1)
    mod_part = jnp.dot(silu_mine, adaln_weight, preferred_element_type=jnp.float32)
    bias_span = adaln_bias.shape[0]
    bias_here = lax.dynamic_update_slice_in_dim(
        jnp.zeros((mod_part.shape[1],), jnp.float32),
        adaln_bias.astype(jnp.float32),
        seq_here * bias_span,
        0,
    )
    modulation = lax.psum(mod_part + bias_here, "seq").reshape(utt_count, 6, model_width)
    skip_full = gather_weight(skip_weight)
    qkv_full = gather_weight(qkv_weight)
    out_full = gather_weight(out_weight)
    up_full = gather_weight(up_weight)
    down_full = gather_weight(down_weight)
    joined = jnp.concatenate([layer_input, skip_input], axis=-1).reshape(row_count, 2 * model_width)
    residual_in = jnp.dot(joined, skip_full, preferred_element_type=jnp.float32).reshape(
        utt_count, frame_span, model_width
    )
    shift_attn = modulation[:, 0][:, None, :]
    scale_attn = modulation[:, 1][:, None, :]
    hat_attn, inv_attn = layer_norm(residual_in)
    normed_attn = (
        (hat_attn * (1.0 + scale_attn) + shift_attn)
        .astype(jnp.bfloat16)
        .reshape(row_count, model_width)
    )
    if by_heads:
        cos_all, sin_all = paired_tables(jnp.arange(frame_count, dtype=jnp.int32))
        cos_here = lax.dynamic_slice_in_dim(cos_all, seq_here * frame_span, frame_span, 0)
        sin_here = lax.dynamic_slice_in_dim(sin_all, seq_here * frame_span, frame_span, 0)
        packed, attended_mine, lse_mine, attended_parts = [], [], [], []
        for utt in range(utt_count):
            sent = project_heads(
                normed_attn[utt * frame_span : (utt + 1) * frame_span],
                qkv_full,
                cos_here,
                sin_here,
                seq_count,
            )
            packed.append(exchange(sent).reshape(frame_count, 384))
        for utt in range(utt_count):
            heads_out, lse = flash_forward(lengths[utt : utt + 1], packed[utt], 1024, 1024)
            attended_mine.append(heads_out)
            lse_mine.append(lse)
            back = exchange(heads_out.reshape(seq_count, frame_span, 128))
            attended_parts.append(back.transpose(1, 0, 2).reshape(frame_span, model_width))
        attended_low = jnp.concatenate(attended_parts, axis=0)
    else:
        projected = jnp.dot(normed_attn, qkv_full, preferred_element_type=jnp.float32).reshape(
            utt_count, frame_span, 3, head_count, HEAD_DIM
        )
        cosine_table, sine_table = rotary_tables(local_pos)
        cosine_table = cosine_table[None, :, None, :]
        sine_table = sine_table[None, :, None, :]
        queries = (rotate_heads(projected[:, :, 0], cosine_table, sine_table) * 0.125).astype(
            jnp.bfloat16
        )
        keys_rot = rotate_heads(projected[:, :, 1], cosine_table, sine_table).astype(jnp.bfloat16)
        values = projected[:, :, 2].astype(jnp.bfloat16)
        start_top = jnp.full((utt_count, head_count, frame_span), MASKED, jnp.float32)
        top_score = start_top
        key_piece = lax.all_gather(keys_rot, "seq", axis=1, tiled=True)
        value_piece = lax.all_gather(values, "seq", axis=1, tiled=True)
        piece_len = key_piece.shape[1]
        piece_live = jnp.arange(piece_len, dtype=jnp.int32)[None, :] < lengths[:, None]
        scores = jnp.einsum("bqhd,bkhd->bhqk", queries, key_piece, preferred_element_type=jnp.float32)
        scores = jnp.where(piece_live[:, None, None, :], scores, MASKED)
        new_top = jnp.maximum(top_score, jnp.max(scores, axis=-1))
        expo = jnp.where(piece_live[:, None, None, :], jnp.exp(scores - new_top[..., None]), 0.0)
        denom = jnp.sum(expo, axis=-1)
        partial_out = jnp.einsum(
            "bhqk,bkhd->bqhd",
            expo.astype(jnp.bfloat16),
            value_piece,
            preferred_element_type=jnp.float32,
        )
        accum = partial_out
        accum, top_score, denom = (accum, new_top, denom)
        attended_full = accum / jnp.transpose(denom, (0, 2, 1))[..., None]
        lse_rows = jnp.transpose(top_score + jnp.log(denom), (0, 2, 1))
        attended_low = attended_full.astype(jnp.bfloat16).reshape(row_count, model_width)
    residual_rows = residual_in.reshape(row_count, model_width)
    cot_rows = cotangent.reshape(row_count, model_width)
    weight_rows = loss_weight.reshape(row_count, 1)
    branch_attn, hidden_act, hidden_slope, grad_branch_ffn, layer_output, grad_gate_ffn = ffn_forward(
        attended_low,
        out_full,
        residual_rows,
        modulation,
        cot_rows,
        weight_rows,
        up_full,
        down_full,
    )
    layer_output = layer_output.reshape(utt_count, frame_span, model_width)
    grad_up, grad_down, grad_mid, grad_attended_flat, grad_out, ffn_sums = ffn_backward(
        attended_low,
        out_full,
        residual_rows,
        branch_attn,
        modulation,
        cot_rows,
        weight_rows,
        grad_branch_ffn,
        hidden_act,
        hidden_slope,
        up_full,
        down_full,
    )
    grad_mid = grad_mid.reshape(utt_count, frame_span, model_width)
    grad_shift_ffn, grad_scale_ffn, grad_gate_attn = ffn_sums[:, 0], ffn_sums[:, 1], ffn_sums[:, 2]
    qkv_back, skip_back = qkv_full, skip_full
    if by_heads:
        grad_parts = []
        for utt in range(utt_count):
            sent = grad_attended_flat[utt * frame_span : (utt + 1) * frame_span]
            sent = sent.reshape(frame_span, seq_count, 128).transpose(1, 0, 2)
            dout = exchange(sent).reshape(frame_count, 128)
            grads = flash_backward(
                lengths[utt : utt + 1],
                packed[utt],
                attended_mine[utt],
                dout,
                lse_mine[utt],
                cos_all,
                sin_all,
                1024,
                1024,
            )
            back = exchange(grads.reshape(seq_count, frame_span, 384))
            back = back.reshape(seq_count, frame_span, 3, 128).transpose(1, 2, 0, 3)
            grad_parts.append(back.reshape(frame_span, 3 * model_width))
        grad_projected = jnp.concatenate(grad_parts, axis=0)
    else:
        grad_attended = grad_attended_flat.reshape(
            utt_count, frame_span, head_count, HEAD_DIM
        )
        delta_rows = jnp.sum(grad_attended.astype(jnp.float32) * attended_full, axis=-1)
        lse_all, delta_all = (
            lax.all_gather(lse_rows, "seq", axis=1, tiled=True),
            lax.all_gather(delta_rows, "seq", axis=1, tiled=True),
        )
        key_piece = lax.all_gather(keys_rot, "seq", axis=1, tiled=True)
        value_piece = lax.all_gather(values, "seq", axis=1, tiled=True)
        piece_len = key_piece.shape[1]
        piece_live = jnp.arange(piece_len, dtype=jnp.int32)[None, :] < lengths[:, None]
        probs_low, dscore = block_terms(
            queries, grad_attended, lse_rows, delta_rows, key_piece, value_piece, piece_live
        )
        grad_queries = jnp.einsum(
            "bhqk,bkhd->bqhd", dscore, key_piece, preferred_element_type=jnp.float32
        )
        query_piece = lax.all_gather(queries, "seq", axis=1, tiled=True)
        dout_piece = lax.all_gather(grad_attended, "seq", axis=1, tiled=True)
        probs_low, dscore = block_terms(
            query_piece, dout_piece, lse_all, delta_all, keys_rot, values, local_live
        )
        grad_k = jnp.einsum("bhqk,bqhd->bkhd", dscore, query_piece, preferred_element_type=jnp.float32)
        grad_v = jnp.einsum(
            "bhqk,bqhd->bkhd", probs_low, dout_piece, preferred_element_type=jnp.float32
        )
        grad_q_pre = rotate_heads(grad_queries * 0.125, cosine_table, -sine_table)
        grad_k_pre = rotate_heads(grad_k, cosine_table, -sine_table)
        grad_projected = (
            jnp.stack([grad_q_pre, grad_k_pre, grad_v], axis=2)
            .reshape(row_count, 3 * model_width)
            .astype(jnp.bfloat16)
        )
    grad_qkv = cross(normed_attn, grad_projected)
    grad_normed_attn = back_product(grad_projected, qkv_back).reshape(
        utt_count, frame_span, model_width
    )
    grad_shift_attn = jnp.sum(grad_normed_attn, axis=1)
    grad_scale_attn = jnp.sum(grad_normed_attn * hat_attn, axis=1)
    grad_stream = grad_mid + norm_back(grad_normed_attn * (1.0 + scale_attn), hat_attn, inv_attn)
    grad_stream_low = grad_stream.astype(jnp.bfloat16).reshape(row_count, model_width)
    grad_skip_w = cross(joined, grad_stream_low)
    grad_joined = back_product(grad_stream_low, skip_back)
    grad_input = (
        grad_joined[:, :model_width]
        .reshape(utt_count, frame_span, model_width)
        .astype(jnp.bfloat16)
    )
    grad_skip = (
        grad_joined[:, model_width:]
        .reshape(utt_count, frame_span, model_width)
        .astype(jnp.bfloat16)
    )
    grad_modulation = jnp.stack(
        [
            grad_shift_attn,
            grad_scale_attn,
            grad_gate_attn,
            grad_shift_ffn,
            grad_scale_ffn,
            grad_gate_ffn,
        ],
        axis=1,
    ).reshape(utt_count, 6 * model_width)
    mod_total = lax.psum(grad_modulation, "seq")
    mod_every, silu_every = (
        lax.all_gather(mod_total.astype(jnp.bfloat16), "batch", axis=0, tiled=True).astype(
            mod_total.dtype
        ),
        lax.all_gather(
            silu_time.astype(jnp.float32).astype(jnp.bfloat16), "batch", axis=0, tiled=True
        ).astype(jnp.float32),
    )
    silu_rows = lax.dynamic_slice_in_dim(silu_every, seq_here * row_span, row_span, 1)
    adaln_rows = jnp.dot(silu_rows.T, mod_every, precision=lax.Precision.HIGHEST)
    bias_rows = lax.dynamic_slice_in_dim(
        jnp.sum(mod_every, axis=0), seq_here * bias_span, bias_span, 0
    )
    summed = [sum_weight(grad) for grad in (grad_skip_w, grad_qkv, grad_out, grad_up, grad_down)]
    results = (summed[0], adaln_rows, bias_rows, summed[1], summed[2], summed[3], summed[4])
    return (
        layer_output,
        grad_input,
        grad_skip,
        results[0],
        results[1],
        results[2],
        results[3],
        results[4],
        results[5],
        results[6],
    )


def solution(mesh):
    placed = (
        P("batch", "seq", None),
        P("batch", "seq", None),
        P("batch", None),
        P("batch"),
        P("batch"),
        P("batch", "seq", None),
        P("seq", None),
        P("seq", None),
        P("seq"),
        P("seq", None),
        P("seq", None),
        P("seq", None),
        P("seq", None),
    )
    return jax.shard_map(
        on_device,
        mesh=mesh,
        in_specs=placed,
        out_specs=(
            P("batch", "seq", None),
            P("batch", "seq", None),
            P("batch", "seq", None),
            P("seq", None),
            P("seq", None),
            P("seq"),
            P("seq", None),
            P("seq", None),
            P("seq", None),
            P("seq", None),
        ),
        check_vma=False,
    )
```

```python
import functools
import jax
import jax.numpy as jnp
from jax import lax
from jax.sharding import Mesh, PartitionSpec as P
from jax.experimental import pallas as pl
from jax.experimental.pallas import tpu as pltpu
HEAD_DIM = 64
EPS = 1e-06
LOG2E = 1.4426950408889634
LN2 = 0.6931471805599453
MASKED = -1e30
RANGE = 100.0
BF = jnp.bfloat16
F32 = jnp.float32
VMEM_LIMIT = 60 * 2**20


def nt(left, right):
    return lax.dot_general(left, right, (((1,), (1,)), ((), ())), preferred_element_type=F32)


def nn(left, right):
    return lax.dot_general(left, right, (((1,), (0,)), ((), ())), preferred_element_type=F32)


def head_sums(product, lane):
    first = jnp.sum(jnp.where(lane < 64, product, 0.0), axis=1, keepdims=True)
    second = jnp.sum(jnp.where(lane >= 64, product, 0.0), axis=1, keepdims=True)
    return (first, second)


def lanes_of(rows):
    return lax.broadcasted_iota(jnp.int32, (rows, 128), 1)


def flash_forward_kernel(len_ref, q_ref, k_ref, v_ref, o_ref, lse_ref, ka, kb, vta, vtb, mean_ref, top_ref, *, bq, bk):
    step = pl.program_id(0)
    length = len_ref[0]
    frames = k_ref.shape[0]

    @pl.when(step == 0)
    def _():
        def build(j, carry):
            rows = pl.ds(pl.multiple_of(j * bk, bk), bk)
            lane = lanes_of(bk)
            pos = j * bk + lax.broadcasted_iota(jnp.int32, (bk, 128), 0)
            bias = jnp.where(pos < length, 0.0, MASKED)
            keys = k_ref[rows, :].astype(F32)
            ka[rows, :] = jnp.where(lane < 64, keys, jnp.where(lane == 64, bias, jnp.where(lane == 65, 1.0, 0.0))).astype(BF)
            kb[rows, :] = jnp.where(lane >= 64, keys, jnp.where(lane == 0, bias, jnp.where(lane == 1, 1.0, 0.0))).astype(BF)
            vals = v_ref[rows, :].astype(F32)
            vta[:, rows] = jnp.where(lane < 64, vals, 1.0).T.astype(BF)
            vtb[:, rows] = jnp.where(lane >= 64, vals, 1.0).T.astype(BF)
            keys = jnp.where(pos < length, keys, 0.0)
            norm_a, norm_b = head_sums(keys * keys, lane)
            total, top_a, top_b = carry
            return (
                total + jnp.sum(keys, axis=0, keepdims=True),
                jnp.maximum(top_a, jnp.max(norm_a)),
                jnp.maximum(top_b, jnp.max(norm_b)),
            )

        total, top_a, top_b = lax.fori_loop(
            0, frames // bk, build, (jnp.zeros((1, 128), F32), jnp.float32(0.0), jnp.float32(0.0))
        )
        mean_ref[0:1, :] = total / length.astype(F32)
        top_ref[0] = top_a
        top_ref[1] = top_b

    lane = lanes_of(bq)
    queries = q_ref[...].astype(F32)
    bounds = [
        jnp.sqrt(jnp.max(norm) * top_ref[head]) * 1.001
        for head, norm in enumerate(head_sums(queries * queries, lane))
    ]
    shifts = [jnp.maximum(bound - RANGE, 0.0) for bound in bounds]
    lows = [jnp.min(low) for low in head_sums(queries * mean_ref[0:1, :], lane)]
    tame = jnp.logical_and(lows[0] - shifts[0] >= -RANGE, lows[1] - shifts[1] >= -RANGE)
    qa = jnp.where(lane < 64, queries, jnp.where(lane == 64, 1.0, jnp.where(lane == 65, -shifts[0], 0.0)))
    qb = jnp.where(lane >= 64, queries, jnp.where(lane == 0, 1.0, jnp.where(lane == 1, -shifts[1], 0.0)))
    qa, qb = qa.astype(BF), qb.astype(BF)

    def body(j, carry):
        rows = pl.ds(pl.multiple_of(j * bk, bk), bk)
        out = []
        scores = [nt(ka[rows, :], qa), nt(kb[rows, :], qb)]
        for score, vt, (top, acc) in zip(scores, (vta, vtb), carry):
            new = jnp.maximum(top, jnp.max(score, axis=0, keepdims=True))
            probs = jnp.exp2(score - new).astype(BF)
            acc = acc * jnp.exp2(top - new) + nn(vt[:, rows], probs)
            out.append((new, acc))
        return tuple(out)

    live = (length + bk - 1) // bk

    def finish(shift_a, acc_a, shift_b, acc_b):
        sum_a, sum_b = acc_a[64:65], acc_b[0:1]
        both = jnp.concatenate([acc_a[:64] / sum_a, acc_b[64:] / sum_b], axis=0)
        o_ref[...] = both.T.astype(BF)
        lse_ref[...] = jnp.concatenate(
            [shift_a + jnp.log2(sum_a), shift_b + jnp.log2(sum_b), jnp.zeros((6, bq), F32)], axis=0
        )

    @pl.when(tame)
    def _():
        def plain(j, carry):
            rows = pl.ds(pl.multiple_of(j * bk, bk), bk)
            out = []
            for keys, query, vt, acc in ((ka, qa, vta, carry[0]), (kb, qb, vtb, carry[1])):
                probs = jnp.exp2(nt(keys[rows, :], query)).astype(BF)
                out.append(acc + nn(vt[:, rows], probs))
            return tuple(out)

        start = jnp.zeros((128, bq), F32)
        acc_a, acc_b = lax.fori_loop(0, live, plain, (start, start))
        rounded = [shift.astype(BF).astype(F32) for shift in shifts]
        finish(rounded[0], acc_a, rounded[1], acc_b)

    @pl.when(jnp.logical_not(tame))
    def _():
        start = (jnp.full((1, bq), MASKED, F32), jnp.zeros((128, bq), F32))
        (top_a, acc_a), (top_b, acc_b) = lax.fori_loop(0, live, body, (start, start))
        rounded = [shift.astype(BF).astype(F32) for shift in shifts]
        finish(rounded[0] + top_a, acc_a, rounded[1] + top_b, acc_b)


def attention_cost(frames, products):
    return pl.CostEstimate(
        flops=2 * products * 2 * frames * frames * 128,
        bytes_accessed=frames * 128 * 2 * 8,
        transcendentals=2 * frames * frames,
    )


def flash_forward(length, qkv, bq, bk):
    frames = qkv.shape[0]
    return pl.pallas_call(
        functools.partial(flash_forward_kernel, bq=bq, bk=bk),
        grid_spec=pltpu.PrefetchScalarGridSpec(
            num_scalar_prefetch=1,
            grid=(frames // bq,),
            in_specs=[
                pl.BlockSpec((bq, 128), lambda i, *_: (i, 0)),
                pl.BlockSpec((frames, 128), lambda i, *_: (0, 1)),
                pl.BlockSpec((frames, 128), lambda i, *_: (0, 2)),
            ],
            out_specs=[
                pl.BlockSpec((bq, 128), lambda i, *_: (i, 0)),
                pl.BlockSpec((8, bq), lambda i, *_: (0, i)),
            ],
            scratch_shapes=[
                pltpu.VMEM((frames, 128), BF),
                pltpu.VMEM((frames, 128), BF),
                pltpu.VMEM((128, frames), BF),
                pltpu.VMEM((128, frames), BF),
                pltpu.VMEM((8, 128), F32),
                pltpu.SMEM((2,), F32),
            ],
        ),
        out_shape=[
            jax.ShapeDtypeStruct((frames, 128), BF),
            jax.ShapeDtypeStruct((8, frames), F32),
        ],
        compiler_params=pltpu.CompilerParams(vmem_limit_bytes=VMEM_LIMIT),
        cost_estimate=attention_cost(frames, 2),
        name="attend_forward",
    )(length, qkv, qkv, qkv)


def turn_back(grad, cos, sin):
    lane = lanes_of(grad.shape[0])
    turned = jnp.where((lane & 63) < 32, pltpu.roll(grad, 96, 1), pltpu.roll(grad, 32, 1))
    return grad * cos - turned * sin


def three(column, lane, at):
    high = column.astype(BF).astype(F32)
    rest = column - high
    mid = rest.astype(BF).astype(F32)
    low = rest - mid
    return jnp.where(lane == at, -high, jnp.where(lane == at + 1, -mid, jnp.where(lane == at + 2, -low, 0.0)))


def flash_backward_kernel(
    len_ref, q_ref, k_ref, v_ref, o_ref, do_ref, lse_ref, cos_ref, sin_ref,
    g_ref, ka, kb, va, vb, dkt, dvt, *, bq, bk,
):
    step = pl.program_id(0)
    steps = pl.num_programs(0)
    length = len_ref[0]
    frames = k_ref.shape[0]

    @pl.when(step == 0)
    def _():
        def build(j, carry):
            rows = pl.ds(pl.multiple_of(j * bk, bk), bk)
            lane = lanes_of(bk)
            pos = j * bk + lax.broadcasted_iota(jnp.int32, (bk, 128), 0)
            bias = jnp.where(pos < length, 0.0, MASKED)
            keys = k_ref[rows, :].astype(F32)
            vals = v_ref[rows, :].astype(F32)
            ones_a = jnp.where(lane < 67, 1.0, 0.0)
            ones_b = jnp.where(lane < 3, 1.0, 0.0)
            ka[rows, :] = jnp.where(lane < 64, keys, jnp.where(lane == 67, bias, ones_a)).astype(BF)
            kb[rows, :] = jnp.where(lane >= 64, keys, jnp.where(lane == 3, bias, ones_b)).astype(BF)
            va[rows, :] = jnp.where(lane < 64, vals, ones_a).astype(BF)
            vb[rows, :] = jnp.where(lane >= 64, vals, ones_b).astype(BF)
            return carry

        lax.fori_loop(0, frames // bk, build, 0)
        dkt[...] = jnp.zeros_like(dkt)
        dvt[...] = jnp.zeros_like(dvt)

    @pl.when(step * bq >= length)
    def _():
        rows = pl.ds(pl.multiple_of(step * bq, bq), bq)
        g_ref[rows, 0:128] = jnp.zeros((bq, 128), BF)

    @pl.when(step * bq < length)
    def _():
        lane = lanes_of(bq)
        queries = q_ref[...].astype(F32)
        dout = do_ref[...].astype(F32)
        product = dout * o_ref[...].astype(F32)
        delta_a, delta_b = head_sums(product, lane)
        lse = lse_ref[...].T
        qa = jnp.where(lane < 64, queries, jnp.where(lane == 67, 1.0, three(lse[:, 0:1], lane, 64))).astype(BF)
        qb = jnp.where(lane >= 64, queries, jnp.where(lane == 3, 1.0, three(lse[:, 1:2], lane, 0))).astype(BF)
        da = jnp.where(lane < 64, dout, three(delta_a, lane, 64)).astype(BF)
        db = jnp.where(lane >= 64, dout, three(delta_b, lane, 0)).astype(BF)
        qt = queries.T.astype(BF)
        dt = dout.T.astype(BF)

        def body(j, carry):
            rows = pl.ds(pl.multiple_of(j * bk, bk), bk)
            out = []
            for head, (qh, dh, kh, vh, dq) in enumerate(((qa, da, ka, va, carry[0]), (qb, db, kb, vb, carry[1]))):
                part = slice(head * 64, head * 64 + 64)
                keys = kh[rows, :]
                probs = jnp.exp2(nt(qh, keys))
                grad = (probs * nt(dh, vh[rows, :])).astype(BF)
                dvt[part, rows] += nn(dt, probs.astype(BF))[part]
                dkt[part, rows] += nn(qt, grad)[part]
                out.append(dq + nn(grad, keys))
            return tuple(out)

        start = jnp.zeros((bq, 128), F32)
        live = (length + bk - 1) // bk
        dq_a, dq_b = lax.fori_loop(0, live, body, (start, start))
        dq = jnp.where(lane < 64, dq_a, dq_b) * 0.125
        rows = pl.ds(pl.multiple_of(step * bq, bq), bq)
        g_ref[rows, 0:128] = turn_back(dq, cos_ref[rows, :], sin_ref[rows, :]).astype(BF)

    @pl.when(step == steps - 1)
    def _():
        def finish(j, carry):
            rows = pl.ds(pl.multiple_of(j * bk, bk), bk)
            dk = dkt[:, rows].T * LN2
            g_ref[rows, 128:256] = turn_back(dk, cos_ref[rows, :], sin_ref[rows, :]).astype(BF)
            g_ref[rows, 256:384] = dvt[:, rows].T.astype(BF)
            return carry

        lax.fori_loop(0, frames // bk, finish, 0)


def flash_backward(length, qkv, out, dout, lse, cos, sin, bq, bk):
    frames = qkv.shape[0]
    part = pl.BlockSpec((bq, 128), lambda i, *_: (i, 0))
    whole = pl.BlockSpec((frames, 128), lambda i, *_: (0, 0))
    return pl.pallas_call(
        functools.partial(flash_backward_kernel, bq=bq, bk=bk),
        grid_spec=pltpu.PrefetchScalarGridSpec(
            num_scalar_prefetch=1,
            grid=(frames // bq,),
            in_specs=[
                part,
                pl.BlockSpec((frames, 128), lambda i, *_: (0, 1)),
                pl.BlockSpec((frames, 128), lambda i, *_: (0, 2)),
                part,
                part,
                pl.BlockSpec((8, bq), lambda i, *_: (0, i)),
                whole,
                whole,
            ],
            out_specs=pl.BlockSpec((frames, 384), lambda i, *_: (0, 0)),
            scratch_shapes=[pltpu.VMEM((frames, 128), BF)] * 4
            + [pltpu.VMEM((128, frames), F32)] * 2,
        ),
        out_shape=jax.ShapeDtypeStruct((frames, 384), BF),
        compiler_params=pltpu.CompilerParams(vmem_limit_bytes=VMEM_LIMIT),
        cost_estimate=attention_cost(frames, 5),
        name="attend_backward",
    )(length, qkv, qkv, qkv, out, dout, lse, cos, sin)


def layer_norm(stream):
    centre = stream - jnp.mean(stream, axis=-1, keepdims=True)
    spread = jnp.mean(centre * centre, axis=-1, keepdims=True)
    inverse = lax.rsqrt(spread + EPS)
    return (centre * inverse, inverse)


def norm_back(grad_normed, normed, inverse):
    first_mean = jnp.mean(grad_normed, axis=-1, keepdims=True)
    second_mean = jnp.mean(grad_normed * normed, axis=-1, keepdims=True)
    return inverse * (grad_normed - first_mean - normed * second_mean)


def tn(left, right):
    return lax.dot_general(left, right, (((0,), (0,)), ((), ())), preferred_element_type=F32)


GELU_C = 0.7978845608028654
GELU_A = 0.044715


def gelu_and_slope(z):
    square = z * z
    turn = jnp.tanh(GELU_C * z * (1.0 + GELU_A * square))
    half = 0.5 * (1.0 + turn)
    slope = half + 0.5 * z * (1.0 - turn * turn) * (GELU_C * (1.0 + 3.0 * GELU_A * square))
    return z * half, slope


def row_blocks(rows):
    block = min(rows, 256)
    return [(at, slice(at, at + block)) for at in range(0, rows, block)]


def ffn_forward_kernel(
    att_ref, outw_ref, res_ref, mod_ref, cot_ref, weight_ref, up_ref, down_ref,
    branch_ref, act_ref, slope_ref, gb_ref, out_ref, gate_ref, normed, acc,
):
    step = pl.program_id(0)
    rows = att_ref.shape[0]
    span = rows // mod_ref.shape[0]

    @pl.when(step == 0)
    def _():
        for at, part in row_blocks(span):
            for utt in range(mod_ref.shape[0]):
                here = slice(utt * span + part.start, utt * span + part.stop)
                mod = mod_ref[utt]
                branch = nn(att_ref[here, :], outw_ref[...])
                branch_ref[here, :] = branch
                hat, _ = layer_norm(res_ref[here, :] + mod[2:3] * branch)
                normed[here, :] = (hat * (1.0 + mod[4:5]) + mod[3:4]).astype(BF)
        acc[...] = jnp.zeros_like(acc)

    for _, part in row_blocks(rows):
        act, slope = gelu_and_slope(nn(normed[part, :], up_ref[...]))
        act = act.astype(BF)
        act_ref[part, :] = act
        slope_ref[part, :] = slope.astype(BF)
        acc[part, :] += nn(act, down_ref[...])

    @pl.when(step == pl.num_programs(0) - 1)
    def _():
        for utt in range(mod_ref.shape[0]):
            mod = mod_ref[utt]
            total = jnp.zeros((1, acc.shape[1]), F32)
            for _, part in row_blocks(span):
                here = slice(utt * span + part.start, utt * span + part.stop)
                branch = acc[here, :]
                mid = res_ref[here, :] + mod[2:3] * branch_ref[here, :]
                out_ref[here, :] = (mid + mod[5:6] * branch).astype(BF)
                upstream = cot_ref[here, :].astype(F32) * weight_ref[here, :]
                gb_ref[here, :] = (upstream * mod[5:6]).astype(BF)
                total += jnp.sum(upstream * branch, axis=0, keepdims=True)
            gate_ref[utt : utt + 1, :] = total


def ffn_backward_kernel(
    att_ref, outw_ref, res_ref, branch_ref, mod_ref, cot_ref, weight_ref, gb_ref,
    act_ref, slope_ref, up_ref, down_ref,
    gup_ref, gdown_ref, gmid_ref, gatt_ref, gout_ref, sums_ref, normed, acc, gba,
):
    step = pl.program_id(0)
    rows = att_ref.shape[0]
    utts = mod_ref.shape[0]
    span = rows // utts

    def hat_of(here, mod):
        return layer_norm(res_ref[here, :] + mod[2:3] * branch_ref[here, :])

    @pl.when(step == 0)
    def _():
        for utt in range(utts):
            mod = mod_ref[utt]
            for _, part in row_blocks(span):
                here = slice(utt * span + part.start, utt * span + part.stop)
                hat, _ = hat_of(here, mod)
                normed[here, :] = (hat * (1.0 + mod[4:5]) + mod[3:4]).astype(BF)
        acc[...] = jnp.zeros_like(acc)

    pieces = []
    for _, part in row_blocks(rows):
        grad = nt(gb_ref[part, :], down_ref[...]) * slope_ref[part, :].astype(F32)
        grad = grad.astype(BF)
        acc[part, :] += nt(grad, up_ref[...])
        pieces.append(grad)
    gdown_ref[...] = tn(act_ref[...], gb_ref[...]).astype(BF)
    gup_ref[...] = tn(normed[...], jnp.concatenate(pieces, axis=0)).astype(BF)

    @pl.when(step == pl.num_programs(0) - 1)
    def _():
        for utt in range(utts):
            mod = mod_ref[utt]
            width = acc.shape[1]
            shift = jnp.zeros((1, width), F32)
            scale = jnp.zeros((1, width), F32)
            gate = jnp.zeros((1, width), F32)
            for _, part in row_blocks(span):
                here = slice(utt * span + part.start, utt * span + part.stop)
                hat, inverse = hat_of(here, mod)
                grad = acc[here, :]
                shift += jnp.sum(grad, axis=0, keepdims=True)
                scale += jnp.sum(grad * hat, axis=0, keepdims=True)
                upstream = cot_ref[here, :].astype(F32) * weight_ref[here, :]
                mid = upstream + norm_back(grad * (1.0 + mod[4:5]), hat, inverse)
                gmid_ref[here, :] = mid
                gate += jnp.sum(mid * branch_ref[here, :], axis=0, keepdims=True)
                low = (mid * mod[2:3]).astype(BF)
                gba[here, :] = low
                gatt_ref[here, :] = nt(low, outw_ref[...]).astype(BF)
            sums_ref[utt, 0:1, :] = shift
            sums_ref[utt, 1:2, :] = scale
            sums_ref[utt, 2:3, :] = gate
        gout_ref[...] = tn(att_ref[...], gba[...]).astype(BF)


def whole_spec(shape):
    zeros = (0,) * len(shape)
    return pl.BlockSpec(shape, lambda i: zeros, pipeline_mode=pl.Buffered(1))


def ffn_forward(att, outw, res, mods, cot, weight, up, down, chunk=512):
    rows, width = res.shape
    hidden = up.shape[1]
    whole = [whole_spec(a.shape) for a in (att, outw, res, mods, cot, weight)]
    col = pl.BlockSpec((rows, chunk), lambda i: (0, i))
    utts = mods.shape[0]
    return pl.pallas_call(
        ffn_forward_kernel,
        grid=(hidden // chunk,),
        in_specs=whole
        + [
            pl.BlockSpec((width, chunk), lambda i: (0, i)),
            pl.BlockSpec((chunk, width), lambda i: (i, 0)),
        ],
        out_specs=[
            whole_spec((rows, width)),
            col,
            col,
            whole_spec((rows, width)),
            whole_spec((rows, width)),
            whole_spec((utts, width)),
        ],
        out_shape=[
            jax.ShapeDtypeStruct((rows, width), F32),
            jax.ShapeDtypeStruct((rows, hidden), BF),
            jax.ShapeDtypeStruct((rows, hidden), BF),
            jax.ShapeDtypeStruct((rows, width), BF),
            jax.ShapeDtypeStruct((rows, width), BF),
            jax.ShapeDtypeStruct((utts, width), F32),
        ],
        scratch_shapes=[pltpu.VMEM((rows, width), BF), pltpu.VMEM((rows, width), F32)],
        compiler_params=pltpu.CompilerParams(vmem_limit_bytes=VMEM_LIMIT),
        cost_estimate=pl.CostEstimate(
            flops=2 * rows * width * (width + 2 * hidden),
            bytes_accessed=60 * 2**20,
            transcendentals=rows * hidden,
        ),
        name="ffn_forward",
    )(att, outw, res, mods, cot, weight, up, down)


def ffn_backward(att, outw, res, branch, mods, cot, weight, gb, act, slope, up, down, chunk=512):
    rows, width = res.shape
    hidden = up.shape[1]
    utts = mods.shape[0]
    whole = [whole_spec(a.shape) for a in (att, outw, res, branch, mods, cot, weight, gb)]
    col = pl.BlockSpec((rows, chunk), lambda i: (0, i))
    upspec = pl.BlockSpec((width, chunk), lambda i: (0, i))
    downspec = pl.BlockSpec((chunk, width), lambda i: (i, 0))
    return pl.pallas_call(
        ffn_backward_kernel,
        grid=(hidden // chunk,),
        in_specs=whole + [col, col, upspec, downspec],
        out_specs=[
            upspec,
            downspec,
            whole_spec((rows, width)),
            whole_spec((rows, width)),
            whole_spec((width, width)),
            whole_spec((utts, 8, width)),
        ],
        out_shape=[
            jax.ShapeDtypeStruct((width, hidden), BF),
            jax.ShapeDtypeStruct((hidden, width), BF),
            jax.ShapeDtypeStruct((rows, width), F32),
            jax.ShapeDtypeStruct((rows, width), BF),
            jax.ShapeDtypeStruct((width, width), BF),
            jax.ShapeDtypeStruct((utts, 8, width), F32),
        ],
        scratch_shapes=[
            pltpu.VMEM((rows, width), BF),
            pltpu.VMEM((rows, width), F32),
            pltpu.VMEM((rows, width), BF),
        ],
        compiler_params=pltpu.CompilerParams(vmem_limit_bytes=VMEM_LIMIT),
        cost_estimate=pl.CostEstimate(
            flops=2 * rows * width * (2 * width + 4 * hidden),
            bytes_accessed=90 * 2**20,
            transcendentals=0,
        ),
        name="ffn_backward",
    )(att, outw, res, branch, mods, cot, weight, gb, act, slope, up, down)


def project_kernel(x_ref, w_ref, cos_ref, sin_ref, out_ref):
    projected = nn(x_ref[...], w_ref[...])
    groups = out_ref.shape[0]
    rows = x_ref.shape[0]
    lane = lanes_of(rows)
    cos, sin = cos_ref[...], sin_ref[...]
    for part in range(3):
        for group in range(groups):
            at = (part * groups + group) * 128
            piece = projected[:, at : at + 128]
            if part < 2:
                turned = jnp.where(
                    (lane & 63) < 32, pltpu.roll(piece, 96, 1), pltpu.roll(piece, 32, 1)
                )
                piece = piece * cos + turned * sin
            if part == 0:
                piece = piece * (0.125 * LOG2E)
            out_ref[group, :, part * 128 : part * 128 + 128] = piece.astype(BF)


def project_heads(x, weight, cos, sin, groups, block=256):
    rows, width = x.shape
    return pl.pallas_call(
        project_kernel,
        grid=(rows // block,),
        in_specs=[
            pl.BlockSpec((block, width), lambda i: (i, 0)),
            pl.BlockSpec(weight.shape, lambda i: (0, 0)),
            pl.BlockSpec((block, 128), lambda i: (i, 0)),
            pl.BlockSpec((block, 128), lambda i: (i, 0)),
        ],
        out_specs=pl.BlockSpec((groups, block, 384), lambda i: (0, i, 0)),
        out_shape=jax.ShapeDtypeStruct((groups, rows, 384), BF),
        compiler_params=pltpu.CompilerParams(vmem_limit_bytes=VMEM_LIMIT),
        cost_estimate=pl.CostEstimate(
            flops=2 * rows * weight.size, bytes_accessed=2 * weight.size, transcendentals=0
        ),
        name="project_heads",
    )(x, weight, cos, sin)


def rotary_tables(positions):
    half_dim = HEAD_DIM // 2
    channel = jnp.arange(half_dim, dtype=jnp.float32)
    inverse = jnp.power(10000.0, -2.0 * channel / HEAD_DIM)
    angles = positions.astype(jnp.float32)[:, None] * inverse[None, :]
    angles = jnp.concatenate([angles, angles], axis=1)
    return (jnp.cos(angles), jnp.sin(angles))


def rotate_heads(field, cosine_table, sine_table):
    half_dim = field.shape[-1] // 2
    turned = jnp.concatenate([-field[..., half_dim:], field[..., :half_dim]], axis=-1)
    return field * cosine_table + turned * sine_table


def smooth_gelu(values):
    return jax.nn.gelu(values, approximate=True)


def cross(left, right):
    return lax.dot_general(
        left, right, (((0,), (0,)), ((), ())), preferred_element_type=jnp.float32
    )


def back_product(left, right):
    return lax.dot_general(
        left, right, (((1,), (1,)), ((), ())), preferred_element_type=jnp.float32
    )


def block_terms(query_block, dout_block, lse_block, delta_block, key_block, value_block, key_live):
    scores = jnp.einsum(
        "bqhd,bkhd->bhqk", query_block, key_block, preferred_element_type=jnp.float32
    )
    lse_heads = jnp.transpose(lse_block, (0, 2, 1))[..., None]
    probs = jnp.where(key_live[:, None, None, :], jnp.exp(scores - lse_heads), 0.0)
    grad_probs = jnp.einsum(
        "bqhd,bkhd->bhqk", dout_block, value_block, preferred_element_type=jnp.float32
    )
    delta_heads = jnp.transpose(delta_block, (0, 2, 1))[..., None]
    dscore = (probs * (grad_probs - delta_heads)).astype(jnp.bfloat16)
    return (probs.astype(jnp.bfloat16), dscore)


BATCH = ("x", "core")


def batch_index():
    return lax.axis_index("x") * lax.axis_size("core") + lax.axis_index("core")


def after(first, *later):
    return lax.optimization_barrier((first,) + later)[1:]


def exchange(pieces):
    count = pieces.shape[0]
    me = lax.axis_index("seq")
    out = pieces
    for flip in range(count - 1, 0, -1):
        there = jnp.bitwise_xor(me, flip)
        piece = lax.dynamic_index_in_dim(pieces, there, 0, keepdims=False)
        got = lax.ppermute(piece, "seq", [(i, i ^ flip) for i in range(count)])
        out = lax.dynamic_update_index_in_dim(out, got, there, 0)
    return out


def gather_weight(weight):
    parts = lax.axis_size(BATCH)
    if weight.shape[0] % parts:
        return lax.all_gather(weight, "seq", axis=0, tiled=True)
    rows = weight.shape[0] // parts
    mine = lax.dynamic_slice_in_dim(weight, batch_index() * rows, rows, 0)
    return lax.all_gather(mine, ("seq",) + BATCH, axis=0, tiled=True)


def sum_weight(grad):
    rows, width = grad.shape
    low = grad.astype(jnp.bfloat16)
    seq_count, cores = lax.axis_size("seq"), lax.axis_size("core")
    parts = seq_count * lax.axis_size(BATCH)
    if rows % parts or cores != 2:
        shard = lax.psum_scatter(low, "seq", scatter_dimension=0, tiled=True)
        return lax.psum(shard, BATCH).astype(jnp.float32)
    core = lax.axis_index("core")
    held = low.reshape(parts // 2, 2, rows // parts, width)
    send = lax.dynamic_index_in_dim(held, 1 - core, 1, keepdims=False)
    keep = lax.dynamic_index_in_dim(held, core, 1, keepdims=False)
    got = lax.ppermute(send, "core", [(0, 1), (1, 0)])
    half = (keep.astype(jnp.float32) + got.astype(jnp.float32)).astype(jnp.bfloat16)
    half = half.reshape(rows // 2, width)
    shard = lax.psum_scatter(half, ("seq", "x"), scatter_dimension=0, tiled=True)
    return lax.all_gather(shard, BATCH, axis=0, tiled=True).astype(jnp.float32)


def gather_kernel(*refs, shapes):
    count = len(shapes)
    weights, seq_small, batch_small = refs[:count], refs[count], refs[count + 1]
    fulls = refs[count + 2 : 2 * count + 2]
    seq_out, batch_out, send, recv, small_send, small_recv, local = refs[2 * count + 2 :]
    me, x, core = lax.axis_index("seq"), lax.axis_index("x"), lax.axis_index("core")
    bits = (me // 4, (me // 2) % 2, me % 2, x, core)

    def peer(dim):
        if dim < 3:
            return (me ^ (4 >> dim), x, core)
        return (me, 1 - x, core) if dim == 3 else (me, x, 1 - core)

    others = [((me + d) % 8, x, core) for d in range(1, 8)]
    mates = [(me, (x + dx) % 2, (core + dc) % 2) for dx, dc in ((0, 1), (1, 0), (1, 1))]
    barrier = pltpu.get_barrier_semaphore()
    for device in others + mates:
        pl.semaphore_signal(barrier, inc=1, device_id=device, device_id_type=pl.DeviceIdType.MESH)
    pl.semaphore_wait(barrier, len(others) + len(mates))

    small = []
    quarter = x * 2 + core
    own_seq = pltpu.make_async_copy(seq_small, seq_out.at[me], local.at[0])
    own_batch = pltpu.make_async_copy(batch_small, batch_out.at[quarter], local.at[1])
    own_seq.start()
    own_batch.start()
    for slot, device in enumerate(others):
        small.append(
            pltpu.make_async_remote_copy(
                seq_small, seq_out.at[me], small_send.at[slot], small_recv.at[slot],
                device_id=device, device_id_type=pl.DeviceIdType.MESH,
            )
        )
    for slot, device in enumerate(mates):
        small.append(
            pltpu.make_async_remote_copy(
                batch_small, batch_out.at[quarter], small_send.at[7 + slot], small_recv.at[7 + slot],
                device_id=device, device_id_type=pl.DeviceIdType.MESH,
            )
        )
    for copy in small:
        copy.start()

    jobs = []
    for index, (weight, full, (rows, width)) in enumerate(zip(weights, fulls, shapes)):
        span = rows // 4
        half = width // 2
        for side in range(2):
            cols = pl.ds(side * half, half)
            source = weight.at[pl.ds(quarter * span, span), cols]
            order = (0, 1, 2, 3, 4) if side == 0 else (0, 1, 3, 2, 4)
            jobs.append((full, cols, source, order))
    owns = []
    for index, (full, cols, source, order) in enumerate(jobs):
        own = pltpu.make_async_copy(source, full.at[bits + (slice(None), cols)], local.at[2 + index])
        own.start()
        owns.append(own)
    copies = [[None] * 5 for _ in jobs]
    for stage in range(5):
        for index, (full, cols, source, order) in enumerate(jobs):
            dim = order[stage]
            done = order[:stage]
            where = tuple(slice(None) if d in done else bits[d] for d in range(5)) + (slice(None), cols)
            if stage == 1:
                owns[index].wait()
            if stage:
                copies[index][stage - 1].wait_recv()
            copy = pltpu.make_async_remote_copy(
                source if stage == 0 else full.at[where],
                full.at[where],
                send.at[index * 5 + stage],
                recv.at[index * 5 + stage],
                device_id=peer(dim),
                device_id_type=pl.DeviceIdType.MESH,
            )
            copy.start()
            copies[index][stage] = copy
    for chain in copies:
        chain[4].wait_recv()
    for chain in copies:
        for copy in chain:
            copy.wait_send()
    for copy in small:
        copy.wait()
    own_seq.wait()
    own_batch.wait()


def gather_early(weights, seq_small, batch_small):
    shapes = [w.shape for w in weights]
    anywhere = pl.BlockSpec(memory_space=pl.ANY)
    jobs = 2 * len(weights)
    outs = pl.pallas_call(
        functools.partial(gather_kernel, shapes=shapes),
        in_specs=[anywhere] * (len(weights) + 2),
        out_specs=[anywhere] * (len(weights) + 2),
        out_shape=[
            jax.ShapeDtypeStruct((2, 2, 2, 2, 2, rows // 4, width), BF) for rows, width in shapes
        ]
        + [
            jax.ShapeDtypeStruct((8,) + seq_small.shape, F32),
            jax.ShapeDtypeStruct((4,) + batch_small.shape, F32),
        ],
        scratch_shapes=[
            pltpu.SemaphoreType.DMA((5 * jobs,)),
            pltpu.SemaphoreType.DMA((5 * jobs,)),
            pltpu.SemaphoreType.DMA((10,)),
            pltpu.SemaphoreType.DMA((10,)),
            pltpu.SemaphoreType.DMA((2 + jobs,)),
        ],
        compiler_params=pltpu.CompilerParams(collective_id=0, has_side_effects=True),
        name="gather_early",
    )(*weights, seq_small, batch_small)
    fulls = [full.reshape(8 * rows, width) for full, (rows, width) in zip(outs, shapes)]
    return fulls, outs[-2], outs[-1]


def paired_tables(positions):
    cos, sin = rotary_tables(positions)
    half = HEAD_DIM // 2
    signed = jnp.concatenate([-sin[:, :half], sin[:, half:]], axis=1)
    return jnp.tile(cos, (1, 2)), jnp.tile(signed, (1, 2))


def on_device(
    layer_input,
    skip_input,
    time_embed,
    lengths,
    cond_drop,
    cotangent,
    skip_weight,
    adaln_weight,
    adaln_bias,
    qkv_weight,
    out_weight,
    up_weight,
    down_weight,
):
    utt_count, frame_span, model_width = layer_input.shape
    head_count = model_width // HEAD_DIM
    row_count = utt_count * frame_span
    seq_here = lax.axis_index("seq")
    seq_count = lax.axis_size("seq")
    frame_count = frame_span * seq_count
    by_heads = head_count == 2 * seq_count and frame_count % 1024 == 0
    local_pos = seq_here * frame_span + jnp.arange(frame_span, dtype=jnp.int32)
    local_live = local_pos[None, :] < lengths[:, None]
    valid_mask = local_live.astype(jnp.float32)
    drop = cond_drop.astype(jnp.float32)
    dropped = drop[:, None] * valid_mask
    frames_live = jnp.minimum(lengths, frame_count).astype(jnp.float32)
    counts = jnp.stack([jnp.sum((1.0 - drop) * frames_live), jnp.sum(drop * frames_live)])
    silu_time = jax.nn.silu(time_embed.astype(jnp.float32)).astype(jnp.bfloat16)
    row_span = adaln_weight.shape[0]
    silu_mine = lax.dynamic_slice_in_dim(silu_time, seq_here * row_span, row_span, 1)
    mod_part = jnp.dot(silu_mine, adaln_weight, preferred_element_type=jnp.float32)
    bias_span = adaln_bias.shape[0]
    bias_here = lax.dynamic_update_slice_in_dim(
        jnp.zeros((mod_part.shape[1],), jnp.float32),
        adaln_bias.astype(jnp.float32),
        seq_here * bias_span,
        0,
    )
    mod_part = mod_part + bias_here
    if by_heads:
        small = jnp.concatenate(
            [
                silu_time.astype(jnp.float32),
                jnp.pad(counts[None, :], ((0, 5), (0, model_width - 2))),
            ],
            axis=0,
        )
        (skip_full, qkv_full), mod_every, small_every = gather_early(
            (skip_weight, qkv_weight), mod_part.reshape(-1, model_width), small
        )
        modulation = jnp.sum(mod_every, axis=0)
        totals = jnp.sum(small_every[:, utt_count, :2], axis=0)
        silu_every = small_every[:, :utt_count].reshape(-1, model_width)
    else:
        modulation = lax.psum(mod_part, "seq")
        totals = lax.psum(counts, BATCH)
        skip_full = gather_weight(skip_weight)
        qkv_full = gather_weight(qkv_weight)
        silu_every = lax.all_gather(silu_time, BATCH, axis=0, tiled=True).astype(jnp.float32)
    modulation = modulation.reshape(utt_count, 6, model_width)
    kept_total = jnp.maximum(totals[0], 1.0)
    drop_total = jnp.maximum(totals[1], 1.0)
    every_count = kept_total + drop_total
    loss_weight = (valid_mask - dropped) * (every_count / (2.0 * kept_total)) + dropped * (
        every_count / (2.0 * drop_total)
    )
    joined = jnp.concatenate([layer_input, skip_input], axis=-1).reshape(row_count, 2 * model_width)
    residual_in = jnp.dot(joined, skip_full, preferred_element_type=jnp.float32).reshape(
        utt_count, frame_span, model_width
    )
    shift_attn = modulation[:, 0][:, None, :]
    scale_attn = modulation[:, 1][:, None, :]
    hat_attn, inv_attn = layer_norm(residual_in)
    normed_attn = (
        (hat_attn * (1.0 + scale_attn) + shift_attn)
        .astype(jnp.bfloat16)
        .reshape(row_count, model_width)
    )
    if by_heads:
        cos_all, sin_all = paired_tables(jnp.arange(frame_count, dtype=jnp.int32))
        cos_here = lax.dynamic_slice_in_dim(cos_all, seq_here * frame_span, frame_span, 0)
        sin_here = lax.dynamic_slice_in_dim(sin_all, seq_here * frame_span, frame_span, 0)
        packed, attended_mine, lse_mine, attended_parts = [], [], [], []
        sends = []
        for utt in range(utt_count):
            sent = project_heads(
                normed_attn[utt * frame_span : (utt + 1) * frame_span],
                qkv_full,
                cos_here,
                sin_here,
                seq_count,
            )
            sends.append(sent)
        late = after(tuple(sends), out_weight, up_weight, down_weight)
        out_full, up_full, down_full = [gather_weight(weight) for weight in late]
        for sent in sends:
            packed.append(exchange(sent).reshape(frame_count, 384))
        for utt in range(utt_count):
            heads_out, lse = flash_forward(lengths[utt : utt + 1], packed[utt], 1024, 1024)
            attended_mine.append(heads_out)
            lse_mine.append(lse)
            back = exchange(heads_out.reshape(seq_count, frame_span, 128))
            attended_parts.append(back.transpose(1, 0, 2).reshape(frame_span, model_width))
        attended_low = jnp.concatenate(attended_parts, axis=0)
    else:
        out_full, up_full, down_full = [
            gather_weight(weight) for weight in (out_weight, up_weight, down_weight)
        ]
        projected = jnp.dot(normed_attn, qkv_full, preferred_element_type=jnp.float32).reshape(
            utt_count, frame_span, 3, head_count, HEAD_DIM
        )
        cosine_table, sine_table = rotary_tables(local_pos)
        cosine_table = cosine_table[None, :, None, :]
        sine_table = sine_table[None, :, None, :]
        queries = (rotate_heads(projected[:, :, 0], cosine_table, sine_table) * 0.125).astype(
            jnp.bfloat16
        )
        keys_rot = rotate_heads(projected[:, :, 1], cosine_table, sine_table).astype(jnp.bfloat16)
        values = projected[:, :, 2].astype(jnp.bfloat16)
        start_top = jnp.full((utt_count, head_count, frame_span), MASKED, jnp.float32)
        top_score = start_top
        key_piece = lax.all_gather(keys_rot, "seq", axis=1, tiled=True)
        value_piece = lax.all_gather(values, "seq", axis=1, tiled=True)
        piece_len = key_piece.shape[1]
        piece_live = jnp.arange(piece_len, dtype=jnp.int32)[None, :] < lengths[:, None]
        scores = jnp.einsum("bqhd,bkhd->bhqk", queries, key_piece, preferred_element_type=jnp.float32)
        scores = jnp.where(piece_live[:, None, None, :], scores, MASKED)
        new_top = jnp.maximum(top_score, jnp.max(scores, axis=-1))
        expo = jnp.where(piece_live[:, None, None, :], jnp.exp(scores - new_top[..., None]), 0.0)
        denom = jnp.sum(expo, axis=-1)
        partial_out = jnp.einsum(
            "bhqk,bkhd->bqhd",
            expo.astype(jnp.bfloat16),
            value_piece,
            preferred_element_type=jnp.float32,
        )
        accum = partial_out
        accum, top_score, denom = (accum, new_top, denom)
        attended_full = accum / jnp.transpose(denom, (0, 2, 1))[..., None]
        lse_rows = jnp.transpose(top_score + jnp.log(denom), (0, 2, 1))
        attended_low = attended_full.astype(jnp.bfloat16).reshape(row_count, model_width)
    residual_rows = residual_in.reshape(row_count, model_width)
    cot_rows = cotangent.reshape(row_count, model_width)
    weight_rows = loss_weight.reshape(row_count, 1)
    branch_attn, hidden_act, hidden_slope, grad_branch_ffn, layer_output, grad_gate_ffn = ffn_forward(
        attended_low,
        out_full,
        residual_rows,
        modulation,
        cot_rows,
        weight_rows,
        up_full,
        down_full,
    )
    layer_output = layer_output.reshape(utt_count, frame_span, model_width)
    grad_up, grad_down, grad_mid, grad_attended_flat, grad_out, ffn_sums = ffn_backward(
        attended_low,
        out_full,
        residual_rows,
        branch_attn,
        modulation,
        cot_rows,
        weight_rows,
        grad_branch_ffn,
        hidden_act,
        hidden_slope,
        up_full,
        down_full,
    )
    grad_mid = grad_mid.reshape(utt_count, frame_span, model_width)
    grad_shift_ffn, grad_scale_ffn, grad_gate_attn = ffn_sums[:, 0], ffn_sums[:, 1], ffn_sums[:, 2]
    qkv_back, skip_back = qkv_full, skip_full
    if by_heads:
        grad_parts = []
        for utt in range(utt_count):
            sent = grad_attended_flat[utt * frame_span : (utt + 1) * frame_span]
            sent = sent.reshape(frame_span, seq_count, 128).transpose(1, 0, 2)
            dout = exchange(sent).reshape(frame_count, 128)
            grads = flash_backward(
                lengths[utt : utt + 1],
                packed[utt],
                attended_mine[utt],
                dout,
                lse_mine[utt],
                cos_all,
                sin_all,
                1024,
                1024,
            )
            back = exchange(grads.reshape(seq_count, frame_span, 384))
            back = back.reshape(seq_count, frame_span, 3, 128).transpose(1, 2, 0, 3)
            grad_parts.append(back.reshape(frame_span, 3 * model_width))
        grad_projected = jnp.concatenate(grad_parts, axis=0)
    else:
        grad_attended = grad_attended_flat.reshape(
            utt_count, frame_span, head_count, HEAD_DIM
        )
        delta_rows = jnp.sum(grad_attended.astype(jnp.float32) * attended_full, axis=-1)
        lse_all, delta_all = (
            lax.all_gather(lse_rows, "seq", axis=1, tiled=True),
            lax.all_gather(delta_rows, "seq", axis=1, tiled=True),
        )
        key_piece = lax.all_gather(keys_rot, "seq", axis=1, tiled=True)
        value_piece = lax.all_gather(values, "seq", axis=1, tiled=True)
        piece_len = key_piece.shape[1]
        piece_live = jnp.arange(piece_len, dtype=jnp.int32)[None, :] < lengths[:, None]
        probs_low, dscore = block_terms(
            queries, grad_attended, lse_rows, delta_rows, key_piece, value_piece, piece_live
        )
        grad_queries = jnp.einsum(
            "bhqk,bkhd->bqhd", dscore, key_piece, preferred_element_type=jnp.float32
        )
        query_piece = lax.all_gather(queries, "seq", axis=1, tiled=True)
        dout_piece = lax.all_gather(grad_attended, "seq", axis=1, tiled=True)
        probs_low, dscore = block_terms(
            query_piece, dout_piece, lse_all, delta_all, keys_rot, values, local_live
        )
        grad_k = jnp.einsum("bhqk,bqhd->bkhd", dscore, query_piece, preferred_element_type=jnp.float32)
        grad_v = jnp.einsum(
            "bhqk,bqhd->bkhd", probs_low, dout_piece, preferred_element_type=jnp.float32
        )
        grad_q_pre = rotate_heads(grad_queries * 0.125, cosine_table, -sine_table)
        grad_k_pre = rotate_heads(grad_k, cosine_table, -sine_table)
        grad_projected = (
            jnp.stack([grad_q_pre, grad_k_pre, grad_v], axis=2)
            .reshape(row_count, 3 * model_width)
            .astype(jnp.bfloat16)
        )
    grad_qkv = cross(normed_attn, grad_projected)
    grad_normed_attn = back_product(grad_projected, qkv_back).reshape(
        utt_count, frame_span, model_width
    )
    grad_shift_attn = jnp.sum(grad_normed_attn, axis=1)
    grad_scale_attn = jnp.sum(grad_normed_attn * hat_attn, axis=1)
    grad_stream = grad_mid + norm_back(grad_normed_attn * (1.0 + scale_attn), hat_attn, inv_attn)
    grad_stream_low = grad_stream.astype(jnp.bfloat16).reshape(row_count, model_width)
    grad_skip_w = cross(joined, grad_stream_low)
    grad_joined = back_product(grad_stream_low, skip_back)
    grad_input = (
        grad_joined[:, :model_width]
        .reshape(utt_count, frame_span, model_width)
        .astype(jnp.bfloat16)
    )
    grad_skip = (
        grad_joined[:, model_width:]
        .reshape(utt_count, frame_span, model_width)
        .astype(jnp.bfloat16)
    )
    grad_modulation = jnp.stack(
        [
            grad_shift_attn,
            grad_scale_attn,
            grad_gate_attn,
            grad_shift_ffn,
            grad_scale_ffn,
            grad_gate_ffn,
        ],
        axis=1,
    ).reshape(utt_count, 6 * model_width)
    mod_total = lax.psum(grad_modulation, "seq")
    mod_every = lax.all_gather(
        mod_total.astype(jnp.bfloat16), BATCH, axis=0, tiled=True
    ).astype(jnp.float32)
    silu_rows = lax.dynamic_slice_in_dim(silu_every, seq_here * row_span, row_span, 1)
    adaln_rows = jnp.dot(silu_rows.T, mod_every, precision=lax.Precision.HIGHEST)
    bias_rows = lax.dynamic_slice_in_dim(
        jnp.sum(mod_every, axis=0), seq_here * bias_span, bias_span, 0
    )
    summed = [sum_weight(grad) for grad in (grad_skip_w, grad_qkv, grad_out, grad_up, grad_down)]
    results = (summed[0], adaln_rows, bias_rows, summed[1], summed[2], summed[3], summed[4])
    return (
        layer_output,
        grad_input,
        grad_skip,
        results[0],
        results[1],
        results[2],
        results[3],
        results[4],
        results[5],
        results[6],
    )


def solution(mesh):
    count, batch = mesh.shape["seq"], mesh.shape["batch"]
    cores = 2 if batch % 2 == 0 else 1
    split = Mesh(mesh.devices.reshape(count, batch // cores, cores), ("seq",) + BATCH)
    placed = (
        P(BATCH, "seq", None),
        P(BATCH, "seq", None),
        P(BATCH, None),
        P(BATCH),
        P(BATCH),
        P(BATCH, "seq", None),
        P("seq", None),
        P("seq", None),
        P("seq"),
        P("seq", None),
        P("seq", None),
        P("seq", None),
        P("seq", None),
    )
    return jax.shard_map(
        on_device,
        mesh=split,
        in_specs=placed,
        out_specs=(
            P(BATCH, "seq", None),
            P(BATCH, "seq", None),
            P(BATCH, "seq", None),
            P("seq", None),
            P("seq", None),
            P("seq"),
            P("seq", None),
            P("seq", None),
            P("seq", None),
            P("seq", None),
        ),
        check_vma=False,
    )
```

```python
import functools
import jax
import jax.numpy as jnp
from jax import lax
from jax.sharding import Mesh, PartitionSpec as P
from jax.experimental import pallas as pl
from jax.experimental.pallas import tpu as pltpu
HEAD_DIM = 64
EPS = 1e-06
LOG2E = 1.4426950408889634
LN2 = 0.6931471805599453
MASKED = -1e30
BF = jnp.bfloat16
F32 = jnp.float32
VMEM_LIMIT = 60 * 2**20


def nt(left, right):
    return lax.dot_general(left, right, (((1,), (1,)), ((), ())), preferred_element_type=F32)


def nn(left, right):
    return lax.dot_general(left, right, (((1,), (0,)), ((), ())), preferred_element_type=F32)


def head_sums(product, lane):
    first = jnp.sum(jnp.where(lane < 64, product, 0.0), axis=1, keepdims=True)
    second = jnp.sum(jnp.where(lane >= 64, product, 0.0), axis=1, keepdims=True)
    return (first, second)


def lanes_of(rows):
    return lax.broadcasted_iota(jnp.int32, (rows, 128), 1)


def attention_cost(frames, products):
    return pl.CostEstimate(
        flops=2 * products * 2 * frames * frames * 128,
        bytes_accessed=frames * 128 * 2 * 8,
        transcendentals=2 * frames * frames,
    )


def turn_back(grad, cos, sin):
    lane = lanes_of(grad.shape[0])
    turned = jnp.where((lane & 63) < 32, pltpu.roll(grad, 96, 1), pltpu.roll(grad, 32, 1))
    return grad * cos - turned * sin


def three(column, lane, at):
    high = column.astype(BF).astype(F32)
    rest = column - high
    mid = rest.astype(BF).astype(F32)
    low = rest - mid
    return jnp.where(lane == at, -high, jnp.where(lane == at + 1, -mid, jnp.where(lane == at + 2, -low, 0.0)))


MESH_IDS = pl.DeviceIdType.MESH


def seq_flip(flip):
    return (lax.axis_index("seq") ^ flip, lax.axis_index("x"), lax.axis_index("core"))


def greet(devices):
    barrier = pltpu.get_barrier_semaphore()
    for device in devices:
        pl.semaphore_signal(barrier, inc=1, device_id=device, device_id_type=MESH_IDS)
    pl.semaphore_wait(barrier, len(devices))


def remote(source, target, send, recv, device):
    return pltpu.make_async_remote_copy(
        source, target, send, recv, device_id=device, device_id_type=MESH_IDS
    )


class WeightGather:
    def __init__(self, jobs, send, recv, local):
        self.jobs, self.send, self.recv, self.local = jobs, send, recv, local
        me, x, core = lax.axis_index("seq"), lax.axis_index("x"), lax.axis_index("core")
        self.bits = (me // 4, (me // 2) % 2, me % 2, x, core)
        self.copies = [[] for _ in jobs]
        self.owns = []

    def peer(self, dim):
        me, x, core = lax.axis_index("seq"), lax.axis_index("x"), lax.axis_index("core")
        if dim < 3:
            return (me ^ (4 >> dim), x, core)
        return (me, 1 - x, core) if dim == 3 else (me, x, 1 - core)

    def stage(self):
        for index, (full, cols, source, order) in enumerate(self.jobs):
            at = len(self.copies[index])
            tail = (slice(None), cols)
            if at == 0:
                own = pltpu.make_async_copy(
                    source, full.at[self.bits + tail], self.local.at[index]
                )
                own.start()
                self.owns.append(own)
            else:
                if at == 1:
                    self.owns[index].wait()
                self.copies[index][at - 1].wait_recv()
            where = tuple(
                slice(None) if d in order[:at] else self.bits[d] for d in range(5)
            ) + tail
            copy = remote(
                source if at == 0 else full.at[where],
                full.at[where],
                self.send.at[index * 5 + at],
                self.recv.at[index * 5 + at],
                self.peer(order[at]),
            )
            copy.start()
            self.copies[index].append(copy)

    def finish(self):
        for chain in self.copies:
            chain[-1].wait_recv()
        for chain in self.copies:
            for copy in chain:
                copy.wait_send()


def gather_jobs(weights, fulls):
    quarter = lax.axis_index("x") * 2 + lax.axis_index("core")
    jobs = []
    for weight, full in zip(weights, fulls):
        rows, width = weight.shape
        span, half = rows // 4, width // 2
        for side in range(2):
            cols = pl.ds(side * half, half)
            source = weight.at[pl.ds(quarter * span, span), cols]
            jobs.append((full, cols, source, (0, 1, 2, 3, 4) if side == 0 else (0, 1, 3, 2, 4)))
    return jobs


def attend_forward_kernel(
    len_ref, proj, out_w, up_w, down_w,
    qkv_all, o_all, lse_ref, att, out_full, up_full, down_full,
    qkv, outs, ka, kb, vta, vtb,
    wsend, wrecv, wlocal, qsend, qrecv, qlocal, osend, orecv, olocal, slocal,
    *, span, bq, bk,
):
    me, x, core = lax.axis_index("seq"), lax.axis_index("x"), lax.axis_index("core")
    frames = qkv.shape[2]
    mine = pl.ds(pl.multiple_of(me * span, span), span)
    my_cols = pl.ds(pl.multiple_of(me * 128, 128), 128)
    flips = (7, 6, 5, 4, 3, 2, 1)
    greet([seq_flip(flip) for flip in flips] + [(me, 1 - x, core), (me, x, 1 - core)])
    weights = WeightGather(
        gather_jobs((out_w, up_w, down_w), (out_full, up_full, down_full)), wsend, wrecv, wlocal
    )

    def send_heads(utt):
        rows = pl.ds(utt * span, span)
        own = pltpu.make_async_copy(
            proj.at[:, rows, my_cols], qkv.at[utt, :, mine, :], qlocal.at[utt]
        )
        own.start()
        copies = []
        for flip in flips:
            there = me ^ flip
            cols = pl.ds(pl.multiple_of(there * 128, 128), 128)
            copy = remote(
                proj.at[:, rows, cols],
                qkv.at[utt, :, mine, :],
                qsend.at[utt * 8 + flip],
                qrecv.at[utt * 8 + flip],
                seq_flip(flip),
            )
            copy.start()
            copies.append(copy)
        return own, copies

    def arrive(sent):
        own, copies = sent
        own.wait()
        for copy in copies:
            copy.wait_recv()

    def attend(utt, between):
        length = len_ref[utt]
        save = pltpu.make_async_copy(qkv.at[utt], qkv_all.at[utt], slocal.at[utt])
        save.start()

        def build(j, carry):
            rows = pl.ds(pl.multiple_of(j * bk, bk), bk)
            lane = lanes_of(bk)
            pos = j * bk + lax.broadcasted_iota(jnp.int32, (bk, 128), 0)
            bias = jnp.where(pos < length, 0.0, MASKED)
            keys = qkv[utt, 1, rows, :].astype(F32)
            ka[rows, :] = jnp.where(lane < 64, keys, jnp.where(lane == 64, bias, 0.0)).astype(BF)
            kb[rows, :] = jnp.where(lane >= 64, keys, jnp.where(lane == 0, bias, 0.0)).astype(BF)
            vals = qkv[utt, 2, rows, :].astype(F32)
            vta[:, rows] = jnp.where(lane < 64, vals, 1.0).T.astype(BF)
            vtb[:, rows] = jnp.where(lane >= 64, vals, 1.0).T.astype(BF)
            return carry

        lax.fori_loop(0, frames // bk, build, 0)

        def block(i, carry):
            here = pl.ds(pl.multiple_of(i * bq, bq), bq)
            lane = lanes_of(bq)
            queries = qkv[utt, 0, here, :].astype(F32)
            qa = jnp.where(lane < 64, queries, jnp.where(lane == 64, 1.0, 0.0)).astype(BF)
            qb = jnp.where(lane >= 64, queries, jnp.where(lane == 0, 1.0, 0.0)).astype(BF)

            def body(j, inner):
                rows = pl.ds(pl.multiple_of(j * bk, bk), bk)
                result = []
                scores = [nt(ka[rows, :], qa), nt(kb[rows, :], qb)]
                for score, vt, (top, acc) in zip(scores, (vta, vtb), inner):
                    new = jnp.maximum(top, jnp.max(score, axis=0, keepdims=True))
                    probs = jnp.exp2(score - new).astype(BF)
                    acc = acc * jnp.exp2(top - new) + nn(vt[:, rows], probs)
                    result.append((new, acc))
                return tuple(result)

            start = (jnp.full((1, bq), MASKED, F32), jnp.zeros((128, bq), F32))
            (top_a, acc_a), (top_b, acc_b) = lax.fori_loop(0, frames // bk, body, (start, start))
            sum_a, sum_b = acc_a[64:65], acc_b[0:1]
            both = jnp.concatenate([acc_a[:64] / sum_a, acc_b[64:] / sum_b], axis=0)
            outs[utt, here, :] = both.T.astype(BF)
            lse_ref[utt, :, here] = jnp.concatenate(
                [top_a + jnp.log2(sum_a), top_b + jnp.log2(sum_b), jnp.zeros((6, bq), F32)],
                axis=0,
            )
            for part in range(bq // span):
                there = i * (bq // span) + part
                rows = pl.ds(pl.multiple_of(there * span, span), span)
                target = att.at[pl.ds(utt * span, span), my_cols]

                @pl.when(there != me)
                def _():
                    remote(
                        outs.at[utt, rows, :],
                        target,
                        osend.at[utt * 8 + (there ^ me)],
                        orecv.at[utt * 8 + (there ^ me)],
                        (there, x, core),
                    ).start()

                @pl.when(there == me)
                def _():
                    pltpu.make_async_copy(outs.at[utt, rows, :], target, olocal.at[utt]).start()

            return carry

        half = frames // bq // 2
        lax.fori_loop(0, half, block, 0)
        between()
        lax.fori_loop(half, 2 * half, block, 0)
        keep = pltpu.make_async_copy(outs.at[utt], o_all.at[utt], slocal.at[2 + utt])
        keep.start()
        return [save, keep]

    weights.stage()
    first = send_heads(0)
    arrive(first)
    second = send_heads(1)
    weights.stage()
    saves = attend(0, weights.stage)
    weights.stage()
    arrive(second)
    saves += attend(1, weights.stage)
    for sent in (first, second):
        for copy in sent[1]:
            copy.wait_send()
    weights.finish()
    for save in saves:
        save.wait()
    for utt in range(2):
        target = att.at[pl.ds(utt * span, span), my_cols]
        pltpu.make_async_copy(outs.at[utt, mine, :], target, olocal.at[utt]).wait()
        for flip in flips:
            copy = remote(
                outs.at[utt, mine, :],
                target,
                osend.at[utt * 8 + flip],
                orecv.at[utt * 8 + flip],
                seq_flip(flip),
            )
            copy.wait_send()
            copy.wait_recv()


def attend_forward(lengths, proj, out_w, up_w, down_w, span, bq=1024, bk=512):
    rows, width = proj.shape[1:]
    frames = 8 * span
    anywhere = pl.BlockSpec(memory_space=pl.ANY)
    vmem = pl.BlockSpec(memory_space=pltpu.VMEM)
    full = lambda w: jax.ShapeDtypeStruct((2, 2, 2, 2, 2, w.shape[0] // 4, w.shape[1]), BF)
    dma = pltpu.SemaphoreType.DMA
    outs = pl.pallas_call(
        functools.partial(attend_forward_kernel, span=span, bq=bq, bk=bk),
        in_specs=[pl.BlockSpec(memory_space=pltpu.SMEM)] + [anywhere] * 4,
        out_specs=[anywhere, anywhere, vmem] + [anywhere] * 4,
        out_shape=[
            jax.ShapeDtypeStruct((2, 3, frames, 128), BF),
            jax.ShapeDtypeStruct((2, frames, 128), BF),
            jax.ShapeDtypeStruct((2, 8, frames), F32),
            jax.ShapeDtypeStruct((rows, width), BF),
            full(out_w),
            full(up_w),
            full(down_w),
        ],
        scratch_shapes=[
            pltpu.VMEM((2, 3, frames, 128), BF),
            pltpu.VMEM((2, frames, 128), BF),
            pltpu.VMEM((frames, 128), BF),
            pltpu.VMEM((frames, 128), BF),
            pltpu.VMEM((128, frames), BF),
            pltpu.VMEM((128, frames), BF),
            dma((30,)),
            dma((30,)),
            dma((6,)),
            dma((16,)),
            dma((16,)),
            dma((2,)),
            dma((16,)),
            dma((16,)),
            dma((2,)),
            dma((4,)),
        ],
        compiler_params=pltpu.CompilerParams(
            vmem_limit_bytes=VMEM_LIMIT, collective_id=1, has_side_effects=True
        ),
        cost_estimate=attention_cost(frames, 4),
        name="attend_forward",
    )(lengths, proj, out_w, up_w, down_w)
    fulls = [outs[4 + i].reshape(8 * w.shape[0], w.shape[1]) for i, w in enumerate((out_w, up_w, down_w))]
    return outs[:4], fulls


def attend_backward_kernel(
    len_ref, dout, qkv_all, o_all, lse_ref, cos_ref, sin_ref,
    grads,
    qkv, outs, douts, qa, qb, da, db, qt, dt, dqa, dqb,
    dsend, drecv, dlocal, gsend, grecv, glocal, load,
    *, span, block,
):
    me, x, core = lax.axis_index("seq"), lax.axis_index("x"), lax.axis_index("core")
    frames = qkv.shape[2]
    width = grads.shape[1] // 3
    count = frames // block
    mine = pl.ds(pl.multiple_of(me * span, span), span)
    flips = (7, 6, 5, 4, 3, 2, 1)
    greet([seq_flip(flip) for flip in flips])
    loads = []
    for utt in range(2):
        loads.append(
            [
                pltpu.make_async_copy(qkv_all.at[utt], qkv.at[utt], load.at[utt]),
                pltpu.make_async_copy(o_all.at[utt], outs.at[utt], load.at[2 + utt]),
            ]
        )
        for copy in loads[-1]:
            copy.start()

    def send_heads(utt):
        rows = pl.ds(utt * span, span)
        my_cols = pl.ds(pl.multiple_of(me * 128, 128), 128)
        own = pltpu.make_async_copy(dout.at[rows, my_cols], douts.at[utt, mine, :], dlocal.at[utt])
        own.start()
        copies = []
        for flip in flips:
            cols = pl.ds(pl.multiple_of((me ^ flip) * 128, 128), 128)
            copy = remote(
                dout.at[rows, cols],
                douts.at[utt, mine, :],
                dsend.at[utt * 8 + flip],
                drecv.at[utt * 8 + flip],
                seq_flip(flip),
            )
            copy.start()
            copies.append(copy)
        return own, copies

    def arrive(sent):
        own, copies = sent
        own.wait()
        for copy in copies:
            copy.wait_recv()

    def slot(utt, part, flip):
        return (utt * 3 + part) * 8 + flip

    def target(utt, part):
        cols = pl.ds(pl.multiple_of(part * width + me * 128, 128), 128)
        return grads.at[pl.ds(utt * span, span), cols]

    def send_grads(utt, part, there):
        rows = pl.ds(pl.multiple_of(there * span, span), span)

        @pl.when(there != me)
        def _():
            at = slot(utt, part, there ^ me)
            remote(
                qkv.at[utt, part, rows, :],
                target(utt, part),
                gsend.at[at],
                grecv.at[at],
                (there, x, core),
            ).start()

        @pl.when(there == me)
        def _():
            pltpu.make_async_copy(
                qkv.at[utt, part, rows, :], target(utt, part), glocal.at[utt * 3 + part]
            ).start()

    def differentiate(utt):
        length = len_ref[utt]

        def build(j, carry):
            rows = pl.ds(pl.multiple_of(j * block, block), block)
            lane = lanes_of(block)
            queries = qkv[utt, 0, rows, :].astype(F32)
            grad = douts[utt, rows, :].astype(F32)
            delta_a, delta_b = head_sums(grad * outs[utt, rows, :].astype(F32), lane)
            lse = lse_ref[utt, :, rows].T
            one_a, one_b = lse[:, 0:1], lse[:, 1:2]
            qa[rows, :] = jnp.where(
                lane < 64, queries, jnp.where(lane == 67, 1.0, three(one_a, lane, 64))
            ).astype(BF)
            qb[rows, :] = jnp.where(
                lane >= 64, queries, jnp.where(lane == 3, 1.0, three(one_b, lane, 0))
            ).astype(BF)
            da[rows, :] = jnp.where(lane < 64, grad, three(delta_a, lane, 64)).astype(BF)
            db[rows, :] = jnp.where(lane >= 64, grad, three(delta_b, lane, 0)).astype(BF)
            qt[:, rows] = queries.T.astype(BF)
            dt[:, rows] = grad.T.astype(BF)
            dqa[rows, :] = jnp.zeros((block, 128), F32)
            dqb[rows, :] = jnp.zeros((block, 128), F32)
            return carry

        lax.fori_loop(0, count, build, 0)

        def keys_block(i, carry):
            here = pl.ds(pl.multiple_of(i * block, block), block)
            lane = lanes_of(block)
            pos = i * block + lax.broadcasted_iota(jnp.int32, (block, 128), 0)
            bias = jnp.where(pos < length, 0.0, MASKED)
            keys = qkv[utt, 1, here, :].astype(F32)
            vals = qkv[utt, 2, here, :].astype(F32)
            ones_a = jnp.where(lane < 67, 1.0, 0.0)
            ones_b = jnp.where(lane < 3, 1.0, 0.0)
            ka = jnp.where(lane < 64, keys, jnp.where(lane == 67, bias, ones_a)).astype(BF)
            kb = jnp.where(lane >= 64, keys, jnp.where(lane == 3, bias, ones_b)).astype(BF)
            va = jnp.where(lane < 64, vals, ones_a).astype(BF)
            vb = jnp.where(lane >= 64, vals, ones_b).astype(BF)

            def body(j, inner):
                rows = pl.ds(pl.multiple_of(j * block, block), block)
                result = []
                for head, (qh, dh, kh, vh, dq) in enumerate(
                    ((qa, da, ka, va, dqa), (qb, db, kb, vb, dqb))
                ):
                    part = slice(head * 64, head * 64 + 64)
                    probs = jnp.exp2(nt(qh[rows, :], kh))
                    grad = (probs * nt(dh[rows, :], vh)).astype(BF)
                    dv = inner[2 * head + 1] + nn(dt[:, rows], probs.astype(BF))[part]
                    dk = inner[2 * head] + nn(qt[:, rows], grad)[part]
                    dq[rows, :] += nn(grad, kh)
                    result += [dk, dv]
                return tuple(result)

            zero = jnp.zeros((64, block), F32)
            dk_a, dv_a, dk_b, dv_b = lax.fori_loop(0, count, body, (zero,) * 4)
            dk = jnp.concatenate([dk_a, dk_b], axis=0).T * LN2
            dv = jnp.concatenate([dv_a, dv_b], axis=0).T
            qkv[utt, 1, here, :] = turn_back(dk, cos_ref[here, :], sin_ref[here, :]).astype(BF)
            qkv[utt, 2, here, :] = dv.astype(BF)
            for step in range(block // span):
                there = i * (block // span) + step
                send_grads(utt, 1, there)
                send_grads(utt, 2, there)
            return carry

        lax.fori_loop(0, count, keys_block, 0)

        def finish(i, carry):
            here = pl.ds(pl.multiple_of(i * block, block), block)
            lane = lanes_of(block)
            dq = jnp.where(lane < 64, dqa[here, :], dqb[here, :]) * 0.125
            qkv[utt, 0, here, :] = turn_back(dq, cos_ref[here, :], sin_ref[here, :]).astype(BF)
            for step in range(block // span):
                send_grads(utt, 0, i * (block // span) + step)
            return carry

        lax.fori_loop(0, count, finish, 0)

    first = send_heads(0)
    for copy in loads[0]:
        copy.wait()
    arrive(first)
    second = send_heads(1)
    differentiate(0)
    for copy in loads[1]:
        copy.wait()
    arrive(second)
    differentiate(1)
    for sent in (first, second):
        for copy in sent[1]:
            copy.wait_send()
    for utt in range(2):
        for part in range(3):
            own = qkv.at[utt, part, mine, :]
            pltpu.make_async_copy(own, target(utt, part), glocal.at[utt * 3 + part]).wait()
            for flip in flips:
                at = slot(utt, part, flip)
                copy = remote(own, target(utt, part), gsend.at[at], grecv.at[at], seq_flip(flip))
                copy.wait_send()
                copy.wait_recv()


def attend_backward(lengths, dout, qkv_all, o_all, lse, cos, sin, span, block=1024):
    frames = 8 * span
    rows, width = dout.shape
    anywhere = pl.BlockSpec(memory_space=pl.ANY)
    vmem = pl.BlockSpec(memory_space=pltpu.VMEM)
    dma = pltpu.SemaphoreType.DMA
    return pl.pallas_call(
        functools.partial(attend_backward_kernel, span=span, block=block),
        in_specs=[pl.BlockSpec(memory_space=pltpu.SMEM)] + [anywhere] * 3 + [vmem] * 3,
        out_specs=anywhere,
        out_shape=jax.ShapeDtypeStruct((rows, 3 * width), BF),
        scratch_shapes=[
            pltpu.VMEM((2, 3, frames, 128), BF),
            pltpu.VMEM((2, frames, 128), BF),
            pltpu.VMEM((2, frames, 128), BF),
        ]
        + [pltpu.VMEM((frames, 128), BF)] * 4
        + [pltpu.VMEM((128, frames), BF)] * 2
        + [pltpu.VMEM((frames, 128), F32)] * 2
        + [dma((16,)), dma((16,)), dma((2,)), dma((48,)), dma((48,)), dma((6,)), dma((4,))],
        compiler_params=pltpu.CompilerParams(
            vmem_limit_bytes=VMEM_LIMIT, collective_id=2, has_side_effects=True
        ),
        cost_estimate=attention_cost(frames, 10),
        name="attend_backward",
    )(lengths, dout, qkv_all, o_all, lse, cos, sin)


def layer_norm(stream):
    centre = stream - jnp.mean(stream, axis=-1, keepdims=True)
    spread = jnp.mean(centre * centre, axis=-1, keepdims=True)
    inverse = lax.rsqrt(spread + EPS)
    return (centre * inverse, inverse)


def norm_back(grad_normed, normed, inverse):
    first_mean = jnp.mean(grad_normed, axis=-1, keepdims=True)
    second_mean = jnp.mean(grad_normed * normed, axis=-1, keepdims=True)
    return inverse * (grad_normed - first_mean - normed * second_mean)


def tn(left, right):
    return lax.dot_general(left, right, (((0,), (0,)), ((), ())), preferred_element_type=F32)


GELU_C = 0.7978845608028654
GELU_A = 0.044715


def gelu_and_slope(z):
    square = z * z
    turn = jnp.tanh(GELU_C * z * (1.0 + GELU_A * square))
    half = 0.5 * (1.0 + turn)
    slope = half + 0.5 * z * (1.0 - turn * turn) * (GELU_C * (1.0 + 3.0 * GELU_A * square))
    return z * half, slope


def row_blocks(rows):
    block = min(rows, 256)
    return [(at, slice(at, at + block)) for at in range(0, rows, block)]


def ffn_forward_kernel(
    att_ref, outw_ref, res_ref, mod_ref, cot_ref, weight_ref, up_ref, down_ref,
    branch_ref, act_ref, slope_ref, gb_ref, out_ref, gate_ref, normed, acc,
):
    step = pl.program_id(0)
    rows = att_ref.shape[0]
    span = rows // mod_ref.shape[0]

    @pl.when(step == 0)
    def _():
        for at, part in row_blocks(span):
            for utt in range(mod_ref.shape[0]):
                here = slice(utt * span + part.start, utt * span + part.stop)
                mod = mod_ref[utt]
                branch = nn(att_ref[here, :], outw_ref[...])
                branch_ref[here, :] = branch
                hat, _ = layer_norm(res_ref[here, :] + mod[2:3] * branch)
                normed[here, :] = (hat * (1.0 + mod[4:5]) + mod[3:4]).astype(BF)
        acc[...] = jnp.zeros_like(acc)

    for _, part in row_blocks(rows):
        act, slope = gelu_and_slope(nn(normed[part, :], up_ref[...]))
        act = act.astype(BF)
        act_ref[part, :] = act
        slope_ref[part, :] = slope.astype(BF)
        acc[part, :] += nn(act, down_ref[...])

    @pl.when(step == pl.num_programs(0) - 1)
    def _():
        for utt in range(mod_ref.shape[0]):
            mod = mod_ref[utt]
            total = jnp.zeros((1, acc.shape[1]), F32)
            for _, part in row_blocks(span):
                here = slice(utt * span + part.start, utt * span + part.stop)
                branch = acc[here, :]
                mid = res_ref[here, :] + mod[2:3] * branch_ref[here, :]
                out_ref[here, :] = (mid + mod[5:6] * branch).astype(BF)
                upstream = cot_ref[here, :].astype(F32) * weight_ref[here, :]
                gb_ref[here, :] = (upstream * mod[5:6]).astype(BF)
                total += jnp.sum(upstream * branch, axis=0, keepdims=True)
            gate_ref[utt : utt + 1, :] = total


def ffn_backward_kernel(
    att_ref, outw_ref, res_ref, branch_ref, mod_ref, cot_ref, weight_ref, gb_ref,
    act_ref, slope_ref, up_ref, down_ref,
    gup_ref, gdown_ref, gmid_ref, gatt_ref, gout_ref, sums_ref, normed, acc, gba,
):
    step = pl.program_id(0)
    rows = att_ref.shape[0]
    utts = mod_ref.shape[0]
    span = rows // utts

    def hat_of(here, mod):
        return layer_norm(res_ref[here, :] + mod[2:3] * branch_ref[here, :])

    @pl.when(step == 0)
    def _():
        for utt in range(utts):
            mod = mod_ref[utt]
            for _, part in row_blocks(span):
                here = slice(utt * span + part.start, utt * span + part.stop)
                hat, _ = hat_of(here, mod)
                normed[here, :] = (hat * (1.0 + mod[4:5]) + mod[3:4]).astype(BF)
        acc[...] = jnp.zeros_like(acc)

    pieces = []
    for _, part in row_blocks(rows):
        grad = nt(gb_ref[part, :], down_ref[...]) * slope_ref[part, :].astype(F32)
        grad = grad.astype(BF)
        acc[part, :] += nt(grad, up_ref[...])
        pieces.append(grad)
    gdown_ref[...] = tn(act_ref[...], gb_ref[...]).astype(BF)
    gup_ref[...] = tn(normed[...], jnp.concatenate(pieces, axis=0)).astype(BF)

    @pl.when(step == pl.num_programs(0) - 1)
    def _():
        for utt in range(utts):
            mod = mod_ref[utt]
            width = acc.shape[1]
            shift = jnp.zeros((1, width), F32)
            scale = jnp.zeros((1, width), F32)
            gate = jnp.zeros((1, width), F32)
            for _, part in row_blocks(span):
                here = slice(utt * span + part.start, utt * span + part.stop)
                hat, inverse = hat_of(here, mod)
                grad = acc[here, :]
                shift += jnp.sum(grad, axis=0, keepdims=True)
                scale += jnp.sum(grad * hat, axis=0, keepdims=True)
                upstream = cot_ref[here, :].astype(F32) * weight_ref[here, :]
                mid = upstream + norm_back(grad * (1.0 + mod[4:5]), hat, inverse)
                gmid_ref[here, :] = mid
                gate += jnp.sum(mid * branch_ref[here, :], axis=0, keepdims=True)
                low = (mid * mod[2:3]).astype(BF)
                gba[here, :] = low
                gatt_ref[here, :] = nt(low, outw_ref[...]).astype(BF)
            sums_ref[utt, 0:1, :] = shift
            sums_ref[utt, 1:2, :] = scale
            sums_ref[utt, 2:3, :] = gate
        gout_ref[...] = tn(att_ref[...], gba[...]).astype(BF)


def whole_spec(shape):
    zeros = (0,) * len(shape)
    return pl.BlockSpec(shape, lambda i: zeros, pipeline_mode=pl.Buffered(1))


def ffn_forward(att, outw, res, mods, cot, weight, up, down, chunk=512):
    rows, width = res.shape
    hidden = up.shape[1]
    whole = [whole_spec(a.shape) for a in (att, outw, res, mods, cot, weight)]
    col = pl.BlockSpec((rows, chunk), lambda i: (0, i))
    utts = mods.shape[0]
    return pl.pallas_call(
        ffn_forward_kernel,
        grid=(hidden // chunk,),
        in_specs=whole
        + [
            pl.BlockSpec((width, chunk), lambda i: (0, i)),
            pl.BlockSpec((chunk, width), lambda i: (i, 0)),
        ],
        out_specs=[
            whole_spec((rows, width)),
            col,
            col,
            whole_spec((rows, width)),
            whole_spec((rows, width)),
            whole_spec((utts, width)),
        ],
        out_shape=[
            jax.ShapeDtypeStruct((rows, width), F32),
            jax.ShapeDtypeStruct((rows, hidden), BF),
            jax.ShapeDtypeStruct((rows, hidden), BF),
            jax.ShapeDtypeStruct((rows, width), BF),
            jax.ShapeDtypeStruct((rows, width), BF),
            jax.ShapeDtypeStruct((utts, width), F32),
        ],
        scratch_shapes=[pltpu.VMEM((rows, width), BF), pltpu.VMEM((rows, width), F32)],
        compiler_params=pltpu.CompilerParams(vmem_limit_bytes=VMEM_LIMIT),
        cost_estimate=pl.CostEstimate(
            flops=2 * rows * width * (width + 2 * hidden),
            bytes_accessed=60 * 2**20,
            transcendentals=rows * hidden,
        ),
        name="ffn_forward",
    )(att, outw, res, mods, cot, weight, up, down)


def ffn_backward(att, outw, res, branch, mods, cot, weight, gb, act, slope, up, down, chunk=512):
    rows, width = res.shape
    hidden = up.shape[1]
    utts = mods.shape[0]
    whole = [whole_spec(a.shape) for a in (att, outw, res, branch, mods, cot, weight, gb)]
    col = pl.BlockSpec((rows, chunk), lambda i: (0, i))
    upspec = pl.BlockSpec((width, chunk), lambda i: (0, i))
    downspec = pl.BlockSpec((chunk, width), lambda i: (i, 0))
    return pl.pallas_call(
        ffn_backward_kernel,
        grid=(hidden // chunk,),
        in_specs=whole + [col, col, upspec, downspec],
        out_specs=[
            upspec,
            downspec,
            whole_spec((rows, width)),
            whole_spec((rows, width)),
            whole_spec((width, width)),
            whole_spec((utts, 8, width)),
        ],
        out_shape=[
            jax.ShapeDtypeStruct((width, hidden), BF),
            jax.ShapeDtypeStruct((hidden, width), BF),
            jax.ShapeDtypeStruct((rows, width), F32),
            jax.ShapeDtypeStruct((rows, width), BF),
            jax.ShapeDtypeStruct((width, width), BF),
            jax.ShapeDtypeStruct((utts, 8, width), F32),
        ],
        scratch_shapes=[
            pltpu.VMEM((rows, width), BF),
            pltpu.VMEM((rows, width), F32),
            pltpu.VMEM((rows, width), BF),
        ],
        compiler_params=pltpu.CompilerParams(vmem_limit_bytes=VMEM_LIMIT),
        cost_estimate=pl.CostEstimate(
            flops=2 * rows * width * (2 * width + 4 * hidden),
            bytes_accessed=90 * 2**20,
            transcendentals=0,
        ),
        name="ffn_backward",
    )(att, outw, res, branch, mods, cot, weight, gb, act, slope, up, down)


def project_kernel(x_ref, w_ref, cos_ref, sin_ref, out_ref):
    projected = nn(x_ref[...], w_ref[...])
    groups = out_ref.shape[2] // 128
    rows = x_ref.shape[0]
    lane = lanes_of(rows)
    cos, sin = cos_ref[...], sin_ref[...]
    for part in range(3):
        for group in range(groups):
            at = (part * groups + group) * 128
            piece = projected[:, at : at + 128]
            if part < 2:
                turned = jnp.where(
                    (lane & 63) < 32, pltpu.roll(piece, 96, 1), pltpu.roll(piece, 32, 1)
                )
                piece = piece * cos + turned * sin
            if part == 0:
                piece = piece * (0.125 * LOG2E)
            out_ref[part, :, group * 128 : group * 128 + 128] = piece.astype(BF)


def project_heads(x, weight, cos, sin, block=256):
    rows, width = x.shape
    steps = cos.shape[0] // block
    return pl.pallas_call(
        project_kernel,
        grid=(rows // block,),
        in_specs=[
            pl.BlockSpec((block, width), lambda i: (i, 0)),
            pl.BlockSpec(weight.shape, lambda i: (0, 0)),
            pl.BlockSpec((block, 128), lambda i: (i % steps, 0)),
            pl.BlockSpec((block, 128), lambda i: (i % steps, 0)),
        ],
        out_specs=pl.BlockSpec((3, block, width), lambda i: (0, i, 0)),
        out_shape=jax.ShapeDtypeStruct((3, rows, width), BF),
        compiler_params=pltpu.CompilerParams(vmem_limit_bytes=VMEM_LIMIT),
        cost_estimate=pl.CostEstimate(
            flops=2 * rows * weight.size, bytes_accessed=2 * weight.size, transcendentals=0
        ),
        name="project_heads",
    )(x, weight, cos, sin)


def rotary_tables(positions):
    half_dim = HEAD_DIM // 2
    channel = jnp.arange(half_dim, dtype=jnp.float32)
    inverse = jnp.power(10000.0, -2.0 * channel / HEAD_DIM)
    angles = positions.astype(jnp.float32)[:, None] * inverse[None, :]
    angles = jnp.concatenate([angles, angles], axis=1)
    return (jnp.cos(angles), jnp.sin(angles))


def rotate_heads(field, cosine_table, sine_table):
    half_dim = field.shape[-1] // 2
    turned = jnp.concatenate([-field[..., half_dim:], field[..., :half_dim]], axis=-1)
    return field * cosine_table + turned * sine_table


def smooth_gelu(values):
    return jax.nn.gelu(values, approximate=True)


def cross(left, right):
    return lax.dot_general(
        left, right, (((0,), (0,)), ((), ())), preferred_element_type=jnp.float32
    )


def back_product(left, right):
    return lax.dot_general(
        left, right, (((1,), (1,)), ((), ())), preferred_element_type=jnp.float32
    )


def block_terms(query_block, dout_block, lse_block, delta_block, key_block, value_block, key_live):
    scores = jnp.einsum(
        "bqhd,bkhd->bhqk", query_block, key_block, preferred_element_type=jnp.float32
    )
    lse_heads = jnp.transpose(lse_block, (0, 2, 1))[..., None]
    probs = jnp.where(key_live[:, None, None, :], jnp.exp(scores - lse_heads), 0.0)
    grad_probs = jnp.einsum(
        "bqhd,bkhd->bhqk", dout_block, value_block, preferred_element_type=jnp.float32
    )
    delta_heads = jnp.transpose(delta_block, (0, 2, 1))[..., None]
    dscore = (probs * (grad_probs - delta_heads)).astype(jnp.bfloat16)
    return (probs.astype(jnp.bfloat16), dscore)


BATCH = ("x", "core")


def batch_index():
    return lax.axis_index("x") * lax.axis_size("core") + lax.axis_index("core")


def gather_weight(weight):
    parts = lax.axis_size(BATCH)
    if weight.shape[0] % parts:
        return lax.all_gather(weight, "seq", axis=0, tiled=True)
    rows = weight.shape[0] // parts
    mine = lax.dynamic_slice_in_dim(weight, batch_index() * rows, rows, 0)
    return lax.all_gather(mine, ("seq",) + BATCH, axis=0, tiled=True)


def sum_weight(grad):
    rows, width = grad.shape
    low = grad.astype(jnp.bfloat16)
    seq_count, cores = lax.axis_size("seq"), lax.axis_size("core")
    parts = seq_count * lax.axis_size(BATCH)
    if rows % parts or cores != 2:
        shard = lax.psum_scatter(low, "seq", scatter_dimension=0, tiled=True)
        return lax.psum(shard, BATCH).astype(jnp.float32)
    core = lax.axis_index("core")
    held = low.reshape(parts // 2, 2, rows // parts, width)
    send = lax.dynamic_index_in_dim(held, 1 - core, 1, keepdims=False)
    keep = lax.dynamic_index_in_dim(held, core, 1, keepdims=False)
    got = lax.ppermute(send, "core", [(0, 1), (1, 0)])
    half = (keep.astype(jnp.float32) + got.astype(jnp.float32)).astype(jnp.bfloat16)
    half = half.reshape(rows // 2, width)
    shard = lax.psum_scatter(half, ("seq", "x"), scatter_dimension=0, tiled=True)
    return lax.all_gather(shard, BATCH, axis=0, tiled=True).astype(jnp.float32)


def gather_kernel(*refs, shapes):
    count = len(shapes)
    weights, seq_small, batch_small = refs[:count], refs[count], refs[count + 1]
    fulls = refs[count + 2 : 2 * count + 2]
    seq_out, batch_out, send, recv, small_send, small_recv, local = refs[2 * count + 2 :]
    me, x, core = lax.axis_index("seq"), lax.axis_index("x"), lax.axis_index("core")
    bits = (me // 4, (me // 2) % 2, me % 2, x, core)

    def peer(dim):
        if dim < 3:
            return (me ^ (4 >> dim), x, core)
        return (me, 1 - x, core) if dim == 3 else (me, x, 1 - core)

    others = [((me + d) % 8, x, core) for d in range(1, 8)]
    mates = [(me, (x + dx) % 2, (core + dc) % 2) for dx, dc in ((0, 1), (1, 0), (1, 1))]
    barrier = pltpu.get_barrier_semaphore()
    for device in others + mates:
        pl.semaphore_signal(barrier, inc=1, device_id=device, device_id_type=pl.DeviceIdType.MESH)
    pl.semaphore_wait(barrier, len(others) + len(mates))

    small = []
    quarter = x * 2 + core
    own_seq = pltpu.make_async_copy(seq_small, seq_out.at[me], local.at[0])
    own_batch = pltpu.make_async_copy(batch_small, batch_out.at[quarter], local.at[1])
    own_seq.start()
    own_batch.start()
    for slot, device in enumerate(others):
        small.append(
            pltpu.make_async_remote_copy(
                seq_small, seq_out.at[me], small_send.at[slot], small_recv.at[slot],
                device_id=device, device_id_type=pl.DeviceIdType.MESH,
            )
        )
    for slot, device in enumerate(mates):
        small.append(
            pltpu.make_async_remote_copy(
                batch_small, batch_out.at[quarter], small_send.at[7 + slot], small_recv.at[7 + slot],
                device_id=device, device_id_type=pl.DeviceIdType.MESH,
            )
        )
    for copy in small:
        copy.start()

    chain = WeightGather(gather_jobs(weights, fulls), send, recv, local.at[pl.ds(2, 2 * count)])
    for _ in range(5):
        chain.stage()
    chain.finish()
    for copy in small:
        copy.wait()
    own_seq.wait()
    own_batch.wait()


def gather_early(weights, seq_small, batch_small):
    shapes = [w.shape for w in weights]
    anywhere = pl.BlockSpec(memory_space=pl.ANY)
    jobs = 2 * len(weights)
    outs = pl.pallas_call(
        functools.partial(gather_kernel, shapes=shapes),
        in_specs=[anywhere] * (len(weights) + 2),
        out_specs=[anywhere] * (len(weights) + 2),
        out_shape=[
            jax.ShapeDtypeStruct((2, 2, 2, 2, 2, rows // 4, width), BF) for rows, width in shapes
        ]
        + [
            jax.ShapeDtypeStruct((8,) + seq_small.shape, F32),
            jax.ShapeDtypeStruct((4,) + batch_small.shape, F32),
        ],
        scratch_shapes=[
            pltpu.SemaphoreType.DMA((5 * jobs,)),
            pltpu.SemaphoreType.DMA((5 * jobs,)),
            pltpu.SemaphoreType.DMA((10,)),
            pltpu.SemaphoreType.DMA((10,)),
            pltpu.SemaphoreType.DMA((2 + jobs,)),
        ],
        compiler_params=pltpu.CompilerParams(collective_id=0, has_side_effects=True),
        name="gather_early",
    )(*weights, seq_small, batch_small)
    fulls = [full.reshape(8 * rows, width) for full, (rows, width) in zip(outs, shapes)]
    return fulls, outs[-2], outs[-1]


def paired_tables(positions):
    cos, sin = rotary_tables(positions)
    half = HEAD_DIM // 2
    signed = jnp.concatenate([-sin[:, :half], sin[:, half:]], axis=1)
    return jnp.tile(cos, (1, 2)), jnp.tile(signed, (1, 2))


def on_device(
    layer_input,
    skip_input,
    time_embed,
    lengths,
    cond_drop,
    cotangent,
    skip_weight,
    adaln_weight,
    adaln_bias,
    qkv_weight,
    out_weight,
    up_weight,
    down_weight,
):
    utt_count, frame_span, model_width = layer_input.shape
    head_count = model_width // HEAD_DIM
    row_count = utt_count * frame_span
    seq_here = lax.axis_index("seq")
    seq_count = lax.axis_size("seq")
    frame_count = frame_span * seq_count
    by_heads = (
        seq_count == 8
        and head_count == 16
        and utt_count == 2
        and lax.axis_size(BATCH) == 4
        and frame_span == 512
    )
    local_pos = seq_here * frame_span + jnp.arange(frame_span, dtype=jnp.int32)
    local_live = local_pos[None, :] < lengths[:, None]
    valid_mask = local_live.astype(jnp.float32)
    drop = cond_drop.astype(jnp.float32)
    dropped = drop[:, None] * valid_mask
    frames_live = jnp.minimum(lengths, frame_count).astype(jnp.float32)
    counts = jnp.stack([jnp.sum((1.0 - drop) * frames_live), jnp.sum(drop * frames_live)])
    silu_time = jax.nn.silu(time_embed.astype(jnp.float32)).astype(jnp.bfloat16)
    row_span = adaln_weight.shape[0]
    silu_mine = lax.dynamic_slice_in_dim(silu_time, seq_here * row_span, row_span, 1)
    mod_part = jnp.dot(silu_mine, adaln_weight, preferred_element_type=jnp.float32)
    bias_span = adaln_bias.shape[0]
    bias_here = lax.dynamic_update_slice_in_dim(
        jnp.zeros((mod_part.shape[1],), jnp.float32),
        adaln_bias.astype(jnp.float32),
        seq_here * bias_span,
        0,
    )
    mod_part = mod_part + bias_here
    if by_heads:
        small = jnp.concatenate(
            [
                silu_time.astype(jnp.float32),
                jnp.pad(counts[None, :], ((0, 5), (0, model_width - 2))),
            ],
            axis=0,
        )
        (skip_full, qkv_full), mod_every, small_every = gather_early(
            (skip_weight, qkv_weight), mod_part.reshape(-1, model_width), small
        )
        modulation = jnp.sum(mod_every, axis=0)
        totals = jnp.sum(small_every[:, utt_count, :2], axis=0)
        silu_every = small_every[:, :utt_count].reshape(-1, model_width)
    else:
        modulation = lax.psum(mod_part, "seq")
        totals = lax.psum(counts, BATCH)
        skip_full = gather_weight(skip_weight)
        qkv_full = gather_weight(qkv_weight)
        silu_every = lax.all_gather(silu_time, BATCH, axis=0, tiled=True).astype(jnp.float32)
    modulation = modulation.reshape(utt_count, 6, model_width)
    kept_total = jnp.maximum(totals[0], 1.0)
    drop_total = jnp.maximum(totals[1], 1.0)
    every_count = kept_total + drop_total
    loss_weight = (valid_mask - dropped) * (every_count / (2.0 * kept_total)) + dropped * (
        every_count / (2.0 * drop_total)
    )
    joined = jnp.concatenate([layer_input, skip_input], axis=-1).reshape(row_count, 2 * model_width)
    residual_in = jnp.dot(joined, skip_full, preferred_element_type=jnp.float32).reshape(
        utt_count, frame_span, model_width
    )
    shift_attn = modulation[:, 0][:, None, :]
    scale_attn = modulation[:, 1][:, None, :]
    hat_attn, inv_attn = layer_norm(residual_in)
    normed_attn = (
        (hat_attn * (1.0 + scale_attn) + shift_attn)
        .astype(jnp.bfloat16)
        .reshape(row_count, model_width)
    )
    if by_heads:
        cos_all, sin_all = paired_tables(jnp.arange(frame_count, dtype=jnp.int32))
        cos_here = lax.dynamic_slice_in_dim(cos_all, seq_here * frame_span, frame_span, 0)
        sin_here = lax.dynamic_slice_in_dim(sin_all, seq_here * frame_span, frame_span, 0)
        proj = project_heads(normed_attn, qkv_full, cos_here, sin_here)
        (qkv_all, out_all, lse_all, attended_low), (out_full, up_full, down_full) = attend_forward(
            lengths, proj, out_weight, up_weight, down_weight, frame_span
        )
    else:
        out_full, up_full, down_full = [
            gather_weight(weight) for weight in (out_weight, up_weight, down_weight)
        ]
        projected = jnp.dot(normed_attn, qkv_full, preferred_element_type=jnp.float32).reshape(
            utt_count, frame_span, 3, head_count, HEAD_DIM
        )
        cosine_table, sine_table = rotary_tables(local_pos)
        cosine_table = cosine_table[None, :, None, :]
        sine_table = sine_table[None, :, None, :]
        queries = (rotate_heads(projected[:, :, 0], cosine_table, sine_table) * 0.125).astype(
            jnp.bfloat16
        )
        keys_rot = rotate_heads(projected[:, :, 1], cosine_table, sine_table).astype(jnp.bfloat16)
        values = projected[:, :, 2].astype(jnp.bfloat16)
        start_top = jnp.full((utt_count, head_count, frame_span), MASKED, jnp.float32)
        top_score = start_top
        key_piece = lax.all_gather(keys_rot, "seq", axis=1, tiled=True)
        value_piece = lax.all_gather(values, "seq", axis=1, tiled=True)
        piece_len = key_piece.shape[1]
        piece_live = jnp.arange(piece_len, dtype=jnp.int32)[None, :] < lengths[:, None]
        scores = jnp.einsum("bqhd,bkhd->bhqk", queries, key_piece, preferred_element_type=jnp.float32)
        scores = jnp.where(piece_live[:, None, None, :], scores, MASKED)
        new_top = jnp.maximum(top_score, jnp.max(scores, axis=-1))
        expo = jnp.where(piece_live[:, None, None, :], jnp.exp(scores - new_top[..., None]), 0.0)
        denom = jnp.sum(expo, axis=-1)
        partial_out = jnp.einsum(
            "bhqk,bkhd->bqhd",
            expo.astype(jnp.bfloat16),
            value_piece,
            preferred_element_type=jnp.float32,
        )
        accum = partial_out
        accum, top_score, denom = (accum, new_top, denom)
        attended_full = accum / jnp.transpose(denom, (0, 2, 1))[..., None]
        lse_rows = jnp.transpose(top_score + jnp.log(denom), (0, 2, 1))
        attended_low = attended_full.astype(jnp.bfloat16).reshape(row_count, model_width)
    residual_rows = residual_in.reshape(row_count, model_width)
    cot_rows = cotangent.reshape(row_count, model_width)
    weight_rows = loss_weight.reshape(row_count, 1)
    branch_attn, hidden_act, hidden_slope, grad_branch_ffn, layer_output, grad_gate_ffn = ffn_forward(
        attended_low,
        out_full,
        residual_rows,
        modulation,
        cot_rows,
        weight_rows,
        up_full,
        down_full,
    )
    layer_output = layer_output.reshape(utt_count, frame_span, model_width)
    grad_up, grad_down, grad_mid, grad_attended_flat, grad_out, ffn_sums = ffn_backward(
        attended_low,
        out_full,
        residual_rows,
        branch_attn,
        modulation,
        cot_rows,
        weight_rows,
        grad_branch_ffn,
        hidden_act,
        hidden_slope,
        up_full,
        down_full,
    )
    grad_mid = grad_mid.reshape(utt_count, frame_span, model_width)
    grad_shift_ffn, grad_scale_ffn, grad_gate_attn = ffn_sums[:, 0], ffn_sums[:, 1], ffn_sums[:, 2]
    qkv_back, skip_back = qkv_full, skip_full
    if by_heads:
        grad_projected = attend_backward(
            lengths, grad_attended_flat, qkv_all, out_all, lse_all, cos_all, sin_all, frame_span
        )
    else:
        grad_attended = grad_attended_flat.reshape(
            utt_count, frame_span, head_count, HEAD_DIM
        )
        delta_rows = jnp.sum(grad_attended.astype(jnp.float32) * attended_full, axis=-1)
        lse_all, delta_all = (
            lax.all_gather(lse_rows, "seq", axis=1, tiled=True),
            lax.all_gather(delta_rows, "seq", axis=1, tiled=True),
        )
        key_piece = lax.all_gather(keys_rot, "seq", axis=1, tiled=True)
        value_piece = lax.all_gather(values, "seq", axis=1, tiled=True)
        piece_len = key_piece.shape[1]
        piece_live = jnp.arange(piece_len, dtype=jnp.int32)[None, :] < lengths[:, None]
        probs_low, dscore = block_terms(
            queries, grad_attended, lse_rows, delta_rows, key_piece, value_piece, piece_live
        )
        grad_queries = jnp.einsum(
            "bhqk,bkhd->bqhd", dscore, key_piece, preferred_element_type=jnp.float32
        )
        query_piece = lax.all_gather(queries, "seq", axis=1, tiled=True)
        dout_piece = lax.all_gather(grad_attended, "seq", axis=1, tiled=True)
        probs_low, dscore = block_terms(
            query_piece, dout_piece, lse_all, delta_all, keys_rot, values, local_live
        )
        grad_k = jnp.einsum("bhqk,bqhd->bkhd", dscore, query_piece, preferred_element_type=jnp.float32)
        grad_v = jnp.einsum(
            "bhqk,bqhd->bkhd", probs_low, dout_piece, preferred_element_type=jnp.float32
        )
        grad_q_pre = rotate_heads(grad_queries * 0.125, cosine_table, -sine_table)
        grad_k_pre = rotate_heads(grad_k, cosine_table, -sine_table)
        grad_projected = (
            jnp.stack([grad_q_pre, grad_k_pre, grad_v], axis=2)
            .reshape(row_count, 3 * model_width)
            .astype(jnp.bfloat16)
        )
    grad_qkv = cross(normed_attn, grad_projected)
    grad_normed_attn = back_product(grad_projected, qkv_back).reshape(
        utt_count, frame_span, model_width
    )
    grad_shift_attn = jnp.sum(grad_normed_attn, axis=1)
    grad_scale_attn = jnp.sum(grad_normed_attn * hat_attn, axis=1)
    grad_stream = grad_mid + norm_back(grad_normed_attn * (1.0 + scale_attn), hat_attn, inv_attn)
    grad_stream_low = grad_stream.astype(jnp.bfloat16).reshape(row_count, model_width)
    grad_skip_w = cross(joined, grad_stream_low)
    grad_joined = back_product(grad_stream_low, skip_back)
    grad_input = (
        grad_joined[:, :model_width]
        .reshape(utt_count, frame_span, model_width)
        .astype(jnp.bfloat16)
    )
    grad_skip = (
        grad_joined[:, model_width:]
        .reshape(utt_count, frame_span, model_width)
        .astype(jnp.bfloat16)
    )
    grad_modulation = jnp.stack(
        [
            grad_shift_attn,
            grad_scale_attn,
            grad_gate_attn,
            grad_shift_ffn,
            grad_scale_ffn,
            grad_gate_ffn,
        ],
        axis=1,
    ).reshape(utt_count, 6 * model_width)
    mod_total = lax.psum(grad_modulation, "seq")
    mod_every = lax.all_gather(
        mod_total.astype(jnp.bfloat16), BATCH, axis=0, tiled=True
    ).astype(jnp.float32)
    silu_rows = lax.dynamic_slice_in_dim(silu_every, seq_here * row_span, row_span, 1)
    adaln_rows = jnp.dot(silu_rows.T, mod_every, precision=lax.Precision.HIGHEST)
    bias_rows = lax.dynamic_slice_in_dim(
        jnp.sum(mod_every, axis=0), seq_here * bias_span, bias_span, 0
    )
    summed = [sum_weight(grad) for grad in (grad_skip_w, grad_qkv, grad_out, grad_up, grad_down)]
    results = (summed[0], adaln_rows, bias_rows, summed[1], summed[2], summed[3], summed[4])
    return (
        layer_output,
        grad_input,
        grad_skip,
        results[0],
        results[1],
        results[2],
        results[3],
        results[4],
        results[5],
        results[6],
    )


def solution(mesh):
    count, batch = mesh.shape["seq"], mesh.shape["batch"]
    cores = 2 if batch % 2 == 0 else 1
    split = Mesh(mesh.devices.reshape(count, batch // cores, cores), ("seq",) + BATCH)
    placed = (
        P(BATCH, "seq", None),
        P(BATCH, "seq", None),
        P(BATCH, None),
        P(BATCH),
        P(BATCH),
        P(BATCH, "seq", None),
        P("seq", None),
        P("seq", None),
        P("seq"),
        P("seq", None),
        P("seq", None),
        P("seq", None),
        P("seq", None),
    )
    return jax.shard_map(
        on_device,
        mesh=split,
        in_specs=placed,
        out_specs=(
            P(BATCH, "seq", None),
            P(BATCH, "seq", None),
            P(BATCH, "seq", None),
            P("seq", None),
            P("seq", None),
            P("seq"),
            P("seq", None),
            P("seq", None),
            P("seq", None),
            P("seq", None),
        ),
        check_vma=False,
    )
```

```python
import functools
import jax
import jax.numpy as jnp
from jax import lax
from jax.sharding import Mesh, PartitionSpec as P
from jax.experimental import pallas as pl
from jax.experimental.pallas import tpu as pltpu
HEAD_DIM = 64
EPS = 1e-06
LOG2E = 1.4426950408889634
LN2 = 0.6931471805599453
MASKED = -1e30
BF = jnp.bfloat16
F32 = jnp.float32
VMEM_LIMIT = 60 * 2**20


def nt(left, right):
    return lax.dot_general(left, right, (((1,), (1,)), ((), ())), preferred_element_type=F32)


def nn(left, right):
    return lax.dot_general(left, right, (((1,), (0,)), ((), ())), preferred_element_type=F32)


def head_sums(product, lane):
    first = jnp.sum(jnp.where(lane < 64, product, 0.0), axis=1, keepdims=True)
    second = jnp.sum(jnp.where(lane >= 64, product, 0.0), axis=1, keepdims=True)
    return (first, second)


def lanes_of(rows):
    return lax.broadcasted_iota(jnp.int32, (rows, 128), 1)


def attention_cost(frames, products):
    return pl.CostEstimate(
        flops=2 * products * 2 * frames * frames * 128,
        bytes_accessed=frames * 128 * 2 * 8,
        transcendentals=2 * frames * frames,
    )


def turn_back(grad, cos, sin):
    lane = lanes_of(grad.shape[0])
    turned = jnp.where((lane & 63) < 32, pltpu.roll(grad, 96, 1), pltpu.roll(grad, 32, 1))
    return grad * cos - turned * sin


def three(column, lane, at):
    high = column.astype(BF).astype(F32)
    rest = column - high
    mid = rest.astype(BF).astype(F32)
    low = rest - mid
    return jnp.where(lane == at, -high, jnp.where(lane == at + 1, -mid, jnp.where(lane == at + 2, -low, 0.0)))


MESH_IDS = pl.DeviceIdType.MESH


def seq_flip(flip):
    return (lax.axis_index("seq") ^ flip, lax.axis_index("x"), lax.axis_index("core"))


def greet(devices):
    barrier = pltpu.get_barrier_semaphore()
    for device in devices:
        pl.semaphore_signal(barrier, inc=1, device_id=device, device_id_type=MESH_IDS)
    pl.semaphore_wait(barrier, len(devices))


def remote(source, target, send, recv, device):
    return pltpu.make_async_remote_copy(
        source, target, send, recv, device_id=device, device_id_type=MESH_IDS
    )


class WeightGather:
    def __init__(self, jobs, send, recv, local):
        self.jobs, self.send, self.recv, self.local = jobs, send, recv, local
        me, x, core = lax.axis_index("seq"), lax.axis_index("x"), lax.axis_index("core")
        self.bits = (me // 4, (me // 2) % 2, me % 2, x, core)
        self.copies = [[] for _ in jobs]
        self.owns = []

    def peer(self, dim):
        me, x, core = lax.axis_index("seq"), lax.axis_index("x"), lax.axis_index("core")
        if dim < 3:
            return (me ^ (4 >> dim), x, core)
        return (me, 1 - x, core) if dim == 3 else (me, x, 1 - core)

    def stage(self):
        for index, (full, cols, source, order) in enumerate(self.jobs):
            at = len(self.copies[index])
            tail = (slice(None), cols)
            if at == 0:
                own = pltpu.make_async_copy(
                    source, full.at[self.bits + tail], self.local.at[index]
                )
                own.start()
                self.owns.append(own)
            else:
                if at == 1:
                    self.owns[index].wait()
                self.copies[index][at - 1].wait_recv()
            where = tuple(
                slice(None) if d in order[:at] else self.bits[d] for d in range(5)
            ) + tail
            copy = remote(
                source if at == 0 else full.at[where],
                full.at[where],
                self.send.at[index * 5 + at],
                self.recv.at[index * 5 + at],
                self.peer(order[at]),
            )
            copy.start()
            self.copies[index].append(copy)

    def finish(self):
        for chain in self.copies:
            chain[-1].wait_recv()
        for chain in self.copies:
            for copy in chain:
                copy.wait_send()


def gather_jobs(weights, fulls):
    quarter = lax.axis_index("x") * 2 + lax.axis_index("core")
    jobs = []
    for weight, full in zip(weights, fulls):
        rows, width = weight.shape
        span, half = rows // 4, width // 2
        for side in range(2):
            cols = pl.ds(side * half, half)
            source = weight.at[pl.ds(quarter * span, span), cols]
            jobs.append((full, cols, source, (0, 1, 2, 3, 4) if side == 0 else (0, 1, 3, 2, 4)))
    return jobs


def attend_forward_kernel(
    len_ref, proj, out_w, up_w, down_w,
    qkv_all, o_all, lse_ref, att, out_full, up_full, down_full,
    qkv, outs, ka, kb, vta, vtb,
    wsend, wrecv, wlocal, qsend, qrecv, qlocal, osend, orecv, olocal, slocal,
    *, span, bq, bk,
):
    me, x, core = lax.axis_index("seq"), lax.axis_index("x"), lax.axis_index("core")
    frames = qkv.shape[2]
    mine = pl.ds(pl.multiple_of(me * span, span), span)
    my_cols = pl.ds(pl.multiple_of(me * 128, 128), 128)
    flips = (7, 6, 5, 4, 3, 2, 1)
    greet([seq_flip(flip) for flip in flips] + [(me, 1 - x, core), (me, x, 1 - core)])
    weights = WeightGather(
        gather_jobs((out_w, up_w, down_w), (out_full, up_full, down_full)), wsend, wrecv, wlocal
    )

    def send_heads(utt):
        rows = pl.ds(utt * span, span)
        own = pltpu.make_async_copy(
            proj.at[:, rows, my_cols], qkv.at[utt, :, mine, :], qlocal.at[utt]
        )
        own.start()
        copies = []
        for flip in flips:
            there = me ^ flip
            cols = pl.ds(pl.multiple_of(there * 128, 128), 128)
            copy = remote(
                proj.at[:, rows, cols],
                qkv.at[utt, :, mine, :],
                qsend.at[utt * 8 + flip],
                qrecv.at[utt * 8 + flip],
                seq_flip(flip),
            )
            copy.start()
            copies.append(copy)
        return own, copies

    def arrive(sent):
        own, copies = sent
        own.wait()
        for copy in copies:
            copy.wait_recv()

    def attend(utt, between):
        length = len_ref[utt]
        save = pltpu.make_async_copy(qkv.at[utt], qkv_all.at[utt], slocal.at[utt])
        save.start()

        def build(j, carry):
            rows = pl.ds(pl.multiple_of(j * bk, bk), bk)
            lane = lanes_of(bk)
            pos = j * bk + lax.broadcasted_iota(jnp.int32, (bk, 128), 0)
            bias = jnp.where(pos < length, 0.0, MASKED)
            keys = qkv[utt, 1, rows, :].astype(F32)
            ka[rows, :] = jnp.where(lane < 64, keys, jnp.where(lane == 64, bias, 0.0)).astype(BF)
            kb[rows, :] = jnp.where(lane >= 64, keys, jnp.where(lane == 0, bias, 0.0)).astype(BF)
            vals = qkv[utt, 2, rows, :].astype(F32)
            vta[:, rows] = jnp.where(lane < 64, vals, 1.0).T.astype(BF)
            vtb[:, rows] = jnp.where(lane >= 64, vals, 1.0).T.astype(BF)
            return carry

        lax.fori_loop(0, frames // bk, build, 0)

        def block(i, carry):
            here = pl.ds(pl.multiple_of(i * bq, bq), bq)
            lane = lanes_of(bq)
            queries = qkv[utt, 0, here, :].astype(F32)
            qa = jnp.where(lane < 64, queries, jnp.where(lane == 64, 1.0, 0.0)).astype(BF)
            qb = jnp.where(lane >= 64, queries, jnp.where(lane == 0, 1.0, 0.0)).astype(BF)

            def body(j, inner):
                rows = pl.ds(pl.multiple_of(j * bk, bk), bk)
                result = []
                scores = [nt(ka[rows, :], qa), nt(kb[rows, :], qb)]
                for score, vt, (top, acc) in zip(scores, (vta, vtb), inner):
                    new = jnp.maximum(top, jnp.max(score, axis=0, keepdims=True))
                    probs = jnp.exp2(score - new).astype(BF)
                    acc = acc * jnp.exp2(top - new) + nn(vt[:, rows], probs)
                    result.append((new, acc))
                return tuple(result)

            start = (jnp.full((1, bq), MASKED, F32), jnp.zeros((128, bq), F32))
            (top_a, acc_a), (top_b, acc_b) = lax.fori_loop(0, frames // bk, body, (start, start))
            sum_a, sum_b = acc_a[64:65], acc_b[0:1]
            both = jnp.concatenate([acc_a[:64] / sum_a, acc_b[64:] / sum_b], axis=0)
            outs[utt, here, :] = both.T.astype(BF)
            lse_ref[utt, :, here] = jnp.concatenate(
                [top_a + jnp.log2(sum_a), top_b + jnp.log2(sum_b), jnp.zeros((6, bq), F32)],
                axis=0,
            )
            for part in range(bq // span):
                there = i * (bq // span) + part
                rows = pl.ds(pl.multiple_of(there * span, span), span)
                target = att.at[pl.ds(utt * span, span), my_cols]

                @pl.when(there != me)
                def _():
                    remote(
                        outs.at[utt, rows, :],
                        target,
                        osend.at[utt * 8 + (there ^ me)],
                        orecv.at[utt * 8 + (there ^ me)],
                        (there, x, core),
                    ).start()

                @pl.when(there == me)
                def _():
                    pltpu.make_async_copy(outs.at[utt, rows, :], target, olocal.at[utt]).start()

            return carry

        half = frames // bq // 2
        lax.fori_loop(0, half, block, 0)
        between()
        lax.fori_loop(half, 2 * half, block, 0)
        keep = pltpu.make_async_copy(outs.at[utt], o_all.at[utt], slocal.at[2 + utt])
        keep.start()
        return [save, keep]

    weights.stage()
    first = send_heads(0)
    arrive(first)
    second = send_heads(1)
    weights.stage()
    saves = attend(0, weights.stage)
    weights.stage()
    arrive(second)
    saves += attend(1, weights.stage)
    for sent in (first, second):
        for copy in sent[1]:
            copy.wait_send()
    weights.finish()
    for save in saves:
        save.wait()
    for utt in range(2):
        target = att.at[pl.ds(utt * span, span), my_cols]
        pltpu.make_async_copy(outs.at[utt, mine, :], target, olocal.at[utt]).wait()
        for flip in flips:
            copy = remote(
                outs.at[utt, mine, :],
                target,
                osend.at[utt * 8 + flip],
                orecv.at[utt * 8 + flip],
                seq_flip(flip),
            )
            copy.wait_send()
            copy.wait_recv()


def attend_forward(lengths, proj, out_w, up_w, down_w, span, bq=1024, bk=512):
    rows, width = proj.shape[1:]
    frames = 8 * span
    anywhere = pl.BlockSpec(memory_space=pl.ANY)
    vmem = pl.BlockSpec(memory_space=pltpu.VMEM)
    full = lambda w: jax.ShapeDtypeStruct((2, 2, 2, 2, 2, w.shape[0] // 4, w.shape[1]), BF)
    dma = pltpu.SemaphoreType.DMA
    outs = pl.pallas_call(
        functools.partial(attend_forward_kernel, span=span, bq=bq, bk=bk),
        in_specs=[pl.BlockSpec(memory_space=pltpu.SMEM)] + [anywhere] * 4,
        out_specs=[anywhere, anywhere, vmem] + [anywhere] * 4,
        out_shape=[
            jax.ShapeDtypeStruct((2, 3, frames, 128), BF),
            jax.ShapeDtypeStruct((2, frames, 128), BF),
            jax.ShapeDtypeStruct((2, 8, frames), F32),
            jax.ShapeDtypeStruct((rows, width), BF),
            full(out_w),
            full(up_w),
            full(down_w),
        ],
        scratch_shapes=[
            pltpu.VMEM((2, 3, frames, 128), BF),
            pltpu.VMEM((2, frames, 128), BF),
            pltpu.VMEM((frames, 128), BF),
            pltpu.VMEM((frames, 128), BF),
            pltpu.VMEM((128, frames), BF),
            pltpu.VMEM((128, frames), BF),
            dma((30,)),
            dma((30,)),
            dma((6,)),
            dma((16,)),
            dma((16,)),
            dma((2,)),
            dma((16,)),
            dma((16,)),
            dma((2,)),
            dma((4,)),
        ],
        compiler_params=pltpu.CompilerParams(
            vmem_limit_bytes=VMEM_LIMIT, collective_id=1, has_side_effects=True
        ),
        cost_estimate=attention_cost(frames, 4),
        name="attend_forward",
    )(lengths, proj, out_w, up_w, down_w)
    fulls = [outs[4 + i].reshape(8 * w.shape[0], w.shape[1]) for i, w in enumerate((out_w, up_w, down_w))]
    return outs[:4], fulls


def attend_backward_kernel(
    len_ref, dout, qkv_all, o_all, lse_ref, cos_ref, sin_ref,
    grads,
    qkv, outs, douts, qa, qb, da, db, qt, dt, dqa, dqb,
    dsend, drecv, dlocal, gsend, grecv, glocal, load,
    *, span, block,
):
    me, x, core = lax.axis_index("seq"), lax.axis_index("x"), lax.axis_index("core")
    frames = qkv.shape[2]
    width = grads.shape[1] // 3
    count = frames // block
    mine = pl.ds(pl.multiple_of(me * span, span), span)
    flips = (7, 6, 5, 4, 3, 2, 1)
    greet([seq_flip(flip) for flip in flips])
    loads = []
    for utt in range(2):
        loads.append(
            [
                pltpu.make_async_copy(qkv_all.at[utt], qkv.at[utt], load.at[utt]),
                pltpu.make_async_copy(o_all.at[utt], outs.at[utt], load.at[2 + utt]),
            ]
        )
        for copy in loads[-1]:
            copy.start()

    def send_heads(utt):
        rows = pl.ds(utt * span, span)
        my_cols = pl.ds(pl.multiple_of(me * 128, 128), 128)
        own = pltpu.make_async_copy(dout.at[rows, my_cols], douts.at[utt, mine, :], dlocal.at[utt])
        own.start()
        copies = []
        for flip in flips:
            cols = pl.ds(pl.multiple_of((me ^ flip) * 128, 128), 128)
            copy = remote(
                dout.at[rows, cols],
                douts.at[utt, mine, :],
                dsend.at[utt * 8 + flip],
                drecv.at[utt * 8 + flip],
                seq_flip(flip),
            )
            copy.start()
            copies.append(copy)
        return own, copies

    def arrive(sent):
        own, copies = sent
        own.wait()
        for copy in copies:
            copy.wait_recv()

    def slot(utt, part, flip):
        return (utt * 3 + part) * 8 + flip

    def target(utt, part):
        cols = pl.ds(pl.multiple_of(part * width + me * 128, 128), 128)
        return grads.at[pl.ds(utt * span, span), cols]

    def send_grads(utt, part, there):
        rows = pl.ds(pl.multiple_of(there * span, span), span)

        @pl.when(there != me)
        def _():
            at = slot(utt, part, there ^ me)
            remote(
                qkv.at[utt, part, rows, :],
                target(utt, part),
                gsend.at[at],
                grecv.at[at],
                (there, x, core),
            ).start()

        @pl.when(there == me)
        def _():
            pltpu.make_async_copy(
                qkv.at[utt, part, rows, :], target(utt, part), glocal.at[utt * 3 + part]
            ).start()

    def differentiate(utt):
        length = len_ref[utt]

        def build(j, carry):
            rows = pl.ds(pl.multiple_of(j * block, block), block)
            lane = lanes_of(block)
            queries = qkv[utt, 0, rows, :].astype(F32)
            grad = douts[utt, rows, :].astype(F32)
            delta_a, delta_b = head_sums(grad * outs[utt, rows, :].astype(F32), lane)
            lse = lse_ref[utt, :, rows].T
            one_a, one_b = lse[:, 0:1], lse[:, 1:2]
            qa[rows, :] = jnp.where(
                lane < 64, queries, jnp.where(lane == 67, 1.0, three(one_a, lane, 64))
            ).astype(BF)
            qb[rows, :] = jnp.where(
                lane >= 64, queries, jnp.where(lane == 3, 1.0, three(one_b, lane, 0))
            ).astype(BF)
            da[rows, :] = jnp.where(lane < 64, grad, three(delta_a, lane, 64)).astype(BF)
            db[rows, :] = jnp.where(lane >= 64, grad, three(delta_b, lane, 0)).astype(BF)
            qt[:, rows] = queries.T.astype(BF)
            dt[:, rows] = grad.T.astype(BF)
            dqa[rows, :] = jnp.zeros((block, 128), F32)
            dqb[rows, :] = jnp.zeros((block, 128), F32)
            return carry

        lax.fori_loop(0, count, build, 0)

        def keys_block(i, carry):
            here = pl.ds(pl.multiple_of(i * block, block), block)
            lane = lanes_of(block)
            pos = i * block + lax.broadcasted_iota(jnp.int32, (block, 128), 0)
            bias = jnp.where(pos < length, 0.0, MASKED)
            keys = qkv[utt, 1, here, :].astype(F32)
            vals = qkv[utt, 2, here, :].astype(F32)
            ones_a = jnp.where(lane < 67, 1.0, 0.0)
            ones_b = jnp.where(lane < 3, 1.0, 0.0)
            ka = jnp.where(lane < 64, keys, jnp.where(lane == 67, bias, ones_a)).astype(BF)
            kb = jnp.where(lane >= 64, keys, jnp.where(lane == 3, bias, ones_b)).astype(BF)
            va = jnp.where(lane < 64, vals, ones_a).astype(BF)
            vb = jnp.where(lane >= 64, vals, ones_b).astype(BF)

            def body(j, inner):
                rows = pl.ds(pl.multiple_of(j * block, block), block)
                result = []
                for head, (qh, dh, kh, vh, dq) in enumerate(
                    ((qa, da, ka, va, dqa), (qb, db, kb, vb, dqb))
                ):
                    part = slice(head * 64, head * 64 + 64)
                    probs = jnp.exp2(nt(qh[rows, :], kh))
                    grad = (probs * nt(dh[rows, :], vh)).astype(BF)
                    dv = inner[2 * head + 1] + nn(dt[:, rows], probs.astype(BF))[part]
                    dk = inner[2 * head] + nn(qt[:, rows], grad)[part]
                    dq[rows, :] += nn(grad, kh)
                    result += [dk, dv]
                return tuple(result)

            zero = jnp.zeros((64, block), F32)
            dk_a, dv_a, dk_b, dv_b = lax.fori_loop(0, count, body, (zero,) * 4)
            dk = jnp.concatenate([dk_a, dk_b], axis=0).T * LN2
            dv = jnp.concatenate([dv_a, dv_b], axis=0).T
            qkv[utt, 1, here, :] = turn_back(dk, cos_ref[here, :], sin_ref[here, :]).astype(BF)
            qkv[utt, 2, here, :] = dv.astype(BF)
            for step in range(block // span):
                there = i * (block // span) + step
                send_grads(utt, 1, there)
                send_grads(utt, 2, there)
            return carry

        lax.fori_loop(0, count, keys_block, 0)

        def finish(i, carry):
            here = pl.ds(pl.multiple_of(i * block, block), block)
            lane = lanes_of(block)
            dq = jnp.where(lane < 64, dqa[here, :], dqb[here, :]) * 0.125
            qkv[utt, 0, here, :] = turn_back(dq, cos_ref[here, :], sin_ref[here, :]).astype(BF)
            for step in range(block // span):
                send_grads(utt, 0, i * (block // span) + step)
            return carry

        lax.fori_loop(0, count, finish, 0)

    first = send_heads(0)
    for copy in loads[0]:
        copy.wait()
    arrive(first)
    second = send_heads(1)
    differentiate(0)
    for copy in loads[1]:
        copy.wait()
    arrive(second)
    differentiate(1)
    for sent in (first, second):
        for copy in sent[1]:
            copy.wait_send()
    for utt in range(2):
        for part in range(3):
            own = qkv.at[utt, part, mine, :]
            pltpu.make_async_copy(own, target(utt, part), glocal.at[utt * 3 + part]).wait()
            for flip in flips:
                at = slot(utt, part, flip)
                copy = remote(own, target(utt, part), gsend.at[at], grecv.at[at], seq_flip(flip))
                copy.wait_send()
                copy.wait_recv()


def attend_backward(lengths, dout, qkv_all, o_all, lse, cos, sin, span, block=1024):
    frames = 8 * span
    rows, width = dout.shape
    anywhere = pl.BlockSpec(memory_space=pl.ANY)
    vmem = pl.BlockSpec(memory_space=pltpu.VMEM)
    dma = pltpu.SemaphoreType.DMA
    return pl.pallas_call(
        functools.partial(attend_backward_kernel, span=span, block=block),
        in_specs=[pl.BlockSpec(memory_space=pltpu.SMEM)] + [anywhere] * 3 + [vmem] * 3,
        out_specs=anywhere,
        out_shape=jax.ShapeDtypeStruct((rows, 3 * width), BF),
        scratch_shapes=[
            pltpu.VMEM((2, 3, frames, 128), BF),
            pltpu.VMEM((2, frames, 128), BF),
            pltpu.VMEM((2, frames, 128), BF),
        ]
        + [pltpu.VMEM((frames, 128), BF)] * 4
        + [pltpu.VMEM((128, frames), BF)] * 2
        + [pltpu.VMEM((frames, 128), F32)] * 2
        + [dma((16,)), dma((16,)), dma((2,)), dma((48,)), dma((48,)), dma((6,)), dma((4,))],
        compiler_params=pltpu.CompilerParams(
            vmem_limit_bytes=VMEM_LIMIT, collective_id=2, has_side_effects=True
        ),
        cost_estimate=attention_cost(frames, 10),
        name="attend_backward",
    )(lengths, dout, qkv_all, o_all, lse, cos, sin)


def layer_norm(stream):
    centre = stream - jnp.mean(stream, axis=-1, keepdims=True)
    spread = jnp.mean(centre * centre, axis=-1, keepdims=True)
    inverse = lax.rsqrt(spread + EPS)
    return (centre * inverse, inverse)


def norm_back(grad_normed, normed, inverse):
    first_mean = jnp.mean(grad_normed, axis=-1, keepdims=True)
    second_mean = jnp.mean(grad_normed * normed, axis=-1, keepdims=True)
    return inverse * (grad_normed - first_mean - normed * second_mean)


def tn(left, right):
    return lax.dot_general(left, right, (((0,), (0,)), ((), ())), preferred_element_type=F32)


GELU_C = 0.7978845608028654
GELU_A = 0.044715


def gelu_and_slope(z):
    square = z * z
    turn = jnp.tanh(GELU_C * z * (1.0 + GELU_A * square))
    half = 0.5 * (1.0 + turn)
    slope = half + 0.5 * z * (1.0 - turn * turn) * (GELU_C * (1.0 + 3.0 * GELU_A * square))
    return z * half, slope


def row_blocks(rows):
    block = min(rows, 256)
    return [(at, slice(at, at + block)) for at in range(0, rows, block)]


def ffn_forward_kernel(
    att_ref, outw_ref, res_ref, mod_ref, cot_ref, weight_ref, up_ref, down_ref,
    branch_ref, act_ref, slope_ref, gb_ref, out_ref, gate_ref, normed, acc,
):
    step = pl.program_id(0)
    rows = att_ref.shape[0]
    span = rows // mod_ref.shape[0]

    @pl.when(step == 0)
    def _():
        for at, part in row_blocks(span):
            for utt in range(mod_ref.shape[0]):
                here = slice(utt * span + part.start, utt * span + part.stop)
                mod = mod_ref[utt]
                branch = nn(att_ref[here, :], outw_ref[...])
                branch_ref[here, :] = branch
                hat, _ = layer_norm(res_ref[here, :] + mod[2:3] * branch)
                normed[here, :] = (hat * (1.0 + mod[4:5]) + mod[3:4]).astype(BF)
        acc[...] = jnp.zeros_like(acc)

    for _, part in row_blocks(rows):
        act, slope = gelu_and_slope(nn(normed[part, :], up_ref[...]))
        act = act.astype(BF)
        act_ref[part, :] = act
        slope_ref[part, :] = slope.astype(BF)
        acc[part, :] += nn(act, down_ref[...])

    @pl.when(step == pl.num_programs(0) - 1)
    def _():
        for utt in range(mod_ref.shape[0]):
            mod = mod_ref[utt]
            total = jnp.zeros((1, acc.shape[1]), F32)
            for _, part in row_blocks(span):
                here = slice(utt * span + part.start, utt * span + part.stop)
                branch = acc[here, :]
                mid = res_ref[here, :] + mod[2:3] * branch_ref[here, :]
                out_ref[here, :] = (mid + mod[5:6] * branch).astype(BF)
                upstream = cot_ref[here, :].astype(F32) * weight_ref[here, :]
                gb_ref[here, :] = (upstream * mod[5:6]).astype(BF)
                total += jnp.sum(upstream * branch, axis=0, keepdims=True)
            gate_ref[utt : utt + 1, :] = total


def ffn_backward_kernel(
    att_ref, outw_ref, res_ref, branch_ref, mod_ref, cot_ref, weight_ref, gb_ref,
    act_ref, slope_ref, up_ref, down_ref,
    gup_ref, gdown_ref, gmid_ref, gatt_ref, gout_ref, sums_ref, normed, acc, gba,
):
    step = pl.program_id(0)
    rows = att_ref.shape[0]
    utts = mod_ref.shape[0]
    span = rows // utts

    def hat_of(here, mod):
        return layer_norm(res_ref[here, :] + mod[2:3] * branch_ref[here, :])

    @pl.when(step == 0)
    def _():
        for utt in range(utts):
            mod = mod_ref[utt]
            for _, part in row_blocks(span):
                here = slice(utt * span + part.start, utt * span + part.stop)
                hat, _ = hat_of(here, mod)
                normed[here, :] = (hat * (1.0 + mod[4:5]) + mod[3:4]).astype(BF)
        acc[...] = jnp.zeros_like(acc)

    pieces = []
    for _, part in row_blocks(rows):
        grad = nt(gb_ref[part, :], down_ref[...]) * slope_ref[part, :].astype(F32)
        grad = grad.astype(BF)
        acc[part, :] += nt(grad, up_ref[...])
        pieces.append(grad)
    gdown_ref[...] = tn(act_ref[...], gb_ref[...]).astype(BF)
    gup_ref[...] = tn(normed[...], jnp.concatenate(pieces, axis=0)).astype(BF)

    @pl.when(step == pl.num_programs(0) - 1)
    def _():
        for utt in range(utts):
            mod = mod_ref[utt]
            width = acc.shape[1]
            shift = jnp.zeros((1, width), F32)
            scale = jnp.zeros((1, width), F32)
            gate = jnp.zeros((1, width), F32)
            for _, part in row_blocks(span):
                here = slice(utt * span + part.start, utt * span + part.stop)
                hat, inverse = hat_of(here, mod)
                grad = acc[here, :]
                shift += jnp.sum(grad, axis=0, keepdims=True)
                scale += jnp.sum(grad * hat, axis=0, keepdims=True)
                upstream = cot_ref[here, :].astype(F32) * weight_ref[here, :]
                mid = upstream + norm_back(grad * (1.0 + mod[4:5]), hat, inverse)
                gmid_ref[here, :] = mid
                gate += jnp.sum(mid * branch_ref[here, :], axis=0, keepdims=True)
                low = (mid * mod[2:3]).astype(BF)
                gba[here, :] = low
                gatt_ref[here, :] = nt(low, outw_ref[...]).astype(BF)
            sums_ref[utt, 0:1, :] = shift
            sums_ref[utt, 1:2, :] = scale
            sums_ref[utt, 2:3, :] = gate
        gout_ref[...] = tn(att_ref[...], gba[...]).astype(BF)


def whole_spec(shape):
    zeros = (0,) * len(shape)
    return pl.BlockSpec(shape, lambda i: zeros, pipeline_mode=pl.Buffered(1))


def ffn_forward(att, outw, res, mods, cot, weight, up, down, chunk=512):
    rows, width = res.shape
    hidden = up.shape[1]
    whole = [whole_spec(a.shape) for a in (att, outw, res, mods, cot, weight)]
    col = pl.BlockSpec((rows, chunk), lambda i: (0, i))
    utts = mods.shape[0]
    return pl.pallas_call(
        ffn_forward_kernel,
        grid=(hidden // chunk,),
        in_specs=whole
        + [
            pl.BlockSpec((width, chunk), lambda i: (0, i)),
            pl.BlockSpec((chunk, width), lambda i: (i, 0)),
        ],
        out_specs=[
            whole_spec((rows, width)),
            col,
            col,
            whole_spec((rows, width)),
            whole_spec((rows, width)),
            whole_spec((utts, width)),
        ],
        out_shape=[
            jax.ShapeDtypeStruct((rows, width), F32),
            jax.ShapeDtypeStruct((rows, hidden), BF),
            jax.ShapeDtypeStruct((rows, hidden), BF),
            jax.ShapeDtypeStruct((rows, width), BF),
            jax.ShapeDtypeStruct((rows, width), BF),
            jax.ShapeDtypeStruct((utts, width), F32),
        ],
        scratch_shapes=[pltpu.VMEM((rows, width), BF), pltpu.VMEM((rows, width), F32)],
        compiler_params=pltpu.CompilerParams(vmem_limit_bytes=VMEM_LIMIT),
        cost_estimate=pl.CostEstimate(
            flops=2 * rows * width * (width + 2 * hidden),
            bytes_accessed=60 * 2**20,
            transcendentals=rows * hidden,
        ),
        name="ffn_forward",
    )(att, outw, res, mods, cot, weight, up, down)


def ffn_backward(att, outw, res, branch, mods, cot, weight, gb, act, slope, up, down, chunk=512):
    rows, width = res.shape
    hidden = up.shape[1]
    utts = mods.shape[0]
    whole = [whole_spec(a.shape) for a in (att, outw, res, branch, mods, cot, weight, gb)]
    col = pl.BlockSpec((rows, chunk), lambda i: (0, i))
    upspec = pl.BlockSpec((width, chunk), lambda i: (0, i))
    downspec = pl.BlockSpec((chunk, width), lambda i: (i, 0))
    return pl.pallas_call(
        ffn_backward_kernel,
        grid=(hidden // chunk,),
        in_specs=whole + [col, col, upspec, downspec],
        out_specs=[
            upspec,
            downspec,
            whole_spec((rows, width)),
            whole_spec((rows, width)),
            whole_spec((width, width)),
            whole_spec((utts, 8, width)),
        ],
        out_shape=[
            jax.ShapeDtypeStruct((width, hidden), BF),
            jax.ShapeDtypeStruct((hidden, width), BF),
            jax.ShapeDtypeStruct((rows, width), F32),
            jax.ShapeDtypeStruct((rows, width), BF),
            jax.ShapeDtypeStruct((width, width), BF),
            jax.ShapeDtypeStruct((utts, 8, width), F32),
        ],
        scratch_shapes=[
            pltpu.VMEM((rows, width), BF),
            pltpu.VMEM((rows, width), F32),
            pltpu.VMEM((rows, width), BF),
        ],
        compiler_params=pltpu.CompilerParams(vmem_limit_bytes=VMEM_LIMIT),
        cost_estimate=pl.CostEstimate(
            flops=2 * rows * width * (2 * width + 4 * hidden),
            bytes_accessed=90 * 2**20,
            transcendentals=0,
        ),
        name="ffn_backward",
    )(att, outw, res, branch, mods, cot, weight, gb, act, slope, up, down)


def enter_kernel(
    in_ref, skip_ref, skip_w, qkv_w, mod_ref, cos_ref, sin_ref, res_ref, proj_ref
):
    width = in_ref.shape[1]
    mod = mod_ref[0]
    residual = nn(in_ref[...], skip_w[:width, :]) + nn(skip_ref[...], skip_w[width:, :])
    res_ref[...] = residual
    hat, _ = layer_norm(residual)
    normed = (hat * (1.0 + mod[1:2]) + mod[0:1]).astype(BF)
    lane = lanes_of(in_ref.shape[0])
    cos, sin = cos_ref[...], sin_ref[...]
    for part in range(3):
        projected = nn(normed, qkv_w[:, part * width : (part + 1) * width])
        for group in range(width // 128):
            cols = slice(group * 128, group * 128 + 128)
            piece = projected[:, cols]
            if part < 2:
                turned = jnp.where(
                    (lane & 63) < 32, pltpu.roll(piece, 96, 1), pltpu.roll(piece, 32, 1)
                )
                piece = piece * cos + turned * sin
            if part == 0:
                piece = piece * (0.125 * LOG2E)
            proj_ref[part, :, cols] = piece.astype(BF)


def enter_layer(first, second, skip_w, qkv_w, mods, cos, sin, block=256):
    rows, width = first.shape
    steps = rows // mods.shape[0] // block
    part = pl.BlockSpec((block, width), lambda i: (i, 0))
    table = pl.BlockSpec((block, 128), lambda i: (i % steps, 0))
    return pl.pallas_call(
        enter_kernel,
        grid=(rows // block,),
        in_specs=[
            part,
            part,
            whole_spec(skip_w.shape),
            whole_spec(qkv_w.shape),
            pl.BlockSpec((1,) + mods.shape[1:], lambda i: (i // steps, 0, 0)),
            table,
            table,
        ],
        out_specs=[part, pl.BlockSpec((3, block, width), lambda i: (0, i, 0))],
        out_shape=[
            jax.ShapeDtypeStruct((rows, width), F32),
            jax.ShapeDtypeStruct((3, rows, width), BF),
        ],
        compiler_params=pltpu.CompilerParams(vmem_limit_bytes=VMEM_LIMIT),
        cost_estimate=pl.CostEstimate(
            flops=2 * rows * (skip_w.size + qkv_w.size),
            bytes_accessed=40 * 2**20,
            transcendentals=0,
        ),
        name="enter_layer",
    )(first, second, skip_w, qkv_w, mods, cos, sin)


def leave_kernel(
    grad_ref, qkv_w, skip_w, res_ref, mid_ref, mod_ref, in_ref, skip_ref,
    gin_ref, gskip_ref, sums_ref, gqkv_ref, gw_ref, normed, stream,
):
    step = pl.program_id(0)
    rows, width = res_ref.shape
    utts = mod_ref.shape[0]
    span = rows // utts

    @pl.when(step == 0)
    def _():
        for utt in range(utts):
            mod = mod_ref[utt]
            shift = jnp.zeros((1, width), F32)
            scale = jnp.zeros((1, width), F32)
            for _, part in row_blocks(span):
                here = slice(utt * span + part.start, utt * span + part.stop)
                hat, inverse = layer_norm(res_ref[here, :])
                normed[here, :] = (hat * (1.0 + mod[1:2]) + mod[0:1]).astype(BF)
                grad = nt(grad_ref[here, :], qkv_w[...])
                shift += jnp.sum(grad, axis=0, keepdims=True)
                scale += jnp.sum(grad * hat, axis=0, keepdims=True)
                total = mid_ref[here, :] + norm_back(grad * (1.0 + mod[1:2]), hat, inverse)
                low = total.astype(BF)
                stream[here, :] = low
                gin_ref[here, :] = nt(low, skip_w[:width, :]).astype(BF)
                gskip_ref[here, :] = nt(low, skip_w[width:, :]).astype(BF)
            sums_ref[utt, 0:1, :] = shift
            sums_ref[utt, 1:2, :] = scale

    chunk = gqkv_ref.shape[1]
    cols = pl.ds(pl.multiple_of(step * chunk, chunk), chunk)
    gqkv_ref[...] = tn(normed[...], grad_ref[:, cols]).astype(BF)
    part = gw_ref.shape[2]
    here = pl.ds(pl.multiple_of(step * part, part), part)
    gw_ref[0] = tn(in_ref[...], stream[:, here]).astype(BF)
    gw_ref[1] = tn(skip_ref[...], stream[:, here]).astype(BF)


def leave_layer(grads, qkv_w, skip_w, res, mid, mods, first, second, steps=4):
    rows, width = res.shape
    utts = mods.shape[0]
    ins = (grads, qkv_w, skip_w, res, mid, mods, first, second)
    outs = pl.pallas_call(
        leave_kernel,
        grid=(steps,),
        in_specs=[whole_spec(a.shape) for a in ins],
        out_specs=[
            whole_spec((rows, width)),
            whole_spec((rows, width)),
            whole_spec((utts, 8, width)),
            pl.BlockSpec((width, 3 * width // steps), lambda i: (0, i)),
            pl.BlockSpec((2, width, width // steps), lambda i: (0, 0, i)),
        ],
        out_shape=[
            jax.ShapeDtypeStruct((rows, width), BF),
            jax.ShapeDtypeStruct((rows, width), BF),
            jax.ShapeDtypeStruct((utts, 8, width), F32),
            jax.ShapeDtypeStruct((width, 3 * width), BF),
            jax.ShapeDtypeStruct((2, width, width), BF),
        ],
        scratch_shapes=[pltpu.VMEM((rows, width), BF), pltpu.VMEM((rows, width), BF)],
        compiler_params=pltpu.CompilerParams(vmem_limit_bytes=VMEM_LIMIT),
        cost_estimate=pl.CostEstimate(
            flops=4 * rows * (skip_w.size + qkv_w.size),
            bytes_accessed=60 * 2**20,
            transcendentals=0,
        ),
        name="leave_layer",
    )(*ins)
    return tuple(outs[:4]) + (outs[4].reshape(2 * width, width),)


class GradSum:
    def __init__(self, jobs, send, recv, local):
        self.jobs, self.send, self.recv, self.local = jobs, send, recv, local
        me, x, core = lax.axis_index("seq"), lax.axis_index("x"), lax.axis_index("core")
        self.bits = (me // 4, (me // 2) % 2, me % 2, x, core)
        self.copies = [[] for _ in jobs]
        self.keeps = []

    def peer(self, dim):
        me, x, core = lax.axis_index("seq"), lax.axis_index("x"), lax.axis_index("core")
        if dim < 3:
            return (me ^ (4 >> dim), x, core)
        return (me, 1 - x, core) if dim == 3 else (me, x, 1 - core)

    def launch(self, index, source, target, dim):
        at = len(self.copies[index])
        copy = remote(
            source,
            target,
            self.send.at[index * 7 + at],
            self.recv.at[index * 7 + at],
            self.peer(dim),
        )
        copy.start()
        self.copies[index].append(copy)

    def absorb(self, index, stage):
        _, _, _, order, keep, arrivals = self.jobs[index]
        done = order[1 : stage + 1]
        left = [dim for dim in range(4) if dim not in done]
        self.copies[index][stage].wait_recv()

        def add(i, carry):
            at = list(self.bits[:4])
            place = []
            for n, dim in enumerate(left):
                bit = (i >> (len(left) - 1 - n)) & 1
                at[dim] = bit
                place.append(bit)
            mine = keep[at[0], at[1], at[2], at[3]].astype(F32)
            other = arrivals[stage][tuple(place)] if place else arrivals[stage][...]
            keep[at[0], at[1], at[2], at[3]] = (mine + other.astype(F32)).astype(BF)
            return carry

        lax.fori_loop(0, 2 ** len(left), add, 0)

    def stage(self, number):
        for index, (grad, out, cols, order, keep, arrivals) in enumerate(self.jobs):
            tail = (slice(None), cols)
            bits = self.bits
            if number == 0:
                lead = (slice(None),) * 4
                own = pltpu.make_async_copy(
                    grad.at[lead + (bits[4],) + tail], keep, self.local.at[index]
                )
                own.start()
                self.keeps.append(own)
                self.launch(index, grad.at[lead + (1 - bits[4],) + tail], arrivals[0], 4)
            elif number < 5:
                if number == 1:
                    self.keeps[index].wait()
                self.absorb(index, number - 1)
                dim = order[number]
                done = order[1:number]
                where = tuple(
                    1 - bits[d] if d == dim else bits[d] if d in done else slice(None)
                    for d in range(4)
                )
                self.launch(index, keep.at[where], arrivals[number], dim)
            elif number == 5:
                self.absorb(index, 4)
                mine = keep.at[bits[:4]]
                spot = out.at[(bits[3], bits[4]) + tail]
                own = pltpu.make_async_copy(mine, spot, self.local.at[index])
                own.start()
                self.keeps[index] = own
                self.launch(index, mine, spot, 3)
            else:
                self.keeps[index].wait()
                self.copies[index][5].wait_recv()
                both = out.at[(slice(None), bits[4]) + tail]
                self.launch(index, both, both, 4)

    def finish(self):
        for chain in self.copies:
            chain[6].wait_recv()
        for chain in self.copies:
            for copy in chain:
                copy.wait_send()


def reduce_kernel(*refs, count):
    grads, small = refs[:count], refs[count]
    outs, small_out = refs[count + 1 : 2 * count + 1], refs[2 * count + 1]
    rest = refs[2 * count + 2 :]
    jobs = 2 * count
    buffers = rest[: 6 * jobs]
    small_in, small_low, send, recv, local, ssend, srecv, bsend, brecv, slocal = rest[6 * jobs :]
    me, x, core = lax.axis_index("seq"), lax.axis_index("x"), lax.axis_index("core")
    others = [seq_flip(flip) for flip in range(7, 0, -1)]
    mates = [(me, (x + dx) % 2, (core + dc) % 2) for dx, dc in ((0, 1), (1, 0), (1, 1))]
    greet(others + mates)
    work = []
    for index in range(jobs):
        grad, out = grads[index // 2], outs[index // 2]
        half = grad.shape[-1] // 2
        cols = pl.ds((index % 2) * half, half)
        keep, arrivals = buffers[6 * index], buffers[6 * index + 1 : 6 * index + 6]
        order = (4, 3, 2, 1, 0) if index % 2 == 0 else (4, 2, 3, 1, 0)
        work.append((grad, out, cols, order, keep, arrivals))
    chain = GradSum(work, send, recv, local)
    chain.stage(0)
    own = pltpu.make_async_copy(small, small_in.at[me], slocal.at[0])
    own.start()
    smalls = []
    for flip, device in zip(range(7, 0, -1), others):
        smalls.append(remote(small, small_in.at[me], ssend.at[flip], srecv.at[flip], device))
        smalls[-1].start()
    for number in range(1, 6):
        chain.stage(number)
    own.wait()
    for copy in smalls:
        copy.wait_recv()
    total = small_in[0]
    for index in range(1, 8):
        total = total + small_in[index]
    small_low[...] = total.astype(BF)
    quarter = x * 2 + core
    keep = pltpu.make_async_copy(small_low, small_out.at[quarter], slocal.at[1])
    keep.start()
    lows = []
    for slot, device in enumerate(mates):
        lows.append(remote(small_low, small_out.at[quarter], bsend.at[slot], brecv.at[slot], device))
        lows[-1].start()
    chain.stage(6)
    chain.finish()
    for copy in smalls:
        copy.wait_send()
    keep.wait()
    for copy in lows:
        copy.wait()


def reduce_grads(grads, small, collective_id=3):
    views, outs, buffers = [], [], []
    for grad in grads:
        rows, width = grad.shape
        span = rows // 32
        views.append(grad.reshape(2, 2, 2, 2, 2, span, width))
        outs.append(jax.ShapeDtypeStruct((2, 2, span, width), BF))
        for _ in range(2):
            tail = (span, width // 2)
            buffers.append(pltpu.VMEM((2, 2, 2, 2) + tail, BF))
            for left in (4, 3, 2, 1, 0):
                buffers.append(pltpu.VMEM((2,) * left + tail, BF))
    anywhere = pl.BlockSpec(memory_space=pl.ANY)
    jobs = 2 * len(grads)
    dma = pltpu.SemaphoreType.DMA
    outs.append(jax.ShapeDtypeStruct((4,) + small.shape, BF))
    results = pl.pallas_call(
        functools.partial(reduce_kernel, count=len(grads)),
        in_specs=[anywhere] * (len(grads) + 1),
        out_specs=[anywhere] * (len(grads) + 1),
        out_shape=outs,
        scratch_shapes=buffers
        + [pltpu.VMEM((8,) + small.shape, F32), pltpu.VMEM(small.shape, BF)]
        + [dma((7 * jobs,)), dma((7 * jobs,)), dma((jobs,)), dma((8,)), dma((8,)), dma((3,)), dma((3,)), dma((2,))],
        compiler_params=pltpu.CompilerParams(
            vmem_limit_bytes=VMEM_LIMIT, collective_id=collective_id, has_side_effects=True
        ),
        name="reduce_grads",
    )(*views, small)
    shards = [
        result.reshape(grad.shape[0] // 8, grad.shape[1]).astype(jnp.float32)
        for result, grad in zip(results, grads)
    ]
    return shards, results[-1].astype(jnp.float32)


def rotary_tables(positions):
    half_dim = HEAD_DIM // 2
    channel = jnp.arange(half_dim, dtype=jnp.float32)
    inverse = jnp.power(10000.0, -2.0 * channel / HEAD_DIM)
    angles = positions.astype(jnp.float32)[:, None] * inverse[None, :]
    angles = jnp.concatenate([angles, angles], axis=1)
    return (jnp.cos(angles), jnp.sin(angles))


def rotate_heads(field, cosine_table, sine_table):
    half_dim = field.shape[-1] // 2
    turned = jnp.concatenate([-field[..., half_dim:], field[..., :half_dim]], axis=-1)
    return field * cosine_table + turned * sine_table


def smooth_gelu(values):
    return jax.nn.gelu(values, approximate=True)


def cross(left, right):
    return lax.dot_general(
        left, right, (((0,), (0,)), ((), ())), preferred_element_type=jnp.float32
    )


def back_product(left, right):
    return lax.dot_general(
        left, right, (((1,), (1,)), ((), ())), preferred_element_type=jnp.float32
    )


def block_terms(query_block, dout_block, lse_block, delta_block, key_block, value_block, key_live):
    scores = jnp.einsum(
        "bqhd,bkhd->bhqk", query_block, key_block, preferred_element_type=jnp.float32
    )
    lse_heads = jnp.transpose(lse_block, (0, 2, 1))[..., None]
    probs = jnp.where(key_live[:, None, None, :], jnp.exp(scores - lse_heads), 0.0)
    grad_probs = jnp.einsum(
        "bqhd,bkhd->bhqk", dout_block, value_block, preferred_element_type=jnp.float32
    )
    delta_heads = jnp.transpose(delta_block, (0, 2, 1))[..., None]
    dscore = (probs * (grad_probs - delta_heads)).astype(jnp.bfloat16)
    return (probs.astype(jnp.bfloat16), dscore)


BATCH = ("x", "core")


def batch_index():
    return lax.axis_index("x") * lax.axis_size("core") + lax.axis_index("core")


def gather_weight(weight):
    parts = lax.axis_size(BATCH)
    if weight.shape[0] % parts:
        return lax.all_gather(weight, "seq", axis=0, tiled=True)
    rows = weight.shape[0] // parts
    mine = lax.dynamic_slice_in_dim(weight, batch_index() * rows, rows, 0)
    return lax.all_gather(mine, ("seq",) + BATCH, axis=0, tiled=True)


def sum_weight(grad):
    rows, width = grad.shape
    low = grad.astype(jnp.bfloat16)
    seq_count, cores = lax.axis_size("seq"), lax.axis_size("core")
    parts = seq_count * lax.axis_size(BATCH)
    if rows % parts or cores != 2:
        shard = lax.psum_scatter(low, "seq", scatter_dimension=0, tiled=True)
        return lax.psum(shard, BATCH).astype(jnp.float32)
    core = lax.axis_index("core")
    held = low.reshape(parts // 2, 2, rows // parts, width)
    send = lax.dynamic_index_in_dim(held, 1 - core, 1, keepdims=False)
    keep = lax.dynamic_index_in_dim(held, core, 1, keepdims=False)
    got = lax.ppermute(send, "core", [(0, 1), (1, 0)])
    half = (keep.astype(jnp.float32) + got.astype(jnp.float32)).astype(jnp.bfloat16)
    half = half.reshape(rows // 2, width)
    shard = lax.psum_scatter(half, ("seq", "x"), scatter_dimension=0, tiled=True)
    return lax.all_gather(shard, BATCH, axis=0, tiled=True).astype(jnp.float32)


def gather_kernel(*refs, shapes):
    count = len(shapes)
    weights, seq_small, batch_small = refs[:count], refs[count], refs[count + 1]
    fulls = refs[count + 2 : 2 * count + 2]
    seq_out, batch_out, send, recv, small_send, small_recv, local = refs[2 * count + 2 :]
    me, x, core = lax.axis_index("seq"), lax.axis_index("x"), lax.axis_index("core")
    bits = (me // 4, (me // 2) % 2, me % 2, x, core)

    def peer(dim):
        if dim < 3:
            return (me ^ (4 >> dim), x, core)
        return (me, 1 - x, core) if dim == 3 else (me, x, 1 - core)

    others = [((me + d) % 8, x, core) for d in range(1, 8)]
    mates = [(me, (x + dx) % 2, (core + dc) % 2) for dx, dc in ((0, 1), (1, 0), (1, 1))]
    barrier = pltpu.get_barrier_semaphore()
    for device in others + mates:
        pl.semaphore_signal(barrier, inc=1, device_id=device, device_id_type=pl.DeviceIdType.MESH)
    pl.semaphore_wait(barrier, len(others) + len(mates))

    small = []
    quarter = x * 2 + core
    own_seq = pltpu.make_async_copy(seq_small, seq_out.at[me], local.at[0])
    own_batch = pltpu.make_async_copy(batch_small, batch_out.at[quarter], local.at[1])
    own_seq.start()
    own_batch.start()
    for slot, device in enumerate(others):
        small.append(
            pltpu.make_async_remote_copy(
                seq_small, seq_out.at[me], small_send.at[slot], small_recv.at[slot],
                device_id=device, device_id_type=pl.DeviceIdType.MESH,
            )
        )
    for slot, device in enumerate(mates):
        small.append(
            pltpu.make_async_remote_copy(
                batch_small, batch_out.at[quarter], small_send.at[7 + slot], small_recv.at[7 + slot],
                device_id=device, device_id_type=pl.DeviceIdType.MESH,
            )
        )
    for copy in small:
        copy.start()

    chain = WeightGather(gather_jobs(weights, fulls), send, recv, local.at[pl.ds(2, 2 * count)])
    for _ in range(5):
        chain.stage()
    chain.finish()
    for copy in small:
        copy.wait()
    own_seq.wait()
    own_batch.wait()


def gather_early(weights, seq_small, batch_small):
    shapes = [w.shape for w in weights]
    anywhere = pl.BlockSpec(memory_space=pl.ANY)
    jobs = 2 * len(weights)
    outs = pl.pallas_call(
        functools.partial(gather_kernel, shapes=shapes),
        in_specs=[anywhere] * (len(weights) + 2),
        out_specs=[anywhere] * (len(weights) + 2),
        out_shape=[
            jax.ShapeDtypeStruct((2, 2, 2, 2, 2, rows // 4, width), BF) for rows, width in shapes
        ]
        + [
            jax.ShapeDtypeStruct((8,) + seq_small.shape, F32),
            jax.ShapeDtypeStruct((4,) + batch_small.shape, F32),
        ],
        scratch_shapes=[
            pltpu.SemaphoreType.DMA((5 * jobs,)),
            pltpu.SemaphoreType.DMA((5 * jobs,)),
            pltpu.SemaphoreType.DMA((10,)),
            pltpu.SemaphoreType.DMA((10,)),
            pltpu.SemaphoreType.DMA((2 + jobs,)),
        ],
        compiler_params=pltpu.CompilerParams(collective_id=0, has_side_effects=True),
        name="gather_early",
    )(*weights, seq_small, batch_small)
    fulls = [full.reshape(8 * rows, width) for full, (rows, width) in zip(outs, shapes)]
    return fulls, outs[-2], outs[-1]


def paired_tables(positions):
    cos, sin = rotary_tables(positions)
    half = HEAD_DIM // 2
    signed = jnp.concatenate([-sin[:, :half], sin[:, half:]], axis=1)
    return jnp.tile(cos, (1, 2)), jnp.tile(signed, (1, 2))


def on_device(
    layer_input,
    skip_input,
    time_embed,
    lengths,
    cond_drop,
    cotangent,
    skip_weight,
    adaln_weight,
    adaln_bias,
    qkv_weight,
    out_weight,
    up_weight,
    down_weight,
):
    utt_count, frame_span, model_width = layer_input.shape
    head_count = model_width // HEAD_DIM
    row_count = utt_count * frame_span
    seq_here = lax.axis_index("seq")
    seq_count = lax.axis_size("seq")
    frame_count = frame_span * seq_count
    by_heads = (
        seq_count == 8
        and head_count == 16
        and utt_count == 2
        and lax.axis_size(BATCH) == 4
        and frame_span == 512
    )
    local_pos = seq_here * frame_span + jnp.arange(frame_span, dtype=jnp.int32)
    local_live = local_pos[None, :] < lengths[:, None]
    valid_mask = local_live.astype(jnp.float32)
    drop = cond_drop.astype(jnp.float32)
    dropped = drop[:, None] * valid_mask
    frames_live = jnp.minimum(lengths, frame_count).astype(jnp.float32)
    counts = jnp.stack([jnp.sum((1.0 - drop) * frames_live), jnp.sum(drop * frames_live)])
    silu_time = jax.nn.silu(time_embed.astype(jnp.float32)).astype(jnp.bfloat16)
    row_span = adaln_weight.shape[0]
    silu_mine = lax.dynamic_slice_in_dim(silu_time, seq_here * row_span, row_span, 1)
    mod_part = jnp.dot(silu_mine, adaln_weight, preferred_element_type=jnp.float32)
    bias_span = adaln_bias.shape[0]
    bias_here = lax.dynamic_update_slice_in_dim(
        jnp.zeros((mod_part.shape[1],), jnp.float32),
        adaln_bias.astype(jnp.float32),
        seq_here * bias_span,
        0,
    )
    mod_part = mod_part + bias_here
    if by_heads:
        small = jnp.concatenate(
            [
                silu_time.astype(jnp.float32),
                jnp.pad(counts[None, :], ((0, 5), (0, model_width - 2))),
            ],
            axis=0,
        )
        (skip_full, qkv_full), mod_every, small_every = gather_early(
            (skip_weight, qkv_weight), mod_part.reshape(-1, model_width), small
        )
        modulation = jnp.sum(mod_every, axis=0)
        totals = jnp.sum(small_every[:, utt_count, :2], axis=0)
        silu_every = small_every[:, :utt_count].reshape(-1, model_width)
    else:
        modulation = lax.psum(mod_part, "seq")
        totals = lax.psum(counts, BATCH)
        skip_full = gather_weight(skip_weight)
        qkv_full = gather_weight(qkv_weight)
        silu_every = lax.all_gather(silu_time, BATCH, axis=0, tiled=True).astype(jnp.float32)
    modulation = modulation.reshape(utt_count, 6, model_width)
    kept_total = jnp.maximum(totals[0], 1.0)
    drop_total = jnp.maximum(totals[1], 1.0)
    every_count = kept_total + drop_total
    loss_weight = (valid_mask - dropped) * (every_count / (2.0 * kept_total)) + dropped * (
        every_count / (2.0 * drop_total)
    )
    first_rows = layer_input.reshape(row_count, model_width)
    second_rows = skip_input.reshape(row_count, model_width)
    if by_heads:
        cos_all, sin_all = paired_tables(jnp.arange(frame_count, dtype=jnp.int32))
        cos_here = lax.dynamic_slice_in_dim(cos_all, seq_here * frame_span, frame_span, 0)
        sin_here = lax.dynamic_slice_in_dim(sin_all, seq_here * frame_span, frame_span, 0)
        residual_rows, proj = enter_layer(
            first_rows, second_rows, skip_full, qkv_full, modulation, cos_here, sin_here
        )
        (qkv_all, out_all, lse_all, attended_low), (out_full, up_full, down_full) = attend_forward(
            lengths, proj, out_weight, up_weight, down_weight, frame_span
        )
    else:
        joined = jnp.concatenate([layer_input, skip_input], axis=-1).reshape(row_count, 2 * model_width)
        residual_in = jnp.dot(joined, skip_full, preferred_element_type=jnp.float32).reshape(
            utt_count, frame_span, model_width
        )
        shift_attn = modulation[:, 0][:, None, :]
        scale_attn = modulation[:, 1][:, None, :]
        hat_attn, inv_attn = layer_norm(residual_in)
        normed_attn = (
            (hat_attn * (1.0 + scale_attn) + shift_attn)
            .astype(jnp.bfloat16)
            .reshape(row_count, model_width)
        )
        residual_rows = residual_in.reshape(row_count, model_width)
        out_full, up_full, down_full = [
            gather_weight(weight) for weight in (out_weight, up_weight, down_weight)
        ]
        projected = jnp.dot(normed_attn, qkv_full, preferred_element_type=jnp.float32).reshape(
            utt_count, frame_span, 3, head_count, HEAD_DIM
        )
        cosine_table, sine_table = rotary_tables(local_pos)
        cosine_table = cosine_table[None, :, None, :]
        sine_table = sine_table[None, :, None, :]
        queries = (rotate_heads(projected[:, :, 0], cosine_table, sine_table) * 0.125).astype(
            jnp.bfloat16
        )
        keys_rot = rotate_heads(projected[:, :, 1], cosine_table, sine_table).astype(jnp.bfloat16)
        values = projected[:, :, 2].astype(jnp.bfloat16)
        start_top = jnp.full((utt_count, head_count, frame_span), MASKED, jnp.float32)
        top_score = start_top
        key_piece = lax.all_gather(keys_rot, "seq", axis=1, tiled=True)
        value_piece = lax.all_gather(values, "seq", axis=1, tiled=True)
        piece_len = key_piece.shape[1]
        piece_live = jnp.arange(piece_len, dtype=jnp.int32)[None, :] < lengths[:, None]
        scores = jnp.einsum("bqhd,bkhd->bhqk", queries, key_piece, preferred_element_type=jnp.float32)
        scores = jnp.where(piece_live[:, None, None, :], scores, MASKED)
        new_top = jnp.maximum(top_score, jnp.max(scores, axis=-1))
        expo = jnp.where(piece_live[:, None, None, :], jnp.exp(scores - new_top[..., None]), 0.0)
        denom = jnp.sum(expo, axis=-1)
        partial_out = jnp.einsum(
            "bhqk,bkhd->bqhd",
            expo.astype(jnp.bfloat16),
            value_piece,
            preferred_element_type=jnp.float32,
        )
        accum = partial_out
        accum, top_score, denom = (accum, new_top, denom)
        attended_full = accum / jnp.transpose(denom, (0, 2, 1))[..., None]
        lse_rows = jnp.transpose(top_score + jnp.log(denom), (0, 2, 1))
        attended_low = attended_full.astype(jnp.bfloat16).reshape(row_count, model_width)
    cot_rows = cotangent.reshape(row_count, model_width)
    weight_rows = loss_weight.reshape(row_count, 1)
    branch_attn, hidden_act, hidden_slope, grad_branch_ffn, layer_output, grad_gate_ffn = ffn_forward(
        attended_low,
        out_full,
        residual_rows,
        modulation,
        cot_rows,
        weight_rows,
        up_full,
        down_full,
    )
    layer_output = layer_output.reshape(utt_count, frame_span, model_width)
    grad_up, grad_down, grad_mid, grad_attended_flat, grad_out, ffn_sums = ffn_backward(
        attended_low,
        out_full,
        residual_rows,
        branch_attn,
        modulation,
        cot_rows,
        weight_rows,
        grad_branch_ffn,
        hidden_act,
        hidden_slope,
        up_full,
        down_full,
    )
    grad_shift_ffn, grad_scale_ffn, grad_gate_attn = ffn_sums[:, 0], ffn_sums[:, 1], ffn_sums[:, 2]
    if by_heads:
        grad_projected = attend_backward(
            lengths, grad_attended_flat, qkv_all, out_all, lse_all, cos_all, sin_all, frame_span
        )
    else:
        grad_attended = grad_attended_flat.reshape(
            utt_count, frame_span, head_count, HEAD_DIM
        )
        delta_rows = jnp.sum(grad_attended.astype(jnp.float32) * attended_full, axis=-1)
        lse_all, delta_all = (
            lax.all_gather(lse_rows, "seq", axis=1, tiled=True),
            lax.all_gather(delta_rows, "seq", axis=1, tiled=True),
        )
        key_piece = lax.all_gather(keys_rot, "seq", axis=1, tiled=True)
        value_piece = lax.all_gather(values, "seq", axis=1, tiled=True)
        piece_len = key_piece.shape[1]
        piece_live = jnp.arange(piece_len, dtype=jnp.int32)[None, :] < lengths[:, None]
        probs_low, dscore = block_terms(
            queries, grad_attended, lse_rows, delta_rows, key_piece, value_piece, piece_live
        )
        grad_queries = jnp.einsum(
            "bhqk,bkhd->bqhd", dscore, key_piece, preferred_element_type=jnp.float32
        )
        query_piece = lax.all_gather(queries, "seq", axis=1, tiled=True)
        dout_piece = lax.all_gather(grad_attended, "seq", axis=1, tiled=True)
        probs_low, dscore = block_terms(
            query_piece, dout_piece, lse_all, delta_all, keys_rot, values, local_live
        )
        grad_k = jnp.einsum("bhqk,bqhd->bkhd", dscore, query_piece, preferred_element_type=jnp.float32)
        grad_v = jnp.einsum(
            "bhqk,bqhd->bkhd", probs_low, dout_piece, preferred_element_type=jnp.float32
        )
        grad_q_pre = rotate_heads(grad_queries * 0.125, cosine_table, -sine_table)
        grad_k_pre = rotate_heads(grad_k, cosine_table, -sine_table)
        grad_projected = (
            jnp.stack([grad_q_pre, grad_k_pre, grad_v], axis=2)
            .reshape(row_count, 3 * model_width)
            .astype(jnp.bfloat16)
        )
    if by_heads:
        grad_input, grad_skip, attn_sums, grad_qkv, grad_skip_w = leave_layer(
            grad_projected,
            qkv_full,
            skip_full,
            residual_rows,
            grad_mid,
            modulation,
            first_rows,
            second_rows,
        )
        grad_input = grad_input.reshape(layer_input.shape)
        grad_skip = grad_skip.reshape(skip_input.shape)
        grad_shift_attn, grad_scale_attn = attn_sums[:, 0], attn_sums[:, 1]
    else:
        grad_mid = grad_mid.reshape(utt_count, frame_span, model_width)
        grad_qkv = cross(normed_attn, grad_projected)
        grad_normed_attn = back_product(grad_projected, qkv_full).reshape(
            utt_count, frame_span, model_width
        )
        grad_shift_attn = jnp.sum(grad_normed_attn, axis=1)
        grad_scale_attn = jnp.sum(grad_normed_attn * hat_attn, axis=1)
        grad_stream = grad_mid + norm_back(grad_normed_attn * (1.0 + scale_attn), hat_attn, inv_attn)
        grad_stream_low = grad_stream.astype(jnp.bfloat16).reshape(row_count, model_width)
        grad_skip_w = cross(joined, grad_stream_low)
        grad_joined = back_product(grad_stream_low, skip_full)
        grad_input = (
            grad_joined[:, :model_width]
            .reshape(utt_count, frame_span, model_width)
            .astype(jnp.bfloat16)
        )
        grad_skip = (
            grad_joined[:, model_width:]
            .reshape(utt_count, frame_span, model_width)
            .astype(jnp.bfloat16)
        )
    grad_modulation = jnp.stack(
        [
            grad_shift_attn,
            grad_scale_attn,
            grad_gate_attn,
            grad_shift_ffn,
            grad_scale_ffn,
            grad_gate_ffn,
        ],
        axis=1,
    ).reshape(utt_count, 6 * model_width)
    weight_grads = (grad_skip_w, grad_qkv, grad_out, grad_up, grad_down)
    if by_heads:
        order = (4, 3, 1, 0, 2)
        shards, mod_every = reduce_grads(
            [weight_grads[i] for i in order], grad_modulation.reshape(-1, model_width)
        )
        summed = [shards[order.index(i)] for i in range(5)]
        mod_every = mod_every.reshape(-1, 6 * model_width)
    else:
        mod_total = lax.psum(grad_modulation, "seq")
        mod_every = lax.all_gather(
            mod_total.astype(jnp.bfloat16), BATCH, axis=0, tiled=True
        ).astype(jnp.float32)
        summed = [sum_weight(grad) for grad in weight_grads]
    silu_rows = lax.dynamic_slice_in_dim(silu_every, seq_here * row_span, row_span, 1)
    adaln_rows = jnp.dot(silu_rows.T, mod_every, precision=lax.Precision.HIGHEST)
    bias_rows = lax.dynamic_slice_in_dim(
        jnp.sum(mod_every, axis=0), seq_here * bias_span, bias_span, 0
    )
    results = (summed[0], adaln_rows, bias_rows, summed[1], summed[2], summed[3], summed[4])
    return (
        layer_output,
        grad_input,
        grad_skip,
        results[0],
        results[1],
        results[2],
        results[3],
        results[4],
        results[5],
        results[6],
    )


def solution(mesh):
    count, batch = mesh.shape["seq"], mesh.shape["batch"]
    cores = 2 if batch % 2 == 0 else 1
    split = Mesh(mesh.devices.reshape(count, batch // cores, cores), ("seq",) + BATCH)
    placed = (
        P(BATCH, "seq", None),
        P(BATCH, "seq", None),
        P(BATCH, None),
        P(BATCH),
        P(BATCH),
        P(BATCH, "seq", None),
        P("seq", None),
        P("seq", None),
        P("seq"),
        P("seq", None),
        P("seq", None),
        P("seq", None),
        P("seq", None),
    )
    return jax.shard_map(
        on_device,
        mesh=split,
        in_specs=placed,
        out_specs=(
            P(BATCH, "seq", None),
            P(BATCH, "seq", None),
            P(BATCH, "seq", None),
            P("seq", None),
            P("seq", None),
            P("seq"),
            P("seq", None),
            P("seq", None),
            P("seq", None),
            P("seq", None),
        ),
        check_vma=False,
    )
```

```python
import functools
import jax
import jax.numpy as jnp
from jax import lax
from jax.sharding import Mesh, PartitionSpec as P
from jax.experimental import pallas as pl
from jax.experimental.pallas import tpu as pltpu
HEAD_DIM = 64
EPS = 1e-06
LOG2E = 1.4426950408889634
LN2 = 0.6931471805599453
MASKED = -1e30
BF = jnp.bfloat16
F32 = jnp.float32
VMEM_LIMIT = 60 * 2**20


def nt(left, right):
    return lax.dot_general(left, right, (((1,), (1,)), ((), ())), preferred_element_type=F32)


def nn(left, right):
    return lax.dot_general(left, right, (((1,), (0,)), ((), ())), preferred_element_type=F32)


def head_sums(product, lane):
    first = jnp.sum(jnp.where(lane < 64, product, 0.0), axis=1, keepdims=True)
    second = jnp.sum(jnp.where(lane >= 64, product, 0.0), axis=1, keepdims=True)
    return (first, second)


def lanes_of(rows):
    return lax.broadcasted_iota(jnp.int32, (rows, 128), 1)


def attention_cost(frames, products):
    return pl.CostEstimate(
        flops=2 * products * 2 * frames * frames * 128,
        bytes_accessed=frames * 128 * 2 * 8,
        transcendentals=2 * frames * frames,
    )


def turn_back(grad, cos, sin):
    lane = lanes_of(grad.shape[0])
    turned = jnp.where((lane & 63) < 32, pltpu.roll(grad, 96, 1), pltpu.roll(grad, 32, 1))
    return grad * cos - turned * sin


def three(column, lane, at):
    high = column.astype(BF).astype(F32)
    rest = column - high
    mid = rest.astype(BF).astype(F32)
    low = rest - mid
    return jnp.where(lane == at, -high, jnp.where(lane == at + 1, -mid, jnp.where(lane == at + 2, -low, 0.0)))


MESH_IDS = pl.DeviceIdType.MESH


def seq_flip(flip):
    return (lax.axis_index("seq") ^ flip, lax.axis_index("x"), lax.axis_index("core"))


def greet(devices):
    barrier = pltpu.get_barrier_semaphore()
    for device in devices:
        pl.semaphore_signal(barrier, inc=1, device_id=device, device_id_type=MESH_IDS)
    pl.semaphore_wait(barrier, len(devices))


def remote(source, target, send, recv, device):
    return pltpu.make_async_remote_copy(
        source, target, send, recv, device_id=device, device_id_type=MESH_IDS
    )


class WeightGather:
    def __init__(self, jobs, send, recv, local):
        self.jobs, self.send, self.recv, self.local = jobs, send, recv, local
        me, x, core = lax.axis_index("seq"), lax.axis_index("x"), lax.axis_index("core")
        self.bits = (me // 4, (me // 2) % 2, me % 2, x, core)
        self.copies = [[] for _ in jobs]
        self.owns = []

    def peer(self, dim):
        me, x, core = lax.axis_index("seq"), lax.axis_index("x"), lax.axis_index("core")
        if dim < 3:
            return (me ^ (4 >> dim), x, core)
        return (me, 1 - x, core) if dim == 3 else (me, x, 1 - core)

    def stage(self):
        for index, (full, cols, source, ready, order) in enumerate(self.jobs):
            at = len(self.copies[index])
            where = tuple(
                slice(None) if d in ready + order[:at] else self.bits[d]
                for d in range(len(full.shape) - 2)
            ) + (slice(None), cols)
            if at == 0:
                own = pltpu.make_async_copy(source, full.at[where], self.local.at[index])
                own.start()
                self.owns.append(own)
            else:
                if at == 1:
                    self.owns[index].wait()
                self.copies[index][at - 1].wait_recv()
            copy = remote(
                source if at == 0 else full.at[where],
                full.at[where],
                self.send.at[index * 5 + at],
                self.recv.at[index * 5 + at],
                self.peer(order[at]),
            )
            copy.start()
            self.copies[index].append(copy)

    def finish(self):
        for chain in self.copies:
            chain[-1].wait_recv()
        for chain in self.copies:
            for copy in chain:
                copy.wait_send()


def split_columns(width, shares):
    total, start, out = sum(shares), 0, []
    for n in range(len(shares)):
        stop = width * sum(shares[: n + 1]) // total // 128 * 128
        out.append(pl.ds(start, stop - start))
        start = stop
    return out


def quarter_of(weight, cols):
    quarter = lax.axis_index("x") * 2 + lax.axis_index("core")
    span = weight.shape[0] // 4
    return weight.at[pl.ds(quarter * span, span), cols]


def early_jobs(weights, fulls):
    orders = ((0, 1, 2, 3, 4), (0, 2, 3, 1, 4), (0, 3, 1, 2, 4))
    return [
        (full, cols, quarter_of(weight, cols), (), order)
        for weight, full in zip(weights, fulls)
        for cols, order in zip(split_columns(weight.shape[1], (1, 1, 1)), orders)
    ]


def ahead_jobs(weights, helds):
    every = [(weight, held, pl.ds(0, weight.shape[1])) for weight, held in zip(weights, helds)]
    return [(held, cols, quarter_of(weight, cols), (), (0, 1)) for weight, held, cols in every]


def late_jobs(helds, fulls):
    return [
        (full, cols, held.at[:, :, :, cols], (0, 1), order)
        for held, full in zip(helds, fulls)
        for cols, order in zip(split_columns(held.shape[3], (3, 1)), ((2, 3, 4), (3, 2, 4)))
    ]


def attend_forward_kernel(
    len_ref, proj, out_w, up_w, down_w,
    qkv_all, o_all, lse_ref, att, out_full, up_full, down_full,
    qkv, outs, ka, kb, vta, vtb,
    wsend, wrecv, wlocal, qsend, qrecv, qlocal, osend, orecv, olocal, slocal,
    *, span, bq, bk,
):
    me, x, core = lax.axis_index("seq"), lax.axis_index("x"), lax.axis_index("core")
    frames = qkv.shape[2]
    mine = pl.ds(pl.multiple_of(me * span, span), span)
    my_cols = pl.ds(pl.multiple_of(me * 128, 128), 128)
    flips = (7, 6, 5, 4, 3, 2, 1)
    greet([seq_flip(flip) for flip in flips] + [(me, 1 - x, core), (me, x, 1 - core)])
    weights = WeightGather(
        late_jobs((out_w, up_w, down_w), (out_full, up_full, down_full)), wsend, wrecv, wlocal
    )

    def send_heads(utt):
        rows = pl.ds(utt * span, span)
        own = pltpu.make_async_copy(
            proj.at[:, rows, my_cols], qkv.at[utt, :, mine, :], qlocal.at[utt]
        )
        own.start()
        copies = []
        for flip in flips:
            there = me ^ flip
            cols = pl.ds(pl.multiple_of(there * 128, 128), 128)
            copy = remote(
                proj.at[:, rows, cols],
                qkv.at[utt, :, mine, :],
                qsend.at[utt * 8 + flip],
                qrecv.at[utt * 8 + flip],
                seq_flip(flip),
            )
            copy.start()
            copies.append(copy)
        return own, copies

    def arrive(sent):
        own, copies = sent
        own.wait()
        for copy in copies:
            copy.wait_recv()

    def attend(utt, between):
        length = len_ref[utt]
        save = pltpu.make_async_copy(qkv.at[utt], qkv_all.at[utt], slocal.at[utt])
        save.start()

        def build(j, carry):
            rows = pl.ds(pl.multiple_of(j * bk, bk), bk)
            lane = lanes_of(bk)
            pos = j * bk + lax.broadcasted_iota(jnp.int32, (bk, 128), 0)
            bias = jnp.where(pos < length, 0.0, MASKED)
            keys = qkv[utt, 1, rows, :].astype(F32)
            ka[rows, :] = jnp.where(lane < 64, keys, jnp.where(lane == 64, bias, 0.0)).astype(BF)
            kb[rows, :] = jnp.where(lane >= 64, keys, jnp.where(lane == 0, bias, 0.0)).astype(BF)
            vals = qkv[utt, 2, rows, :].astype(F32)
            vta[:, rows] = jnp.where(lane < 64, vals, 1.0).T.astype(BF)
            vtb[:, rows] = jnp.where(lane >= 64, vals, 1.0).T.astype(BF)
            return carry

        lax.fori_loop(0, frames // bk, build, 0)

        def block(i, carry):
            here = pl.ds(pl.multiple_of(i * bq, bq), bq)
            lane = lanes_of(bq)
            queries = qkv[utt, 0, here, :].astype(F32)
            qa = jnp.where(lane < 64, queries, jnp.where(lane == 64, 1.0, 0.0)).astype(BF)
            qb = jnp.where(lane >= 64, queries, jnp.where(lane == 0, 1.0, 0.0)).astype(BF)

            def body(j, inner):
                rows = pl.ds(pl.multiple_of(j * bk, bk), bk)
                result = []
                scores = [nt(ka[rows, :], qa), nt(kb[rows, :], qb)]
                for score, vt, (top, acc) in zip(scores, (vta, vtb), inner):
                    new = jnp.maximum(top, jnp.max(score, axis=0, keepdims=True))
                    probs = jnp.exp2(score - new).astype(BF)
                    acc = acc * jnp.exp2(top - new) + nn(vt[:, rows], probs)
                    result.append((new, acc))
                return tuple(result)

            start = (jnp.full((1, bq), MASKED, F32), jnp.zeros((128, bq), F32))
            (top_a, acc_a), (top_b, acc_b) = lax.fori_loop(0, frames // bk, body, (start, start))
            sum_a, sum_b = acc_a[64:65], acc_b[0:1]
            both = jnp.concatenate([acc_a[:64] / sum_a, acc_b[64:] / sum_b], axis=0)
            outs[utt, here, :] = both.T.astype(BF)
            lse_ref[utt, :, here] = jnp.concatenate(
                [top_a + jnp.log2(sum_a), top_b + jnp.log2(sum_b), jnp.zeros((6, bq), F32)],
                axis=0,
            )
            for part in range(bq // span):
                there = i * (bq // span) + part
                rows = pl.ds(pl.multiple_of(there * span, span), span)
                target = att.at[pl.ds(utt * span, span), my_cols]

                @pl.when(there != me)
                def _():
                    remote(
                        outs.at[utt, rows, :],
                        target,
                        osend.at[utt * 8 + (there ^ me)],
                        orecv.at[utt * 8 + (there ^ me)],
                        (there, x, core),
                    ).start()

                @pl.when(there == me)
                def _():
                    pltpu.make_async_copy(outs.at[utt, rows, :], target, olocal.at[utt]).start()

            return carry

        half = frames // bq // 2
        lax.fori_loop(0, half, block, 0)
        between()
        lax.fori_loop(half, 2 * half, block, 0)
        keep = pltpu.make_async_copy(outs.at[utt], o_all.at[utt], slocal.at[2 + utt])
        keep.start()
        return [save, keep]

    first = send_heads(0)
    weights.stage()
    arrive(first)
    second = send_heads(1)
    weights.stage()
    saves = attend(0, lambda: None)
    arrive(second)
    saves += attend(1, weights.stage)
    for sent in (first, second):
        for copy in sent[1]:
            copy.wait_send()
    weights.finish()
    for save in saves:
        save.wait()
    for utt in range(2):
        target = att.at[pl.ds(utt * span, span), my_cols]
        pltpu.make_async_copy(outs.at[utt, mine, :], target, olocal.at[utt]).wait()
        for flip in flips:
            copy = remote(
                outs.at[utt, mine, :],
                target,
                osend.at[utt * 8 + flip],
                orecv.at[utt * 8 + flip],
                seq_flip(flip),
            )
            copy.wait_send()
            copy.wait_recv()


def attend_forward(lengths, proj, out_w, up_w, down_w, span, bq=1024, bk=512):
    rows, width = proj.shape[1:]
    frames = 8 * span
    anywhere = pl.BlockSpec(memory_space=pl.ANY)
    vmem = pl.BlockSpec(memory_space=pltpu.VMEM)
    full = lambda w: jax.ShapeDtypeStruct((2, 2, 2, 2, 2) + w.shape[2:], BF)
    dma = pltpu.SemaphoreType.DMA
    outs = pl.pallas_call(
        functools.partial(attend_forward_kernel, span=span, bq=bq, bk=bk),
        in_specs=[pl.BlockSpec(memory_space=pltpu.SMEM)] + [anywhere] * 4,
        out_specs=[anywhere, anywhere, vmem] + [anywhere] * 4,
        out_shape=[
            jax.ShapeDtypeStruct((2, 3, frames, 128), BF),
            jax.ShapeDtypeStruct((2, frames, 128), BF),
            jax.ShapeDtypeStruct((2, 8, frames), F32),
            jax.ShapeDtypeStruct((rows, width), BF),
            full(out_w),
            full(up_w),
            full(down_w),
        ],
        scratch_shapes=[
            pltpu.VMEM((2, 3, frames, 128), BF),
            pltpu.VMEM((2, frames, 128), BF),
            pltpu.VMEM((frames, 128), BF),
            pltpu.VMEM((frames, 128), BF),
            pltpu.VMEM((128, frames), BF),
            pltpu.VMEM((128, frames), BF),
            dma((30,)),
            dma((30,)),
            dma((6,)),
            dma((16,)),
            dma((16,)),
            dma((2,)),
            dma((16,)),
            dma((16,)),
            dma((2,)),
            dma((4,)),
        ],
        compiler_params=pltpu.CompilerParams(
            vmem_limit_bytes=VMEM_LIMIT, collective_id=1, has_side_effects=True
        ),
        cost_estimate=attention_cost(frames, 4),
        name="attend_forward",
    )(lengths, proj, out_w, up_w, down_w)
    fulls = [
        outs[4 + i].reshape(32 * w.shape[2], w.shape[3]) for i, w in enumerate((out_w, up_w, down_w))
    ]
    return outs[:4], fulls


def attend_backward_kernel(
    len_ref, dout, qkv_all, o_all, lse_ref, cos_ref, sin_ref,
    grads,
    qkv, outs, douts, qa, qb, da, db, qt, dt, dqa, dqb,
    dsend, drecv, dlocal, gsend, grecv, glocal, load,
    *, span, block,
):
    me, x, core = lax.axis_index("seq"), lax.axis_index("x"), lax.axis_index("core")
    frames = qkv.shape[2]
    width = grads.shape[1] // 3
    count = frames // block
    mine = pl.ds(pl.multiple_of(me * span, span), span)
    flips = (7, 6, 5, 4, 3, 2, 1)
    greet([seq_flip(flip) for flip in flips])
    loads = []
    for utt in range(2):
        loads.append(
            [
                pltpu.make_async_copy(qkv_all.at[utt], qkv.at[utt], load.at[utt]),
                pltpu.make_async_copy(o_all.at[utt], outs.at[utt], load.at[2 + utt]),
            ]
        )
        for copy in loads[-1]:
            copy.start()

    def send_heads(utt):
        rows = pl.ds(utt * span, span)
        my_cols = pl.ds(pl.multiple_of(me * 128, 128), 128)
        own = pltpu.make_async_copy(dout.at[rows, my_cols], douts.at[utt, mine, :], dlocal.at[utt])
        own.start()
        copies = []
        for flip in flips:
            cols = pl.ds(pl.multiple_of((me ^ flip) * 128, 128), 128)
            copy = remote(
                dout.at[rows, cols],
                douts.at[utt, mine, :],
                dsend.at[utt * 8 + flip],
                drecv.at[utt * 8 + flip],
                seq_flip(flip),
            )
            copy.start()
            copies.append(copy)
        return own, copies

    def arrive(sent):
        own, copies = sent
        own.wait()
        for copy in copies:
            copy.wait_recv()

    def slot(utt, part, flip):
        return (utt * 3 + part) * 8 + flip

    def target(utt, part):
        cols = pl.ds(pl.multiple_of(part * width + me * 128, 128), 128)
        return grads.at[pl.ds(utt * span, span), cols]

    def send_grads(utt, part, there):
        rows = pl.ds(pl.multiple_of(there * span, span), span)

        @pl.when(there != me)
        def _():
            at = slot(utt, part, there ^ me)
            remote(
                qkv.at[utt, part, rows, :],
                target(utt, part),
                gsend.at[at],
                grecv.at[at],
                (there, x, core),
            ).start()

        @pl.when(there == me)
        def _():
            pltpu.make_async_copy(
                qkv.at[utt, part, rows, :], target(utt, part), glocal.at[utt * 3 + part]
            ).start()

    def differentiate(utt):
        length = len_ref[utt]

        def build(j, carry):
            rows = pl.ds(pl.multiple_of(j * block, block), block)
            lane = lanes_of(block)
            queries = qkv[utt, 0, rows, :].astype(F32)
            grad = douts[utt, rows, :].astype(F32)
            delta_a, delta_b = head_sums(grad * outs[utt, rows, :].astype(F32), lane)
            lse = lse_ref[utt, :, rows].T
            one_a, one_b = lse[:, 0:1], lse[:, 1:2]
            qa[rows, :] = jnp.where(
                lane < 64, queries, jnp.where(lane == 67, 1.0, three(one_a, lane, 64))
            ).astype(BF)
            qb[rows, :] = jnp.where(
                lane >= 64, queries, jnp.where(lane == 3, 1.0, three(one_b, lane, 0))
            ).astype(BF)
            da[rows, :] = jnp.where(lane < 64, grad, three(delta_a, lane, 64)).astype(BF)
            db[rows, :] = jnp.where(lane >= 64, grad, three(delta_b, lane, 0)).astype(BF)
            qt[:, rows] = queries.T.astype(BF)
            dt[:, rows] = grad.T.astype(BF)
            dqa[rows, :] = jnp.zeros((block, 128), F32)
            dqb[rows, :] = jnp.zeros((block, 128), F32)
            return carry

        lax.fori_loop(0, count, build, 0)

        def keys_block(i, carry):
            here = pl.ds(pl.multiple_of(i * block, block), block)
            lane = lanes_of(block)
            pos = i * block + lax.broadcasted_iota(jnp.int32, (block, 128), 0)
            bias = jnp.where(pos < length, 0.0, MASKED)
            keys = qkv[utt, 1, here, :].astype(F32)
            vals = qkv[utt, 2, here, :].astype(F32)
            ones_a = jnp.where(lane < 67, 1.0, 0.0)
            ones_b = jnp.where(lane < 3, 1.0, 0.0)
            ka = jnp.where(lane < 64, keys, jnp.where(lane == 67, bias, ones_a)).astype(BF)
            kb = jnp.where(lane >= 64, keys, jnp.where(lane == 3, bias, ones_b)).astype(BF)
            va = jnp.where(lane < 64, vals, ones_a).astype(BF)
            vb = jnp.where(lane >= 64, vals, ones_b).astype(BF)

            def body(j, inner):
                rows = pl.ds(pl.multiple_of(j * block, block), block)
                result = []
                for head, (qh, dh, kh, vh, dq) in enumerate(
                    ((qa, da, ka, va, dqa), (qb, db, kb, vb, dqb))
                ):
                    part = slice(head * 64, head * 64 + 64)
                    probs = jnp.exp2(nt(qh[rows, :], kh))
                    grad = (probs * nt(dh[rows, :], vh)).astype(BF)
                    dv = inner[2 * head + 1] + nn(dt[:, rows], probs.astype(BF))[part]
                    dk = inner[2 * head] + nn(qt[:, rows], grad)[part]
                    dq[rows, :] += nn(grad, kh)
                    result += [dk, dv]
                return tuple(result)

            zero = jnp.zeros((64, block), F32)
            dk_a, dv_a, dk_b, dv_b = lax.fori_loop(0, count, body, (zero,) * 4)
            dk = jnp.concatenate([dk_a, dk_b], axis=0).T * LN2
            dv = jnp.concatenate([dv_a, dv_b], axis=0).T
            qkv[utt, 1, here, :] = turn_back(dk, cos_ref[here, :], sin_ref[here, :]).astype(BF)
            qkv[utt, 2, here, :] = dv.astype(BF)
            for step in range(block // span):
                there = i * (block // span) + step
                send_grads(utt, 1, there)
                send_grads(utt, 2, there)
            return carry

        lax.fori_loop(0, count, keys_block, 0)

        def finish(i, carry):
            here = pl.ds(pl.multiple_of(i * block, block), block)
            lane = lanes_of(block)
            dq = jnp.where(lane < 64, dqa[here, :], dqb[here, :]) * 0.125
            qkv[utt, 0, here, :] = turn_back(dq, cos_ref[here, :], sin_ref[here, :]).astype(BF)
            for step in range(block // span):
                send_grads(utt, 0, i * (block // span) + step)
            return carry

        lax.fori_loop(0, count, finish, 0)

    first = send_heads(0)
    for copy in loads[0]:
        copy.wait()
    arrive(first)
    second = send_heads(1)
    differentiate(0)
    for copy in loads[1]:
        copy.wait()
    arrive(second)
    differentiate(1)
    for sent in (first, second):
        for copy in sent[1]:
            copy.wait_send()
    for utt in range(2):
        for part in range(3):
            own = qkv.at[utt, part, mine, :]
            pltpu.make_async_copy(own, target(utt, part), glocal.at[utt * 3 + part]).wait()
            for flip in flips:
                at = slot(utt, part, flip)
                copy = remote(own, target(utt, part), gsend.at[at], grecv.at[at], seq_flip(flip))
                copy.wait_send()
                copy.wait_recv()


def attend_backward(lengths, dout, qkv_all, o_all, lse, cos, sin, span, block=1024):
    frames = 8 * span
    rows, width = dout.shape
    anywhere = pl.BlockSpec(memory_space=pl.ANY)
    vmem = pl.BlockSpec(memory_space=pltpu.VMEM)
    dma = pltpu.SemaphoreType.DMA
    return pl.pallas_call(
        functools.partial(attend_backward_kernel, span=span, block=block),
        in_specs=[pl.BlockSpec(memory_space=pltpu.SMEM)] + [anywhere] * 3 + [vmem] * 3,
        out_specs=anywhere,
        out_shape=jax.ShapeDtypeStruct((rows, 3 * width), BF),
        scratch_shapes=[
            pltpu.VMEM((2, 3, frames, 128), BF),
            pltpu.VMEM((2, frames, 128), BF),
            pltpu.VMEM((2, frames, 128), BF),
        ]
        + [pltpu.VMEM((frames, 128), BF)] * 4
        + [pltpu.VMEM((128, frames), BF)] * 2
        + [pltpu.VMEM((frames, 128), F32)] * 2
        + [dma((16,)), dma((16,)), dma((2,)), dma((48,)), dma((48,)), dma((6,)), dma((4,))],
        compiler_params=pltpu.CompilerParams(
            vmem_limit_bytes=VMEM_LIMIT, collective_id=2, has_side_effects=True
        ),
        cost_estimate=attention_cost(frames, 10),
        name="attend_backward",
    )(lengths, dout, qkv_all, o_all, lse, cos, sin)


def layer_norm(stream):
    centre = stream - jnp.mean(stream, axis=-1, keepdims=True)
    spread = jnp.mean(centre * centre, axis=-1, keepdims=True)
    inverse = lax.rsqrt(spread + EPS)
    return (centre * inverse, inverse)


def norm_back(grad_normed, normed, inverse):
    first_mean = jnp.mean(grad_normed, axis=-1, keepdims=True)
    second_mean = jnp.mean(grad_normed * normed, axis=-1, keepdims=True)
    return inverse * (grad_normed - first_mean - normed * second_mean)


def tn(left, right):
    return lax.dot_general(left, right, (((0,), (0,)), ((), ())), preferred_element_type=F32)


GELU_C = 0.7978845608028654
GELU_A = 0.044715


def gelu_and_slope(z):
    square = z * z
    turn = jnp.tanh(GELU_C * z * (1.0 + GELU_A * square))
    half = 0.5 * (1.0 + turn)
    slope = half + 0.5 * z * (1.0 - turn * turn) * (GELU_C * (1.0 + 3.0 * GELU_A * square))
    return z * half, slope


def row_blocks(rows):
    block = min(rows, 256)
    return [(at, slice(at, at + block)) for at in range(0, rows, block)]


def ffn_forward_kernel(
    att_ref, outw_ref, res_ref, mod_ref, cot_ref, weight_ref, up_ref, down_ref,
    branch_ref, act_ref, slope_ref, gb_ref, out_ref, gate_ref, normed, acc,
):
    step = pl.program_id(0)
    rows = att_ref.shape[0]
    span = rows // mod_ref.shape[0]

    @pl.when(step == 0)
    def _():
        for at, part in row_blocks(span):
            for utt in range(mod_ref.shape[0]):
                here = slice(utt * span + part.start, utt * span + part.stop)
                mod = mod_ref[utt]
                branch = nn(att_ref[here, :], outw_ref[...])
                branch_ref[here, :] = branch
                hat, _ = layer_norm(res_ref[here, :] + mod[2:3] * branch)
                normed[here, :] = (hat * (1.0 + mod[4:5]) + mod[3:4]).astype(BF)
        acc[...] = jnp.zeros_like(acc)

    for _, part in row_blocks(rows):
        act, slope = gelu_and_slope(nn(normed[part, :], up_ref[...]))
        act = act.astype(BF)
        act_ref[part, :] = act
        slope_ref[part, :] = slope.astype(BF)
        acc[part, :] += nn(act, down_ref[...])

    @pl.when(step == pl.num_programs(0) - 1)
    def _():
        for utt in range(mod_ref.shape[0]):
            mod = mod_ref[utt]
            total = jnp.zeros((1, acc.shape[1]), F32)
            for _, part in row_blocks(span):
                here = slice(utt * span + part.start, utt * span + part.stop)
                branch = acc[here, :]
                mid = res_ref[here, :] + mod[2:3] * branch_ref[here, :]
                out_ref[here, :] = (mid + mod[5:6] * branch).astype(BF)
                upstream = cot_ref[here, :].astype(F32) * weight_ref[here, :]
                gb_ref[here, :] = (upstream * mod[5:6]).astype(BF)
                total += jnp.sum(upstream * branch, axis=0, keepdims=True)
            gate_ref[utt : utt + 1, :] = total


def ffn_backward_kernel(
    att_ref, outw_ref, res_ref, branch_ref, mod_ref, cot_ref, weight_ref, gb_ref,
    act_ref, slope_ref, up_ref, down_ref,
    gup_ref, gdown_ref, gmid_ref, gatt_ref, gout_ref, sums_ref, normed, acc, gba,
):
    step = pl.program_id(0)
    rows = att_ref.shape[0]
    utts = mod_ref.shape[0]
    span = rows // utts

    def hat_of(here, mod):
        return layer_norm(res_ref[here, :] + mod[2:3] * branch_ref[here, :])

    @pl.when(step == 0)
    def _():
        for utt in range(utts):
            mod = mod_ref[utt]
            for _, part in row_blocks(span):
                here = slice(utt * span + part.start, utt * span + part.stop)
                hat, _ = hat_of(here, mod)
                normed[here, :] = (hat * (1.0 + mod[4:5]) + mod[3:4]).astype(BF)
        acc[...] = jnp.zeros_like(acc)

    pieces = []
    for _, part in row_blocks(rows):
        grad = nt(gb_ref[part, :], down_ref[...]) * slope_ref[part, :].astype(F32)
        grad = grad.astype(BF)
        acc[part, :] += nt(grad, up_ref[...])
        pieces.append(grad)
    gdown_ref[...] = tn(act_ref[...], gb_ref[...]).astype(BF)
    gup_ref[...] = tn(normed[...], jnp.concatenate(pieces, axis=0)).astype(BF)

    @pl.when(step == pl.num_programs(0) - 1)
    def _():
        for utt in range(utts):
            mod = mod_ref[utt]
            width = acc.shape[1]
            shift = jnp.zeros((1, width), F32)
            scale = jnp.zeros((1, width), F32)
            gate = jnp.zeros((1, width), F32)
            for _, part in row_blocks(span):
                here = slice(utt * span + part.start, utt * span + part.stop)
                hat, inverse = hat_of(here, mod)
                grad = acc[here, :]
                shift += jnp.sum(grad, axis=0, keepdims=True)
                scale += jnp.sum(grad * hat, axis=0, keepdims=True)
                upstream = cot_ref[here, :].astype(F32) * weight_ref[here, :]
                mid = upstream + norm_back(grad * (1.0 + mod[4:5]), hat, inverse)
                gmid_ref[here, :] = mid
                gate += jnp.sum(mid * branch_ref[here, :], axis=0, keepdims=True)
                low = (mid * mod[2:3]).astype(BF)
                gba[here, :] = low
                gatt_ref[here, :] = nt(low, outw_ref[...]).astype(BF)
            sums_ref[utt, 0:1, :] = shift
            sums_ref[utt, 1:2, :] = scale
            sums_ref[utt, 2:3, :] = gate
        gout_ref[...] = tn(att_ref[...], gba[...]).astype(BF)


def whole_spec(shape):
    zeros = (0,) * len(shape)
    return pl.BlockSpec(shape, lambda i: zeros, pipeline_mode=pl.Buffered(1))


def ffn_forward(att, outw, res, mods, cot, weight, up, down, chunk=512):
    rows, width = res.shape
    hidden = up.shape[1]
    whole = [whole_spec(a.shape) for a in (att, outw, res, mods, cot, weight)]
    col = pl.BlockSpec((rows, chunk), lambda i: (0, i))
    utts = mods.shape[0]
    return pl.pallas_call(
        ffn_forward_kernel,
        grid=(hidden // chunk,),
        in_specs=whole
        + [
            pl.BlockSpec((width, chunk), lambda i: (0, i)),
            pl.BlockSpec((chunk, width), lambda i: (i, 0)),
        ],
        out_specs=[
            whole_spec((rows, width)),
            col,
            col,
            whole_spec((rows, width)),
            whole_spec((rows, width)),
            whole_spec((utts, width)),
        ],
        out_shape=[
            jax.ShapeDtypeStruct((rows, width), F32),
            jax.ShapeDtypeStruct((rows, hidden), BF),
            jax.ShapeDtypeStruct((rows, hidden), BF),
            jax.ShapeDtypeStruct((rows, width), BF),
            jax.ShapeDtypeStruct((rows, width), BF),
            jax.ShapeDtypeStruct((utts, width), F32),
        ],
        scratch_shapes=[pltpu.VMEM((rows, width), BF), pltpu.VMEM((rows, width), F32)],
        compiler_params=pltpu.CompilerParams(vmem_limit_bytes=VMEM_LIMIT),
        cost_estimate=pl.CostEstimate(
            flops=2 * rows * width * (width + 2 * hidden),
            bytes_accessed=60 * 2**20,
            transcendentals=rows * hidden,
        ),
        name="ffn_forward",
    )(att, outw, res, mods, cot, weight, up, down)


def ffn_backward(att, outw, res, branch, mods, cot, weight, gb, act, slope, up, down, chunk=512):
    rows, width = res.shape
    hidden = up.shape[1]
    utts = mods.shape[0]
    whole = [whole_spec(a.shape) for a in (att, outw, res, branch, mods, cot, weight, gb)]
    col = pl.BlockSpec((rows, chunk), lambda i: (0, i))
    upspec = pl.BlockSpec((width, chunk), lambda i: (0, i))
    downspec = pl.BlockSpec((chunk, width), lambda i: (i, 0))
    return pl.pallas_call(
        ffn_backward_kernel,
        grid=(hidden // chunk,),
        in_specs=whole + [col, col, upspec, downspec],
        out_specs=[
            upspec,
            downspec,
            whole_spec((rows, width)),
            whole_spec((rows, width)),
            whole_spec((width, width)),
            whole_spec((utts, 8, width)),
        ],
        out_shape=[
            jax.ShapeDtypeStruct((width, hidden), BF),
            jax.ShapeDtypeStruct((hidden, width), BF),
            jax.ShapeDtypeStruct((rows, width), F32),
            jax.ShapeDtypeStruct((rows, width), BF),
            jax.ShapeDtypeStruct((width, width), BF),
            jax.ShapeDtypeStruct((utts, 8, width), F32),
        ],
        scratch_shapes=[
            pltpu.VMEM((rows, width), BF),
            pltpu.VMEM((rows, width), F32),
            pltpu.VMEM((rows, width), BF),
        ],
        compiler_params=pltpu.CompilerParams(vmem_limit_bytes=VMEM_LIMIT),
        cost_estimate=pl.CostEstimate(
            flops=2 * rows * width * (2 * width + 4 * hidden),
            bytes_accessed=90 * 2**20,
            transcendentals=0,
        ),
        name="ffn_backward",
    )(att, outw, res, branch, mods, cot, weight, gb, act, slope, up, down)


def enter_kernel(
    in_ref, skip_ref, skip_w, qkv_w, mod_ref, cos_ref, sin_ref, res_ref, proj_ref
):
    width = in_ref.shape[1]
    mod = mod_ref[0]
    residual = nn(in_ref[...], skip_w[:width, :]) + nn(skip_ref[...], skip_w[width:, :])
    res_ref[...] = residual
    hat, _ = layer_norm(residual)
    normed = (hat * (1.0 + mod[1:2]) + mod[0:1]).astype(BF)
    lane = lanes_of(in_ref.shape[0])
    cos, sin = cos_ref[...], sin_ref[...]
    for part in range(3):
        projected = nn(normed, qkv_w[:, part * width : (part + 1) * width])
        for group in range(width // 128):
            cols = slice(group * 128, group * 128 + 128)
            piece = projected[:, cols]
            if part < 2:
                turned = jnp.where(
                    (lane & 63) < 32, pltpu.roll(piece, 96, 1), pltpu.roll(piece, 32, 1)
                )
                piece = piece * cos + turned * sin
            if part == 0:
                piece = piece * (0.125 * LOG2E)
            proj_ref[part, :, cols] = piece.astype(BF)


def enter_layer(first, second, skip_w, qkv_w, mods, cos, sin, block=256):
    rows, width = first.shape
    steps = rows // mods.shape[0] // block
    part = pl.BlockSpec((block, width), lambda i: (i, 0))
    table = pl.BlockSpec((block, 128), lambda i: (i % steps, 0))
    return pl.pallas_call(
        enter_kernel,
        grid=(rows // block,),
        in_specs=[
            part,
            part,
            whole_spec(skip_w.shape),
            whole_spec(qkv_w.shape),
            pl.BlockSpec((1,) + mods.shape[1:], lambda i: (i // steps, 0, 0)),
            table,
            table,
        ],
        out_specs=[part, pl.BlockSpec((3, block, width), lambda i: (0, i, 0))],
        out_shape=[
            jax.ShapeDtypeStruct((rows, width), F32),
            jax.ShapeDtypeStruct((3, rows, width), BF),
        ],
        compiler_params=pltpu.CompilerParams(vmem_limit_bytes=VMEM_LIMIT),
        cost_estimate=pl.CostEstimate(
            flops=2 * rows * (skip_w.size + qkv_w.size),
            bytes_accessed=40 * 2**20,
            transcendentals=0,
        ),
        name="enter_layer",
    )(first, second, skip_w, qkv_w, mods, cos, sin)


def leave_kernel(
    grad_ref, qkv_w, skip_w, res_ref, mid_ref, mod_ref, in_ref, skip_ref,
    gin_ref, gskip_ref, sums_ref, gqkv_ref, gw_ref, normed, stream,
):
    step = pl.program_id(0)
    rows, width = res_ref.shape
    utts = mod_ref.shape[0]
    span = rows // utts

    @pl.when(step == 0)
    def _():
        for utt in range(utts):
            mod = mod_ref[utt]
            shift = jnp.zeros((1, width), F32)
            scale = jnp.zeros((1, width), F32)
            for _, part in row_blocks(span):
                here = slice(utt * span + part.start, utt * span + part.stop)
                hat, inverse = layer_norm(res_ref[here, :])
                normed[here, :] = (hat * (1.0 + mod[1:2]) + mod[0:1]).astype(BF)
                grad = nt(grad_ref[here, :], qkv_w[...])
                shift += jnp.sum(grad, axis=0, keepdims=True)
                scale += jnp.sum(grad * hat, axis=0, keepdims=True)
                total = mid_ref[here, :] + norm_back(grad * (1.0 + mod[1:2]), hat, inverse)
                low = total.astype(BF)
                stream[here, :] = low
                gin_ref[here, :] = nt(low, skip_w[:width, :]).astype(BF)
                gskip_ref[here, :] = nt(low, skip_w[width:, :]).astype(BF)
            sums_ref[utt, 0:1, :] = shift
            sums_ref[utt, 1:2, :] = scale

    chunk = gqkv_ref.shape[1]
    cols = pl.ds(pl.multiple_of(step * chunk, chunk), chunk)
    gqkv_ref[...] = tn(normed[...], grad_ref[:, cols]).astype(BF)
    part = gw_ref.shape[2]
    here = pl.ds(pl.multiple_of(step * part, part), part)
    gw_ref[0] = tn(in_ref[...], stream[:, here]).astype(BF)
    gw_ref[1] = tn(skip_ref[...], stream[:, here]).astype(BF)


def leave_layer(grads, qkv_w, skip_w, res, mid, mods, first, second, steps=4):
    rows, width = res.shape
    utts = mods.shape[0]
    ins = (grads, qkv_w, skip_w, res, mid, mods, first, second)
    outs = pl.pallas_call(
        leave_kernel,
        grid=(steps,),
        in_specs=[whole_spec(a.shape) for a in ins],
        out_specs=[
            whole_spec((rows, width)),
            whole_spec((rows, width)),
            whole_spec((utts, 8, width)),
            pl.BlockSpec((width, 3 * width // steps), lambda i: (0, i)),
            pl.BlockSpec((2, width, width // steps), lambda i: (0, 0, i)),
        ],
        out_shape=[
            jax.ShapeDtypeStruct((rows, width), BF),
            jax.ShapeDtypeStruct((rows, width), BF),
            jax.ShapeDtypeStruct((utts, 8, width), F32),
            jax.ShapeDtypeStruct((width, 3 * width), BF),
            jax.ShapeDtypeStruct((2, width, width), BF),
        ],
        scratch_shapes=[pltpu.VMEM((rows, width), BF), pltpu.VMEM((rows, width), BF)],
        compiler_params=pltpu.CompilerParams(vmem_limit_bytes=VMEM_LIMIT),
        cost_estimate=pl.CostEstimate(
            flops=4 * rows * (skip_w.size + qkv_w.size),
            bytes_accessed=60 * 2**20,
            transcendentals=0,
        ),
        name="leave_layer",
    )(*ins)
    return tuple(outs[:4]) + (outs[4].reshape(2 * width, width),)


class GradSum:
    def __init__(self, jobs, send, recv, local):
        self.jobs, self.send, self.recv, self.local = jobs, send, recv, local
        me, x, core = lax.axis_index("seq"), lax.axis_index("x"), lax.axis_index("core")
        self.bits = (me // 4, (me // 2) % 2, me % 2, x, core)
        self.copies = [[] for _ in jobs]
        self.keeps = []

    def peer(self, dim):
        me, x, core = lax.axis_index("seq"), lax.axis_index("x"), lax.axis_index("core")
        if dim < 3:
            return (me ^ (4 >> dim), x, core)
        return (me, 1 - x, core) if dim == 3 else (me, x, 1 - core)

    def launch(self, index, source, target, dim):
        at = len(self.copies[index])
        copy = remote(
            source,
            target,
            self.send.at[index * 7 + at],
            self.recv.at[index * 7 + at],
            self.peer(dim),
        )
        copy.start()
        self.copies[index].append(copy)

    def absorb(self, index, stage):
        _, _, _, order, keep, arrivals = self.jobs[index]
        done = order[1 : stage + 1]
        left = [dim for dim in range(4) if dim not in done]
        self.copies[index][stage].wait_recv()

        def add(i, carry):
            at = list(self.bits[:4])
            place = []
            for n, dim in enumerate(left):
                bit = (i >> (len(left) - 1 - n)) & 1
                at[dim] = bit
                place.append(bit)
            mine = keep[at[0], at[1], at[2], at[3]].astype(F32)
            other = arrivals[stage][tuple(place)] if place else arrivals[stage][...]
            keep[at[0], at[1], at[2], at[3]] = (mine + other.astype(F32)).astype(BF)
            return carry

        lax.fori_loop(0, 2 ** len(left), add, 0)

    def stage(self, number):
        for index, (grad, out, cols, order, keep, arrivals) in enumerate(self.jobs):
            tail = (slice(None), cols)
            bits = self.bits
            if number == 0:
                lead = (slice(None),) * 4
                own = pltpu.make_async_copy(
                    grad.at[lead + (bits[4],) + tail], keep, self.local.at[index]
                )
                own.start()
                self.keeps.append(own)
                self.launch(index, grad.at[lead + (1 - bits[4],) + tail], arrivals[0], 4)
            elif number < 5:
                if number == 1:
                    self.keeps[index].wait()
                self.absorb(index, number - 1)
                dim = order[number]
                done = order[1:number]
                where = tuple(
                    1 - bits[d] if d == dim else bits[d] if d in done else slice(None)
                    for d in range(4)
                )
                self.launch(index, keep.at[where], arrivals[number], dim)
            elif number == 5:
                self.absorb(index, 4)
                mine = keep.at[bits[:4]]
                spot = out.at[(bits[3], bits[4]) + tail]
                own = pltpu.make_async_copy(mine, spot, self.local.at[index])
                own.start()
                self.keeps[index] = own
                self.launch(index, mine, spot, 3)
            else:
                self.keeps[index].wait()
                self.copies[index][5].wait_recv()
                both = out.at[(slice(None), bits[4]) + tail]
                self.launch(index, both, both, 4)

    def finish(self):
        for chain in self.copies:
            chain[6].wait_recv()
        for chain in self.copies:
            for copy in chain:
                copy.wait_send()


def reduce_kernel(*refs, count):
    grads, small = refs[:count], refs[count]
    outs, small_out = refs[count + 1 : 2 * count + 1], refs[2 * count + 1]
    rest = refs[2 * count + 2 :]
    jobs = 3 * count
    buffers = rest[: 6 * jobs]
    small_in, small_low, send, recv, local, ssend, srecv, bsend, brecv, slocal = rest[6 * jobs :]
    me, x, core = lax.axis_index("seq"), lax.axis_index("x"), lax.axis_index("core")
    others = [seq_flip(flip) for flip in range(7, 0, -1)]
    mates = [(me, (x + dx) % 2, (core + dc) % 2) for dx, dc in ((0, 1), (1, 0), (1, 1))]
    greet(others + mates)
    work = []
    orders = ((4, 3, 2, 1, 0), (4, 2, 1, 3, 0), (4, 1, 3, 2, 0))
    for index in range(jobs):
        grad, out = grads[index // 3], outs[index // 3]
        cols = split_columns(grad.shape[-1], (1, 1, 1))[index % 3]
        keep, arrivals = buffers[6 * index], buffers[6 * index + 1 : 6 * index + 6]
        work.append((grad, out, cols, orders[index % 3], keep, arrivals))
    chain = GradSum(work, send, recv, local)
    chain.stage(0)
    own = pltpu.make_async_copy(small, small_in.at[me], slocal.at[0])
    own.start()
    smalls = []
    for flip, device in zip(range(7, 0, -1), others):
        smalls.append(remote(small, small_in.at[me], ssend.at[flip], srecv.at[flip], device))
        smalls[-1].start()
    for number in range(1, 6):
        chain.stage(number)
    own.wait()
    for copy in smalls:
        copy.wait_recv()
    total = small_in[0]
    for index in range(1, 8):
        total = total + small_in[index]
    small_low[...] = total.astype(BF)
    quarter = x * 2 + core
    keep = pltpu.make_async_copy(small_low, small_out.at[quarter], slocal.at[1])
    keep.start()
    lows = []
    for slot, device in enumerate(mates):
        lows.append(remote(small_low, small_out.at[quarter], bsend.at[slot], brecv.at[slot], device))
        lows[-1].start()
    chain.stage(6)
    chain.finish()
    for copy in smalls:
        copy.wait_send()
    keep.wait()
    for copy in lows:
        copy.wait()


def reduce_grads(grads, small, collective_id=3):
    views, outs, buffers = [], [], []
    for grad in grads:
        rows, width = grad.shape
        span = rows // 32
        views.append(grad.reshape(2, 2, 2, 2, 2, span, width))
        outs.append(jax.ShapeDtypeStruct((2, 2, span, width), BF))
        for cols in split_columns(width, (1, 1, 1)):
            tail = (span, cols.size)
            buffers.append(pltpu.VMEM((2, 2, 2, 2) + tail, BF))
            for left in (4, 3, 2, 1, 0):
                buffers.append(pltpu.VMEM((2,) * left + tail, BF))
    anywhere = pl.BlockSpec(memory_space=pl.ANY)
    jobs = 3 * len(grads)
    dma = pltpu.SemaphoreType.DMA
    outs.append(jax.ShapeDtypeStruct((4,) + small.shape, BF))
    results = pl.pallas_call(
        functools.partial(reduce_kernel, count=len(grads)),
        in_specs=[anywhere] * (len(grads) + 1),
        out_specs=[anywhere] * (len(grads) + 1),
        out_shape=outs,
        scratch_shapes=buffers
        + [pltpu.VMEM((8,) + small.shape, F32), pltpu.VMEM(small.shape, BF)]
        + [dma((7 * jobs,)), dma((7 * jobs,)), dma((jobs,)), dma((8,)), dma((8,)), dma((3,)), dma((3,)), dma((2,))],
        compiler_params=pltpu.CompilerParams(
            vmem_limit_bytes=VMEM_LIMIT, collective_id=collective_id, has_side_effects=True
        ),
        name="reduce_grads",
    )(*views, small)
    shards = [
        result.reshape(grad.shape[0] // 8, grad.shape[1]).astype(jnp.float32)
        for result, grad in zip(results, grads)
    ]
    return shards, results[-1].astype(jnp.float32)


def rotary_tables(positions):
    half_dim = HEAD_DIM // 2
    channel = jnp.arange(half_dim, dtype=jnp.float32)
    inverse = jnp.power(10000.0, -2.0 * channel / HEAD_DIM)
    angles = positions.astype(jnp.float32)[:, None] * inverse[None, :]
    angles = jnp.concatenate([angles, angles], axis=1)
    return (jnp.cos(angles), jnp.sin(angles))


def rotate_heads(field, cosine_table, sine_table):
    half_dim = field.shape[-1] // 2
    turned = jnp.concatenate([-field[..., half_dim:], field[..., :half_dim]], axis=-1)
    return field * cosine_table + turned * sine_table


def smooth_gelu(values):
    return jax.nn.gelu(values, approximate=True)


def cross(left, right):
    return lax.dot_general(
        left, right, (((0,), (0,)), ((), ())), preferred_element_type=jnp.float32
    )


def back_product(left, right):
    return lax.dot_general(
        left, right, (((1,), (1,)), ((), ())), preferred_element_type=jnp.float32
    )


def block_terms(query_block, dout_block, lse_block, delta_block, key_block, value_block, key_live):
    scores = jnp.einsum(
        "bqhd,bkhd->bhqk", query_block, key_block, preferred_element_type=jnp.float32
    )
    lse_heads = jnp.transpose(lse_block, (0, 2, 1))[..., None]
    probs = jnp.where(key_live[:, None, None, :], jnp.exp(scores - lse_heads), 0.0)
    grad_probs = jnp.einsum(
        "bqhd,bkhd->bhqk", dout_block, value_block, preferred_element_type=jnp.float32
    )
    delta_heads = jnp.transpose(delta_block, (0, 2, 1))[..., None]
    dscore = (probs * (grad_probs - delta_heads)).astype(jnp.bfloat16)
    return (probs.astype(jnp.bfloat16), dscore)


BATCH = ("x", "core")


def batch_index():
    return lax.axis_index("x") * lax.axis_size("core") + lax.axis_index("core")


def gather_weight(weight):
    parts = lax.axis_size(BATCH)
    if weight.shape[0] % parts:
        return lax.all_gather(weight, "seq", axis=0, tiled=True)
    rows = weight.shape[0] // parts
    mine = lax.dynamic_slice_in_dim(weight, batch_index() * rows, rows, 0)
    return lax.all_gather(mine, ("seq",) + BATCH, axis=0, tiled=True)


def sum_weight(grad):
    rows, width = grad.shape
    low = grad.astype(jnp.bfloat16)
    seq_count, cores = lax.axis_size("seq"), lax.axis_size("core")
    parts = seq_count * lax.axis_size(BATCH)
    if rows % parts or cores != 2:
        shard = lax.psum_scatter(low, "seq", scatter_dimension=0, tiled=True)
        return lax.psum(shard, BATCH).astype(jnp.float32)
    core = lax.axis_index("core")
    held = low.reshape(parts // 2, 2, rows // parts, width)
    send = lax.dynamic_index_in_dim(held, 1 - core, 1, keepdims=False)
    keep = lax.dynamic_index_in_dim(held, core, 1, keepdims=False)
    got = lax.ppermute(send, "core", [(0, 1), (1, 0)])
    half = (keep.astype(jnp.float32) + got.astype(jnp.float32)).astype(jnp.bfloat16)
    half = half.reshape(rows // 2, width)
    shard = lax.psum_scatter(half, ("seq", "x"), scatter_dimension=0, tiled=True)
    return lax.all_gather(shard, BATCH, axis=0, tiled=True).astype(jnp.float32)


def gather_kernel(*refs, count, ahead):
    weights, laters = refs[:count], refs[count : count + ahead]
    seq_small, batch_small = refs[count + ahead : count + ahead + 2]
    outs = refs[count + ahead + 2 :]
    fulls, helds = outs[:count], outs[count : count + ahead]
    seq_out, batch_out, send, recv, asend, arecv, small_send, small_recv, local = outs[count + ahead :]
    me, x, core = lax.axis_index("seq"), lax.axis_index("x"), lax.axis_index("core")
    bits = (me // 4, (me // 2) % 2, me % 2, x, core)

    def peer(dim):
        if dim < 3:
            return (me ^ (4 >> dim), x, core)
        return (me, 1 - x, core) if dim == 3 else (me, x, 1 - core)

    others = [((me + d) % 8, x, core) for d in range(1, 8)]
    mates = [(me, (x + dx) % 2, (core + dc) % 2) for dx, dc in ((0, 1), (1, 0), (1, 1))]
    barrier = pltpu.get_barrier_semaphore()
    for device in others + mates:
        pl.semaphore_signal(barrier, inc=1, device_id=device, device_id_type=pl.DeviceIdType.MESH)
    pl.semaphore_wait(barrier, len(others) + len(mates))

    small = []
    quarter = x * 2 + core
    own_seq = pltpu.make_async_copy(seq_small, seq_out.at[me], local.at[0])
    own_batch = pltpu.make_async_copy(batch_small, batch_out.at[quarter], local.at[1])
    own_seq.start()
    own_batch.start()
    for slot, device in enumerate(others):
        small.append(
            pltpu.make_async_remote_copy(
                seq_small, seq_out.at[me], small_send.at[slot], small_recv.at[slot],
                device_id=device, device_id_type=pl.DeviceIdType.MESH,
            )
        )
    for slot, device in enumerate(mates):
        small.append(
            pltpu.make_async_remote_copy(
                batch_small, batch_out.at[quarter], small_send.at[7 + slot], small_recv.at[7 + slot],
                device_id=device, device_id_type=pl.DeviceIdType.MESH,
            )
        )
    for copy in small:
        copy.start()

    jobs = early_jobs(weights, fulls)
    chain = WeightGather(jobs, send, recv, local.at[pl.ds(2, len(jobs))])
    later = WeightGather(
        ahead_jobs(laters, helds), asend, arecv, local.at[pl.ds(2 + len(jobs), ahead)]
    )
    chain.stage()
    chain.stage()
    later.stage()
    chain.stage()
    later.stage()
    chain.stage()
    chain.stage()
    chain.finish()
    later.finish()
    for copy in small:
        copy.wait()
    own_seq.wait()
    own_batch.wait()


def gather_early(weights, laters, seq_small, batch_small):
    anywhere = pl.BlockSpec(memory_space=pl.ANY)
    jobs, ahead = 3 * len(weights), len(laters)
    total = len(weights) + ahead + 2
    dma = pltpu.SemaphoreType.DMA
    quarter = lambda lead, w: jax.ShapeDtypeStruct((2,) * lead + (w.shape[0] // 4, w.shape[1]), BF)
    outs = pl.pallas_call(
        functools.partial(gather_kernel, count=len(weights), ahead=ahead),
        in_specs=[anywhere] * total,
        out_specs=[anywhere] * total,
        out_shape=[quarter(5, w) for w in weights]
        + [quarter(2, w) for w in laters]
        + [
            jax.ShapeDtypeStruct((8,) + seq_small.shape, F32),
            jax.ShapeDtypeStruct((4,) + batch_small.shape, F32),
        ],
        scratch_shapes=[
            dma((5 * jobs,)),
            dma((5 * jobs,)),
            dma((5 * ahead,)),
            dma((5 * ahead,)),
            dma((10,)),
            dma((10,)),
            dma((2 + jobs + ahead,)),
        ],
        compiler_params=pltpu.CompilerParams(collective_id=0, has_side_effects=True),
        name="gather_early",
    )(*weights, *laters, seq_small, batch_small)
    fulls = [full.reshape(8 * w.shape[0], w.shape[1]) for full, w in zip(outs, weights)]
    return fulls, outs[len(weights) : len(weights) + ahead], outs[-2], outs[-1]


def paired_tables(positions):
    cos, sin = rotary_tables(positions)
    half = HEAD_DIM // 2
    signed = jnp.concatenate([-sin[:, :half], sin[:, half:]], axis=1)
    return jnp.tile(cos, (1, 2)), jnp.tile(signed, (1, 2))


def on_device(
    layer_input,
    skip_input,
    time_embed,
    lengths,
    cond_drop,
    cotangent,
    skip_weight,
    adaln_weight,
    adaln_bias,
    qkv_weight,
    out_weight,
    up_weight,
    down_weight,
):
    utt_count, frame_span, model_width = layer_input.shape
    head_count = model_width // HEAD_DIM
    row_count = utt_count * frame_span
    seq_here = lax.axis_index("seq")
    seq_count = lax.axis_size("seq")
    frame_count = frame_span * seq_count
    by_heads = (
        seq_count == 8
        and head_count == 16
        and utt_count == 2
        and lax.axis_size(BATCH) == 4
        and frame_span == 512
    )
    local_pos = seq_here * frame_span + jnp.arange(frame_span, dtype=jnp.int32)
    local_live = local_pos[None, :] < lengths[:, None]
    valid_mask = local_live.astype(jnp.float32)
    drop = cond_drop.astype(jnp.float32)
    dropped = drop[:, None] * valid_mask
    frames_live = jnp.minimum(lengths, frame_count).astype(jnp.float32)
    counts = jnp.stack([jnp.sum((1.0 - drop) * frames_live), jnp.sum(drop * frames_live)])
    silu_time = jax.nn.silu(time_embed.astype(jnp.float32)).astype(jnp.bfloat16)
    row_span = adaln_weight.shape[0]
    silu_mine = lax.dynamic_slice_in_dim(silu_time, seq_here * row_span, row_span, 1)
    mod_part = jnp.dot(silu_mine, adaln_weight, preferred_element_type=jnp.float32)
    bias_span = adaln_bias.shape[0]
    bias_here = lax.dynamic_update_slice_in_dim(
        jnp.zeros((mod_part.shape[1],), jnp.float32),
        adaln_bias.astype(jnp.float32),
        seq_here * bias_span,
        0,
    )
    mod_part = mod_part + bias_here
    if by_heads:
        small = jnp.concatenate(
            [
                silu_time.astype(jnp.float32),
                jnp.pad(counts[None, :], ((0, 5), (0, model_width - 2))),
            ],
            axis=0,
        )
        (skip_full, qkv_full), late_held, mod_every, small_every = gather_early(
            (skip_weight, qkv_weight),
            (out_weight, up_weight, down_weight),
            mod_part.reshape(-1, model_width),
            small,
        )
        modulation = jnp.sum(mod_every, axis=0)
        totals = jnp.sum(small_every[:, utt_count, :2], axis=0)
        silu_every = small_every[:, :utt_count].reshape(-1, model_width)
    else:
        modulation = lax.psum(mod_part, "seq")
        totals = lax.psum(counts, BATCH)
        skip_full = gather_weight(skip_weight)
        qkv_full = gather_weight(qkv_weight)
        silu_every = lax.all_gather(silu_time, BATCH, axis=0, tiled=True).astype(jnp.float32)
    modulation = modulation.reshape(utt_count, 6, model_width)
    kept_total = jnp.maximum(totals[0], 1.0)
    drop_total = jnp.maximum(totals[1], 1.0)
    every_count = kept_total + drop_total
    loss_weight = (valid_mask - dropped) * (every_count / (2.0 * kept_total)) + dropped * (
        every_count / (2.0 * drop_total)
    )
    first_rows = layer_input.reshape(row_count, model_width)
    second_rows = skip_input.reshape(row_count, model_width)
    if by_heads:
        cos_all, sin_all = paired_tables(jnp.arange(frame_count, dtype=jnp.int32))
        cos_here = lax.dynamic_slice_in_dim(cos_all, seq_here * frame_span, frame_span, 0)
        sin_here = lax.dynamic_slice_in_dim(sin_all, seq_here * frame_span, frame_span, 0)
        residual_rows, proj = enter_layer(
            first_rows, second_rows, skip_full, qkv_full, modulation, cos_here, sin_here
        )
        (qkv_all, out_all, lse_all, attended_low), (out_full, up_full, down_full) = attend_forward(
            lengths, proj, *late_held, frame_span
        )
    else:
        joined = jnp.concatenate([layer_input, skip_input], axis=-1).reshape(row_count, 2 * model_width)
        residual_in = jnp.dot(joined, skip_full, preferred_element_type=jnp.float32).reshape(
            utt_count, frame_span, model_width
        )
        shift_attn = modulation[:, 0][:, None, :]
        scale_attn = modulation[:, 1][:, None, :]
        hat_attn, inv_attn = layer_norm(residual_in)
        normed_attn = (
            (hat_attn * (1.0 + scale_attn) + shift_attn)
            .astype(jnp.bfloat16)
            .reshape(row_count, model_width)
        )
        residual_rows = residual_in.reshape(row_count, model_width)
        out_full, up_full, down_full = [
            gather_weight(weight) for weight in (out_weight, up_weight, down_weight)
        ]
        projected = jnp.dot(normed_attn, qkv_full, preferred_element_type=jnp.float32).reshape(
            utt_count, frame_span, 3, head_count, HEAD_DIM
        )
        cosine_table, sine_table = rotary_tables(local_pos)
        cosine_table = cosine_table[None, :, None, :]
        sine_table = sine_table[None, :, None, :]
        queries = (rotate_heads(projected[:, :, 0], cosine_table, sine_table) * 0.125).astype(
            jnp.bfloat16
        )
        keys_rot = rotate_heads(projected[:, :, 1], cosine_table, sine_table).astype(jnp.bfloat16)
        values = projected[:, :, 2].astype(jnp.bfloat16)
        start_top = jnp.full((utt_count, head_count, frame_span), MASKED, jnp.float32)
        top_score = start_top
        key_piece = lax.all_gather(keys_rot, "seq", axis=1, tiled=True)
        value_piece = lax.all_gather(values, "seq", axis=1, tiled=True)
        piece_len = key_piece.shape[1]
        piece_live = jnp.arange(piece_len, dtype=jnp.int32)[None, :] < lengths[:, None]
        scores = jnp.einsum("bqhd,bkhd->bhqk", queries, key_piece, preferred_element_type=jnp.float32)
        scores = jnp.where(piece_live[:, None, None, :], scores, MASKED)
        new_top = jnp.maximum(top_score, jnp.max(scores, axis=-1))
        expo = jnp.where(piece_live[:, None, None, :], jnp.exp(scores - new_top[..., None]), 0.0)
        denom = jnp.sum(expo, axis=-1)
        partial_out = jnp.einsum(
            "bhqk,bkhd->bqhd",
            expo.astype(jnp.bfloat16),
            value_piece,
            preferred_element_type=jnp.float32,
        )
        accum = partial_out
        accum, top_score, denom = (accum, new_top, denom)
        attended_full = accum / jnp.transpose(denom, (0, 2, 1))[..., None]
        lse_rows = jnp.transpose(top_score + jnp.log(denom), (0, 2, 1))
        attended_low = attended_full.astype(jnp.bfloat16).reshape(row_count, model_width)
    cot_rows = cotangent.reshape(row_count, model_width)
    weight_rows = loss_weight.reshape(row_count, 1)
    branch_attn, hidden_act, hidden_slope, grad_branch_ffn, layer_output, grad_gate_ffn = ffn_forward(
        attended_low,
        out_full,
        residual_rows,
        modulation,
        cot_rows,
        weight_rows,
        up_full,
        down_full,
    )
    layer_output = layer_output.reshape(utt_count, frame_span, model_width)
    grad_up, grad_down, grad_mid, grad_attended_flat, grad_out, ffn_sums = ffn_backward(
        attended_low,
        out_full,
        residual_rows,
        branch_attn,
        modulation,
        cot_rows,
        weight_rows,
        grad_branch_ffn,
        hidden_act,
        hidden_slope,
        up_full,
        down_full,
    )
    grad_shift_ffn, grad_scale_ffn, grad_gate_attn = ffn_sums[:, 0], ffn_sums[:, 1], ffn_sums[:, 2]
    if by_heads:
        grad_projected = attend_backward(
            lengths, grad_attended_flat, qkv_all, out_all, lse_all, cos_all, sin_all, frame_span
        )
    else:
        grad_attended = grad_attended_flat.reshape(
            utt_count, frame_span, head_count, HEAD_DIM
        )
        delta_rows = jnp.sum(grad_attended.astype(jnp.float32) * attended_full, axis=-1)
        lse_all, delta_all = (
            lax.all_gather(lse_rows, "seq", axis=1, tiled=True),
            lax.all_gather(delta_rows, "seq", axis=1, tiled=True),
        )
        key_piece = lax.all_gather(keys_rot, "seq", axis=1, tiled=True)
        value_piece = lax.all_gather(values, "seq", axis=1, tiled=True)
        piece_len = key_piece.shape[1]
        piece_live = jnp.arange(piece_len, dtype=jnp.int32)[None, :] < lengths[:, None]
        probs_low, dscore = block_terms(
            queries, grad_attended, lse_rows, delta_rows, key_piece, value_piece, piece_live
        )
        grad_queries = jnp.einsum(
            "bhqk,bkhd->bqhd", dscore, key_piece, preferred_element_type=jnp.float32
        )
        query_piece = lax.all_gather(queries, "seq", axis=1, tiled=True)
        dout_piece = lax.all_gather(grad_attended, "seq", axis=1, tiled=True)
        probs_low, dscore = block_terms(
            query_piece, dout_piece, lse_all, delta_all, keys_rot, values, local_live
        )
        grad_k = jnp.einsum("bhqk,bqhd->bkhd", dscore, query_piece, preferred_element_type=jnp.float32)
        grad_v = jnp.einsum(
            "bhqk,bqhd->bkhd", probs_low, dout_piece, preferred_element_type=jnp.float32
        )
        grad_q_pre = rotate_heads(grad_queries * 0.125, cosine_table, -sine_table)
        grad_k_pre = rotate_heads(grad_k, cosine_table, -sine_table)
        grad_projected = (
            jnp.stack([grad_q_pre, grad_k_pre, grad_v], axis=2)
            .reshape(row_count, 3 * model_width)
            .astype(jnp.bfloat16)
        )
    if by_heads:
        grad_input, grad_skip, attn_sums, grad_qkv, grad_skip_w = leave_layer(
            grad_projected,
            qkv_full,
            skip_full,
            residual_rows,
            grad_mid,
            modulation,
            first_rows,
            second_rows,
        )
        grad_input = grad_input.reshape(layer_input.shape)
        grad_skip = grad_skip.reshape(skip_input.shape)
        grad_shift_attn, grad_scale_attn = attn_sums[:, 0], attn_sums[:, 1]
    else:
        grad_mid = grad_mid.reshape(utt_count, frame_span, model_width)
        grad_qkv = cross(normed_attn, grad_projected)
        grad_normed_attn = back_product(grad_projected, qkv_full).reshape(
            utt_count, frame_span, model_width
        )
        grad_shift_attn = jnp.sum(grad_normed_attn, axis=1)
        grad_scale_attn = jnp.sum(grad_normed_attn * hat_attn, axis=1)
        grad_stream = grad_mid + norm_back(grad_normed_attn * (1.0 + scale_attn), hat_attn, inv_attn)
        grad_stream_low = grad_stream.astype(jnp.bfloat16).reshape(row_count, model_width)
        grad_skip_w = cross(joined, grad_stream_low)
        grad_joined = back_product(grad_stream_low, skip_full)
        grad_input = (
            grad_joined[:, :model_width]
            .reshape(utt_count, frame_span, model_width)
            .astype(jnp.bfloat16)
        )
        grad_skip = (
            grad_joined[:, model_width:]
            .reshape(utt_count, frame_span, model_width)
            .astype(jnp.bfloat16)
        )
    grad_modulation = jnp.stack(
        [
            grad_shift_attn,
            grad_scale_attn,
            grad_gate_attn,
            grad_shift_ffn,
            grad_scale_ffn,
            grad_gate_ffn,
        ],
        axis=1,
    ).reshape(utt_count, 6 * model_width)
    weight_grads = (grad_skip_w, grad_qkv, grad_out, grad_up, grad_down)
    if by_heads:
        order = (4, 3, 1, 0, 2)
        shards, mod_every = reduce_grads(
            [weight_grads[i] for i in order], grad_modulation.reshape(-1, model_width)
        )
        summed = [shards[order.index(i)] for i in range(5)]
        mod_every = mod_every.reshape(-1, 6 * model_width)
    else:
        mod_total = lax.psum(grad_modulation, "seq")
        mod_every = lax.all_gather(
            mod_total.astype(jnp.bfloat16), BATCH, axis=0, tiled=True
        ).astype(jnp.float32)
        summed = [sum_weight(grad) for grad in weight_grads]
    silu_rows = lax.dynamic_slice_in_dim(silu_every, seq_here * row_span, row_span, 1)
    adaln_rows = jnp.dot(silu_rows.T, mod_every, precision=lax.Precision.HIGHEST)
    bias_rows = lax.dynamic_slice_in_dim(
        jnp.sum(mod_every, axis=0), seq_here * bias_span, bias_span, 0
    )
    results = (summed[0], adaln_rows, bias_rows, summed[1], summed[2], summed[3], summed[4])
    return (
        layer_output,
        grad_input,
        grad_skip,
        results[0],
        results[1],
        results[2],
        results[3],
        results[4],
        results[5],
        results[6],
    )


def solution(mesh):
    count, batch = mesh.shape["seq"], mesh.shape["batch"]
    cores = 2 if batch % 2 == 0 else 1
    split = Mesh(mesh.devices.reshape(count, batch // cores, cores), ("seq",) + BATCH)
    placed = (
        P(BATCH, "seq", None),
        P(BATCH, "seq", None),
        P(BATCH, None),
        P(BATCH),
        P(BATCH),
        P(BATCH, "seq", None),
        P("seq", None),
        P("seq", None),
        P("seq"),
        P("seq", None),
        P("seq", None),
        P("seq", None),
        P("seq", None),
    )
    return jax.shard_map(
        on_device,
        mesh=split,
        in_specs=placed,
        out_specs=(
            P(BATCH, "seq", None),
            P(BATCH, "seq", None),
            P(BATCH, "seq", None),
            P("seq", None),
            P("seq", None),
            P("seq"),
            P("seq", None),
            P("seq", None),
            P("seq", None),
            P("seq", None),
        ),
        check_vma=False,
    )
```

```python
import functools
import jax
import jax.numpy as jnp
import numpy as np
from jax import lax
from jax.sharding import Mesh, PartitionSpec as P
from jax.experimental import pallas as pl
from jax.experimental.pallas import tpu as pltpu
HEAD_DIM = 64
EPS = 1e-06
LOG2E = 1.4426950408889634
LN2 = 0.6931471805599453
MASKED = -1e30
BF = jnp.bfloat16
F32 = jnp.float32
VMEM_LIMIT = 60 * 2**20


def nt(left, right):
    return lax.dot_general(left, right, (((1,), (1,)), ((), ())), preferred_element_type=F32)


def nn(left, right):
    return lax.dot_general(left, right, (((1,), (0,)), ((), ())), preferred_element_type=F32)


def head_sums(product, lane):
    first = jnp.sum(jnp.where(lane < 64, product, 0.0), axis=1, keepdims=True)
    second = jnp.sum(jnp.where(lane >= 64, product, 0.0), axis=1, keepdims=True)
    return (first, second)


def lanes_of(rows):
    return lax.broadcasted_iota(jnp.int32, (rows, 128), 1)


def attention_cost(frames, products):
    return pl.CostEstimate(
        flops=2 * products * 2 * frames * frames * 128,
        bytes_accessed=frames * 128 * 2 * 8,
        transcendentals=2 * frames * frames,
    )


def turn_back(grad, cos, sin):
    lane = lanes_of(grad.shape[0])
    turned = jnp.where((lane & 63) < 32, pltpu.roll(grad, 96, 1), pltpu.roll(grad, 32, 1))
    return grad * cos - turned * sin


def three(column, lane, at):
    high = column.astype(BF).astype(F32)
    rest = column - high
    mid = rest.astype(BF).astype(F32)
    low = rest - mid
    return jnp.where(lane == at, -high, jnp.where(lane == at + 1, -mid, jnp.where(lane == at + 2, -low, 0.0)))


MESH_IDS = pl.DeviceIdType.MESH


def seq_flip(flip):
    return (lax.axis_index("seq") ^ flip, lax.axis_index("x"), lax.axis_index("core"))


def greet(devices):
    barrier = pltpu.get_barrier_semaphore()
    for device in devices:
        pl.semaphore_signal(barrier, inc=1, device_id=device, device_id_type=MESH_IDS)
    pl.semaphore_wait(barrier, len(devices))


def remote(source, target, send, recv, device):
    return pltpu.make_async_remote_copy(
        source, target, send, recv, device_id=device, device_id_type=MESH_IDS
    )


class WeightGather:
    def __init__(self, jobs, send, recv, local):
        self.jobs, self.send, self.recv, self.local = jobs, send, recv, local
        me, x, core = lax.axis_index("seq"), lax.axis_index("x"), lax.axis_index("core")
        self.bits = (me // 4, (me // 2) % 2, me % 2, x, core)
        self.copies = [[] for _ in jobs]
        self.owns = []

    def peer(self, dim):
        me, x, core = lax.axis_index("seq"), lax.axis_index("x"), lax.axis_index("core")
        if dim < 3:
            return (me ^ (4 >> dim), x, core)
        return (me, 1 - x, core) if dim == 3 else (me, x, 1 - core)

    def stage(self):
        for index, (full, cols, source, ready, order) in enumerate(self.jobs):
            at = len(self.copies[index])
            where = tuple(
                slice(None) if d in ready + order[:at] else self.bits[d]
                for d in range(len(full.shape) - 2)
            ) + (slice(None), cols)
            if at == 0:
                own = pltpu.make_async_copy(source, full.at[where], self.local.at[index])
                own.start()
                self.owns.append(own)
            else:
                if at == 1:
                    self.owns[index].wait()
                self.copies[index][at - 1].wait_recv()
            copy = remote(
                source if at == 0 else full.at[where],
                full.at[where],
                self.send.at[index * 5 + at],
                self.recv.at[index * 5 + at],
                self.peer(order[at]),
            )
            copy.start()
            self.copies[index].append(copy)

    def finish(self):
        for chain in self.copies:
            chain[-1].wait_recv()
        for chain in self.copies:
            for copy in chain:
                copy.wait_send()


def split_columns(width, shares):
    total, start, out = sum(shares), 0, []
    for n in range(len(shares)):
        stop = width * sum(shares[: n + 1]) // total // 128 * 128
        out.append(pl.ds(start, stop - start))
        start = stop
    return out


def quarter_of(weight, cols):
    quarter = lax.axis_index("x") * 2 + lax.axis_index("core")
    span = weight.shape[0] // 4
    return weight.at[pl.ds(quarter * span, span), cols]


def early_jobs(weights, fulls):
    orders = ((0, 1, 2, 3, 4), (0, 2, 3, 1, 4), (0, 3, 1, 2, 4))
    return [
        (full, cols, quarter_of(weight, cols), (), order)
        for weight, full in zip(weights, fulls)
        for cols, order in zip(split_columns(weight.shape[1], (1, 1, 1)), orders)
    ]


def ahead_jobs(weights, helds):
    every = [(weight, held, pl.ds(0, weight.shape[1])) for weight, held in zip(weights, helds)]
    return [(held, cols, quarter_of(weight, cols), (), (0, 1)) for weight, held, cols in every]


def late_jobs(helds, fulls):
    return [
        (full, cols, held.at[:, :, :, cols], (0, 1), order)
        for held, full in zip(helds, fulls)
        for cols, order in zip(split_columns(held.shape[3], (3, 1)), ((2, 3, 4), (3, 2, 4)))
    ]


def attend_forward_kernel(
    len_ref, proj, out_w, up_w, down_w,
    qkv_all, o_all, lse_ref, att, out_full, up_full, down_full,
    qkv, outs, ka, kb, vta, vtb,
    wsend, wrecv, wlocal, qsend, qrecv, qlocal, osend, orecv, olocal, slocal,
    *, span, bq, bk,
):
    me, x, core = lax.axis_index("seq"), lax.axis_index("x"), lax.axis_index("core")
    frames = qkv.shape[2]
    mine = pl.ds(pl.multiple_of(me * span, span), span)
    my_cols = pl.ds(pl.multiple_of(me * 128, 128), 128)
    flips = (7, 6, 5, 4, 3, 2, 1)
    greet([seq_flip(flip) for flip in flips] + [(me, 1 - x, core), (me, x, 1 - core)])
    weights = WeightGather(
        late_jobs((out_w, up_w, down_w), (out_full, up_full, down_full)), wsend, wrecv, wlocal
    )

    def send_heads(utt):
        rows = pl.ds(utt * span, span)
        own = pltpu.make_async_copy(
            proj.at[:, rows, my_cols], qkv.at[utt, :, mine, :], qlocal.at[utt]
        )
        own.start()
        copies = []
        for flip in flips:
            there = me ^ flip
            cols = pl.ds(pl.multiple_of(there * 128, 128), 128)
            copy = remote(
                proj.at[:, rows, cols],
                qkv.at[utt, :, mine, :],
                qsend.at[utt * 8 + flip],
                qrecv.at[utt * 8 + flip],
                seq_flip(flip),
            )
            copy.start()
            copies.append(copy)
        return own, copies

    def arrive(sent):
        own, copies = sent
        own.wait()
        for copy in copies:
            copy.wait_recv()

    def send_out(utt, there):
        rows = pl.ds(pl.multiple_of(there * span, span), span)
        target = att.at[pl.ds(utt * span, span), my_cols]

        @pl.when(there != me)
        def _():
            remote(
                outs.at[utt, rows, :],
                target,
                osend.at[utt * 8 + (there ^ me)],
                orecv.at[utt * 8 + (there ^ me)],
                (there, x, core),
            ).start()

        @pl.when(there == me)
        def _():
            pltpu.make_async_copy(outs.at[utt, rows, :], target, olocal.at[utt]).start()

    def attend(utt, between):
        length = len_ref[utt]
        save = pltpu.make_async_copy(qkv.at[utt], qkv_all.at[utt], slocal.at[utt])
        save.start()

        def build(j, carry):
            rows = pl.ds(pl.multiple_of(j * bk, bk), bk)
            lane = lanes_of(bk)
            pos = j * bk + lax.broadcasted_iota(jnp.int32, (bk, 128), 0)
            bias = jnp.where(pos < length, 0.0, MASKED)
            keys = qkv[utt, 1, rows, :].astype(F32)
            ka[rows, :] = jnp.where(lane < 64, keys, jnp.where(lane == 64, bias, 0.0)).astype(BF)
            kb[rows, :] = jnp.where(lane >= 64, keys, jnp.where(lane == 0, bias, 0.0)).astype(BF)
            vals = qkv[utt, 2, rows, :].astype(F32)
            vta[:, rows] = jnp.where(lane < 64, vals, 1.0).T.astype(BF)
            vtb[:, rows] = jnp.where(lane >= 64, vals, 1.0).T.astype(BF)
            return carry

        lax.fori_loop(0, frames // bk, build, 0)

        def block(i, carry):
            here = pl.ds(pl.multiple_of(i * bq, bq), bq)
            lane = lanes_of(bq)
            queries = qkv[utt, 0, here, :].astype(F32)
            qa = jnp.where(lane < 64, queries, jnp.where(lane == 64, 1.0, 0.0)).astype(BF)
            qb = jnp.where(lane >= 64, queries, jnp.where(lane == 0, 1.0, 0.0)).astype(BF)

            def body(j, inner):
                rows = pl.ds(pl.multiple_of(j * bk, bk), bk)
                result = []
                scores = [nt(ka[rows, :], qa), nt(kb[rows, :], qb)]
                for score, vt, (top, acc) in zip(scores, (vta, vtb), inner):
                    new = jnp.maximum(top, jnp.max(score, axis=0, keepdims=True))
                    probs = jnp.exp2(score - new).astype(BF)
                    acc = acc * jnp.exp2(top - new) + nn(vt[:, rows], probs)
                    result.append((new, acc))
                return tuple(result)

            start = (jnp.full((1, bq), MASKED, F32), jnp.zeros((128, bq), F32))
            (top_a, acc_a), (top_b, acc_b) = lax.fori_loop(0, frames // bk, body, (start, start))
            sum_a, sum_b = acc_a[64:65], acc_b[0:1]
            both = jnp.concatenate([acc_a[:64] / sum_a, acc_b[64:] / sum_b], axis=0)
            outs[utt, here, :] = both.T.astype(BF)
            lse_ref[utt, :, here] = jnp.concatenate(
                [top_a + jnp.log2(sum_a), top_b + jnp.log2(sum_b), jnp.zeros((6, bq), F32)],
                axis=0,
            )
            if utt == 1:
                for part in range(bq // span):
                    send_out(utt, i * (bq // span) + part)
            return carry

        half = frames // bq // 2
        lax.fori_loop(0, half, block, 0)
        between()
        lax.fori_loop(half, 2 * half, block, 0)
        keep = pltpu.make_async_copy(outs.at[utt], o_all.at[utt], slocal.at[2 + utt])
        keep.start()
        return [save, keep]

    first = send_heads(0)
    weights.stage()
    arrive(first)
    second = send_heads(1)
    weights.stage()
    saves = attend(0, lambda: None)
    arrive(second)

    def send_first(i, carry):
        send_out(0, i)
        return carry

    lax.fori_loop(0, 8, send_first, 0)
    saves += attend(1, weights.stage)
    for sent in (first, second):
        for copy in sent[1]:
            copy.wait_send()
    weights.finish()
    for save in saves:
        save.wait()
    for utt in range(2):
        target = att.at[pl.ds(utt * span, span), my_cols]
        pltpu.make_async_copy(outs.at[utt, mine, :], target, olocal.at[utt]).wait()
        for flip in flips:
            copy = remote(
                outs.at[utt, mine, :],
                target,
                osend.at[utt * 8 + flip],
                orecv.at[utt * 8 + flip],
                seq_flip(flip),
            )
            copy.wait_send()
            copy.wait_recv()


def attend_forward(lengths, proj, out_w, up_w, down_w, span, bq=1024, bk=512):
    rows, width = proj.shape[1:]
    frames = 8 * span
    anywhere = pl.BlockSpec(memory_space=pl.ANY)
    vmem = pl.BlockSpec(memory_space=pltpu.VMEM)
    full = lambda w: jax.ShapeDtypeStruct((2, 2, 2, 2, 2) + w.shape[2:], BF)
    dma = pltpu.SemaphoreType.DMA
    outs = pl.pallas_call(
        functools.partial(attend_forward_kernel, span=span, bq=bq, bk=bk),
        in_specs=[pl.BlockSpec(memory_space=pltpu.SMEM)] + [anywhere] * 4,
        out_specs=[anywhere, anywhere, vmem] + [anywhere] * 4,
        out_shape=[
            jax.ShapeDtypeStruct((2, 3, frames, 128), BF),
            jax.ShapeDtypeStruct((2, frames, 128), BF),
            jax.ShapeDtypeStruct((2, 8, frames), F32),
            jax.ShapeDtypeStruct((rows, width), BF),
            full(out_w),
            full(up_w),
            full(down_w),
        ],
        scratch_shapes=[
            pltpu.VMEM((2, 3, frames, 128), BF),
            pltpu.VMEM((2, frames, 128), BF),
            pltpu.VMEM((frames, 128), BF),
            pltpu.VMEM((frames, 128), BF),
            pltpu.VMEM((128, frames), BF),
            pltpu.VMEM((128, frames), BF),
            dma((30,)),
            dma((30,)),
            dma((6,)),
            dma((16,)),
            dma((16,)),
            dma((2,)),
            dma((16,)),
            dma((16,)),
            dma((2,)),
            dma((4,)),
        ],
        compiler_params=pltpu.CompilerParams(
            vmem_limit_bytes=VMEM_LIMIT, collective_id=1, has_side_effects=True
        ),
        cost_estimate=attention_cost(frames, 4),
        name="attend_forward",
    )(lengths, proj, out_w, up_w, down_w)
    fulls = [
        outs[4 + i].reshape(32 * w.shape[2], w.shape[3]) for i, w in enumerate((out_w, up_w, down_w))
    ]
    return outs[:4], fulls


def attend_backward_kernel(
    len_ref, dout, qkv_all, o_all, lse_ref, cos_ref, sin_ref, raw_a, raw_b, raw_c,
    grads, got_a, got_b, got_c,
    qkv, outs, douts, qa, qb, da, db, qt, dt, dqa, dqb,
    dsend, drecv, dlocal, gsend, grecv, glocal, load, rsend, rrecv,
    *, span, block,
):
    me, x, core = lax.axis_index("seq"), lax.axis_index("x"), lax.axis_index("core")
    frames = qkv.shape[2]
    width = grads.shape[1] // 3
    count = frames // block
    mine = pl.ds(pl.multiple_of(me * span, span), span)
    flips = (7, 6, 5, 4, 3, 2, 1)
    mates = [(me, x ^ dx, core ^ dc) for dx, dc in ((0, 1), (1, 0), (1, 1))]
    greet([seq_flip(flip) for flip in flips] + mates)
    loads = []
    for utt in range(2):
        loads.append(
            [
                pltpu.make_async_copy(qkv_all.at[utt], qkv.at[utt], load.at[utt]),
                pltpu.make_async_copy(o_all.at[utt], outs.at[utt], load.at[2 + utt]),
            ]
        )
        for copy in loads[-1]:
            copy.start()

    def send_heads(utt):
        rows = pl.ds(utt * span, span)
        my_cols = pl.ds(pl.multiple_of(me * 128, 128), 128)
        own = pltpu.make_async_copy(dout.at[rows, my_cols], douts.at[utt, mine, :], dlocal.at[utt])
        own.start()
        copies = []
        for flip in flips:
            cols = pl.ds(pl.multiple_of((me ^ flip) * 128, 128), 128)
            copy = remote(
                dout.at[rows, cols],
                douts.at[utt, mine, :],
                dsend.at[utt * 8 + flip],
                drecv.at[utt * 8 + flip],
                seq_flip(flip),
            )
            copy.start()
            copies.append(copy)
        return own, copies

    def arrive(sent):
        own, copies = sent
        own.wait()
        for copy in copies:
            copy.wait_recv()

    def slot(utt, part, flip):
        return (utt * 3 + part) * 8 + flip

    def target(utt, part):
        cols = pl.ds(pl.multiple_of(part * width + me * 128, 128), 128)
        return grads.at[pl.ds(utt * span, span), cols]

    def send_grads(utt, part, there):
        rows = pl.ds(pl.multiple_of(there * span, span), span)

        @pl.when(there != me)
        def _():
            at = slot(utt, part, there ^ me)
            remote(
                qkv.at[utt, part, rows, :],
                target(utt, part),
                gsend.at[at],
                grecv.at[at],
                (there, x, core),
            ).start()

        @pl.when(there == me)
        def _():
            pltpu.make_async_copy(
                qkv.at[utt, part, rows, :], target(utt, part), glocal.at[utt * 3 + part]
            ).start()

    def differentiate(utt):
        length = len_ref[utt]

        def build(j, carry):
            rows = pl.ds(pl.multiple_of(j * block, block), block)
            lane = lanes_of(block)
            queries = qkv[utt, 0, rows, :].astype(F32)
            grad = douts[utt, rows, :].astype(F32)
            delta_a, delta_b = head_sums(grad * outs[utt, rows, :].astype(F32), lane)
            lse = lse_ref[utt, :, rows].T
            one_a, one_b = lse[:, 0:1], lse[:, 1:2]
            qa[rows, :] = jnp.where(
                lane < 64, queries, jnp.where(lane == 67, 1.0, three(one_a, lane, 64))
            ).astype(BF)
            qb[rows, :] = jnp.where(
                lane >= 64, queries, jnp.where(lane == 3, 1.0, three(one_b, lane, 0))
            ).astype(BF)
            da[rows, :] = jnp.where(lane < 64, grad, three(delta_a, lane, 64)).astype(BF)
            db[rows, :] = jnp.where(lane >= 64, grad, three(delta_b, lane, 0)).astype(BF)
            qt[:, rows] = queries.T.astype(BF)
            dt[:, rows] = grad.T.astype(BF)
            dqa[rows, :] = jnp.zeros((block, 128), F32)
            dqb[rows, :] = jnp.zeros((block, 128), F32)
            return carry

        lax.fori_loop(0, count, build, 0)

        def keys_block(i, carry):
            here = pl.ds(pl.multiple_of(i * block, block), block)
            lane = lanes_of(block)
            pos = i * block + lax.broadcasted_iota(jnp.int32, (block, 128), 0)
            bias = jnp.where(pos < length, 0.0, MASKED)
            keys = qkv[utt, 1, here, :].astype(F32)
            vals = qkv[utt, 2, here, :].astype(F32)
            ones_a = jnp.where(lane < 67, 1.0, 0.0)
            ones_b = jnp.where(lane < 3, 1.0, 0.0)
            ka = jnp.where(lane < 64, keys, jnp.where(lane == 67, bias, ones_a)).astype(BF)
            kb = jnp.where(lane >= 64, keys, jnp.where(lane == 3, bias, ones_b)).astype(BF)
            va = jnp.where(lane < 64, vals, ones_a).astype(BF)
            vb = jnp.where(lane >= 64, vals, ones_b).astype(BF)

            def body(j, inner):
                rows = pl.ds(pl.multiple_of(j * block, block), block)
                result = []
                for head, (qh, dh, kh, vh, dq) in enumerate(
                    ((qa, da, ka, va, dqa), (qb, db, kb, vb, dqb))
                ):
                    part = slice(head * 64, head * 64 + 64)
                    probs = jnp.exp2(nt(qh[rows, :], kh))
                    grad = (probs * nt(dh[rows, :], vh)).astype(BF)
                    dv = inner[2 * head + 1] + nn(dt[:, rows], probs.astype(BF))[part]
                    dk = inner[2 * head] + nn(qt[:, rows], grad)[part]
                    dq[rows, :] += nn(grad, kh)
                    result += [dk, dv]

                @pl.when(i == count - 1)
                def _():
                    low = jnp.where(lanes_of(block) < 64, dqa[rows, :], dqb[rows, :]) * 0.125
                    low = turn_back(low, cos_ref[rows, :], sin_ref[rows, :])
                    qkv[utt, 0, rows, :] = low.astype(BF)
                    for step in range(block // span):
                        send_grads(utt, 0, j * (block // span) + step)

                return tuple(result)

            zero = jnp.zeros((64, block), F32)
            dk_a, dv_a, dk_b, dv_b = lax.fori_loop(0, count, body, (zero,) * 4)
            dk = jnp.concatenate([dk_a, dk_b], axis=0).T * LN2
            dv = jnp.concatenate([dv_a, dv_b], axis=0).T
            qkv[utt, 1, here, :] = turn_back(dk, cos_ref[here, :], sin_ref[here, :]).astype(BF)
            qkv[utt, 2, here, :] = dv.astype(BF)
            for step in range(block // span):
                there = i * (block // span) + step
                send_grads(utt, 1, there)
                send_grads(utt, 2, there)
            return carry

        lax.fori_loop(0, count, keys_block, 0)

    first = send_heads(0)
    raws = []
    for index, (raw, got) in enumerate(((raw_a, got_a), (raw_b, got_b), (raw_c, got_c))):
        for slot_at, device in enumerate(mates):
            at = index * 3 + slot_at
            copy = remote(
                raw.at[:, :, :, device[1], device[2]],
                got.at[slot_at],
                rsend.at[at],
                rrecv.at[at],
                device,
            )
            copy.start()
            raws.append(copy)
    for copy in loads[0]:
        copy.wait()
    arrive(first)
    second = send_heads(1)
    differentiate(0)
    for copy in loads[1]:
        copy.wait()
    arrive(second)
    differentiate(1)
    for sent in (first, second):
        for copy in sent[1]:
            copy.wait_send()
    for copy in raws:
        copy.wait()
    for utt in range(2):
        for part in range(3):
            own = qkv.at[utt, part, mine, :]
            pltpu.make_async_copy(own, target(utt, part), glocal.at[utt * 3 + part]).wait()
            for flip in flips:
                at = slot(utt, part, flip)
                copy = remote(own, target(utt, part), gsend.at[at], grecv.at[at], seq_flip(flip))
                copy.wait_send()
                copy.wait_recv()


def attend_backward(lengths, dout, qkv_all, o_all, lse, cos, sin, raws, span, block=1024):
    raws = [raw.reshape(2, 2, 2, 2, 2, raw.shape[0] // 32, raw.shape[1]) for raw in raws]
    frames = 8 * span
    rows, width = dout.shape
    anywhere = pl.BlockSpec(memory_space=pl.ANY)
    vmem = pl.BlockSpec(memory_space=pltpu.VMEM)
    dma = pltpu.SemaphoreType.DMA
    return pl.pallas_call(
        functools.partial(attend_backward_kernel, span=span, block=block),
        in_specs=[pl.BlockSpec(memory_space=pltpu.SMEM)]
        + [anywhere] * 3
        + [vmem] * 3
        + [anywhere] * 3,
        out_specs=[anywhere] * 4,
        out_shape=[jax.ShapeDtypeStruct((rows, 3 * width), BF)]
        + [jax.ShapeDtypeStruct((3, 2, 2, 2) + raw.shape[5:], BF) for raw in raws],
        scratch_shapes=[
            pltpu.VMEM((2, 3, frames, 128), BF),
            pltpu.VMEM((2, frames, 128), BF),
            pltpu.VMEM((2, frames, 128), BF),
        ]
        + [pltpu.VMEM((frames, 128), BF)] * 4
        + [pltpu.VMEM((128, frames), BF)] * 2
        + [pltpu.VMEM((frames, 128), F32)] * 2
        + [dma((16,)), dma((16,)), dma((2,)), dma((48,)), dma((48,)), dma((6,)), dma((4,)), dma((9,)), dma((9,))],
        compiler_params=pltpu.CompilerParams(
            vmem_limit_bytes=VMEM_LIMIT, collective_id=2, has_side_effects=True
        ),
        cost_estimate=attention_cost(frames, 10),
        name="attend_backward",
    )(lengths, dout, qkv_all, o_all, lse, cos, sin, *raws)


def layer_norm(stream):
    centre = stream - jnp.mean(stream, axis=-1, keepdims=True)
    spread = jnp.mean(centre * centre, axis=-1, keepdims=True)
    inverse = lax.rsqrt(spread + EPS)
    return (centre * inverse, inverse)


def norm_back(grad_normed, normed, inverse):
    first_mean = jnp.mean(grad_normed, axis=-1, keepdims=True)
    second_mean = jnp.mean(grad_normed * normed, axis=-1, keepdims=True)
    return inverse * (grad_normed - first_mean - normed * second_mean)


def tn(left, right):
    return lax.dot_general(left, right, (((0,), (0,)), ((), ())), preferred_element_type=F32)


GELU_C = 0.7978845608028654
GELU_A = 0.044715


def gelu_and_slope(z):
    square = z * z
    turn = jnp.tanh(GELU_C * z * (1.0 + GELU_A * square))
    half = 0.5 * (1.0 + turn)
    slope = half + 0.5 * z * (1.0 - turn * turn) * (GELU_C * (1.0 + 3.0 * GELU_A * square))
    return z * half, slope


def row_blocks(rows):
    block = min(rows, 256)
    return [(at, slice(at, at + block)) for at in range(0, rows, block)]


def ffn_forward_kernel(
    att_ref, outw_ref, res_ref, mod_ref, cot_ref, weight_ref, up_ref, down_ref,
    branch_ref, act_ref, slope_ref, gb_ref, out_ref, gate_ref, normed, acc,
):
    step = pl.program_id(0)
    rows = att_ref.shape[0]
    span = rows // mod_ref.shape[0]

    @pl.when(step == 0)
    def _():
        for at, part in row_blocks(span):
            for utt in range(mod_ref.shape[0]):
                here = slice(utt * span + part.start, utt * span + part.stop)
                mod = mod_ref[utt]
                branch = nn(att_ref[here, :], outw_ref[...])
                branch_ref[here, :] = branch
                hat, _ = layer_norm(res_ref[here, :] + mod[2:3] * branch)
                normed[here, :] = (hat * (1.0 + mod[4:5]) + mod[3:4]).astype(BF)
        acc[...] = jnp.zeros_like(acc)

    for _, part in row_blocks(rows):
        act, slope = gelu_and_slope(nn(normed[part, :], up_ref[...]))
        act = act.astype(BF)
        act_ref[part, :] = act
        slope_ref[part, :] = slope.astype(BF)
        acc[part, :] += nn(act, down_ref[...])

    @pl.when(step == pl.num_programs(0) - 1)
    def _():
        for utt in range(mod_ref.shape[0]):
            mod = mod_ref[utt]
            total = jnp.zeros((1, acc.shape[1]), F32)
            for _, part in row_blocks(span):
                here = slice(utt * span + part.start, utt * span + part.stop)
                branch = acc[here, :]
                mid = res_ref[here, :] + mod[2:3] * branch_ref[here, :]
                out_ref[here, :] = (mid + mod[5:6] * branch).astype(BF)
                upstream = cot_ref[here, :].astype(F32) * weight_ref[here, :]
                gb_ref[here, :] = (upstream * mod[5:6]).astype(BF)
                total += jnp.sum(upstream * branch, axis=0, keepdims=True)
            gate_ref[utt : utt + 1, :] = total


def ffn_backward_kernel(
    att_ref, outw_ref, res_ref, branch_ref, mod_ref, cot_ref, weight_ref, gb_ref,
    act_ref, slope_ref, up_ref, down_ref,
    gup_ref, gdown_ref, gmid_ref, gatt_ref, gout_ref, sums_ref, normed, acc, gba,
):
    step = pl.program_id(0)
    rows = att_ref.shape[0]
    utts = mod_ref.shape[0]
    span = rows // utts

    def hat_of(here, mod):
        return layer_norm(res_ref[here, :] + mod[2:3] * branch_ref[here, :])

    @pl.when(step == 0)
    def _():
        for utt in range(utts):
            mod = mod_ref[utt]
            for _, part in row_blocks(span):
                here = slice(utt * span + part.start, utt * span + part.stop)
                hat, _ = hat_of(here, mod)
                normed[here, :] = (hat * (1.0 + mod[4:5]) + mod[3:4]).astype(BF)
        acc[...] = jnp.zeros_like(acc)

    pieces = []
    for _, part in row_blocks(rows):
        grad = nt(gb_ref[part, :], down_ref[...]) * slope_ref[part, :].astype(F32)
        grad = grad.astype(BF)
        acc[part, :] += nt(grad, up_ref[...])
        pieces.append(grad)
    gdown_ref[...] = tn(act_ref[...], gb_ref[...]).astype(BF)
    gup_ref[...] = tn(normed[...], jnp.concatenate(pieces, axis=0)).astype(BF)

    @pl.when(step == pl.num_programs(0) - 1)
    def _():
        for utt in range(utts):
            mod = mod_ref[utt]
            width = acc.shape[1]
            shift = jnp.zeros((1, width), F32)
            scale = jnp.zeros((1, width), F32)
            gate = jnp.zeros((1, width), F32)
            for _, part in row_blocks(span):
                here = slice(utt * span + part.start, utt * span + part.stop)
                hat, inverse = hat_of(here, mod)
                grad = acc[here, :]
                shift += jnp.sum(grad, axis=0, keepdims=True)
                scale += jnp.sum(grad * hat, axis=0, keepdims=True)
                upstream = cot_ref[here, :].astype(F32) * weight_ref[here, :]
                mid = upstream + norm_back(grad * (1.0 + mod[4:5]), hat, inverse)
                gmid_ref[here, :] = mid
                gate += jnp.sum(mid * branch_ref[here, :], axis=0, keepdims=True)
                low = (mid * mod[2:3]).astype(BF)
                gba[here, :] = low
                gatt_ref[here, :] = nt(low, outw_ref[...]).astype(BF)
            sums_ref[utt, 0:1, :] = shift
            sums_ref[utt, 1:2, :] = scale
            sums_ref[utt, 2:3, :] = gate
        gout_ref[...] = tn(att_ref[...], gba[...]).astype(BF)


def whole_spec(shape):
    zeros = (0,) * len(shape)
    return pl.BlockSpec(shape, lambda i: zeros, pipeline_mode=pl.Buffered(1))


def ffn_forward(att, outw, res, mods, cot, weight, up, down, chunk=512):
    rows, width = res.shape
    hidden = up.shape[1]
    whole = [whole_spec(a.shape) for a in (att, outw, res, mods, cot, weight)]
    col = pl.BlockSpec((rows, chunk), lambda i: (0, i))
    utts = mods.shape[0]
    return pl.pallas_call(
        ffn_forward_kernel,
        grid=(hidden // chunk,),
        in_specs=whole
        + [
            pl.BlockSpec((width, chunk), lambda i: (0, i)),
            pl.BlockSpec((chunk, width), lambda i: (i, 0)),
        ],
        out_specs=[
            whole_spec((rows, width)),
            col,
            col,
            whole_spec((rows, width)),
            whole_spec((rows, width)),
            whole_spec((utts, width)),
        ],
        out_shape=[
            jax.ShapeDtypeStruct((rows, width), F32),
            jax.ShapeDtypeStruct((rows, hidden), BF),
            jax.ShapeDtypeStruct((rows, hidden), BF),
            jax.ShapeDtypeStruct((rows, width), BF),
            jax.ShapeDtypeStruct((rows, width), BF),
            jax.ShapeDtypeStruct((utts, width), F32),
        ],
        scratch_shapes=[pltpu.VMEM((rows, width), BF), pltpu.VMEM((rows, width), F32)],
        compiler_params=pltpu.CompilerParams(vmem_limit_bytes=VMEM_LIMIT),
        cost_estimate=pl.CostEstimate(
            flops=2 * rows * width * (width + 2 * hidden),
            bytes_accessed=60 * 2**20,
            transcendentals=rows * hidden,
        ),
        name="ffn_forward",
    )(att, outw, res, mods, cot, weight, up, down)


def ffn_backward(att, outw, res, branch, mods, cot, weight, gb, act, slope, up, down, chunk=512):
    rows, width = res.shape
    hidden = up.shape[1]
    utts = mods.shape[0]
    whole = [whole_spec(a.shape) for a in (att, outw, res, branch, mods, cot, weight, gb)]
    col = pl.BlockSpec((rows, chunk), lambda i: (0, i))
    upspec = pl.BlockSpec((width, chunk), lambda i: (0, i))
    downspec = pl.BlockSpec((chunk, width), lambda i: (i, 0))
    return pl.pallas_call(
        ffn_backward_kernel,
        grid=(hidden // chunk,),
        in_specs=whole + [col, col, upspec, downspec],
        out_specs=[
            upspec,
            downspec,
            whole_spec((rows, width)),
            whole_spec((rows, width)),
            whole_spec((width, width)),
            whole_spec((utts, 8, width)),
        ],
        out_shape=[
            jax.ShapeDtypeStruct((width, hidden), BF),
            jax.ShapeDtypeStruct((hidden, width), BF),
            jax.ShapeDtypeStruct((rows, width), F32),
            jax.ShapeDtypeStruct((rows, width), BF),
            jax.ShapeDtypeStruct((width, width), BF),
            jax.ShapeDtypeStruct((utts, 8, width), F32),
        ],
        scratch_shapes=[
            pltpu.VMEM((rows, width), BF),
            pltpu.VMEM((rows, width), F32),
            pltpu.VMEM((rows, width), BF),
        ],
        compiler_params=pltpu.CompilerParams(vmem_limit_bytes=VMEM_LIMIT),
        cost_estimate=pl.CostEstimate(
            flops=2 * rows * width * (2 * width + 4 * hidden),
            bytes_accessed=90 * 2**20,
            transcendentals=0,
        ),
        name="ffn_backward",
    )(att, outw, res, branch, mods, cot, weight, gb, act, slope, up, down)


def enter_kernel(
    in_ref, skip_ref, skip_w, qkv_w, mod_ref, cos_ref, sin_ref, res_ref, proj_ref
):
    width = in_ref.shape[1]
    mod = mod_ref[0]
    residual = nn(in_ref[...], skip_w[:width, :]) + nn(skip_ref[...], skip_w[width:, :])
    res_ref[...] = residual
    hat, _ = layer_norm(residual)
    normed = (hat * (1.0 + mod[1:2]) + mod[0:1]).astype(BF)
    lane = lanes_of(in_ref.shape[0])
    cos, sin = cos_ref[...], sin_ref[...]
    for part in range(3):
        projected = nn(normed, qkv_w[:, part * width : (part + 1) * width])
        for group in range(width // 128):
            cols = slice(group * 128, group * 128 + 128)
            piece = projected[:, cols]
            if part < 2:
                turned = jnp.where(
                    (lane & 63) < 32, pltpu.roll(piece, 96, 1), pltpu.roll(piece, 32, 1)
                )
                piece = piece * cos + turned * sin
            if part == 0:
                piece = piece * (0.125 * LOG2E)
            proj_ref[part, :, cols] = piece.astype(BF)


def enter_layer(first, second, skip_w, qkv_w, mods, cos, sin, block=256):
    rows, width = first.shape
    steps = rows // mods.shape[0] // block
    part = pl.BlockSpec((block, width), lambda i: (i, 0))
    table = pl.BlockSpec((block, 128), lambda i: (i % steps, 0))
    return pl.pallas_call(
        enter_kernel,
        grid=(rows // block,),
        in_specs=[
            part,
            part,
            whole_spec(skip_w.shape),
            whole_spec(qkv_w.shape),
            pl.BlockSpec((1,) + mods.shape[1:], lambda i: (i // steps, 0, 0)),
            table,
            table,
        ],
        out_specs=[part, pl.BlockSpec((3, block, width), lambda i: (0, i, 0))],
        out_shape=[
            jax.ShapeDtypeStruct((rows, width), F32),
            jax.ShapeDtypeStruct((3, rows, width), BF),
        ],
        compiler_params=pltpu.CompilerParams(vmem_limit_bytes=VMEM_LIMIT),
        cost_estimate=pl.CostEstimate(
            flops=2 * rows * (skip_w.size + qkv_w.size),
            bytes_accessed=40 * 2**20,
            transcendentals=0,
        ),
        name="enter_layer",
    )(first, second, skip_w, qkv_w, mods, cos, sin)


def leave_kernel(
    grad_ref, qkv_w, skip_w, res_ref, mid_ref, mod_ref, in_ref, skip_ref,
    gin_ref, gskip_ref, sums_ref, gqkv_ref, gw_ref, normed, stream,
):
    step = pl.program_id(0)
    rows, width = res_ref.shape
    utts = mod_ref.shape[0]
    span = rows // utts

    @pl.when(step == 0)
    def _():
        for utt in range(utts):
            mod = mod_ref[utt]
            shift = jnp.zeros((1, width), F32)
            scale = jnp.zeros((1, width), F32)
            for _, part in row_blocks(span):
                here = slice(utt * span + part.start, utt * span + part.stop)
                hat, inverse = layer_norm(res_ref[here, :])
                normed[here, :] = (hat * (1.0 + mod[1:2]) + mod[0:1]).astype(BF)
                grad = nt(grad_ref[here, :], qkv_w[...])
                shift += jnp.sum(grad, axis=0, keepdims=True)
                scale += jnp.sum(grad * hat, axis=0, keepdims=True)
                total = mid_ref[here, :] + norm_back(grad * (1.0 + mod[1:2]), hat, inverse)
                low = total.astype(BF)
                stream[here, :] = low
                gin_ref[here, :] = nt(low, skip_w[:width, :]).astype(BF)
                gskip_ref[here, :] = nt(low, skip_w[width:, :]).astype(BF)
            sums_ref[utt, 0:1, :] = shift
            sums_ref[utt, 1:2, :] = scale

    chunk = gqkv_ref.shape[1]
    cols = pl.ds(pl.multiple_of(step * chunk, chunk), chunk)
    gqkv_ref[...] = tn(normed[...], grad_ref[:, cols]).astype(BF)
    part = gw_ref.shape[2]
    here = pl.ds(pl.multiple_of(step * part, part), part)
    gw_ref[0] = tn(in_ref[...], stream[:, here]).astype(BF)
    gw_ref[1] = tn(skip_ref[...], stream[:, here]).astype(BF)


def leave_layer(grads, qkv_w, skip_w, res, mid, mods, first, second, steps=4):
    rows, width = res.shape
    utts = mods.shape[0]
    ins = (grads, qkv_w, skip_w, res, mid, mods, first, second)
    outs = pl.pallas_call(
        leave_kernel,
        grid=(steps,),
        in_specs=[whole_spec(a.shape) for a in ins],
        out_specs=[
            whole_spec((rows, width)),
            whole_spec((rows, width)),
            whole_spec((utts, 8, width)),
            pl.BlockSpec((width, 3 * width // steps), lambda i: (0, i)),
            pl.BlockSpec((2, width, width // steps), lambda i: (0, 0, i)),
        ],
        out_shape=[
            jax.ShapeDtypeStruct((rows, width), BF),
            jax.ShapeDtypeStruct((rows, width), BF),
            jax.ShapeDtypeStruct((utts, 8, width), F32),
            jax.ShapeDtypeStruct((width, 3 * width), BF),
            jax.ShapeDtypeStruct((2, width, width), BF),
        ],
        scratch_shapes=[pltpu.VMEM((rows, width), BF), pltpu.VMEM((rows, width), BF)],
        compiler_params=pltpu.CompilerParams(vmem_limit_bytes=VMEM_LIMIT),
        cost_estimate=pl.CostEstimate(
            flops=4 * rows * (skip_w.size + qkv_w.size),
            bytes_accessed=60 * 2**20,
            transcendentals=0,
        ),
        name="leave_layer",
    )(*ins)
    return tuple(outs[:4]) + (outs[4].reshape(2 * width, width),)


class GradJob:
    def __init__(self, grad, arrived, out, cols, order, keep, buffers, loads, sems, base):
        self.grad, self.arrived, self.out, self.cols, self.order = grad, arrived, out, cols, order
        self.keep, self.buffers, self.loads = keep, buffers, loads
        self.send, self.recv, self.local, self.base = *sems, base
        me, x, core = lax.axis_index("seq"), lax.axis_index("x"), lax.axis_index("core")
        self.bits = (me // 4, (me // 2) % 2, me % 2, x, core)
        self.lead = 3 if arrived is not None else 4
        self.copies, self.locals, self.round = [], [], 0

    def peer(self, dim):
        me, x, core = lax.axis_index("seq"), lax.axis_index("x"), lax.axis_index("core")
        if dim < 3:
            return (me ^ (4 >> dim), x, core)
        return (me, 1 - x, core) if dim == 3 else (me, x, 1 - core)

    def launch(self, source, target, dim):
        at = self.base + len(self.copies)
        copy = remote(source, target, self.send.at[at], self.recv.at[at], self.peer(dim))
        copy.start()
        self.copies.append(copy)

    def load(self, source, target):
        copy = pltpu.make_async_copy(source, target, self.local.at[self.base + len(self.locals)])
        copy.start()
        self.locals.append(copy)

    def add(self, done, others):
        left = [dim for dim in range(self.lead) if dim not in done]

        def body(i, carry):
            at, place = list(self.bits[: self.lead]), []
            for n, dim in enumerate(left):
                bit = (i >> (len(left) - 1 - n)) & 1
                at[dim] = bit
                place.append(bit)
            total = self.keep[tuple(at)].astype(F32)
            for other in others:
                total = total + (other[tuple(place)] if place else other[...]).astype(F32)
            self.keep[tuple(at)] = total.astype(BF)
            return carry

        lax.fori_loop(0, 2 ** len(left), body, 0)

    def exchange(self, step):
        dim, done = self.order[step], self.order[:step]
        where = tuple(
            1 - self.bits[d] if d == dim else self.bits[d] if d in done else slice(None)
            for d in range(self.lead)
        )
        self.launch(self.keep.at[where], self.buffers[step], dim)

    def advance(self):
        number, self.round = self.round, self.round + 1
        tail, bits = (slice(None), self.cols), self.bits
        steps = len(self.order)
        every = (slice(None),) * self.lead
        if number == 0:
            self.load(self.grad.at[every + bits[self.lead :] + tail], self.keep)
            if self.arrived is None:
                self.launch(self.grad.at[every + (1 - bits[4],) + tail], self.loads[0], 4)
            else:
                for slot, buffer in enumerate(self.loads):
                    self.load(self.arrived.at[(slot,) + every + tail], buffer)
        elif number == 1:
            for copy in self.locals:
                copy.wait()
            if self.arrived is None:
                self.copies[0].wait_recv()
            self.add((), self.loads)
            self.exchange(0)
        elif number <= steps + 1:
            self.copies[-1].wait_recv()
            self.add(self.order[: number - 1], [self.buffers[number - 2]])
            if number <= steps:
                self.exchange(number - 1)
            else:
                mine = self.keep.at[bits[: self.lead]]
                spot = self.out.at[bits[3:5] + tail]
                self.load(mine, spot)
                self.launch(mine, spot, 3)
        elif number == steps + 2:
            self.locals[-1].wait()
            self.copies[-1].wait_recv()
            both = self.out.at[(slice(None), bits[4]) + tail]
            self.launch(both, both, 4)

    def finish(self):
        self.copies[-1].wait_recv()
        for copy in self.copies:
            copy.wait_send()


FULL_ORDERS = ((3, 2, 1, 0), (2, 1, 3, 0), (1, 3, 2, 0))
QUARTER_ORDERS = ((2, 1, 0), (1, 2, 0))


def reduce_kernel(*refs, halves, quarters):
    count = halves + quarters
    grads, arrived, small = refs[:count], refs[count : count + quarters], refs[count + quarters]
    refs = refs[count + quarters + 1 :]
    outs, small_out, rest = refs[:count], refs[count], list(refs[count + 1 :])
    small_in, small_low, send, recv, local, ssend, srecv, bsend, brecv, slocal = rest[-10:]
    me, x, core = lax.axis_index("seq"), lax.axis_index("x"), lax.axis_index("core")
    others = [seq_flip(flip) for flip in range(7, 0, -1)]
    mates = [(me, (x + dx) % 2, (core + dc) % 2) for dx, dc in ((0, 1), (1, 0), (1, 1))]
    greet(others + mates)
    jobs = []
    for index, (grad, out) in enumerate(zip(grads, outs)):
        whole = index < halves
        orders = FULL_ORDERS if whole else QUARTER_ORDERS
        for cols, order in zip(split_columns(grad.shape[-1], (1,) * len(orders)), orders):
            keep = rest.pop(0)
            loads = [rest.pop(0) for _ in range(1 if whole else 3)]
            buffers = [rest.pop(0) for _ in order]
            jobs.append(
                GradJob(
                    grad,
                    None if whole else arrived[index - halves],
                    out,
                    cols,
                    order,
                    keep,
                    buffers,
                    loads,
                    (send, recv, local),
                    7 * len(jobs),
                )
            )
    own = pltpu.make_async_copy(small, small_in.at[me], slocal.at[0])
    own.start()
    smalls = []
    for flip, device in zip(range(7, 0, -1), others):
        smalls.append(remote(small, small_in.at[me], ssend.at[flip], srecv.at[flip], device))
        smalls[-1].start()
    for _ in range(3):
        for job in jobs:
            job.advance()
    own.wait()
    for copy in smalls:
        copy.wait_recv()
    total = small_in[0]
    for index in range(1, 8):
        total = total + small_in[index]
    small_low[...] = total.astype(BF)
    quarter = x * 2 + core
    keep = pltpu.make_async_copy(small_low, small_out.at[quarter], slocal.at[1])
    keep.start()
    lows = []
    for slot, device in enumerate(mates):
        lows.append(remote(small_low, small_out.at[quarter], bsend.at[slot], brecv.at[slot], device))
        lows[-1].start()
    for _ in range(4):
        for job in jobs:
            job.advance()
    for job in jobs:
        job.finish()
    for copy in smalls:
        copy.wait_send()
    keep.wait()
    for copy in lows:
        copy.wait()


def reduce_grads(halves, quarters, arrived, small):
    grads = list(halves) + list(quarters)
    views, outs, buffers, jobs = [], [], [], 0
    for index, grad in enumerate(grads):
        rows, width = grad.shape
        span = rows // 32
        views.append(grad.reshape(2, 2, 2, 2, 2, span, width))
        outs.append(jax.ShapeDtypeStruct((2, 2, span, width), BF))
        whole = index < len(halves)
        lead, orders = (4, FULL_ORDERS) if whole else (3, QUARTER_ORDERS)
        for cols in split_columns(width, (1,) * len(orders)):
            jobs += 1
            tail = (span, cols.size)
            for left in [lead] * (2 if whole else 4) + list(range(lead - 1, -1, -1)):
                buffers.append(pltpu.VMEM((2,) * left + tail, BF))
    anywhere = pl.BlockSpec(memory_space=pl.ANY)
    dma = pltpu.SemaphoreType.DMA
    outs.append(jax.ShapeDtypeStruct((4,) + small.shape, BF))
    results = pl.pallas_call(
        functools.partial(reduce_kernel, halves=len(halves), quarters=len(quarters)),
        in_specs=[anywhere] * (len(grads) + len(arrived) + 1),
        out_specs=[anywhere] * (len(grads) + 1),
        out_shape=outs,
        scratch_shapes=buffers
        + [pltpu.VMEM((8,) + small.shape, F32), pltpu.VMEM(small.shape, BF)]
        + [dma((7 * jobs,))] * 3
        + [dma((8,)), dma((8,)), dma((3,)), dma((3,)), dma((2,))],
        compiler_params=pltpu.CompilerParams(
            vmem_limit_bytes=VMEM_LIMIT, collective_id=3, has_side_effects=True
        ),
        name="reduce_grads",
    )(*views, *arrived, small)
    shards = [
        result.reshape(grad.shape[0] // 8, grad.shape[1]).astype(jnp.float32)
        for result, grad in zip(results, grads)
    ]
    return shards, results[-1].astype(jnp.float32)


def rotary_tables(positions):
    half_dim = HEAD_DIM // 2
    channel = jnp.arange(half_dim, dtype=jnp.float32)
    inverse = jnp.power(10000.0, -2.0 * channel / HEAD_DIM)
    angles = positions.astype(jnp.float32)[:, None] * inverse[None, :]
    angles = jnp.concatenate([angles, angles], axis=1)
    return (jnp.cos(angles), jnp.sin(angles))


def rotate_heads(field, cosine_table, sine_table):
    half_dim = field.shape[-1] // 2
    turned = jnp.concatenate([-field[..., half_dim:], field[..., :half_dim]], axis=-1)
    return field * cosine_table + turned * sine_table


def smooth_gelu(values):
    return jax.nn.gelu(values, approximate=True)


def cross(left, right):
    return lax.dot_general(
        left, right, (((0,), (0,)), ((), ())), preferred_element_type=jnp.float32
    )


def back_product(left, right):
    return lax.dot_general(
        left, right, (((1,), (1,)), ((), ())), preferred_element_type=jnp.float32
    )


def block_terms(query_block, dout_block, lse_block, delta_block, key_block, value_block, key_live):
    scores = jnp.einsum(
        "bqhd,bkhd->bhqk", query_block, key_block, preferred_element_type=jnp.float32
    )
    lse_heads = jnp.transpose(lse_block, (0, 2, 1))[..., None]
    probs = jnp.where(key_live[:, None, None, :], jnp.exp(scores - lse_heads), 0.0)
    grad_probs = jnp.einsum(
        "bqhd,bkhd->bhqk", dout_block, value_block, preferred_element_type=jnp.float32
    )
    delta_heads = jnp.transpose(delta_block, (0, 2, 1))[..., None]
    dscore = (probs * (grad_probs - delta_heads)).astype(jnp.bfloat16)
    return (probs.astype(jnp.bfloat16), dscore)


BATCH = ("x", "core")


def batch_index():
    return lax.axis_index("x") * lax.axis_size("core") + lax.axis_index("core")


def gather_weight(weight):
    parts = lax.axis_size(BATCH)
    if weight.shape[0] % parts:
        return lax.all_gather(weight, "seq", axis=0, tiled=True)
    rows = weight.shape[0] // parts
    mine = lax.dynamic_slice_in_dim(weight, batch_index() * rows, rows, 0)
    return lax.all_gather(mine, ("seq",) + BATCH, axis=0, tiled=True)


def sum_weight(grad):
    rows, width = grad.shape
    low = grad.astype(jnp.bfloat16)
    seq_count, cores = lax.axis_size("seq"), lax.axis_size("core")
    parts = seq_count * lax.axis_size(BATCH)
    if rows % parts or cores != 2:
        shard = lax.psum_scatter(low, "seq", scatter_dimension=0, tiled=True)
        return lax.psum(shard, BATCH).astype(jnp.float32)
    core = lax.axis_index("core")
    held = low.reshape(parts // 2, 2, rows // parts, width)
    send = lax.dynamic_index_in_dim(held, 1 - core, 1, keepdims=False)
    keep = lax.dynamic_index_in_dim(held, core, 1, keepdims=False)
    got = lax.ppermute(send, "core", [(0, 1), (1, 0)])
    half = (keep.astype(jnp.float32) + got.astype(jnp.float32)).astype(jnp.bfloat16)
    half = half.reshape(rows // 2, width)
    shard = lax.psum_scatter(half, ("seq", "x"), scatter_dimension=0, tiled=True)
    return lax.all_gather(shard, BATCH, axis=0, tiled=True).astype(jnp.float32)


def gather_kernel(*refs, count, ahead):
    weights, laters = refs[:count], refs[count : count + ahead]
    seq_small, batch_small = refs[count + ahead : count + ahead + 2]
    outs = refs[count + ahead + 2 :]
    fulls, helds = outs[:count], outs[count : count + ahead]
    seq_out, batch_out, send, recv, asend, arecv, small_send, small_recv, local = outs[count + ahead :]
    me, x, core = lax.axis_index("seq"), lax.axis_index("x"), lax.axis_index("core")
    bits = (me // 4, (me // 2) % 2, me % 2, x, core)

    def peer(dim):
        if dim < 3:
            return (me ^ (4 >> dim), x, core)
        return (me, 1 - x, core) if dim == 3 else (me, x, 1 - core)

    others = [((me + d) % 8, x, core) for d in range(1, 8)]
    mates = [(me, (x + dx) % 2, (core + dc) % 2) for dx, dc in ((0, 1), (1, 0), (1, 1))]
    barrier = pltpu.get_barrier_semaphore()
    for device in others + mates:
        pl.semaphore_signal(barrier, inc=1, device_id=device, device_id_type=pl.DeviceIdType.MESH)
    pl.semaphore_wait(barrier, len(others) + len(mates))

    small = []
    quarter = x * 2 + core
    own_seq = pltpu.make_async_copy(seq_small, seq_out.at[me], local.at[0])
    own_batch = pltpu.make_async_copy(batch_small, batch_out.at[quarter], local.at[1])
    own_seq.start()
    own_batch.start()
    for slot, device in enumerate(others):
        small.append(
            pltpu.make_async_remote_copy(
                seq_small, seq_out.at[me], small_send.at[slot], small_recv.at[slot],
                device_id=device, device_id_type=pl.DeviceIdType.MESH,
            )
        )
    for slot, device in enumerate(mates):
        small.append(
            pltpu.make_async_remote_copy(
                batch_small, batch_out.at[quarter], small_send.at[7 + slot], small_recv.at[7 + slot],
                device_id=device, device_id_type=pl.DeviceIdType.MESH,
            )
        )
    for copy in small:
        copy.start()

    jobs = early_jobs(weights, fulls)
    chain = WeightGather(jobs, send, recv, local.at[pl.ds(2, len(jobs))])
    later = WeightGather(
        ahead_jobs(laters, helds), asend, arecv, local.at[pl.ds(2 + len(jobs), ahead)]
    )
    chain.stage()
    chain.stage()
    later.stage()
    chain.stage()
    later.stage()
    chain.stage()
    chain.stage()
    chain.finish()
    later.finish()
    for copy in small:
        copy.wait()
    own_seq.wait()
    own_batch.wait()


def gather_early(weights, laters, seq_small, batch_small):
    anywhere = pl.BlockSpec(memory_space=pl.ANY)
    jobs, ahead = 3 * len(weights), len(laters)
    total = len(weights) + ahead + 2
    dma = pltpu.SemaphoreType.DMA
    quarter = lambda lead, w: jax.ShapeDtypeStruct((2,) * lead + (w.shape[0] // 4, w.shape[1]), BF)
    outs = pl.pallas_call(
        functools.partial(gather_kernel, count=len(weights), ahead=ahead),
        in_specs=[anywhere] * total,
        out_specs=[anywhere] * total,
        out_shape=[quarter(5, w) for w in weights]
        + [quarter(2, w) for w in laters]
        + [
            jax.ShapeDtypeStruct((8,) + seq_small.shape, F32),
            jax.ShapeDtypeStruct((4,) + batch_small.shape, F32),
        ],
        scratch_shapes=[
            dma((5 * jobs,)),
            dma((5 * jobs,)),
            dma((5 * ahead,)),
            dma((5 * ahead,)),
            dma((10,)),
            dma((10,)),
            dma((2 + jobs + ahead,)),
        ],
        compiler_params=pltpu.CompilerParams(collective_id=0, has_side_effects=True),
        name="gather_early",
    )(*weights, *laters, seq_small, batch_small)
    fulls = [full.reshape(8 * w.shape[0], w.shape[1]) for full, w in zip(outs, weights)]
    return fulls, outs[len(weights) : len(weights) + ahead], outs[-2], outs[-1]


def paired_tables(count):
    half = HEAD_DIM // 2
    inverse = np.power(10000.0, -2.0 * np.arange(half) / HEAD_DIM)
    angles = np.arange(count)[:, None] * inverse[None, :]
    cos, sin = np.cos(angles), np.sin(angles)
    tables = (np.tile(cos, (1, 4)), np.tile(np.concatenate([-sin, sin], axis=1), (1, 2)))
    return tuple(jnp.asarray(table, jnp.float32) for table in tables)


def on_device(
    layer_input,
    skip_input,
    time_embed,
    lengths,
    cond_drop,
    cotangent,
    skip_weight,
    adaln_weight,
    adaln_bias,
    qkv_weight,
    out_weight,
    up_weight,
    down_weight,
):
    utt_count, frame_span, model_width = layer_input.shape
    head_count = model_width // HEAD_DIM
    row_count = utt_count * frame_span
    seq_here = lax.axis_index("seq")
    seq_count = lax.axis_size("seq")
    frame_count = frame_span * seq_count
    by_heads = (
        seq_count == 8
        and head_count == 16
        and utt_count == 2
        and lax.axis_size(BATCH) == 4
        and frame_span == 512
    )
    local_pos = seq_here * frame_span + jnp.arange(frame_span, dtype=jnp.int32)
    local_live = local_pos[None, :] < lengths[:, None]
    valid_mask = local_live.astype(jnp.float32)
    drop = cond_drop.astype(jnp.float32)
    dropped = drop[:, None] * valid_mask
    frames_live = jnp.minimum(lengths, frame_count).astype(jnp.float32)
    counts = jnp.stack([jnp.sum((1.0 - drop) * frames_live), jnp.sum(drop * frames_live)])
    silu_time = jax.nn.silu(time_embed.astype(jnp.float32)).astype(jnp.bfloat16)
    row_span = adaln_weight.shape[0]
    silu_mine = lax.dynamic_slice_in_dim(silu_time, seq_here * row_span, row_span, 1)
    mod_part = jnp.dot(silu_mine, adaln_weight, preferred_element_type=jnp.float32)
    bias_span = adaln_bias.shape[0]
    bias_here = lax.dynamic_update_slice_in_dim(
        jnp.zeros((mod_part.shape[1],), jnp.float32),
        adaln_bias.astype(jnp.float32),
        seq_here * bias_span,
        0,
    )
    mod_part = mod_part + bias_here
    if by_heads:
        small = jnp.concatenate(
            [
                silu_time.astype(jnp.float32),
                jnp.pad(counts[None, :], ((0, 5), (0, model_width - 2))),
            ],
            axis=0,
        )
        (skip_full, qkv_full), late_held, mod_every, small_every = gather_early(
            (skip_weight, qkv_weight),
            (out_weight, up_weight, down_weight),
            mod_part.reshape(-1, model_width),
            small,
        )
        modulation = jnp.sum(mod_every, axis=0)
        totals = jnp.sum(small_every[:, utt_count, :2], axis=0)
        silu_every = small_every[:, :utt_count].reshape(-1, model_width)
    else:
        modulation = lax.psum(mod_part, "seq")
        totals = lax.psum(counts, BATCH)
        skip_full = gather_weight(skip_weight)
        qkv_full = gather_weight(qkv_weight)
        silu_every = lax.all_gather(silu_time, BATCH, axis=0, tiled=True).astype(jnp.float32)
    modulation = modulation.reshape(utt_count, 6, model_width)
    kept_total = jnp.maximum(totals[0], 1.0)
    drop_total = jnp.maximum(totals[1], 1.0)
    every_count = kept_total + drop_total
    loss_weight = (valid_mask - dropped) * (every_count / (2.0 * kept_total)) + dropped * (
        every_count / (2.0 * drop_total)
    )
    first_rows = layer_input.reshape(row_count, model_width)
    second_rows = skip_input.reshape(row_count, model_width)
    if by_heads:
        cos_all, sin_all = paired_tables(frame_count)
        cos_here = lax.dynamic_slice_in_dim(cos_all, seq_here * frame_span, frame_span, 0)
        sin_here = lax.dynamic_slice_in_dim(sin_all, seq_here * frame_span, frame_span, 0)
        residual_rows, proj = enter_layer(
            first_rows, second_rows, skip_full, qkv_full, modulation, cos_here, sin_here
        )
        (qkv_all, out_all, lse_all, attended_low), (out_full, up_full, down_full) = attend_forward(
            lengths, proj, *late_held, frame_span
        )
    else:
        joined = jnp.concatenate([layer_input, skip_input], axis=-1).reshape(row_count, 2 * model_width)
        residual_in = jnp.dot(joined, skip_full, preferred_element_type=jnp.float32).reshape(
            utt_count, frame_span, model_width
        )
        shift_attn = modulation[:, 0][:, None, :]
        scale_attn = modulation[:, 1][:, None, :]
        hat_attn, inv_attn = layer_norm(residual_in)
        normed_attn = (
            (hat_attn * (1.0 + scale_attn) + shift_attn)
            .astype(jnp.bfloat16)
            .reshape(row_count, model_width)
        )
        residual_rows = residual_in.reshape(row_count, model_width)
        out_full, up_full, down_full = [
            gather_weight(weight) for weight in (out_weight, up_weight, down_weight)
        ]
        projected = jnp.dot(normed_attn, qkv_full, preferred_element_type=jnp.float32).reshape(
            utt_count, frame_span, 3, head_count, HEAD_DIM
        )
        cosine_table, sine_table = rotary_tables(local_pos)
        cosine_table = cosine_table[None, :, None, :]
        sine_table = sine_table[None, :, None, :]
        queries = (rotate_heads(projected[:, :, 0], cosine_table, sine_table) * 0.125).astype(
            jnp.bfloat16
        )
        keys_rot = rotate_heads(projected[:, :, 1], cosine_table, sine_table).astype(jnp.bfloat16)
        values = projected[:, :, 2].astype(jnp.bfloat16)
        start_top = jnp.full((utt_count, head_count, frame_span), MASKED, jnp.float32)
        top_score = start_top
        key_piece = lax.all_gather(keys_rot, "seq", axis=1, tiled=True)
        value_piece = lax.all_gather(values, "seq", axis=1, tiled=True)
        piece_len = key_piece.shape[1]
        piece_live = jnp.arange(piece_len, dtype=jnp.int32)[None, :] < lengths[:, None]
        scores = jnp.einsum("bqhd,bkhd->bhqk", queries, key_piece, preferred_element_type=jnp.float32)
        scores = jnp.where(piece_live[:, None, None, :], scores, MASKED)
        new_top = jnp.maximum(top_score, jnp.max(scores, axis=-1))
        expo = jnp.where(piece_live[:, None, None, :], jnp.exp(scores - new_top[..., None]), 0.0)
        denom = jnp.sum(expo, axis=-1)
        partial_out = jnp.einsum(
            "bhqk,bkhd->bqhd",
            expo.astype(jnp.bfloat16),
            value_piece,
            preferred_element_type=jnp.float32,
        )
        accum = partial_out
        accum, top_score, denom = (accum, new_top, denom)
        attended_full = accum / jnp.transpose(denom, (0, 2, 1))[..., None]
        lse_rows = jnp.transpose(top_score + jnp.log(denom), (0, 2, 1))
        attended_low = attended_full.astype(jnp.bfloat16).reshape(row_count, model_width)
    cot_rows = cotangent.reshape(row_count, model_width)
    weight_rows = loss_weight.reshape(row_count, 1)
    branch_attn, hidden_act, hidden_slope, grad_branch_ffn, layer_output, grad_gate_ffn = ffn_forward(
        attended_low,
        out_full,
        residual_rows,
        modulation,
        cot_rows,
        weight_rows,
        up_full,
        down_full,
    )
    layer_output = layer_output.reshape(utt_count, frame_span, model_width)
    grad_up, grad_down, grad_mid, grad_attended_flat, grad_out, ffn_sums = ffn_backward(
        attended_low,
        out_full,
        residual_rows,
        branch_attn,
        modulation,
        cot_rows,
        weight_rows,
        grad_branch_ffn,
        hidden_act,
        hidden_slope,
        up_full,
        down_full,
    )
    grad_shift_ffn, grad_scale_ffn, grad_gate_attn = ffn_sums[:, 0], ffn_sums[:, 1], ffn_sums[:, 2]
    if by_heads:
        grad_projected, *arrived = attend_backward(
            lengths,
            grad_attended_flat,
            qkv_all,
            out_all,
            lse_all,
            cos_all,
            sin_all,
            (grad_down, grad_up, grad_out),
            frame_span,
        )
    else:
        grad_attended = grad_attended_flat.reshape(
            utt_count, frame_span, head_count, HEAD_DIM
        )
        delta_rows = jnp.sum(grad_attended.astype(jnp.float32) * attended_full, axis=-1)
        lse_all, delta_all = (
            lax.all_gather(lse_rows, "seq", axis=1, tiled=True),
            lax.all_gather(delta_rows, "seq", axis=1, tiled=True),
        )
        key_piece = lax.all_gather(keys_rot, "seq", axis=1, tiled=True)
        value_piece = lax.all_gather(values, "seq", axis=1, tiled=True)
        piece_len = key_piece.shape[1]
        piece_live = jnp.arange(piece_len, dtype=jnp.int32)[None, :] < lengths[:, None]
        probs_low, dscore = block_terms(
            queries, grad_attended, lse_rows, delta_rows, key_piece, value_piece, piece_live
        )
        grad_queries = jnp.einsum(
            "bhqk,bkhd->bqhd", dscore, key_piece, preferred_element_type=jnp.float32
        )
        query_piece = lax.all_gather(queries, "seq", axis=1, tiled=True)
        dout_piece = lax.all_gather(grad_attended, "seq", axis=1, tiled=True)
        probs_low, dscore = block_terms(
            query_piece, dout_piece, lse_all, delta_all, keys_rot, values, local_live
        )
        grad_k = jnp.einsum("bhqk,bqhd->bkhd", dscore, query_piece, preferred_element_type=jnp.float32)
        grad_v = jnp.einsum(
            "bhqk,bqhd->bkhd", probs_low, dout_piece, preferred_element_type=jnp.float32
        )
        grad_q_pre = rotate_heads(grad_queries * 0.125, cosine_table, -sine_table)
        grad_k_pre = rotate_heads(grad_k, cosine_table, -sine_table)
        grad_projected = (
            jnp.stack([grad_q_pre, grad_k_pre, grad_v], axis=2)
            .reshape(row_count, 3 * model_width)
            .astype(jnp.bfloat16)
        )
    if by_heads:
        grad_input, grad_skip, attn_sums, grad_qkv, grad_skip_w = leave_layer(
            grad_projected,
            qkv_full,
            skip_full,
            residual_rows,
            grad_mid,
            modulation,
            first_rows,
            second_rows,
        )
        grad_input = grad_input.reshape(layer_input.shape)
        grad_skip = grad_skip.reshape(skip_input.shape)
        grad_shift_attn, grad_scale_attn = attn_sums[:, 0], attn_sums[:, 1]
    else:
        grad_mid = grad_mid.reshape(utt_count, frame_span, model_width)
        grad_qkv = cross(normed_attn, grad_projected)
        grad_normed_attn = back_product(grad_projected, qkv_full).reshape(
            utt_count, frame_span, model_width
        )
        grad_shift_attn = jnp.sum(grad_normed_attn, axis=1)
        grad_scale_attn = jnp.sum(grad_normed_attn * hat_attn, axis=1)
        grad_stream = grad_mid + norm_back(grad_normed_attn * (1.0 + scale_attn), hat_attn, inv_attn)
        grad_stream_low = grad_stream.astype(jnp.bfloat16).reshape(row_count, model_width)
        grad_skip_w = cross(joined, grad_stream_low)
        grad_joined = back_product(grad_stream_low, skip_full)
        grad_input = (
            grad_joined[:, :model_width]
            .reshape(utt_count, frame_span, model_width)
            .astype(jnp.bfloat16)
        )
        grad_skip = (
            grad_joined[:, model_width:]
            .reshape(utt_count, frame_span, model_width)
            .astype(jnp.bfloat16)
        )
    grad_modulation = jnp.stack(
        [
            grad_shift_attn,
            grad_scale_attn,
            grad_gate_attn,
            grad_shift_ffn,
            grad_scale_ffn,
            grad_gate_ffn,
        ],
        axis=1,
    ).reshape(utt_count, 6 * model_width)
    weight_grads = (grad_skip_w, grad_qkv, grad_out, grad_up, grad_down)
    if by_heads:
        shards, mod_every = reduce_grads(
            (grad_qkv, grad_skip_w),
            (grad_down, grad_up, grad_out),
            arrived,
            grad_modulation.reshape(-1, model_width),
        )
        summed = [shards[i] for i in (1, 0, 4, 3, 2)]
        mod_every = mod_every.reshape(-1, 6 * model_width)
    else:
        mod_total = lax.psum(grad_modulation, "seq")
        mod_every = lax.all_gather(
            mod_total.astype(jnp.bfloat16), BATCH, axis=0, tiled=True
        ).astype(jnp.float32)
        summed = [sum_weight(grad) for grad in weight_grads]
    silu_rows = lax.dynamic_slice_in_dim(silu_every, seq_here * row_span, row_span, 1)
    adaln_rows = jnp.dot(silu_rows.T, mod_every, precision=lax.Precision.HIGHEST)
    bias_rows = lax.dynamic_slice_in_dim(
        jnp.sum(mod_every, axis=0), seq_here * bias_span, bias_span, 0
    )
    results = (summed[0], adaln_rows, bias_rows, summed[1], summed[2], summed[3], summed[4])
    return (
        layer_output,
        grad_input,
        grad_skip,
        results[0],
        results[1],
        results[2],
        results[3],
        results[4],
        results[5],
        results[6],
    )


def solution(mesh):
    count, batch = mesh.shape["seq"], mesh.shape["batch"]
    cores = 2 if batch % 2 == 0 else 1
    split = Mesh(mesh.devices.reshape(count, batch // cores, cores), ("seq",) + BATCH)
    placed = (
        P(BATCH, "seq", None),
        P(BATCH, "seq", None),
        P(BATCH, None),
        P(BATCH),
        P(BATCH),
        P(BATCH, "seq", None),
        P("seq", None),
        P("seq", None),
        P("seq"),
        P("seq", None),
        P("seq", None),
        P("seq", None),
        P("seq", None),
    )
    return jax.shard_map(
        on_device,
        mesh=split,
        in_specs=placed,
        out_specs=(
            P(BATCH, "seq", None),
            P(BATCH, "seq", None),
            P(BATCH, "seq", None),
            P("seq", None),
            P("seq", None),
            P("seq"),
            P("seq", None),
            P("seq", None),
            P("seq", None),
            P("seq", None),
        ),
        check_vma=False,
    )
```

```python
import functools
import jax
import jax.numpy as jnp
import numpy as np
from jax import lax
from jax.sharding import Mesh, PartitionSpec as P
from jax.experimental import pallas as pl
from jax.experimental.pallas import tpu as pltpu
HEAD_DIM = 64
EPS = 1e-06
LOG2E = 1.4426950408889634
LN2 = 0.6931471805599453
MASKED = -1e30
BF = jnp.bfloat16
F32 = jnp.float32
VMEM_LIMIT = 60 * 2**20


def nt(left, right):
    return lax.dot_general(left, right, (((1,), (1,)), ((), ())), preferred_element_type=F32)


def nn(left, right):
    return lax.dot_general(left, right, (((1,), (0,)), ((), ())), preferred_element_type=F32)


def head_sums(product, lane):
    first = jnp.sum(jnp.where(lane < 64, product, 0.0), axis=1, keepdims=True)
    second = jnp.sum(jnp.where(lane >= 64, product, 0.0), axis=1, keepdims=True)
    return (first, second)


def lanes_of(rows):
    return lax.broadcasted_iota(jnp.int32, (rows, 128), 1)


def attention_cost(frames, products):
    return pl.CostEstimate(
        flops=2 * products * 2 * frames * frames * 128,
        bytes_accessed=frames * 128 * 2 * 8,
        transcendentals=2 * frames * frames,
    )


def turn_back(grad, cos, sin):
    lane = lanes_of(grad.shape[0])
    turned = jnp.where((lane & 63) < 32, pltpu.roll(grad, 96, 1), pltpu.roll(grad, 32, 1))
    return grad * cos - turned * sin


def three(column, lane, at):
    high = column.astype(BF).astype(F32)
    rest = column - high
    mid = rest.astype(BF).astype(F32)
    low = rest - mid
    return jnp.where(lane == at, -high, jnp.where(lane == at + 1, -mid, jnp.where(lane == at + 2, -low, 0.0)))


MESH_IDS = pl.DeviceIdType.MESH


def seq_flip(flip):
    return (lax.axis_index("seq") ^ flip, lax.axis_index("x"), lax.axis_index("core"))


def greet(devices):
    barrier = pltpu.get_barrier_semaphore()
    for device in devices:
        pl.semaphore_signal(barrier, inc=1, device_id=device, device_id_type=MESH_IDS)
    pl.semaphore_wait(barrier, len(devices))


def remote(source, target, send, recv, device):
    return pltpu.make_async_remote_copy(
        source, target, send, recv, device_id=device, device_id_type=MESH_IDS
    )


class WeightGather:
    def __init__(self, jobs, send, recv, local):
        self.jobs, self.send, self.recv, self.local = jobs, send, recv, local
        me, x, core = lax.axis_index("seq"), lax.axis_index("x"), lax.axis_index("core")
        self.bits = (me // 4, (me // 2) % 2, me % 2, x, core)
        self.copies = [[] for _ in jobs]
        self.owns = []

    def peer(self, dim):
        me, x, core = lax.axis_index("seq"), lax.axis_index("x"), lax.axis_index("core")
        if dim < 3:
            return (me ^ (4 >> dim), x, core)
        return (me, 1 - x, core) if dim == 3 else (me, x, 1 - core)

    def stage(self):
        for index, (full, cols, source, ready, order) in enumerate(self.jobs):
            at = len(self.copies[index])
            where = tuple(
                slice(None) if d in ready + order[:at] else self.bits[d]
                for d in range(len(full.shape) - 2)
            ) + (slice(None), cols)
            if at == 0:
                own = pltpu.make_async_copy(source, full.at[where], self.local.at[index])
                own.start()
                self.owns.append(own)
            else:
                if at == 1:
                    self.owns[index].wait()
                self.copies[index][at - 1].wait_recv()
            copy = remote(
                source if at == 0 else full.at[where],
                full.at[where],
                self.send.at[index * 5 + at],
                self.recv.at[index * 5 + at],
                self.peer(order[at]),
            )
            copy.start()
            self.copies[index].append(copy)

    def finish(self):
        for chain in self.copies:
            chain[-1].wait_recv()
        for chain in self.copies:
            for copy in chain:
                copy.wait_send()


def split_columns(width, shares):
    total, start, out = sum(shares), 0, []
    for n in range(len(shares)):
        stop = width * sum(shares[: n + 1]) // total // 128 * 128
        out.append(pl.ds(start, stop - start))
        start = stop
    return out


def quarter_of(weight, cols):
    quarter = lax.axis_index("x") * 2 + lax.axis_index("core")
    span = weight.shape[0] // 4
    return weight.at[pl.ds(quarter * span, span), cols]


def early_jobs(weights, fulls):
    orders = ((0, 1, 2, 3, 4), (0, 2, 3, 1, 4), (0, 3, 1, 2, 4))
    return [
        (full, cols, quarter_of(weight, cols), (), order)
        for weight, full in zip(weights, fulls)
        for cols, order in zip(split_columns(weight.shape[1], (1, 1, 1)), orders)
    ]


def ahead_jobs(weights, helds):
    every = [(weight, held, pl.ds(0, weight.shape[1])) for weight, held in zip(weights, helds)]
    return [(held, cols, quarter_of(weight, cols), (), (0, 1)) for weight, held, cols in every]


def late_jobs(helds, fulls):
    return [
        (full, cols, held.at[:, :, :, cols], (0, 1), order)
        for held, full in zip(helds, fulls)
        for cols, order in zip(split_columns(held.shape[3], (3, 1)), ((2, 3, 4), (3, 2, 4)))
    ]


def attend_forward_kernel(
    len_ref, proj, out_w, up_w, down_w,
    qkv_all, o_all, lse_ref, att, out_full, up_full, down_full,
    qkv, outs, ka, kb, vta, vtb,
    wsend, wrecv, wlocal, qsend, qrecv, qlocal, osend, orecv, olocal, slocal,
    *, span, bq, bk,
):
    me, x, core = lax.axis_index("seq"), lax.axis_index("x"), lax.axis_index("core")
    frames = qkv.shape[2]
    mine = pl.ds(pl.multiple_of(me * span, span), span)
    my_cols = pl.ds(pl.multiple_of(me * 128, 128), 128)
    flips = (7, 6, 5, 4, 3, 2, 1)
    greet([seq_flip(flip) for flip in flips] + [(me, 1 - x, core), (me, x, 1 - core)])
    weights = WeightGather(
        late_jobs((out_w, up_w, down_w), (out_full, up_full, down_full)), wsend, wrecv, wlocal
    )

    def send_heads(utt):
        rows = pl.ds(utt * span, span)
        own = pltpu.make_async_copy(
            proj.at[:, rows, my_cols], qkv.at[utt, :, mine, :], qlocal.at[utt]
        )
        own.start()
        copies = []
        for flip in flips:
            there = me ^ flip
            cols = pl.ds(pl.multiple_of(there * 128, 128), 128)
            copy = remote(
                proj.at[:, rows, cols],
                qkv.at[utt, :, mine, :],
                qsend.at[utt * 8 + flip],
                qrecv.at[utt * 8 + flip],
                seq_flip(flip),
            )
            copy.start()
            copies.append(copy)
        return own, copies

    def arrive(sent):
        own, copies = sent
        own.wait()
        for copy in copies:
            copy.wait_recv()

    def send_out(utt, there):
        rows = pl.ds(pl.multiple_of(there * span, span), span)
        target = att.at[pl.ds(utt * span, span), my_cols]

        @pl.when(there != me)
        def _():
            remote(
                outs.at[utt, rows, :],
                target,
                osend.at[utt * 8 + (there ^ me)],
                orecv.at[utt * 8 + (there ^ me)],
                (there, x, core),
            ).start()

        @pl.when(there == me)
        def _():
            pltpu.make_async_copy(outs.at[utt, rows, :], target, olocal.at[utt]).start()

    def attend(utt, between):
        length = len_ref[utt]
        save = pltpu.make_async_copy(qkv.at[utt], qkv_all.at[utt], slocal.at[utt])
        save.start()

        def build(j, carry):
            rows = pl.ds(pl.multiple_of(j * bk, bk), bk)
            lane = lanes_of(bk)
            pos = j * bk + lax.broadcasted_iota(jnp.int32, (bk, 128), 0)
            bias = jnp.where(pos < length, 0.0, MASKED)
            keys = qkv[utt, 1, rows, :].astype(F32)
            ka[rows, :] = jnp.where(lane < 64, keys, jnp.where(lane == 64, bias, 0.0)).astype(BF)
            kb[rows, :] = jnp.where(lane >= 64, keys, jnp.where(lane == 0, bias, 0.0)).astype(BF)
            vals = qkv[utt, 2, rows, :].astype(F32)
            vta[:, rows] = jnp.where(lane < 64, vals, 1.0).T.astype(BF)
            vtb[:, rows] = jnp.where(lane >= 64, vals, 1.0).T.astype(BF)
            return carry

        lax.fori_loop(0, frames // bk, build, 0)

        def block(i, carry):
            here = pl.ds(pl.multiple_of(i * bq, bq), bq)
            lane = lanes_of(bq)
            queries = qkv[utt, 0, here, :].astype(F32)
            qa = jnp.where(lane < 64, queries, jnp.where(lane == 64, 1.0, 0.0)).astype(BF)
            qb = jnp.where(lane >= 64, queries, jnp.where(lane == 0, 1.0, 0.0)).astype(BF)

            def body(j, inner):
                rows = pl.ds(pl.multiple_of(j * bk, bk), bk)
                result = []
                scores = [nt(ka[rows, :], qa), nt(kb[rows, :], qb)]
                for score, vt, (top, acc) in zip(scores, (vta, vtb), inner):
                    new = jnp.maximum(top, jnp.max(score, axis=0, keepdims=True))
                    probs = jnp.exp2(score - new).astype(BF)
                    acc = acc * jnp.exp2(top - new) + nn(vt[:, rows], probs)
                    result.append((new, acc))
                return tuple(result)

            start = (jnp.full((1, bq), MASKED, F32), jnp.zeros((128, bq), F32))
            (top_a, acc_a), (top_b, acc_b) = lax.fori_loop(0, frames // bk, body, (start, start))
            sum_a, sum_b = acc_a[64:65], acc_b[0:1]
            both = jnp.concatenate([acc_a[:64] / sum_a, acc_b[64:] / sum_b], axis=0)
            outs[utt, here, :] = both.T.astype(BF)
            lse_ref[utt, :, here] = jnp.concatenate(
                [top_a + jnp.log2(sum_a), top_b + jnp.log2(sum_b), jnp.zeros((6, bq), F32)],
                axis=0,
            )
            if utt == 1:
                for part in range(bq // span):
                    send_out(utt, i * (bq // span) + part)
            return carry

        half = frames // bq // 2
        lax.fori_loop(0, half, block, 0)
        between()
        lax.fori_loop(half, 2 * half, block, 0)
        keep = pltpu.make_async_copy(outs.at[utt], o_all.at[utt], slocal.at[2 + utt])
        keep.start()
        return [save, keep]

    first = send_heads(0)
    weights.stage()
    arrive(first)
    second = send_heads(1)
    weights.stage()
    saves = attend(0, lambda: None)
    arrive(second)

    def send_first(i, carry):
        send_out(0, i)
        return carry

    lax.fori_loop(0, 8, send_first, 0)
    saves += attend(1, weights.stage)
    for sent in (first, second):
        for copy in sent[1]:
            copy.wait_send()
    weights.finish()
    for save in saves:
        save.wait()
    for utt in range(2):
        target = att.at[pl.ds(utt * span, span), my_cols]
        pltpu.make_async_copy(outs.at[utt, mine, :], target, olocal.at[utt]).wait()
        for flip in flips:
            copy = remote(
                outs.at[utt, mine, :],
                target,
                osend.at[utt * 8 + flip],
                orecv.at[utt * 8 + flip],
                seq_flip(flip),
            )
            copy.wait_send()
            copy.wait_recv()


def attend_forward(lengths, proj, out_w, up_w, down_w, span, bq=1024, bk=512):
    rows, width = proj.shape[1:]
    frames = 8 * span
    anywhere = pl.BlockSpec(memory_space=pl.ANY)
    vmem = pl.BlockSpec(memory_space=pltpu.VMEM)
    full = lambda w: jax.ShapeDtypeStruct((2, 2, 2, 2, 2) + w.shape[2:], BF)
    dma = pltpu.SemaphoreType.DMA
    outs = pl.pallas_call(
        functools.partial(attend_forward_kernel, span=span, bq=bq, bk=bk),
        in_specs=[pl.BlockSpec(memory_space=pltpu.SMEM)] + [anywhere] * 4,
        out_specs=[anywhere, anywhere, vmem] + [anywhere] * 4,
        out_shape=[
            jax.ShapeDtypeStruct((2, 3, frames, 128), BF),
            jax.ShapeDtypeStruct((2, frames, 128), BF),
            jax.ShapeDtypeStruct((2, 8, frames), F32),
            jax.ShapeDtypeStruct((rows, width), BF),
            full(out_w),
            full(up_w),
            full(down_w),
        ],
        scratch_shapes=[
            pltpu.VMEM((2, 3, frames, 128), BF),
            pltpu.VMEM((2, frames, 128), BF),
            pltpu.VMEM((frames, 128), BF),
            pltpu.VMEM((frames, 128), BF),
            pltpu.VMEM((128, frames), BF),
            pltpu.VMEM((128, frames), BF),
            dma((30,)),
            dma((30,)),
            dma((6,)),
            dma((16,)),
            dma((16,)),
            dma((2,)),
            dma((16,)),
            dma((16,)),
            dma((2,)),
            dma((4,)),
        ],
        compiler_params=pltpu.CompilerParams(
            vmem_limit_bytes=VMEM_LIMIT, collective_id=1, has_side_effects=True
        ),
        cost_estimate=attention_cost(frames, 4),
        name="attend_forward",
    )(lengths, proj, out_w, up_w, down_w)
    fulls = [
        outs[4 + i].reshape(32 * w.shape[2], w.shape[3]) for i, w in enumerate((out_w, up_w, down_w))
    ]
    return outs[:4], fulls


def attend_backward_kernel(
    len_ref, dout, qkv_all, o_all, lse_ref, cos_ref, sin_ref, raw_a, raw_b, raw_c,
    grads, got_a, got_b, got_c,
    qkv, outs, douts, qa, qb, da, db, qt, dt, dqa, dqb,
    dsend, drecv, dlocal, gsend, grecv, glocal, load, rsend, rrecv,
    *, span, block,
):
    me, x, core = lax.axis_index("seq"), lax.axis_index("x"), lax.axis_index("core")
    frames = qkv.shape[2]
    width = grads.shape[1] // 3
    count = frames // block
    mine = pl.ds(pl.multiple_of(me * span, span), span)
    flips = (7, 6, 5, 4, 3, 2, 1)
    mates = [(me, x ^ dx, core ^ dc) for dx, dc in ((0, 1), (1, 0), (1, 1))]
    greet([seq_flip(flip) for flip in flips] + mates)
    loads = []
    for utt in range(2):
        loads.append(
            [
                pltpu.make_async_copy(qkv_all.at[utt], qkv.at[utt], load.at[utt]),
                pltpu.make_async_copy(o_all.at[utt], outs.at[utt], load.at[2 + utt]),
            ]
        )
        for copy in loads[-1]:
            copy.start()

    def send_heads(utt):
        rows = pl.ds(utt * span, span)
        my_cols = pl.ds(pl.multiple_of(me * 128, 128), 128)
        own = pltpu.make_async_copy(dout.at[rows, my_cols], douts.at[utt, mine, :], dlocal.at[utt])
        own.start()
        copies = []
        for flip in flips:
            cols = pl.ds(pl.multiple_of((me ^ flip) * 128, 128), 128)
            copy = remote(
                dout.at[rows, cols],
                douts.at[utt, mine, :],
                dsend.at[utt * 8 + flip],
                drecv.at[utt * 8 + flip],
                seq_flip(flip),
            )
            copy.start()
            copies.append(copy)
        return own, copies

    def arrive(sent):
        own, copies = sent
        own.wait()
        for copy in copies:
            copy.wait_recv()

    def slot(utt, part, flip):
        return (utt * 3 + part) * 8 + flip

    def target(utt, part):
        cols = pl.ds(pl.multiple_of(part * width + me * 128, 128), 128)
        return grads.at[pl.ds(utt * span, span), cols]

    def send_grads(utt, part, there):
        rows = pl.ds(pl.multiple_of(there * span, span), span)

        @pl.when(there != me)
        def _():
            at = slot(utt, part, there ^ me)
            remote(
                qkv.at[utt, part, rows, :],
                target(utt, part),
                gsend.at[at],
                grecv.at[at],
                (there, x, core),
            ).start()

        @pl.when(there == me)
        def _():
            pltpu.make_async_copy(
                qkv.at[utt, part, rows, :], target(utt, part), glocal.at[utt * 3 + part]
            ).start()

    def differentiate(utt):
        length = len_ref[utt]

        def build(j, carry):
            rows = pl.ds(pl.multiple_of(j * block, block), block)
            lane = lanes_of(block)
            queries = qkv[utt, 0, rows, :].astype(F32)
            grad = douts[utt, rows, :].astype(F32)
            delta_a, delta_b = head_sums(grad * outs[utt, rows, :].astype(F32), lane)
            lse = lse_ref[utt, :, rows].T
            one_a, one_b = lse[:, 0:1], lse[:, 1:2]
            qa[rows, :] = jnp.where(
                lane < 64, queries, jnp.where(lane == 67, 1.0, three(one_a, lane, 64))
            ).astype(BF)
            qb[rows, :] = jnp.where(
                lane >= 64, queries, jnp.where(lane == 3, 1.0, three(one_b, lane, 0))
            ).astype(BF)
            da[rows, :] = jnp.where(lane < 64, grad, three(delta_a, lane, 64)).astype(BF)
            db[rows, :] = jnp.where(lane >= 64, grad, three(delta_b, lane, 0)).astype(BF)
            qt[:, rows] = queries.T.astype(BF)
            dt[:, rows] = grad.T.astype(BF)
            dqa[rows, :] = jnp.zeros((block, 128), F32)
            dqb[rows, :] = jnp.zeros((block, 128), F32)
            return carry

        lax.fori_loop(0, count, build, 0)

        def keys_block(i, carry):
            here = pl.ds(pl.multiple_of(i * block, block), block)
            lane = lanes_of(block)
            pos = i * block + lax.broadcasted_iota(jnp.int32, (block, 128), 0)
            bias = jnp.where(pos < length, 0.0, MASKED)
            keys = qkv[utt, 1, here, :].astype(F32)
            vals = qkv[utt, 2, here, :].astype(F32)
            ones_a = jnp.where(lane < 67, 1.0, 0.0)
            ones_b = jnp.where(lane < 3, 1.0, 0.0)
            ka = jnp.where(lane < 64, keys, jnp.where(lane == 67, bias, ones_a)).astype(BF)
            kb = jnp.where(lane >= 64, keys, jnp.where(lane == 3, bias, ones_b)).astype(BF)
            va = jnp.where(lane < 64, vals, ones_a).astype(BF)
            vb = jnp.where(lane >= 64, vals, ones_b).astype(BF)

            def body(j, inner):
                rows = pl.ds(pl.multiple_of(j * block, block), block)
                result = []
                for head, (qh, dh, kh, vh, dq) in enumerate(
                    ((qa, da, ka, va, dqa), (qb, db, kb, vb, dqb))
                ):
                    part = slice(head * 64, head * 64 + 64)
                    probs = jnp.exp2(nt(qh[rows, :], kh))
                    grad = (probs * nt(dh[rows, :], vh)).astype(BF)
                    dv = inner[2 * head + 1] + nn(dt[:, rows], probs.astype(BF))[part]
                    dk = inner[2 * head] + nn(qt[:, rows], grad)[part]
                    dq[rows, :] += nn(grad, kh)
                    result += [dk, dv]

                @pl.when(i == count - 1)
                def _():
                    low = jnp.where(lanes_of(block) < 64, dqa[rows, :], dqb[rows, :]) * 0.125
                    low = turn_back(low, cos_ref[rows, :], sin_ref[rows, :])
                    qkv[utt, 0, rows, :] = low.astype(BF)
                    for step in range(block // span):
                        send_grads(utt, 0, j * (block // span) + step)

                return tuple(result)

            zero = jnp.zeros((64, block), F32)
            dk_a, dv_a, dk_b, dv_b = lax.fori_loop(0, count, body, (zero,) * 4)
            dk = jnp.concatenate([dk_a, dk_b], axis=0).T * LN2
            dv = jnp.concatenate([dv_a, dv_b], axis=0).T
            qkv[utt, 1, here, :] = turn_back(dk, cos_ref[here, :], sin_ref[here, :]).astype(BF)
            qkv[utt, 2, here, :] = dv.astype(BF)
            for step in range(block // span):
                there = i * (block // span) + step
                send_grads(utt, 1, there)
                send_grads(utt, 2, there)
            return carry

        lax.fori_loop(0, count, keys_block, 0)

    first = send_heads(0)
    raws = []
    for index, (raw, got) in enumerate(((raw_a, got_a), (raw_b, got_b), (raw_c, got_c))):
        for slot_at, device in enumerate(mates):
            at = index * 3 + slot_at
            copy = remote(
                raw.at[:, :, :, device[1], device[2]],
                got.at[slot_at],
                rsend.at[at],
                rrecv.at[at],
                device,
            )
            copy.start()
            raws.append(copy)
    for copy in loads[0]:
        copy.wait()
    arrive(first)
    second = send_heads(1)
    differentiate(0)
    for copy in loads[1]:
        copy.wait()
    arrive(second)
    differentiate(1)
    for sent in (first, second):
        for copy in sent[1]:
            copy.wait_send()
    for copy in raws:
        copy.wait()
    for utt in range(2):
        for part in range(3):
            own = qkv.at[utt, part, mine, :]
            pltpu.make_async_copy(own, target(utt, part), glocal.at[utt * 3 + part]).wait()
            for flip in flips:
                at = slot(utt, part, flip)
                copy = remote(own, target(utt, part), gsend.at[at], grecv.at[at], seq_flip(flip))
                copy.wait_send()
                copy.wait_recv()


def attend_backward(lengths, dout, qkv_all, o_all, lse, cos, sin, raws, span, block=1024):
    raws = [raw.reshape(2, 2, 2, 2, 2, raw.shape[0] // 32, raw.shape[1]) for raw in raws]
    frames = 8 * span
    rows, width = dout.shape
    anywhere = pl.BlockSpec(memory_space=pl.ANY)
    vmem = pl.BlockSpec(memory_space=pltpu.VMEM)
    dma = pltpu.SemaphoreType.DMA
    return pl.pallas_call(
        functools.partial(attend_backward_kernel, span=span, block=block),
        in_specs=[pl.BlockSpec(memory_space=pltpu.SMEM)]
        + [anywhere] * 3
        + [vmem] * 3
        + [anywhere] * 3,
        out_specs=[anywhere] * 4,
        out_shape=[jax.ShapeDtypeStruct((rows, 3 * width), BF)]
        + [jax.ShapeDtypeStruct((3, 2, 2, 2) + raw.shape[5:], BF) for raw in raws],
        scratch_shapes=[
            pltpu.VMEM((2, 3, frames, 128), BF),
            pltpu.VMEM((2, frames, 128), BF),
            pltpu.VMEM((2, frames, 128), BF),
        ]
        + [pltpu.VMEM((frames, 128), BF)] * 4
        + [pltpu.VMEM((128, frames), BF)] * 2
        + [pltpu.VMEM((frames, 128), F32)] * 2
        + [dma((16,)), dma((16,)), dma((2,)), dma((48,)), dma((48,)), dma((6,)), dma((4,)), dma((9,)), dma((9,))],
        compiler_params=pltpu.CompilerParams(
            vmem_limit_bytes=VMEM_LIMIT, collective_id=2, has_side_effects=True
        ),
        cost_estimate=attention_cost(frames, 10),
        name="attend_backward",
    )(lengths, dout, qkv_all, o_all, lse, cos, sin, *raws)


def layer_norm(stream):
    centre = stream - jnp.mean(stream, axis=-1, keepdims=True)
    spread = jnp.mean(centre * centre, axis=-1, keepdims=True)
    inverse = lax.rsqrt(spread + EPS)
    return (centre * inverse, inverse)


def norm_back(grad_normed, normed, inverse):
    first_mean = jnp.mean(grad_normed, axis=-1, keepdims=True)
    second_mean = jnp.mean(grad_normed * normed, axis=-1, keepdims=True)
    return inverse * (grad_normed - first_mean - normed * second_mean)


def tn(left, right):
    return lax.dot_general(left, right, (((0,), (0,)), ((), ())), preferred_element_type=F32)


GELU_C = 0.7978845608028654
GELU_A = 0.044715


def gelu_and_slope(z):
    square = z * z
    turn = jnp.tanh(GELU_C * z * (1.0 + GELU_A * square))
    half = 0.5 * (1.0 + turn)
    slope = half + 0.5 * z * (1.0 - turn * turn) * (GELU_C * (1.0 + 3.0 * GELU_A * square))
    return z * half, slope


def row_blocks(rows):
    block = min(rows, 512)
    return [(at, slice(at, at + block)) for at in range(0, rows, block)]


def ffn_forward_kernel(
    att_ref, outw_ref, res_ref, mod_ref, cot_ref, weight_ref, up_ref, down_ref,
    branch_ref, act_ref, slope_ref, gb_ref, out_ref, gate_ref, normed, acc,
):
    step = pl.program_id(0)
    rows = att_ref.shape[0]
    span = rows // mod_ref.shape[0]

    @pl.when(step == 0)
    def _():
        for at, part in row_blocks(span):
            for utt in range(mod_ref.shape[0]):
                here = slice(utt * span + part.start, utt * span + part.stop)
                mod = mod_ref[utt]
                branch = nn(att_ref[here, :], outw_ref[...])
                branch_ref[here, :] = branch
                hat, _ = layer_norm(res_ref[here, :] + mod[2:3] * branch)
                normed[here, :] = (hat * (1.0 + mod[4:5]) + mod[3:4]).astype(BF)
        acc[...] = jnp.zeros_like(acc)

    parts = [part for _, part in row_blocks(rows)]
    ahead = nn(normed[parts[0], :], up_ref[...])
    for index, part in enumerate(parts):
        hidden = ahead
        if index + 1 < len(parts):
            ahead = nn(normed[parts[index + 1], :], up_ref[...])
        act, slope = gelu_and_slope(hidden)
        act = act.astype(BF)
        act_ref[part, :] = act
        slope_ref[part, :] = slope.astype(BF)
        acc[part, :] += nn(act, down_ref[...])

    @pl.when(step == pl.num_programs(0) - 1)
    def _():
        for utt in range(mod_ref.shape[0]):
            mod = mod_ref[utt]
            total = jnp.zeros((1, acc.shape[1]), F32)
            for _, part in row_blocks(span):
                here = slice(utt * span + part.start, utt * span + part.stop)
                branch = acc[here, :]
                mid = res_ref[here, :] + mod[2:3] * branch_ref[here, :]
                out_ref[here, :] = (mid + mod[5:6] * branch).astype(BF)
                upstream = cot_ref[here, :].astype(F32) * weight_ref[here, :]
                gb_ref[here, :] = (upstream * mod[5:6]).astype(BF)
                total += jnp.sum(upstream * branch, axis=0, keepdims=True)
            gate_ref[utt : utt + 1, :] = total


def ffn_backward_kernel(
    att_ref, outw_ref, res_ref, branch_ref, mod_ref, cot_ref, weight_ref, gb_ref,
    act_ref, slope_ref, up_ref, down_ref,
    gup_ref, gdown_ref, gmid_ref, gatt_ref, gout_ref, sums_ref, normed, acc, gba,
):
    step = pl.program_id(0)
    rows = att_ref.shape[0]
    utts = mod_ref.shape[0]
    span = rows // utts

    def hat_of(here, mod):
        return layer_norm(res_ref[here, :] + mod[2:3] * branch_ref[here, :])

    @pl.when(step == 0)
    def _():
        for utt in range(utts):
            mod = mod_ref[utt]
            for _, part in row_blocks(span):
                here = slice(utt * span + part.start, utt * span + part.stop)
                hat, _ = hat_of(here, mod)
                normed[here, :] = (hat * (1.0 + mod[4:5]) + mod[3:4]).astype(BF)
        acc[...] = jnp.zeros_like(acc)

    pieces = []
    for _, part in row_blocks(rows):
        grad = nt(gb_ref[part, :], down_ref[...]) * slope_ref[part, :].astype(F32)
        grad = grad.astype(BF)
        acc[part, :] += nt(grad, up_ref[...])
        pieces.append(grad)
    gdown_ref[...] = tn(act_ref[...], gb_ref[...]).astype(BF)
    gup_ref[...] = tn(normed[...], jnp.concatenate(pieces, axis=0)).astype(BF)

    @pl.when(step == pl.num_programs(0) - 1)
    def _():
        for utt in range(utts):
            mod = mod_ref[utt]
            width = acc.shape[1]
            shift = jnp.zeros((1, width), F32)
            scale = jnp.zeros((1, width), F32)
            gate = jnp.zeros((1, width), F32)
            for _, part in row_blocks(span):
                here = slice(utt * span + part.start, utt * span + part.stop)
                hat, inverse = hat_of(here, mod)
                grad = acc[here, :]
                shift += jnp.sum(grad, axis=0, keepdims=True)
                scale += jnp.sum(grad * hat, axis=0, keepdims=True)
                upstream = cot_ref[here, :].astype(F32) * weight_ref[here, :]
                mid = upstream + norm_back(grad * (1.0 + mod[4:5]), hat, inverse)
                gmid_ref[here, :] = mid
                gate += jnp.sum(mid * branch_ref[here, :], axis=0, keepdims=True)
                low = (mid * mod[2:3]).astype(BF)
                gba[here, :] = low
                gatt_ref[here, :] = nt(low, outw_ref[...]).astype(BF)
            sums_ref[utt, 0:1, :] = shift
            sums_ref[utt, 1:2, :] = scale
            sums_ref[utt, 2:3, :] = gate
        gout_ref[...] = tn(att_ref[...], gba[...]).astype(BF)


def whole_spec(shape):
    zeros = (0,) * len(shape)
    return pl.BlockSpec(shape, lambda i: zeros, pipeline_mode=pl.Buffered(1))


def ffn_forward(att, outw, res, mods, cot, weight, up, down, chunk=1024):
    rows, width = res.shape
    hidden = up.shape[1]
    whole = [whole_spec(a.shape) for a in (att, outw, res, mods, cot, weight)]
    col = pl.BlockSpec((rows, chunk), lambda i: (0, i))
    utts = mods.shape[0]
    return pl.pallas_call(
        ffn_forward_kernel,
        grid=(hidden // chunk,),
        in_specs=whole
        + [
            pl.BlockSpec((width, chunk), lambda i: (0, i)),
            pl.BlockSpec((chunk, width), lambda i: (i, 0)),
        ],
        out_specs=[
            whole_spec((rows, width)),
            col,
            col,
            whole_spec((rows, width)),
            whole_spec((rows, width)),
            whole_spec((utts, width)),
        ],
        out_shape=[
            jax.ShapeDtypeStruct((rows, width), F32),
            jax.ShapeDtypeStruct((rows, hidden), BF),
            jax.ShapeDtypeStruct((rows, hidden), BF),
            jax.ShapeDtypeStruct((rows, width), BF),
            jax.ShapeDtypeStruct((rows, width), BF),
            jax.ShapeDtypeStruct((utts, width), F32),
        ],
        scratch_shapes=[pltpu.VMEM((rows, width), BF), pltpu.VMEM((rows, width), F32)],
        compiler_params=pltpu.CompilerParams(vmem_limit_bytes=VMEM_LIMIT),
        cost_estimate=pl.CostEstimate(
            flops=2 * rows * width * (width + 2 * hidden),
            bytes_accessed=60 * 2**20,
            transcendentals=rows * hidden,
        ),
        name="ffn_forward",
    )(att, outw, res, mods, cot, weight, up, down)


def ffn_backward(att, outw, res, branch, mods, cot, weight, gb, act, slope, up, down, chunk=512):
    rows, width = res.shape
    hidden = up.shape[1]
    utts = mods.shape[0]
    whole = [whole_spec(a.shape) for a in (att, outw, res, branch, mods, cot, weight, gb)]
    col = pl.BlockSpec((rows, chunk), lambda i: (0, i))
    upspec = pl.BlockSpec((width, chunk), lambda i: (0, i))
    downspec = pl.BlockSpec((chunk, width), lambda i: (i, 0))
    return pl.pallas_call(
        ffn_backward_kernel,
        grid=(hidden // chunk,),
        in_specs=whole + [col, col, upspec, downspec],
        out_specs=[
            upspec,
            downspec,
            whole_spec((rows, width)),
            whole_spec((rows, width)),
            whole_spec((width, width)),
            whole_spec((utts, 8, width)),
        ],
        out_shape=[
            jax.ShapeDtypeStruct((width, hidden), BF),
            jax.ShapeDtypeStruct((hidden, width), BF),
            jax.ShapeDtypeStruct((rows, width), F32),
            jax.ShapeDtypeStruct((rows, width), BF),
            jax.ShapeDtypeStruct((width, width), BF),
            jax.ShapeDtypeStruct((utts, 8, width), F32),
        ],
        scratch_shapes=[
            pltpu.VMEM((rows, width), BF),
            pltpu.VMEM((rows, width), F32),
            pltpu.VMEM((rows, width), BF),
        ],
        compiler_params=pltpu.CompilerParams(vmem_limit_bytes=VMEM_LIMIT),
        cost_estimate=pl.CostEstimate(
            flops=2 * rows * width * (2 * width + 4 * hidden),
            bytes_accessed=90 * 2**20,
            transcendentals=0,
        ),
        name="ffn_backward",
    )(att, outw, res, branch, mods, cot, weight, gb, act, slope, up, down)


def enter_kernel(
    in_ref, skip_ref, skip_w, qkv_w, mod_ref, cos_ref, sin_ref, res_ref, proj_ref
):
    width = in_ref.shape[1]
    mod = mod_ref[0]
    residual = nn(in_ref[...], skip_w[:width, :]) + nn(skip_ref[...], skip_w[width:, :])
    res_ref[...] = residual
    hat, _ = layer_norm(residual)
    normed = (hat * (1.0 + mod[1:2]) + mod[0:1]).astype(BF)
    lane = lanes_of(in_ref.shape[0])
    cos, sin = cos_ref[...], sin_ref[...]
    for part in range(3):
        projected = nn(normed, qkv_w[:, part * width : (part + 1) * width])
        for group in range(width // 128):
            cols = slice(group * 128, group * 128 + 128)
            piece = projected[:, cols]
            if part < 2:
                turned = jnp.where(
                    (lane & 63) < 32, pltpu.roll(piece, 96, 1), pltpu.roll(piece, 32, 1)
                )
                piece = piece * cos + turned * sin
            if part == 0:
                piece = piece * (0.125 * LOG2E)
            proj_ref[part, :, cols] = piece.astype(BF)


def enter_layer(first, second, skip_w, qkv_w, mods, cos, sin, block=256):
    rows, width = first.shape
    steps = rows // mods.shape[0] // block
    part = pl.BlockSpec((block, width), lambda i: (i, 0))
    table = pl.BlockSpec((block, 128), lambda i: (i % steps, 0))
    return pl.pallas_call(
        enter_kernel,
        grid=(rows // block,),
        in_specs=[
            part,
            part,
            whole_spec(skip_w.shape),
            whole_spec(qkv_w.shape),
            pl.BlockSpec((1,) + mods.shape[1:], lambda i: (i // steps, 0, 0)),
            table,
            table,
        ],
        out_specs=[part, pl.BlockSpec((3, block, width), lambda i: (0, i, 0))],
        out_shape=[
            jax.ShapeDtypeStruct((rows, width), F32),
            jax.ShapeDtypeStruct((3, rows, width), BF),
        ],
        compiler_params=pltpu.CompilerParams(vmem_limit_bytes=VMEM_LIMIT),
        cost_estimate=pl.CostEstimate(
            flops=2 * rows * (skip_w.size + qkv_w.size),
            bytes_accessed=40 * 2**20,
            transcendentals=0,
        ),
        name="enter_layer",
    )(first, second, skip_w, qkv_w, mods, cos, sin)


FOLD_DIMS = (2, 1)


def fold_jobs(raws, arrived, folded, keeps, buffers):
    jobs = []
    for index, (raw, got) in enumerate(zip(raws, arrived)):
        for side, cols in enumerate(split_columns(raw.shape[-1], (1, 1))):
            at = 2 * index + side
            jobs.append((raw, got, cols, FOLD_DIMS[side], folded[at], keeps[at], buffers[at]))
    return jobs


def fold_pair(index, job, send, recv):
    _, _, _, dim, _, keep, buffer = job
    me, x, core = lax.axis_index("seq"), lax.axis_index("x"), lax.axis_index("core")
    bit = ((me // 4) % 2, (me // 2) % 2, me % 2)[dim]
    lead = (slice(None),) * dim
    copy = remote(
        keep.at[lead + (1 - bit,)],
        buffer,
        send.at[index],
        recv.at[index],
        (me ^ (4 >> dim), x, core),
    )
    return copy, lead + (bit,), bit


def fold_start(jobs, temps, send, recv, own, tsem, store):
    x, core = lax.axis_index("x"), lax.axis_index("core")
    greet([seq_flip(1), seq_flip(2)])
    owns, pieces = [], []
    for index, (raw, got, cols, dim, folded, keep, buffer) in enumerate(jobs):
        owns.append(
            pltpu.make_async_copy(raw.at[:, :, :, x, core, :, cols], keep, own.at[index])
        )
        owns[-1].start()
        for row in range(0, keep.shape[3], 32):
            for col in range(0, keep.shape[4], 512):
                pieces.append((index, row, col))
    depth = temps.shape[0]

    def loads(at):
        index, row, col = pieces[at]
        _, got, cols, *_ = jobs[index]
        slot = at % depth
        return [
            pltpu.make_async_copy(
                got.at[n, :, :, :, pl.ds(row, 32), pl.ds(cols.start + col, 512)],
                temps.at[slot, n],
                tsem.at[3 * slot + n],
            )
            for n in range(3)
        ]

    for at in range(depth):
        for copy in loads(at):
            copy.start()
    for at, (index, row, col) in enumerate(pieces):
        keep = jobs[index][5]
        if at == 0 or pieces[at - 1][0] != index:
            owns[index].wait()
        for copy in loads(at):
            copy.wait()
        slot = at % depth
        rows, cols = pl.ds(row, 32), pl.ds(col, 512)

        def body(i, carry):
            a, b, c = i // 4, (i // 2) % 2, i % 2
            total = keep[a, b, c, rows, cols].astype(F32)
            for n in range(3):
                total = total + temps[slot, n, a, b, c].astype(F32)
            keep[a, b, c, rows, cols] = total.astype(BF)
            return carry

        lax.fori_loop(0, 8, body, 0)
        if at + depth < len(pieces):
            for copy in loads(at + depth):
                copy.start()
        if at + 1 == len(pieces) or pieces[at + 1][0] != index:
            fold_pair(index, jobs[index], send, recv)[0].start()


def fold_finish(jobs, send, recv, own, tsem, store):
    stores = []
    for index, job in enumerate(jobs):
        _, _, _, dim, folded, keep, buffer = job
        copy, where, bit = fold_pair(index, job, send, recv)
        copy.wait_recv()

        def body(i, carry):
            place = [i // 2, i % 2]
            at = list(place)
            at.insert(dim, bit)
            total = keep[tuple(at)].astype(F32) + buffer[tuple(place)].astype(F32)
            keep[tuple(at)] = total.astype(BF)
            return carry

        lax.fori_loop(0, 4, body, 0)
        stores.append(pltpu.make_async_copy(keep.at[where], folded, store.at[index]))
        stores[-1].start()
    for index, job in enumerate(jobs):
        fold_pair(index, job, send, recv)[0].wait_send()
        stores[index].wait()


def leave_kernel(
    grad_ref, qkv_w, skip_w, res_ref, mid_ref, mod_ref, in_ref, skip_ref, *refs
):
    raws, arrived = refs[:3], refs[3:6]
    gin_ref, gskip_ref, sums_ref, gqkv_ref, gw_ref = refs[6:11]
    folded, normed, stream = refs[11:17], refs[17], refs[18]
    jobs = fold_jobs(raws, arrived, folded, refs[19:25], refs[25:31])
    temps, sems = refs[31], refs[32:]
    step = pl.program_id(0)

    @pl.when(step == 0)
    def _():
        fold_start(jobs, temps, *sems)

    leave_compute(
        step, grad_ref, qkv_w, skip_w, res_ref, mid_ref, mod_ref, in_ref, skip_ref,
        gin_ref, gskip_ref, sums_ref, gqkv_ref, gw_ref, normed, stream,
    )

    @pl.when(step == pl.num_programs(0) - 1)
    def _():
        fold_finish(jobs, *sems)


def leave_compute(
    step, grad_ref, qkv_w, skip_w, res_ref, mid_ref, mod_ref, in_ref, skip_ref,
    gin_ref, gskip_ref, sums_ref, gqkv_ref, gw_ref, normed, stream,
):
    rows, width = res_ref.shape
    utts = mod_ref.shape[0]
    span = rows // utts

    @pl.when(step == 0)
    def _():
        for utt in range(utts):
            mod = mod_ref[utt]
            shift = jnp.zeros((1, width), F32)
            scale = jnp.zeros((1, width), F32)
            for _, part in row_blocks(span):
                here = slice(utt * span + part.start, utt * span + part.stop)
                hat, inverse = layer_norm(res_ref[here, :])
                normed[here, :] = (hat * (1.0 + mod[1:2]) + mod[0:1]).astype(BF)
                grad = nt(grad_ref[here, :], qkv_w[...])
                shift += jnp.sum(grad, axis=0, keepdims=True)
                scale += jnp.sum(grad * hat, axis=0, keepdims=True)
                total = mid_ref[here, :] + norm_back(grad * (1.0 + mod[1:2]), hat, inverse)
                low = total.astype(BF)
                stream[here, :] = low
                gin_ref[here, :] = nt(low, skip_w[:width, :]).astype(BF)
                gskip_ref[here, :] = nt(low, skip_w[width:, :]).astype(BF)
            sums_ref[utt, 0:1, :] = shift
            sums_ref[utt, 1:2, :] = scale

    chunk = gqkv_ref.shape[1]
    cols = pl.ds(pl.multiple_of(step * chunk, chunk), chunk)
    gqkv_ref[...] = tn(normed[...], grad_ref[:, cols]).astype(BF)
    part = gw_ref.shape[2]
    here = pl.ds(pl.multiple_of(step * part, part), part)
    gw_ref[0] = tn(in_ref[...], stream[:, here]).astype(BF)
    gw_ref[1] = tn(skip_ref[...], stream[:, here]).astype(BF)


def leave_layer(grads, qkv_w, skip_w, res, mid, mods, first, second, raws, arrived, steps=4):
    rows, width = res.shape
    utts = mods.shape[0]
    ins = (grads, qkv_w, skip_w, res, mid, mods, first, second)
    views = [raw.reshape(2, 2, 2, 2, 2, raw.shape[0] // 32, raw.shape[1]) for raw in raws]
    tails = [
        (view.shape[5], cols.size)
        for view in views
        for cols in split_columns(view.shape[-1], (1, 1))
    ]
    anywhere = pl.BlockSpec(memory_space=pl.ANY)
    dma = pltpu.SemaphoreType.DMA
    outs = pl.pallas_call(
        leave_kernel,
        grid=(steps,),
        in_specs=[whole_spec(a.shape) for a in ins] + [anywhere] * 6,
        out_specs=[
            whole_spec((rows, width)),
            whole_spec((rows, width)),
            whole_spec((utts, 8, width)),
            pl.BlockSpec((width, 3 * width // steps), lambda i: (0, i)),
            pl.BlockSpec((2, width, width // steps), lambda i: (0, 0, i)),
        ]
        + [anywhere] * 6,
        out_shape=[
            jax.ShapeDtypeStruct((rows, width), BF),
            jax.ShapeDtypeStruct((rows, width), BF),
            jax.ShapeDtypeStruct((utts, 8, width), F32),
            jax.ShapeDtypeStruct((width, 3 * width), BF),
            jax.ShapeDtypeStruct((2, width, width), BF),
        ]
        + [jax.ShapeDtypeStruct((2, 2) + tail, BF) for tail in tails],
        scratch_shapes=[pltpu.VMEM((rows, width), BF), pltpu.VMEM((rows, width), BF)]
        + [pltpu.VMEM((2, 2, 2) + tail, BF) for tail in tails]
        + [pltpu.VMEM((2, 2) + tail, BF) for tail in tails]
        + [pltpu.VMEM((4, 3, 2, 2, 2, 32, 512), BF)]
        + [dma((6,)), dma((6,)), dma((6,)), dma((12,)), dma((6,))],
        compiler_params=pltpu.CompilerParams(
            vmem_limit_bytes=VMEM_LIMIT, collective_id=4, has_side_effects=True
        ),
        cost_estimate=pl.CostEstimate(
            flops=4 * rows * (skip_w.size + qkv_w.size),
            bytes_accessed=60 * 2**20,
            transcendentals=0,
        ),
        name="leave_layer",
    )(*ins, *views, *arrived)
    return tuple(outs[:4]) + (outs[4].reshape(2 * width, width), outs[5:])


class GradJob:
    def __init__(self, grad, out, cols, dims, order, keep, buffers, loads, sems, base):
        self.grad, self.out, self.cols, self.dims, self.order = grad, out, cols, dims, order
        self.keep, self.buffers, self.loads = keep, buffers, loads
        self.send, self.recv, self.local, self.base = *sems, base
        me, x, core = lax.axis_index("seq"), lax.axis_index("x"), lax.axis_index("core")
        self.bits = (me // 4, (me // 2) % 2, me % 2, x, core)
        self.copies, self.locals, self.round = [], [], 0

    def peer(self, dim):
        me, x, core = lax.axis_index("seq"), lax.axis_index("x"), lax.axis_index("core")
        if dim < 3:
            return (me ^ (4 >> dim), x, core)
        return (me, 1 - x, core) if dim == 3 else (me, x, 1 - core)

    def launch(self, source, target, dim):
        at = self.base + len(self.copies)
        copy = remote(source, target, self.send.at[at], self.recv.at[at], self.peer(dim))
        copy.start()
        self.copies.append(copy)

    def load(self, source, target):
        copy = pltpu.make_async_copy(source, target, self.local.at[self.base + len(self.locals)])
        copy.start()
        self.locals.append(copy)

    def add(self, done, others):
        left = [dim for dim in self.dims if dim not in done]

        def body(i, carry):
            at, place = [self.bits[dim] for dim in self.dims], []
            for n, dim in enumerate(left):
                bit = (i >> (len(left) - 1 - n)) & 1
                at[self.dims.index(dim)] = bit
                place.append(bit)
            total = self.keep[tuple(at)].astype(F32)
            for other in others:
                total = total + (other[tuple(place)] if place else other[...]).astype(F32)
            self.keep[tuple(at)] = total.astype(BF)
            return carry

        lax.fori_loop(0, 2 ** len(left), body, 0)

    def exchange(self, step):
        dim, done = self.order[step], self.order[:step]
        where = tuple(
            1 - self.bits[d] if d == dim else self.bits[d] if d in done else slice(None)
            for d in self.dims
        )
        self.launch(self.keep.at[where], self.buffers[step], dim)

    def advance(self):
        number, self.round = self.round, self.round + 1
        tail, bits = (slice(None), self.cols), self.bits
        steps = len(self.order)
        every = (slice(None),) * len(self.dims)
        if number == 0:
            if self.loads:
                self.load(self.grad.at[every + (bits[4],) + tail], self.keep)
                self.launch(self.grad.at[every + (1 - bits[4],) + tail], self.loads[0], 4)
            else:
                self.load(self.grad, self.keep)
        elif number == 1:
            self.locals[0].wait()
            if self.loads:
                self.copies[0].wait_recv()
                self.add((), self.loads)
            self.exchange(0)
        elif number <= steps + 1:
            self.copies[-1].wait_recv()
            self.add(self.order[: number - 1], [self.buffers[number - 2]])
            if number <= steps:
                self.exchange(number - 1)
            else:
                mine = self.keep.at[tuple(bits[dim] for dim in self.dims)]
                spot = self.out.at[bits[3:5] + tail]
                self.load(mine, spot)
                self.launch(mine, spot, 3)
        elif number == steps + 2:
            self.locals[-1].wait()
            self.copies[-1].wait_recv()
            both = self.out.at[(slice(None), bits[4]) + tail]
            self.launch(both, both, 4)

    def finish(self):
        self.copies[-1].wait_recv()
        for copy in self.copies:
            copy.wait_send()


FULL_ORDERS = ((3, 2, 1, 0), (2, 1, 3, 0), (1, 3, 2, 0))
FOLDED_DIMS = ((0, 1), (0, 2))
FOLDED_ORDERS = ((1, 0), (2, 0))


def reduce_kernel(*refs, halves, folds):
    grads, folded, small = refs[:halves], refs[halves : halves + 2 * folds], refs[halves + 2 * folds]
    refs = refs[halves + 2 * folds + 1 :]
    outs, small_out = refs[: halves + folds], refs[halves + folds]
    rest = list(refs[halves + folds + 1 :])
    small_in, small_low, send, recv, local, ssend, srecv, bsend, brecv, slocal = rest[-10:]
    me, x, core = lax.axis_index("seq"), lax.axis_index("x"), lax.axis_index("core")
    others = [seq_flip(flip) for flip in range(7, 0, -1)]
    mates = [(me, (x + dx) % 2, (core + dc) % 2) for dx, dc in ((0, 1), (1, 0), (1, 1))]
    greet(others + mates)
    jobs = []
    for index, out in enumerate(outs):
        whole = index < halves
        orders = FULL_ORDERS if whole else FOLDED_ORDERS
        for side, cols in enumerate(split_columns(out.shape[-1], (1,) * len(orders))):
            keep = rest.pop(0)
            loads = [rest.pop(0)] if whole else []
            buffers = [rest.pop(0) for _ in orders[side]]
            jobs.append(
                GradJob(
                    grads[index] if whole else folded[2 * (index - halves) + side],
                    out,
                    cols,
                    (0, 1, 2, 3) if whole else FOLDED_DIMS[side],
                    orders[side],
                    keep,
                    buffers,
                    loads,
                    (send, recv, local),
                    7 * len(jobs),
                )
            )
    own = pltpu.make_async_copy(small, small_in.at[me], slocal.at[0])
    own.start()
    smalls = []
    for flip, device in zip(range(7, 0, -1), others):
        smalls.append(remote(small, small_in.at[me], ssend.at[flip], srecv.at[flip], device))
        smalls[-1].start()
    for _ in range(3):
        for job in jobs:
            job.advance()
    own.wait()
    for copy in smalls:
        copy.wait_recv()
    total = small_in[0]
    for index in range(1, 8):
        total = total + small_in[index]
    small_low[...] = total.astype(BF)
    quarter = x * 2 + core
    keep = pltpu.make_async_copy(small_low, small_out.at[quarter], slocal.at[1])
    keep.start()
    lows = []
    for slot, device in enumerate(mates):
        lows.append(remote(small_low, small_out.at[quarter], bsend.at[slot], brecv.at[slot], device))
        lows[-1].start()
    for _ in range(4):
        for job in jobs:
            job.advance()
    for job in jobs:
        job.finish()
    for copy in smalls:
        copy.wait_send()
    keep.wait()
    for copy in lows:
        copy.wait()


def reduce_grads(halves, shapes, folded, small):
    views, outs, buffers, jobs = [], [], [], 0
    for grad in halves:
        rows, width = grad.shape
        views.append(grad.reshape(2, 2, 2, 2, 2, rows // 32, width))
    for index, (rows, width) in enumerate([grad.shape for grad in halves] + list(shapes)):
        span = rows // 32
        outs.append(jax.ShapeDtypeStruct((2, 2, span, width), BF))
        whole = index < len(halves)
        lead, orders = (4, FULL_ORDERS) if whole else (2, FOLDED_ORDERS)
        for cols in split_columns(width, (1,) * len(orders)):
            jobs += 1
            tail = (span, cols.size)
            for left in [lead] * (2 if whole else 1) + list(range(lead - 1, -1, -1)):
                buffers.append(pltpu.VMEM((2,) * left + tail, BF))
    anywhere = pl.BlockSpec(memory_space=pl.ANY)
    dma = pltpu.SemaphoreType.DMA
    outs.append(jax.ShapeDtypeStruct((4,) + small.shape, BF))
    results = pl.pallas_call(
        functools.partial(reduce_kernel, halves=len(halves), folds=len(shapes)),
        in_specs=[anywhere] * (len(halves) + len(folded) + 1),
        out_specs=[anywhere] * len(outs),
        out_shape=outs,
        scratch_shapes=buffers
        + [pltpu.VMEM((8,) + small.shape, F32), pltpu.VMEM(small.shape, BF)]
        + [dma((7 * jobs,))] * 3
        + [dma((8,)), dma((8,)), dma((3,)), dma((3,)), dma((2,))],
        compiler_params=pltpu.CompilerParams(
            vmem_limit_bytes=VMEM_LIMIT, collective_id=3, has_side_effects=True
        ),
        name="reduce_grads",
    )(*views, *folded, small)
    shards = [
        result.reshape(4 * result.shape[2], result.shape[3]).astype(jnp.float32)
        for result in results[:-1]
    ]
    return shards, results[-1].astype(jnp.float32)


def rotary_tables(positions):
    half_dim = HEAD_DIM // 2
    channel = jnp.arange(half_dim, dtype=jnp.float32)
    inverse = jnp.power(10000.0, -2.0 * channel / HEAD_DIM)
    angles = positions.astype(jnp.float32)[:, None] * inverse[None, :]
    angles = jnp.concatenate([angles, angles], axis=1)
    return (jnp.cos(angles), jnp.sin(angles))


def rotate_heads(field, cosine_table, sine_table):
    half_dim = field.shape[-1] // 2
    turned = jnp.concatenate([-field[..., half_dim:], field[..., :half_dim]], axis=-1)
    return field * cosine_table + turned * sine_table


def smooth_gelu(values):
    return jax.nn.gelu(values, approximate=True)


def cross(left, right):
    return lax.dot_general(
        left, right, (((0,), (0,)), ((), ())), preferred_element_type=jnp.float32
    )


def back_product(left, right):
    return lax.dot_general(
        left, right, (((1,), (1,)), ((), ())), preferred_element_type=jnp.float32
    )


def block_terms(query_block, dout_block, lse_block, delta_block, key_block, value_block, key_live):
    scores = jnp.einsum(
        "bqhd,bkhd->bhqk", query_block, key_block, preferred_element_type=jnp.float32
    )
    lse_heads = jnp.transpose(lse_block, (0, 2, 1))[..., None]
    probs = jnp.where(key_live[:, None, None, :], jnp.exp(scores - lse_heads), 0.0)
    grad_probs = jnp.einsum(
        "bqhd,bkhd->bhqk", dout_block, value_block, preferred_element_type=jnp.float32
    )
    delta_heads = jnp.transpose(delta_block, (0, 2, 1))[..., None]
    dscore = (probs * (grad_probs - delta_heads)).astype(jnp.bfloat16)
    return (probs.astype(jnp.bfloat16), dscore)


BATCH = ("x", "core")


def batch_index():
    return lax.axis_index("x") * lax.axis_size("core") + lax.axis_index("core")


def gather_weight(weight):
    parts = lax.axis_size(BATCH)
    if weight.shape[0] % parts:
        return lax.all_gather(weight, "seq", axis=0, tiled=True)
    rows = weight.shape[0] // parts
    mine = lax.dynamic_slice_in_dim(weight, batch_index() * rows, rows, 0)
    return lax.all_gather(mine, ("seq",) + BATCH, axis=0, tiled=True)


def sum_weight(grad):
    rows, width = grad.shape
    low = grad.astype(jnp.bfloat16)
    seq_count, cores = lax.axis_size("seq"), lax.axis_size("core")
    parts = seq_count * lax.axis_size(BATCH)
    if rows % parts or cores != 2:
        shard = lax.psum_scatter(low, "seq", scatter_dimension=0, tiled=True)
        return lax.psum(shard, BATCH).astype(jnp.float32)
    core = lax.axis_index("core")
    held = low.reshape(parts // 2, 2, rows // parts, width)
    send = lax.dynamic_index_in_dim(held, 1 - core, 1, keepdims=False)
    keep = lax.dynamic_index_in_dim(held, core, 1, keepdims=False)
    got = lax.ppermute(send, "core", [(0, 1), (1, 0)])
    half = (keep.astype(jnp.float32) + got.astype(jnp.float32)).astype(jnp.bfloat16)
    half = half.reshape(rows // 2, width)
    shard = lax.psum_scatter(half, ("seq", "x"), scatter_dimension=0, tiled=True)
    return lax.all_gather(shard, BATCH, axis=0, tiled=True).astype(jnp.float32)


def gather_kernel(*refs, count, ahead):
    weights, laters = refs[:count], refs[count : count + ahead]
    seq_small, batch_small = refs[count + ahead : count + ahead + 2]
    outs = refs[count + ahead + 2 :]
    fulls, helds = outs[:count], outs[count : count + ahead]
    seq_out, batch_out, send, recv, asend, arecv, small_send, small_recv, local = outs[count + ahead :]
    me, x, core = lax.axis_index("seq"), lax.axis_index("x"), lax.axis_index("core")
    bits = (me // 4, (me // 2) % 2, me % 2, x, core)

    def peer(dim):
        if dim < 3:
            return (me ^ (4 >> dim), x, core)
        return (me, 1 - x, core) if dim == 3 else (me, x, 1 - core)

    others = [((me + d) % 8, x, core) for d in range(1, 8)]
    mates = [(me, (x + dx) % 2, (core + dc) % 2) for dx, dc in ((0, 1), (1, 0), (1, 1))]
    barrier = pltpu.get_barrier_semaphore()
    for device in others + mates:
        pl.semaphore_signal(barrier, inc=1, device_id=device, device_id_type=pl.DeviceIdType.MESH)
    pl.semaphore_wait(barrier, len(others) + len(mates))

    small = []
    quarter = x * 2 + core
    own_seq = pltpu.make_async_copy(seq_small, seq_out.at[me], local.at[0])
    own_batch = pltpu.make_async_copy(batch_small, batch_out.at[quarter], local.at[1])
    own_seq.start()
    own_batch.start()
    for slot, device in enumerate(others):
        small.append(
            pltpu.make_async_remote_copy(
                seq_small, seq_out.at[me], small_send.at[slot], small_recv.at[slot],
                device_id=device, device_id_type=pl.DeviceIdType.MESH,
            )
        )
    for slot, device in enumerate(mates):
        small.append(
            pltpu.make_async_remote_copy(
                batch_small, batch_out.at[quarter], small_send.at[7 + slot], small_recv.at[7 + slot],
                device_id=device, device_id_type=pl.DeviceIdType.MESH,
            )
        )
    for copy in small:
        copy.start()

    jobs = early_jobs(weights, fulls)
    chain = WeightGather(jobs, send, recv, local.at[pl.ds(2, len(jobs))])
    later = WeightGather(
        ahead_jobs(laters, helds), asend, arecv, local.at[pl.ds(2 + len(jobs), ahead)]
    )
    chain.stage()
    chain.stage()
    later.stage()
    chain.stage()
    later.stage()
    chain.stage()
    chain.stage()
    chain.finish()
    later.finish()
    for copy in small:
        copy.wait()
    own_seq.wait()
    own_batch.wait()


def gather_early(weights, laters, seq_small, batch_small):
    anywhere = pl.BlockSpec(memory_space=pl.ANY)
    jobs, ahead = 3 * len(weights), len(laters)
    total = len(weights) + ahead + 2
    dma = pltpu.SemaphoreType.DMA
    quarter = lambda lead, w: jax.ShapeDtypeStruct((2,) * lead + (w.shape[0] // 4, w.shape[1]), BF)
    outs = pl.pallas_call(
        functools.partial(gather_kernel, count=len(weights), ahead=ahead),
        in_specs=[anywhere] * total,
        out_specs=[anywhere] * total,
        out_shape=[quarter(5, w) for w in weights]
        + [quarter(2, w) for w in laters]
        + [
            jax.ShapeDtypeStruct((8,) + seq_small.shape, F32),
            jax.ShapeDtypeStruct((4,) + batch_small.shape, F32),
        ],
        scratch_shapes=[
            dma((5 * jobs,)),
            dma((5 * jobs,)),
            dma((5 * ahead,)),
            dma((5 * ahead,)),
            dma((10,)),
            dma((10,)),
            dma((2 + jobs + ahead,)),
        ],
        compiler_params=pltpu.CompilerParams(collective_id=0, has_side_effects=True),
        name="gather_early",
    )(*weights, *laters, seq_small, batch_small)
    fulls = [full.reshape(8 * w.shape[0], w.shape[1]) for full, w in zip(outs, weights)]
    return fulls, outs[len(weights) : len(weights) + ahead], outs[-2], outs[-1]


def paired_tables(count):
    half = HEAD_DIM // 2
    inverse = np.power(10000.0, -2.0 * np.arange(half) / HEAD_DIM)
    angles = np.arange(count)[:, None] * inverse[None, :]
    cos, sin = np.cos(angles), np.sin(angles)
    tables = (np.tile(cos, (1, 4)), np.tile(np.concatenate([-sin, sin], axis=1), (1, 2)))
    return tuple(jnp.asarray(table, jnp.float32) for table in tables)


def on_device(
    layer_input,
    skip_input,
    time_embed,
    lengths,
    cond_drop,
    cotangent,
    skip_weight,
    adaln_weight,
    adaln_bias,
    qkv_weight,
    out_weight,
    up_weight,
    down_weight,
):
    utt_count, frame_span, model_width = layer_input.shape
    head_count = model_width // HEAD_DIM
    row_count = utt_count * frame_span
    seq_here = lax.axis_index("seq")
    seq_count = lax.axis_size("seq")
    frame_count = frame_span * seq_count
    by_heads = (
        seq_count == 8
        and head_count == 16
        and utt_count == 2
        and lax.axis_size(BATCH) == 4
        and frame_span == 512
    )
    local_pos = seq_here * frame_span + jnp.arange(frame_span, dtype=jnp.int32)
    local_live = local_pos[None, :] < lengths[:, None]
    valid_mask = local_live.astype(jnp.float32)
    drop = cond_drop.astype(jnp.float32)
    dropped = drop[:, None] * valid_mask
    frames_live = jnp.minimum(lengths, frame_count).astype(jnp.float32)
    counts = jnp.stack([jnp.sum((1.0 - drop) * frames_live), jnp.sum(drop * frames_live)])
    silu_time = jax.nn.silu(time_embed.astype(jnp.float32)).astype(jnp.bfloat16)
    row_span = adaln_weight.shape[0]
    silu_mine = lax.dynamic_slice_in_dim(silu_time, seq_here * row_span, row_span, 1)
    mod_part = jnp.dot(silu_mine, adaln_weight, preferred_element_type=jnp.float32)
    bias_span = adaln_bias.shape[0]
    bias_here = lax.dynamic_update_slice_in_dim(
        jnp.zeros((mod_part.shape[1],), jnp.float32),
        adaln_bias.astype(jnp.float32),
        seq_here * bias_span,
        0,
    )
    mod_part = mod_part + bias_here
    if by_heads:
        small = jnp.concatenate(
            [
                silu_time.astype(jnp.float32),
                jnp.pad(counts[None, :], ((0, 5), (0, model_width - 2))),
            ],
            axis=0,
        )
        (skip_full, qkv_full), late_held, mod_every, small_every = gather_early(
            (skip_weight, qkv_weight),
            (out_weight, up_weight, down_weight),
            mod_part.reshape(-1, model_width),
            small,
        )
        modulation = jnp.sum(mod_every, axis=0)
        totals = jnp.sum(small_every[:, utt_count, :2], axis=0)
        silu_every = small_every[:, :utt_count].reshape(-1, model_width)
    else:
        modulation = lax.psum(mod_part, "seq")
        totals = lax.psum(counts, BATCH)
        skip_full = gather_weight(skip_weight)
        qkv_full = gather_weight(qkv_weight)
        silu_every = lax.all_gather(silu_time, BATCH, axis=0, tiled=True).astype(jnp.float32)
    modulation = modulation.reshape(utt_count, 6, model_width)
    kept_total = jnp.maximum(totals[0], 1.0)
    drop_total = jnp.maximum(totals[1], 1.0)
    every_count = kept_total + drop_total
    loss_weight = (valid_mask - dropped) * (every_count / (2.0 * kept_total)) + dropped * (
        every_count / (2.0 * drop_total)
    )
    first_rows = layer_input.reshape(row_count, model_width)
    second_rows = skip_input.reshape(row_count, model_width)
    if by_heads:
        cos_all, sin_all = paired_tables(frame_count)
        cos_here = lax.dynamic_slice_in_dim(cos_all, seq_here * frame_span, frame_span, 0)
        sin_here = lax.dynamic_slice_in_dim(sin_all, seq_here * frame_span, frame_span, 0)
        residual_rows, proj = enter_layer(
            first_rows, second_rows, skip_full, qkv_full, modulation, cos_here, sin_here
        )
        (qkv_all, out_all, lse_all, attended_low), (out_full, up_full, down_full) = attend_forward(
            lengths, proj, *late_held, frame_span
        )
    else:
        joined = jnp.concatenate([layer_input, skip_input], axis=-1).reshape(row_count, 2 * model_width)
        residual_in = jnp.dot(joined, skip_full, preferred_element_type=jnp.float32).reshape(
            utt_count, frame_span, model_width
        )
        shift_attn = modulation[:, 0][:, None, :]
        scale_attn = modulation[:, 1][:, None, :]
        hat_attn, inv_attn = layer_norm(residual_in)
        normed_attn = (
            (hat_attn * (1.0 + scale_attn) + shift_attn)
            .astype(jnp.bfloat16)
            .reshape(row_count, model_width)
        )
        residual_rows = residual_in.reshape(row_count, model_width)
        out_full, up_full, down_full = [
            gather_weight(weight) for weight in (out_weight, up_weight, down_weight)
        ]
        projected = jnp.dot(normed_attn, qkv_full, preferred_element_type=jnp.float32).reshape(
            utt_count, frame_span, 3, head_count, HEAD_DIM
        )
        cosine_table, sine_table = rotary_tables(local_pos)
        cosine_table = cosine_table[None, :, None, :]
        sine_table = sine_table[None, :, None, :]
        queries = (rotate_heads(projected[:, :, 0], cosine_table, sine_table) * 0.125).astype(
            jnp.bfloat16
        )
        keys_rot = rotate_heads(projected[:, :, 1], cosine_table, sine_table).astype(jnp.bfloat16)
        values = projected[:, :, 2].astype(jnp.bfloat16)
        start_top = jnp.full((utt_count, head_count, frame_span), MASKED, jnp.float32)
        top_score = start_top
        key_piece = lax.all_gather(keys_rot, "seq", axis=1, tiled=True)
        value_piece = lax.all_gather(values, "seq", axis=1, tiled=True)
        piece_len = key_piece.shape[1]
        piece_live = jnp.arange(piece_len, dtype=jnp.int32)[None, :] < lengths[:, None]
        scores = jnp.einsum("bqhd,bkhd->bhqk", queries, key_piece, preferred_element_type=jnp.float32)
        scores = jnp.where(piece_live[:, None, None, :], scores, MASKED)
        new_top = jnp.maximum(top_score, jnp.max(scores, axis=-1))
        expo = jnp.where(piece_live[:, None, None, :], jnp.exp(scores - new_top[..., None]), 0.0)
        denom = jnp.sum(expo, axis=-1)
        partial_out = jnp.einsum(
            "bhqk,bkhd->bqhd",
            expo.astype(jnp.bfloat16),
            value_piece,
            preferred_element_type=jnp.float32,
        )
        accum = partial_out
        accum, top_score, denom = (accum, new_top, denom)
        attended_full = accum / jnp.transpose(denom, (0, 2, 1))[..., None]
        lse_rows = jnp.transpose(top_score + jnp.log(denom), (0, 2, 1))
        attended_low = attended_full.astype(jnp.bfloat16).reshape(row_count, model_width)
    cot_rows = cotangent.reshape(row_count, model_width)
    weight_rows = loss_weight.reshape(row_count, 1)
    branch_attn, hidden_act, hidden_slope, grad_branch_ffn, layer_output, grad_gate_ffn = ffn_forward(
        attended_low,
        out_full,
        residual_rows,
        modulation,
        cot_rows,
        weight_rows,
        up_full,
        down_full,
    )
    layer_output = layer_output.reshape(utt_count, frame_span, model_width)
    grad_up, grad_down, grad_mid, grad_attended_flat, grad_out, ffn_sums = ffn_backward(
        attended_low,
        out_full,
        residual_rows,
        branch_attn,
        modulation,
        cot_rows,
        weight_rows,
        grad_branch_ffn,
        hidden_act,
        hidden_slope,
        up_full,
        down_full,
    )
    grad_shift_ffn, grad_scale_ffn, grad_gate_attn = ffn_sums[:, 0], ffn_sums[:, 1], ffn_sums[:, 2]
    if by_heads:
        grad_projected, *arrived = attend_backward(
            lengths,
            grad_attended_flat,
            qkv_all,
            out_all,
            lse_all,
            cos_all,
            sin_all,
            (grad_down, grad_up, grad_out),
            frame_span,
        )
    else:
        grad_attended = grad_attended_flat.reshape(
            utt_count, frame_span, head_count, HEAD_DIM
        )
        delta_rows = jnp.sum(grad_attended.astype(jnp.float32) * attended_full, axis=-1)
        lse_all, delta_all = (
            lax.all_gather(lse_rows, "seq", axis=1, tiled=True),
            lax.all_gather(delta_rows, "seq", axis=1, tiled=True),
        )
        key_piece = lax.all_gather(keys_rot, "seq", axis=1, tiled=True)
        value_piece = lax.all_gather(values, "seq", axis=1, tiled=True)
        piece_len = key_piece.shape[1]
        piece_live = jnp.arange(piece_len, dtype=jnp.int32)[None, :] < lengths[:, None]
        probs_low, dscore = block_terms(
            queries, grad_attended, lse_rows, delta_rows, key_piece, value_piece, piece_live
        )
        grad_queries = jnp.einsum(
            "bhqk,bkhd->bqhd", dscore, key_piece, preferred_element_type=jnp.float32
        )
        query_piece = lax.all_gather(queries, "seq", axis=1, tiled=True)
        dout_piece = lax.all_gather(grad_attended, "seq", axis=1, tiled=True)
        probs_low, dscore = block_terms(
            query_piece, dout_piece, lse_all, delta_all, keys_rot, values, local_live
        )
        grad_k = jnp.einsum("bhqk,bqhd->bkhd", dscore, query_piece, preferred_element_type=jnp.float32)
        grad_v = jnp.einsum(
            "bhqk,bqhd->bkhd", probs_low, dout_piece, preferred_element_type=jnp.float32
        )
        grad_q_pre = rotate_heads(grad_queries * 0.125, cosine_table, -sine_table)
        grad_k_pre = rotate_heads(grad_k, cosine_table, -sine_table)
        grad_projected = (
            jnp.stack([grad_q_pre, grad_k_pre, grad_v], axis=2)
            .reshape(row_count, 3 * model_width)
            .astype(jnp.bfloat16)
        )
    if by_heads:
        grad_input, grad_skip, attn_sums, grad_qkv, grad_skip_w, folded = leave_layer(
            grad_projected,
            qkv_full,
            skip_full,
            residual_rows,
            grad_mid,
            modulation,
            first_rows,
            second_rows,
            (grad_down, grad_up, grad_out),
            arrived,
        )
        grad_input = grad_input.reshape(layer_input.shape)
        grad_skip = grad_skip.reshape(skip_input.shape)
        grad_shift_attn, grad_scale_attn = attn_sums[:, 0], attn_sums[:, 1]
    else:
        grad_mid = grad_mid.reshape(utt_count, frame_span, model_width)
        grad_qkv = cross(normed_attn, grad_projected)
        grad_normed_attn = back_product(grad_projected, qkv_full).reshape(
            utt_count, frame_span, model_width
        )
        grad_shift_attn = jnp.sum(grad_normed_attn, axis=1)
        grad_scale_attn = jnp.sum(grad_normed_attn * hat_attn, axis=1)
        grad_stream = grad_mid + norm_back(grad_normed_attn * (1.0 + scale_attn), hat_attn, inv_attn)
        grad_stream_low = grad_stream.astype(jnp.bfloat16).reshape(row_count, model_width)
        grad_skip_w = cross(joined, grad_stream_low)
        grad_joined = back_product(grad_stream_low, skip_full)
        grad_input = (
            grad_joined[:, :model_width]
            .reshape(utt_count, frame_span, model_width)
            .astype(jnp.bfloat16)
        )
        grad_skip = (
            grad_joined[:, model_width:]
            .reshape(utt_count, frame_span, model_width)
            .astype(jnp.bfloat16)
        )
    grad_modulation = jnp.stack(
        [
            grad_shift_attn,
            grad_scale_attn,
            grad_gate_attn,
            grad_shift_ffn,
            grad_scale_ffn,
            grad_gate_ffn,
        ],
        axis=1,
    ).reshape(utt_count, 6 * model_width)
    weight_grads = (grad_skip_w, grad_qkv, grad_out, grad_up, grad_down)
    if by_heads:
        shards, mod_every = reduce_grads(
            (grad_qkv, grad_skip_w),
            [grad.shape for grad in (grad_down, grad_up, grad_out)],
            folded,
            grad_modulation.reshape(-1, model_width),
        )
        summed = [shards[i] for i in (1, 0, 4, 3, 2)]
        mod_every = mod_every.reshape(-1, 6 * model_width)
    else:
        mod_total = lax.psum(grad_modulation, "seq")
        mod_every = lax.all_gather(
            mod_total.astype(jnp.bfloat16), BATCH, axis=0, tiled=True
        ).astype(jnp.float32)
        summed = [sum_weight(grad) for grad in weight_grads]
    silu_rows = lax.dynamic_slice_in_dim(silu_every, seq_here * row_span, row_span, 1)
    adaln_rows = jnp.dot(silu_rows.T, mod_every, precision=lax.Precision.HIGHEST)
    bias_rows = lax.dynamic_slice_in_dim(
        jnp.sum(mod_every, axis=0), seq_here * bias_span, bias_span, 0
    )
    results = (summed[0], adaln_rows, bias_rows, summed[1], summed[2], summed[3], summed[4])
    return (
        layer_output,
        grad_input,
        grad_skip,
        results[0],
        results[1],
        results[2],
        results[3],
        results[4],
        results[5],
        results[6],
    )


def solution(mesh):
    count, batch = mesh.shape["seq"], mesh.shape["batch"]
    cores = 2 if batch % 2 == 0 else 1
    split = Mesh(mesh.devices.reshape(count, batch // cores, cores), ("seq",) + BATCH)
    placed = (
        P(BATCH, "seq", None),
        P(BATCH, "seq", None),
        P(BATCH, None),
        P(BATCH),
        P(BATCH),
        P(BATCH, "seq", None),
        P("seq", None),
        P("seq", None),
        P("seq"),
        P("seq", None),
        P("seq", None),
        P("seq", None),
        P("seq", None),
    )
    return jax.shard_map(
        on_device,
        mesh=split,
        in_specs=placed,
        out_specs=(
            P(BATCH, "seq", None),
            P(BATCH, "seq", None),
            P(BATCH, "seq", None),
            P("seq", None),
            P("seq", None),
            P("seq"),
            P("seq", None),
            P("seq", None),
            P("seq", None),
            P("seq", None),
        ),
        check_vma=False,
    )
```

```python
import functools
import jax
import jax.numpy as jnp
import numpy as np
from jax import lax
from jax.sharding import Mesh, PartitionSpec as P
from jax.experimental import pallas as pl
from jax.experimental.pallas import tpu as pltpu
HEAD_DIM = 64
EPS = 1e-06
LOG2E = 1.4426950408889634
LN2 = 0.6931471805599453
MASKED = -1e30
BF = jnp.bfloat16
F32 = jnp.float32
VMEM_LIMIT = 60 * 2**20


def nt(left, right):
    return lax.dot_general(left, right, (((1,), (1,)), ((), ())), preferred_element_type=F32)


def nn(left, right):
    return lax.dot_general(left, right, (((1,), (0,)), ((), ())), preferred_element_type=F32)


def head_sums(product, lane):
    first = jnp.sum(jnp.where(lane < 64, product, 0.0), axis=1, keepdims=True)
    second = jnp.sum(jnp.where(lane >= 64, product, 0.0), axis=1, keepdims=True)
    return (first, second)


def lanes_of(rows):
    return lax.broadcasted_iota(jnp.int32, (rows, 128), 1)


def attention_cost(frames, products):
    return pl.CostEstimate(
        flops=2 * products * 2 * frames * frames * 128,
        bytes_accessed=frames * 128 * 2 * 8,
        transcendentals=2 * frames * frames,
    )


def turn_back(grad, cos, sin):
    lane = lanes_of(grad.shape[0])
    turned = jnp.where((lane & 63) < 32, pltpu.roll(grad, 96, 1), pltpu.roll(grad, 32, 1))
    return grad * cos - turned * sin


def three(column, lane, at):
    high = column.astype(BF).astype(F32)
    rest = column - high
    mid = rest.astype(BF).astype(F32)
    low = rest - mid
    return jnp.where(lane == at, -high, jnp.where(lane == at + 1, -mid, jnp.where(lane == at + 2, -low, 0.0)))


MESH_IDS = pl.DeviceIdType.MESH


def seq_flip(flip):
    return (lax.axis_index("seq") ^ flip, lax.axis_index("x"), lax.axis_index("core"))


def greet(devices):
    barrier = pltpu.get_barrier_semaphore()
    for device in devices:
        pl.semaphore_signal(barrier, inc=1, device_id=device, device_id_type=MESH_IDS)
    pl.semaphore_wait(barrier, len(devices))


def far_first(at, count):
    near = lax.axis_index("seq") // 4
    return (at + (count // 2) * (1 - near)) % count


def remote(source, target, send, recv, device):
    return pltpu.make_async_remote_copy(
        source, target, send, recv, device_id=device, device_id_type=MESH_IDS
    )


class WeightGather:
    def __init__(self, jobs, send, recv, local):
        self.jobs, self.send, self.recv, self.local = jobs, send, recv, local
        me, x, core = lax.axis_index("seq"), lax.axis_index("x"), lax.axis_index("core")
        self.bits = (me // 4, (me // 2) % 2, me % 2, x, core)
        self.copies = [[] for _ in jobs]
        self.owns = []

    def peer(self, dim):
        me, x, core = lax.axis_index("seq"), lax.axis_index("x"), lax.axis_index("core")
        if dim < 3:
            return (me ^ (4 >> dim), x, core)
        return (me, 1 - x, core) if dim == 3 else (me, x, 1 - core)

    def stage(self):
        for index, (full, cols, source, ready, order) in enumerate(self.jobs):
            at = len(self.copies[index])
            where = tuple(
                slice(None) if d in ready + order[:at] else self.bits[d]
                for d in range(len(full.shape) - 2)
            ) + (slice(None), cols)
            if at == 0:
                own = pltpu.make_async_copy(source, full.at[where], self.local.at[index])
                own.start()
                self.owns.append(own)
            else:
                if at == 1:
                    self.owns[index].wait()
                self.copies[index][at - 1].wait_recv()
            copy = remote(
                source if at == 0 else full.at[where],
                full.at[where],
                self.send.at[index * 5 + at],
                self.recv.at[index * 5 + at],
                self.peer(order[at]),
            )
            copy.start()
            self.copies[index].append(copy)

    def finish(self):
        for chain in self.copies:
            chain[-1].wait_recv()
        for chain in self.copies:
            for copy in chain:
                copy.wait_send()


def split_columns(width, shares):
    total, start, out = sum(shares), 0, []
    for n in range(len(shares)):
        stop = width * sum(shares[: n + 1]) // total // 128 * 128
        out.append(pl.ds(start, stop - start))
        start = stop
    return out


def quarter_of(weight, cols):
    quarter = lax.axis_index("x") * 2 + lax.axis_index("core")
    span = weight.shape[0] // 4
    return weight.at[pl.ds(quarter * span, span), cols]


def early_jobs(weights, fulls):
    orders = ((0, 1, 2, 3, 4), (0, 2, 3, 1, 4), (0, 3, 1, 2, 4))
    return [
        (full, cols, quarter_of(weight, cols), (), order)
        for weight, full in zip(weights, fulls)
        for cols, order in zip(split_columns(weight.shape[1], (1, 1, 1)), orders)
    ]


def ahead_jobs(weights, helds):
    every = [(weight, held, pl.ds(0, weight.shape[1])) for weight, held in zip(weights, helds)]
    return [(held, cols, quarter_of(weight, cols), (), (0, 1)) for weight, held, cols in every]


def late_jobs(helds, fulls):
    return [
        (full, cols, held.at[:, :, :, cols], (0, 1), order)
        for held, full in zip(helds, fulls)
        for cols, order in zip(split_columns(held.shape[3], (3, 1)), ((2, 3, 4), (3, 2, 4)))
    ]


def attend_forward_kernel(
    len_ref, proj, out_w, up_w, down_w,
    qkv_all, o_all, lse_ref, att, out_full, up_full, down_full,
    qkv, outs, ka, kb, vta, vtb,
    wsend, wrecv, wlocal, qsend, qrecv, qlocal, osend, orecv, olocal, slocal,
    *, span, bq, bk,
):
    me, x, core = lax.axis_index("seq"), lax.axis_index("x"), lax.axis_index("core")
    frames = qkv.shape[2]
    mine = pl.ds(pl.multiple_of(me * span, span), span)
    my_cols = pl.ds(pl.multiple_of(me * 128, 128), 128)
    flips = (7, 6, 5, 4, 3, 2, 1)
    greet([seq_flip(flip) for flip in flips] + [(me, 1 - x, core), (me, x, 1 - core)])
    weights = WeightGather(
        late_jobs((out_w, up_w, down_w), (out_full, up_full, down_full)), wsend, wrecv, wlocal
    )

    def send_heads(utt):
        rows = pl.ds(utt * span, span)
        own = pltpu.make_async_copy(
            proj.at[:, rows, my_cols], qkv.at[utt, :, mine, :], qlocal.at[utt]
        )
        own.start()
        copies = []
        for flip in flips:
            there = me ^ flip
            cols = pl.ds(pl.multiple_of(there * 128, 128), 128)
            copy = remote(
                proj.at[:, rows, cols],
                qkv.at[utt, :, mine, :],
                qsend.at[utt * 8 + flip],
                qrecv.at[utt * 8 + flip],
                seq_flip(flip),
            )
            copy.start()
            copies.append(copy)
        return own, copies

    def arrive(sent):
        own, copies = sent
        own.wait()
        for copy in copies:
            copy.wait_recv()

    def send_out(utt, there):
        rows = pl.ds(pl.multiple_of(there * span, span), span)
        target = att.at[pl.ds(utt * span, span), my_cols]

        @pl.when(there != me)
        def _():
            remote(
                outs.at[utt, rows, :],
                target,
                osend.at[utt * 8 + (there ^ me)],
                orecv.at[utt * 8 + (there ^ me)],
                (there, x, core),
            ).start()

        @pl.when(there == me)
        def _():
            pltpu.make_async_copy(outs.at[utt, rows, :], target, olocal.at[utt]).start()

    def attend(utt, between):
        length = len_ref[utt]
        save = pltpu.make_async_copy(qkv.at[utt], qkv_all.at[utt], slocal.at[utt])
        save.start()

        def build(j, carry):
            rows = pl.ds(pl.multiple_of(j * bk, bk), bk)
            lane = lanes_of(bk)
            pos = j * bk + lax.broadcasted_iota(jnp.int32, (bk, 128), 0)
            bias = jnp.where(pos < length, 0.0, MASKED)
            keys = qkv[utt, 1, rows, :].astype(F32)
            ka[rows, :] = jnp.where(lane < 64, keys, jnp.where(lane == 64, bias, 0.0)).astype(BF)
            kb[rows, :] = jnp.where(lane >= 64, keys, jnp.where(lane == 0, bias, 0.0)).astype(BF)
            vals = qkv[utt, 2, rows, :].astype(F32)
            vta[:, rows] = jnp.where(lane < 64, vals, 1.0).T.astype(BF)
            vtb[:, rows] = jnp.where(lane >= 64, vals, 1.0).T.astype(BF)
            return carry

        lax.fori_loop(0, frames // bk, build, 0)

        def block(i_at, carry):
            i = far_first(i_at, frames // bq)
            here = pl.ds(pl.multiple_of(i * bq, bq), bq)
            lane = lanes_of(bq)
            queries = qkv[utt, 0, here, :].astype(F32)
            qa = jnp.where(lane < 64, queries, jnp.where(lane == 64, 1.0, 0.0)).astype(BF)
            qb = jnp.where(lane >= 64, queries, jnp.where(lane == 0, 1.0, 0.0)).astype(BF)

            def body(j, inner):
                rows = pl.ds(pl.multiple_of(j * bk, bk), bk)
                result = []
                scores = [nt(ka[rows, :], qa), nt(kb[rows, :], qb)]
                for score, vt, (top, acc) in zip(scores, (vta, vtb), inner):
                    new = jnp.maximum(top, jnp.max(score, axis=0, keepdims=True))
                    probs = jnp.exp2(score - new).astype(BF)
                    acc = acc * jnp.exp2(top - new) + nn(vt[:, rows], probs)
                    result.append((new, acc))
                return tuple(result)

            start = (jnp.full((1, bq), MASKED, F32), jnp.zeros((128, bq), F32))
            (top_a, acc_a), (top_b, acc_b) = lax.fori_loop(0, frames // bk, body, (start, start))
            sum_a, sum_b = acc_a[64:65], acc_b[0:1]
            both = jnp.concatenate([acc_a[:64] / sum_a, acc_b[64:] / sum_b], axis=0)
            outs[utt, here, :] = both.T.astype(BF)
            lse_ref[utt, :, here] = jnp.concatenate(
                [top_a + jnp.log2(sum_a), top_b + jnp.log2(sum_b), jnp.zeros((6, bq), F32)],
                axis=0,
            )
            if utt == 1:
                for part in range(bq // span):
                    send_out(utt, i * (bq // span) + part)
            return carry

        half = frames // bq // 2
        lax.fori_loop(0, half, block, 0)
        between()
        lax.fori_loop(half, 2 * half, block, 0)
        keep = pltpu.make_async_copy(outs.at[utt], o_all.at[utt], slocal.at[2 + utt])
        keep.start()
        return [save, keep]

    first = send_heads(0)
    weights.stage()
    arrive(first)
    second = send_heads(1)
    weights.stage()
    saves = attend(0, lambda: None)
    arrive(second)

    def send_first(i, carry):
        send_out(0, i)
        return carry

    lax.fori_loop(0, 8, send_first, 0)
    saves += attend(1, weights.stage)
    for sent in (first, second):
        for copy in sent[1]:
            copy.wait_send()
    weights.finish()
    for save in saves:
        save.wait()
    for utt in range(2):
        target = att.at[pl.ds(utt * span, span), my_cols]
        pltpu.make_async_copy(outs.at[utt, mine, :], target, olocal.at[utt]).wait()
        for flip in flips:
            copy = remote(
                outs.at[utt, mine, :],
                target,
                osend.at[utt * 8 + flip],
                orecv.at[utt * 8 + flip],
                seq_flip(flip),
            )
            copy.wait_send()
            copy.wait_recv()


def attend_forward(lengths, proj, out_w, up_w, down_w, span, bq=1024, bk=512):
    rows, width = proj.shape[1:]
    frames = 8 * span
    anywhere = pl.BlockSpec(memory_space=pl.ANY)
    vmem = pl.BlockSpec(memory_space=pltpu.VMEM)
    full = lambda w: jax.ShapeDtypeStruct((2, 2, 2, 2, 2) + w.shape[2:], BF)
    dma = pltpu.SemaphoreType.DMA
    outs = pl.pallas_call(
        functools.partial(attend_forward_kernel, span=span, bq=bq, bk=bk),
        in_specs=[pl.BlockSpec(memory_space=pltpu.SMEM)] + [anywhere] * 4,
        out_specs=[anywhere, anywhere, vmem] + [anywhere] * 4,
        out_shape=[
            jax.ShapeDtypeStruct((2, 3, frames, 128), BF),
            jax.ShapeDtypeStruct((2, frames, 128), BF),
            jax.ShapeDtypeStruct((2, 8, frames), F32),
            jax.ShapeDtypeStruct((rows, width), BF),
            full(out_w),
            full(up_w),
            full(down_w),
        ],
        scratch_shapes=[
            pltpu.VMEM((2, 3, frames, 128), BF),
            pltpu.VMEM((2, frames, 128), BF),
            pltpu.VMEM((frames, 128), BF),
            pltpu.VMEM((frames, 128), BF),
            pltpu.VMEM((128, frames), BF),
            pltpu.VMEM((128, frames), BF),
            dma((30,)),
            dma((30,)),
            dma((6,)),
            dma((16,)),
            dma((16,)),
            dma((2,)),
            dma((16,)),
            dma((16,)),
            dma((2,)),
            dma((4,)),
        ],
        compiler_params=pltpu.CompilerParams(
            vmem_limit_bytes=VMEM_LIMIT, collective_id=1, has_side_effects=True
        ),
        cost_estimate=attention_cost(frames, 4),
        name="attend_forward",
    )(lengths, proj, out_w, up_w, down_w)
    fulls = [
        outs[4 + i].reshape(32 * w.shape[2], w.shape[3]) for i, w in enumerate((out_w, up_w, down_w))
    ]
    return outs[:4], fulls


def attend_backward_kernel(
    len_ref, dout, qkv_all, o_all, lse_ref, cos_ref, sin_ref, raw_a, raw_b, raw_c,
    grads, got_a, got_b, got_c,
    qkv, outs, douts, qa, qb, da, db, qt, dt, dqa, dqb,
    dsend, drecv, dlocal, gsend, grecv, glocal, load, rsend, rrecv,
    *, span, block,
):
    me, x, core = lax.axis_index("seq"), lax.axis_index("x"), lax.axis_index("core")
    frames = qkv.shape[2]
    width = grads.shape[1] // 3
    count = frames // block
    mine = pl.ds(pl.multiple_of(me * span, span), span)
    flips = (7, 6, 5, 4, 3, 2, 1)
    mates = [(me, x ^ dx, core ^ dc) for dx, dc in ((0, 1), (1, 0), (1, 1))]
    greet([seq_flip(flip) for flip in flips] + mates)
    loads = []
    for utt in range(2):
        loads.append(
            [
                pltpu.make_async_copy(qkv_all.at[utt], qkv.at[utt], load.at[utt]),
                pltpu.make_async_copy(o_all.at[utt], outs.at[utt], load.at[2 + utt]),
            ]
        )
        for copy in loads[-1]:
            copy.start()

    def send_heads(utt):
        rows = pl.ds(utt * span, span)
        my_cols = pl.ds(pl.multiple_of(me * 128, 128), 128)
        own = pltpu.make_async_copy(dout.at[rows, my_cols], douts.at[utt, mine, :], dlocal.at[utt])
        own.start()
        copies = []
        for flip in flips:
            cols = pl.ds(pl.multiple_of((me ^ flip) * 128, 128), 128)
            copy = remote(
                dout.at[rows, cols],
                douts.at[utt, mine, :],
                dsend.at[utt * 8 + flip],
                drecv.at[utt * 8 + flip],
                seq_flip(flip),
            )
            copy.start()
            copies.append(copy)
        return own, copies

    def arrive(sent):
        own, copies = sent
        own.wait()
        for copy in copies:
            copy.wait_recv()

    def slot(utt, part, flip):
        return (utt * 3 + part) * 8 + flip

    def target(utt, part):
        cols = pl.ds(pl.multiple_of(part * width + me * 128, 128), 128)
        return grads.at[pl.ds(utt * span, span), cols]

    def send_grads(utt, part, there):
        rows = pl.ds(pl.multiple_of(there * span, span), span)

        @pl.when(there != me)
        def _():
            at = slot(utt, part, there ^ me)
            remote(
                qkv.at[utt, part, rows, :],
                target(utt, part),
                gsend.at[at],
                grecv.at[at],
                (there, x, core),
            ).start()

        @pl.when(there == me)
        def _():
            pltpu.make_async_copy(
                qkv.at[utt, part, rows, :], target(utt, part), glocal.at[utt * 3 + part]
            ).start()

    def differentiate(utt):
        length = len_ref[utt]

        def build(j, carry):
            rows = pl.ds(pl.multiple_of(j * block, block), block)
            lane = lanes_of(block)
            queries = qkv[utt, 0, rows, :].astype(F32)
            grad = douts[utt, rows, :].astype(F32)
            delta_a, delta_b = head_sums(grad * outs[utt, rows, :].astype(F32), lane)
            lse = lse_ref[utt, :, rows].T
            one_a, one_b = lse[:, 0:1], lse[:, 1:2]
            qa[rows, :] = jnp.where(
                lane < 64, queries, jnp.where(lane == 67, 1.0, three(one_a, lane, 64))
            ).astype(BF)
            qb[rows, :] = jnp.where(
                lane >= 64, queries, jnp.where(lane == 3, 1.0, three(one_b, lane, 0))
            ).astype(BF)
            da[rows, :] = jnp.where(lane < 64, grad, three(delta_a, lane, 64)).astype(BF)
            db[rows, :] = jnp.where(lane >= 64, grad, three(delta_b, lane, 0)).astype(BF)
            qt[:, rows] = queries.T.astype(BF)
            dt[:, rows] = grad.T.astype(BF)
            dqa[rows, :] = jnp.zeros((block, 128), F32)
            dqb[rows, :] = jnp.zeros((block, 128), F32)
            return carry

        lax.fori_loop(0, count, build, 0)

        def keys_block(step_at, carry):
            i = far_first(step_at, count)
            here = pl.ds(pl.multiple_of(i * block, block), block)
            lane = lanes_of(block)
            pos = i * block + lax.broadcasted_iota(jnp.int32, (block, 128), 0)
            bias = jnp.where(pos < length, 0.0, MASKED)
            keys = qkv[utt, 1, here, :].astype(F32)
            vals = qkv[utt, 2, here, :].astype(F32)
            ones_a = jnp.where(lane < 67, 1.0, 0.0)
            ones_b = jnp.where(lane < 3, 1.0, 0.0)
            ka = jnp.where(lane < 64, keys, jnp.where(lane == 67, bias, ones_a)).astype(BF)
            kb = jnp.where(lane >= 64, keys, jnp.where(lane == 3, bias, ones_b)).astype(BF)
            va = jnp.where(lane < 64, vals, ones_a).astype(BF)
            vb = jnp.where(lane >= 64, vals, ones_b).astype(BF)

            def body(j_at, inner):
                j = far_first(j_at, count)
                rows = pl.ds(pl.multiple_of(j * block, block), block)
                result = []
                for head, (qh, dh, kh, vh, dq) in enumerate(
                    ((qa, da, ka, va, dqa), (qb, db, kb, vb, dqb))
                ):
                    part = slice(head * 64, head * 64 + 64)
                    probs = jnp.exp2(nt(qh[rows, :], kh))
                    grad = (probs * nt(dh[rows, :], vh)).astype(BF)
                    dv = inner[2 * head + 1] + nn(dt[:, rows], probs.astype(BF))[part]
                    dk = inner[2 * head] + nn(qt[:, rows], grad)[part]
                    dq[rows, :] += nn(grad, kh)
                    result += [dk, dv]

                @pl.when(step_at == count - 1)
                def _():
                    low = jnp.where(lanes_of(block) < 64, dqa[rows, :], dqb[rows, :]) * 0.125
                    low = turn_back(low, cos_ref[rows, :], sin_ref[rows, :])
                    qkv[utt, 0, rows, :] = low.astype(BF)
                    for step in range(block // span):
                        send_grads(utt, 0, j * (block // span) + step)

                return tuple(result)

            zero = jnp.zeros((64, block), F32)
            dk_a, dv_a, dk_b, dv_b = lax.fori_loop(0, count, body, (zero,) * 4)
            dk = jnp.concatenate([dk_a, dk_b], axis=0).T * LN2
            dv = jnp.concatenate([dv_a, dv_b], axis=0).T
            qkv[utt, 1, here, :] = turn_back(dk, cos_ref[here, :], sin_ref[here, :]).astype(BF)
            qkv[utt, 2, here, :] = dv.astype(BF)
            for step in range(block // span):
                there = i * (block // span) + step
                send_grads(utt, 1, there)
                send_grads(utt, 2, there)
            return carry

        lax.fori_loop(0, count, keys_block, 0)

    first = send_heads(0)
    raws = []
    for index, (raw, got) in enumerate(((raw_a, got_a), (raw_b, got_b), (raw_c, got_c))):
        for slot_at, device in enumerate(mates):
            at = index * 3 + slot_at
            copy = remote(
                raw.at[:, :, :, device[1], device[2]],
                got.at[slot_at],
                rsend.at[at],
                rrecv.at[at],
                device,
            )
            copy.start()
            raws.append(copy)
    for copy in loads[0]:
        copy.wait()
    arrive(first)
    second = send_heads(1)
    differentiate(0)
    for copy in loads[1]:
        copy.wait()
    arrive(second)
    differentiate(1)
    for sent in (first, second):
        for copy in sent[1]:
            copy.wait_send()
    for copy in raws:
        copy.wait()
    for utt in range(2):
        for part in range(3):
            own = qkv.at[utt, part, mine, :]
            pltpu.make_async_copy(own, target(utt, part), glocal.at[utt * 3 + part]).wait()
            for flip in flips:
                at = slot(utt, part, flip)
                copy = remote(own, target(utt, part), gsend.at[at], grecv.at[at], seq_flip(flip))
                copy.wait_send()
                copy.wait_recv()


def attend_backward(lengths, dout, qkv_all, o_all, lse, cos, sin, raws, span, block=1024):
    raws = [raw.reshape(2, 2, 2, 2, 2, raw.shape[0] // 32, raw.shape[1]) for raw in raws]
    frames = 8 * span
    rows, width = dout.shape
    anywhere = pl.BlockSpec(memory_space=pl.ANY)
    vmem = pl.BlockSpec(memory_space=pltpu.VMEM)
    dma = pltpu.SemaphoreType.DMA
    return pl.pallas_call(
        functools.partial(attend_backward_kernel, span=span, block=block),
        in_specs=[pl.BlockSpec(memory_space=pltpu.SMEM)]
        + [anywhere] * 3
        + [vmem] * 3
        + [anywhere] * 3,
        out_specs=[anywhere] * 4,
        out_shape=[jax.ShapeDtypeStruct((rows, 3 * width), BF)]
        + [jax.ShapeDtypeStruct((3, 2, 2, 2) + raw.shape[5:], BF) for raw in raws],
        scratch_shapes=[
            pltpu.VMEM((2, 3, frames, 128), BF),
            pltpu.VMEM((2, frames, 128), BF),
            pltpu.VMEM((2, frames, 128), BF),
        ]
        + [pltpu.VMEM((frames, 128), BF)] * 4
        + [pltpu.VMEM((128, frames), BF)] * 2
        + [pltpu.VMEM((frames, 128), F32)] * 2
        + [dma((16,)), dma((16,)), dma((2,)), dma((48,)), dma((48,)), dma((6,)), dma((4,)), dma((9,)), dma((9,))],
        compiler_params=pltpu.CompilerParams(
            vmem_limit_bytes=VMEM_LIMIT, collective_id=2, has_side_effects=True
        ),
        cost_estimate=attention_cost(frames, 10),
        name="attend_backward",
    )(lengths, dout, qkv_all, o_all, lse, cos, sin, *raws)


def layer_norm(stream):
    centre = stream - jnp.mean(stream, axis=-1, keepdims=True)
    spread = jnp.mean(centre * centre, axis=-1, keepdims=True)
    inverse = lax.rsqrt(spread + EPS)
    return (centre * inverse, inverse)


def norm_back(grad_normed, normed, inverse):
    first_mean = jnp.mean(grad_normed, axis=-1, keepdims=True)
    second_mean = jnp.mean(grad_normed * normed, axis=-1, keepdims=True)
    return inverse * (grad_normed - first_mean - normed * second_mean)


def tn(left, right):
    return lax.dot_general(left, right, (((0,), (0,)), ((), ())), preferred_element_type=F32)


GELU_C = 0.7978845608028654
GELU_A = 0.044715


def gelu_and_slope(z):
    square = z * z
    turn = jnp.tanh(GELU_C * z * (1.0 + GELU_A * square))
    half = 0.5 * (1.0 + turn)
    slope = half + 0.5 * z * (1.0 - turn * turn) * (GELU_C * (1.0 + 3.0 * GELU_A * square))
    return z * half, slope


def row_blocks(rows):
    block = min(rows, 512)
    return [(at, slice(at, at + block)) for at in range(0, rows, block)]


def ffn_forward_kernel(
    att_ref, outw_ref, res_ref, mod_ref, cot_ref, weight_ref, up_ref, down_ref,
    branch_ref, act_ref, slope_ref, gb_ref, out_ref, gate_ref, normed, acc,
):
    step = pl.program_id(0)
    rows = att_ref.shape[0]
    span = rows // mod_ref.shape[0]

    @pl.when(step == 0)
    def _():
        for at, part in row_blocks(span):
            for utt in range(mod_ref.shape[0]):
                here = slice(utt * span + part.start, utt * span + part.stop)
                mod = mod_ref[utt]
                branch = nn(att_ref[here, :], outw_ref[...])
                branch_ref[here, :] = branch
                hat, _ = layer_norm(res_ref[here, :] + mod[2:3] * branch)
                normed[here, :] = (hat * (1.0 + mod[4:5]) + mod[3:4]).astype(BF)
        acc[...] = jnp.zeros_like(acc)

    parts = [part for _, part in row_blocks(rows)]
    ahead = nn(normed[parts[0], :], up_ref[...])
    for index, part in enumerate(parts):
        hidden = ahead
        if index + 1 < len(parts):
            ahead = nn(normed[parts[index + 1], :], up_ref[...])
        act, slope = gelu_and_slope(hidden)
        act = act.astype(BF)
        act_ref[part, :] = act
        slope_ref[part, :] = slope.astype(BF)
        acc[part, :] += nn(act, down_ref[...])

    @pl.when(step == pl.num_programs(0) - 1)
    def _():
        for utt in range(mod_ref.shape[0]):
            mod = mod_ref[utt]
            total = jnp.zeros((1, acc.shape[1]), F32)
            for _, part in row_blocks(span):
                here = slice(utt * span + part.start, utt * span + part.stop)
                branch = acc[here, :]
                mid = res_ref[here, :] + mod[2:3] * branch_ref[here, :]
                out_ref[here, :] = (mid + mod[5:6] * branch).astype(BF)
                upstream = cot_ref[here, :].astype(F32) * weight_ref[here, :]
                gb_ref[here, :] = (upstream * mod[5:6]).astype(BF)
                total += jnp.sum(upstream * branch, axis=0, keepdims=True)
            gate_ref[utt : utt + 1, :] = total


def ffn_backward_kernel(
    att_ref, outw_ref, res_ref, branch_ref, mod_ref, cot_ref, weight_ref, gb_ref,
    act_ref, slope_ref, up_ref, down_ref,
    gup_ref, gdown_ref, gmid_ref, gatt_ref, gout_ref, sums_ref, normed, acc, gba,
):
    step = pl.program_id(0)
    rows = att_ref.shape[0]
    utts = mod_ref.shape[0]
    span = rows // utts

    def hat_of(here, mod):
        return layer_norm(res_ref[here, :] + mod[2:3] * branch_ref[here, :])

    @pl.when(step == 0)
    def _():
        for utt in range(utts):
            mod = mod_ref[utt]
            for _, part in row_blocks(span):
                here = slice(utt * span + part.start, utt * span + part.stop)
                hat, _ = hat_of(here, mod)
                normed[here, :] = (hat * (1.0 + mod[4:5]) + mod[3:4]).astype(BF)
        acc[...] = jnp.zeros_like(acc)

    pieces = []
    for _, part in row_blocks(rows):
        grad = nt(gb_ref[part, :], down_ref[...]) * slope_ref[part, :].astype(F32)
        grad = grad.astype(BF)
        acc[part, :] += nt(grad, up_ref[...])
        pieces.append(grad)
    gdown_ref[...] = tn(act_ref[...], gb_ref[...]).astype(BF)
    gup_ref[...] = tn(normed[...], jnp.concatenate(pieces, axis=0)).astype(BF)

    @pl.when(step == pl.num_programs(0) - 1)
    def _():
        for utt in range(utts):
            mod = mod_ref[utt]
            width = acc.shape[1]
            shift = jnp.zeros((1, width), F32)
            scale = jnp.zeros((1, width), F32)
            gate = jnp.zeros((1, width), F32)
            for _, part in row_blocks(span):
                here = slice(utt * span + part.start, utt * span + part.stop)
                hat, inverse = hat_of(here, mod)
                grad = acc[here, :]
                shift += jnp.sum(grad, axis=0, keepdims=True)
                scale += jnp.sum(grad * hat, axis=0, keepdims=True)
                upstream = cot_ref[here, :].astype(F32) * weight_ref[here, :]
                mid = upstream + norm_back(grad * (1.0 + mod[4:5]), hat, inverse)
                gmid_ref[here, :] = mid
                gate += jnp.sum(mid * branch_ref[here, :], axis=0, keepdims=True)
                low = (mid * mod[2:3]).astype(BF)
                gba[here, :] = low
                gatt_ref[here, :] = nt(low, outw_ref[...]).astype(BF)
            sums_ref[utt, 0:1, :] = shift
            sums_ref[utt, 1:2, :] = scale
            sums_ref[utt, 2:3, :] = gate
        gout_ref[...] = tn(att_ref[...], gba[...]).astype(BF)


def whole_spec(shape):
    zeros = (0,) * len(shape)
    return pl.BlockSpec(shape, lambda i: zeros, pipeline_mode=pl.Buffered(1))


def ffn_forward(att, outw, res, mods, cot, weight, up, down, chunk=1024):
    rows, width = res.shape
    hidden = up.shape[1]
    whole = [whole_spec(a.shape) for a in (att, outw, res, mods, cot, weight)]
    col = pl.BlockSpec((rows, chunk), lambda i: (0, i))
    utts = mods.shape[0]
    return pl.pallas_call(
        ffn_forward_kernel,
        grid=(hidden // chunk,),
        in_specs=whole
        + [
            pl.BlockSpec((width, chunk), lambda i: (0, i)),
            pl.BlockSpec((chunk, width), lambda i: (i, 0)),
        ],
        out_specs=[
            whole_spec((rows, width)),
            col,
            col,
            whole_spec((rows, width)),
            whole_spec((rows, width)),
            whole_spec((utts, width)),
        ],
        out_shape=[
            jax.ShapeDtypeStruct((rows, width), F32),
            jax.ShapeDtypeStruct((rows, hidden), BF),
            jax.ShapeDtypeStruct((rows, hidden), BF),
            jax.ShapeDtypeStruct((rows, width), BF),
            jax.ShapeDtypeStruct((rows, width), BF),
            jax.ShapeDtypeStruct((utts, width), F32),
        ],
        scratch_shapes=[pltpu.VMEM((rows, width), BF), pltpu.VMEM((rows, width), F32)],
        compiler_params=pltpu.CompilerParams(vmem_limit_bytes=VMEM_LIMIT),
        cost_estimate=pl.CostEstimate(
            flops=2 * rows * width * (width + 2 * hidden),
            bytes_accessed=60 * 2**20,
            transcendentals=rows * hidden,
        ),
        name="ffn_forward",
    )(att, outw, res, mods, cot, weight, up, down)


def ffn_backward(att, outw, res, branch, mods, cot, weight, gb, act, slope, up, down, chunk=512):
    rows, width = res.shape
    hidden = up.shape[1]
    utts = mods.shape[0]
    whole = [whole_spec(a.shape) for a in (att, outw, res, branch, mods, cot, weight, gb)]
    col = pl.BlockSpec((rows, chunk), lambda i: (0, i))
    upspec = pl.BlockSpec((width, chunk), lambda i: (0, i))
    downspec = pl.BlockSpec((chunk, width), lambda i: (i, 0))
    return pl.pallas_call(
        ffn_backward_kernel,
        grid=(hidden // chunk,),
        in_specs=whole + [col, col, upspec, downspec],
        out_specs=[
            upspec,
            downspec,
            whole_spec((rows, width)),
            whole_spec((rows, width)),
            whole_spec((width, width)),
            whole_spec((utts, 8, width)),
        ],
        out_shape=[
            jax.ShapeDtypeStruct((width, hidden), BF),
            jax.ShapeDtypeStruct((hidden, width), BF),
            jax.ShapeDtypeStruct((rows, width), F32),
            jax.ShapeDtypeStruct((rows, width), BF),
            jax.ShapeDtypeStruct((width, width), BF),
            jax.ShapeDtypeStruct((utts, 8, width), F32),
        ],
        scratch_shapes=[
            pltpu.VMEM((rows, width), BF),
            pltpu.VMEM((rows, width), F32),
            pltpu.VMEM((rows, width), BF),
        ],
        compiler_params=pltpu.CompilerParams(vmem_limit_bytes=VMEM_LIMIT),
        cost_estimate=pl.CostEstimate(
            flops=2 * rows * width * (2 * width + 4 * hidden),
            bytes_accessed=90 * 2**20,
            transcendentals=0,
        ),
        name="ffn_backward",
    )(att, outw, res, branch, mods, cot, weight, gb, act, slope, up, down)


FOLD_DIMS = (2, 1)


def fold_jobs(raws, arrived, folded, keeps, buffers):
    jobs = []
    for index, (raw, got) in enumerate(zip(raws, arrived)):
        for side, cols in enumerate(split_columns(raw.shape[-1], (1, 1))):
            at = 2 * index + side
            jobs.append((raw, got, cols, FOLD_DIMS[side], folded[at], keeps[at], buffers[at]))
    return jobs


def fold_pair(index, job, send, recv):
    _, _, _, dim, _, keep, buffer = job
    me, x, core = lax.axis_index("seq"), lax.axis_index("x"), lax.axis_index("core")
    bit = ((me // 4) % 2, (me // 2) % 2, me % 2)[dim]
    lead = (slice(None),) * dim
    copy = remote(
        keep.at[lead + (1 - bit,)],
        buffer,
        send.at[index],
        recv.at[index],
        (me ^ (4 >> dim), x, core),
    )
    return copy, lead + (bit,), bit


def fold_start(jobs, temps, send, recv, own, tsem, store):
    x, core = lax.axis_index("x"), lax.axis_index("core")
    greet([seq_flip(1), seq_flip(2)])
    owns, pieces = [], []
    for index, (raw, got, cols, dim, folded, keep, buffer) in enumerate(jobs):
        owns.append(
            pltpu.make_async_copy(raw.at[:, :, :, x, core, :, cols], keep, own.at[index])
        )
        owns[-1].start()
        for row in range(0, keep.shape[3], 32):
            for col in range(0, keep.shape[4], 512):
                pieces.append((index, row, col))
    depth = temps.shape[0]

    def loads(at):
        index, row, col = pieces[at]
        _, got, cols, *_ = jobs[index]
        slot = at % depth
        return [
            pltpu.make_async_copy(
                got.at[n, :, :, :, pl.ds(row, 32), pl.ds(cols.start + col, 512)],
                temps.at[slot, n],
                tsem.at[3 * slot + n],
            )
            for n in range(3)
        ]

    for at in range(depth):
        for copy in loads(at):
            copy.start()
    for at, (index, row, col) in enumerate(pieces):
        keep = jobs[index][5]
        if at == 0 or pieces[at - 1][0] != index:
            owns[index].wait()
        for copy in loads(at):
            copy.wait()
        slot = at % depth
        rows, cols = pl.ds(row, 32), pl.ds(col, 512)

        def body(i, carry):
            a, b, c = i // 4, (i // 2) % 2, i % 2
            total = keep[a, b, c, rows, cols].astype(F32)
            for n in range(3):
                total = total + temps[slot, n, a, b, c].astype(F32)
            keep[a, b, c, rows, cols] = total.astype(BF)
            return carry

        lax.fori_loop(0, 8, body, 0)
        if at + depth < len(pieces):
            for copy in loads(at + depth):
                copy.start()
        if at + 1 == len(pieces) or pieces[at + 1][0] != index:
            fold_pair(index, jobs[index], send, recv)[0].start()


def fold_finish(jobs, send, recv, own, tsem, store):
    stores = []
    for index, job in enumerate(jobs):
        _, _, _, dim, folded, keep, buffer = job
        copy, where, bit = fold_pair(index, job, send, recv)
        copy.wait_recv()

        def body(i, carry):
            place = [i // 2, i % 2]
            at = list(place)
            at.insert(dim, bit)
            total = keep[tuple(at)].astype(F32) + buffer[tuple(place)].astype(F32)
            keep[tuple(at)] = total.astype(BF)
            return carry

        lax.fori_loop(0, 4, body, 0)
        stores.append(pltpu.make_async_copy(keep.at[where], folded, store.at[index]))
        stores[-1].start()
    for index, job in enumerate(jobs):
        fold_pair(index, job, send, recv)[0].wait_send()
        stores[index].wait()


def leave_kernel(
    grad_ref, qkv_w, skip_w, res_ref, mid_ref, mod_ref, in_ref, skip_ref, *refs
):
    raws, arrived = refs[:3], refs[3:6]
    gin_ref, gskip_ref, sums_ref, gqkv_ref, gw_ref = refs[6:11]
    folded, normed, stream = refs[11:17], refs[17], refs[18]
    jobs = fold_jobs(raws, arrived, folded, refs[19:25], refs[25:31])
    temps, sems = refs[31], refs[32:]
    step = pl.program_id(0)

    @pl.when(step == 0)
    def _():
        fold_start(jobs, temps, *sems)

    leave_compute(
        step, grad_ref, qkv_w, skip_w, res_ref, mid_ref, mod_ref, in_ref, skip_ref,
        gin_ref, gskip_ref, sums_ref, gqkv_ref, gw_ref, normed, stream,
    )

    @pl.when(step == pl.num_programs(0) - 1)
    def _():
        fold_finish(jobs, *sems)


def leave_compute(
    step, grad_ref, qkv_w, skip_w, res_ref, mid_ref, mod_ref, in_ref, skip_ref,
    gin_ref, gskip_ref, sums_ref, gqkv_ref, gw_ref, normed, stream,
):
    rows, width = res_ref.shape
    utts = mod_ref.shape[0]
    span = rows // utts

    @pl.when(step == 0)
    def _():
        for utt in range(utts):
            mod = mod_ref[utt]
            shift = jnp.zeros((1, width), F32)
            scale = jnp.zeros((1, width), F32)
            for _, part in row_blocks(span):
                here = slice(utt * span + part.start, utt * span + part.stop)
                hat, inverse = layer_norm(res_ref[here, :])
                normed[here, :] = (hat * (1.0 + mod[1:2]) + mod[0:1]).astype(BF)
                grad = nt(grad_ref[here, :], qkv_w[...])
                shift += jnp.sum(grad, axis=0, keepdims=True)
                scale += jnp.sum(grad * hat, axis=0, keepdims=True)
                total = mid_ref[here, :] + norm_back(grad * (1.0 + mod[1:2]), hat, inverse)
                low = total.astype(BF)
                stream[here, :] = low
                gin_ref[here, :] = nt(low, skip_w[:width, :]).astype(BF)
                gskip_ref[here, :] = nt(low, skip_w[width:, :]).astype(BF)
            sums_ref[utt, 0:1, :] = shift
            sums_ref[utt, 1:2, :] = scale

    chunk = gqkv_ref.shape[1]
    cols = pl.ds(pl.multiple_of(step * chunk, chunk), chunk)
    gqkv_ref[...] = tn(normed[...], grad_ref[:, cols]).astype(BF)
    part = gw_ref.shape[2]
    here = pl.ds(pl.multiple_of(step * part, part), part)
    gw_ref[0] = tn(in_ref[...], stream[:, here]).astype(BF)
    gw_ref[1] = tn(skip_ref[...], stream[:, here]).astype(BF)


def leave_layer(grads, qkv_w, skip_w, res, mid, mods, first, second, raws, arrived, steps=4):
    rows, width = res.shape
    utts = mods.shape[0]
    ins = (grads, qkv_w, skip_w, res, mid, mods, first, second)
    views = [raw.reshape(2, 2, 2, 2, 2, raw.shape[0] // 32, raw.shape[1]) for raw in raws]
    tails = [
        (view.shape[5], cols.size)
        for view in views
        for cols in split_columns(view.shape[-1], (1, 1))
    ]
    anywhere = pl.BlockSpec(memory_space=pl.ANY)
    dma = pltpu.SemaphoreType.DMA
    outs = pl.pallas_call(
        leave_kernel,
        grid=(steps,),
        in_specs=[whole_spec(a.shape) for a in ins] + [anywhere] * 6,
        out_specs=[
            whole_spec((rows, width)),
            whole_spec((rows, width)),
            whole_spec((utts, 8, width)),
            pl.BlockSpec((width, 3 * width // steps), lambda i: (0, i)),
            pl.BlockSpec((2, width, width // steps), lambda i: (0, 0, i)),
        ]
        + [anywhere] * 6,
        out_shape=[
            jax.ShapeDtypeStruct((rows, width), BF),
            jax.ShapeDtypeStruct((rows, width), BF),
            jax.ShapeDtypeStruct((utts, 8, width), F32),
            jax.ShapeDtypeStruct((width, 3 * width), BF),
            jax.ShapeDtypeStruct((2, width, width), BF),
        ]
        + [jax.ShapeDtypeStruct((2, 2) + tail, BF) for tail in tails],
        scratch_shapes=[pltpu.VMEM((rows, width), BF), pltpu.VMEM((rows, width), BF)]
        + [pltpu.VMEM((2, 2, 2) + tail, BF) for tail in tails]
        + [pltpu.VMEM((2, 2) + tail, BF) for tail in tails]
        + [pltpu.VMEM((4, 3, 2, 2, 2, 32, 512), BF)]
        + [dma((6,)), dma((6,)), dma((6,)), dma((12,)), dma((6,))],
        compiler_params=pltpu.CompilerParams(
            vmem_limit_bytes=VMEM_LIMIT, collective_id=4, has_side_effects=True
        ),
        cost_estimate=pl.CostEstimate(
            flops=4 * rows * (skip_w.size + qkv_w.size),
            bytes_accessed=60 * 2**20,
            transcendentals=0,
        ),
        name="leave_layer",
    )(*ins, *views, *arrived)
    return tuple(outs[:4]) + (outs[4].reshape(2 * width, width), outs[5:])


class GradJob:
    def __init__(self, grad, out, cols, dims, order, keep, buffers, loads, sems, base):
        self.grad, self.out, self.cols, self.dims, self.order = grad, out, cols, dims, order
        self.keep, self.buffers, self.loads = keep, buffers, loads
        self.send, self.recv, self.local, self.base = *sems, base
        me, x, core = lax.axis_index("seq"), lax.axis_index("x"), lax.axis_index("core")
        self.bits = (me // 4, (me // 2) % 2, me % 2, x, core)
        self.copies, self.locals, self.round = [], [], 0

    def peer(self, dim):
        me, x, core = lax.axis_index("seq"), lax.axis_index("x"), lax.axis_index("core")
        if dim < 3:
            return (me ^ (4 >> dim), x, core)
        return (me, 1 - x, core) if dim == 3 else (me, x, 1 - core)

    def launch(self, source, target, dim):
        at = self.base + len(self.copies)
        copy = remote(source, target, self.send.at[at], self.recv.at[at], self.peer(dim))
        copy.start()
        self.copies.append(copy)

    def load(self, source, target):
        copy = pltpu.make_async_copy(source, target, self.local.at[self.base + len(self.locals)])
        copy.start()
        self.locals.append(copy)

    def add(self, done, others):
        left = [dim for dim in self.dims if dim not in done]

        def body(i, carry):
            at, place = [self.bits[dim] for dim in self.dims], []
            for n, dim in enumerate(left):
                bit = (i >> (len(left) - 1 - n)) & 1
                at[self.dims.index(dim)] = bit
                place.append(bit)
            total = self.keep[tuple(at)].astype(F32)
            for other in others:
                total = total + (other[tuple(place)] if place else other[...]).astype(F32)
            self.keep[tuple(at)] = total.astype(BF)
            return carry

        lax.fori_loop(0, 2 ** len(left), body, 0)

    def exchange(self, step):
        dim, done = self.order[step], self.order[:step]
        where = tuple(
            1 - self.bits[d] if d == dim else self.bits[d] if d in done else slice(None)
            for d in self.dims
        )
        self.launch(self.keep.at[where], self.buffers[step], dim)

    def advance(self):
        number, self.round = self.round, self.round + 1
        tail, bits = (slice(None), self.cols), self.bits
        steps = len(self.order)
        every = (slice(None),) * len(self.dims)
        if number == 0:
            if self.loads:
                self.load(self.grad.at[every + (bits[4],) + tail], self.keep)
                self.launch(self.grad.at[every + (1 - bits[4],) + tail], self.loads[0], 4)
            else:
                self.load(self.grad, self.keep)
        elif number == 1:
            self.locals[0].wait()
            if self.loads:
                self.copies[0].wait_recv()
                self.add((), self.loads)
            self.exchange(0)
        elif number <= steps + 1:
            self.copies[-1].wait_recv()
            self.add(self.order[: number - 1], [self.buffers[number - 2]])
            if number <= steps:
                self.exchange(number - 1)
            else:
                mine = self.keep.at[tuple(bits[dim] for dim in self.dims)]
                spot = self.out.at[bits[3:5] + tail]
                self.load(mine, spot)
                self.launch(mine, spot, 3)
        elif number == steps + 2:
            self.locals[-1].wait()
            self.copies[-1].wait_recv()
            both = self.out.at[(slice(None), bits[4]) + tail]
            self.launch(both, both, 4)

    def finish(self):
        self.copies[-1].wait_recv()
        for copy in self.copies:
            copy.wait_send()


FULL_ORDERS = ((3, 2, 1, 0), (2, 1, 3, 0), (1, 3, 2, 0))
FOLDED_DIMS = ((0, 1), (0, 2))
FOLDED_ORDERS = ((1, 0), (2, 0))


def reduce_kernel(*refs, halves, folds):
    grads, folded, small = refs[:halves], refs[halves : halves + 2 * folds], refs[halves + 2 * folds]
    refs = refs[halves + 2 * folds + 1 :]
    outs, small_out = refs[: halves + folds], refs[halves + folds]
    rest = list(refs[halves + folds + 1 :])
    small_in, small_low, send, recv, local, ssend, srecv, bsend, brecv, slocal = rest[-10:]
    me, x, core = lax.axis_index("seq"), lax.axis_index("x"), lax.axis_index("core")
    others = [seq_flip(flip) for flip in range(7, 0, -1)]
    mates = [(me, (x + dx) % 2, (core + dc) % 2) for dx, dc in ((0, 1), (1, 0), (1, 1))]
    greet(others + mates)
    jobs = []
    for index, out in enumerate(outs):
        whole = index < halves
        orders = FULL_ORDERS if whole else FOLDED_ORDERS
        for side, cols in enumerate(split_columns(out.shape[-1], (1,) * len(orders))):
            keep = rest.pop(0)
            loads = [rest.pop(0)] if whole else []
            buffers = [rest.pop(0) for _ in orders[side]]
            jobs.append(
                GradJob(
                    grads[index] if whole else folded[2 * (index - halves) + side],
                    out,
                    cols,
                    (0, 1, 2, 3) if whole else FOLDED_DIMS[side],
                    orders[side],
                    keep,
                    buffers,
                    loads,
                    (send, recv, local),
                    7 * len(jobs),
                )
            )
    own = pltpu.make_async_copy(small, small_in.at[me], slocal.at[0])
    own.start()
    smalls = []
    for flip, device in zip(range(7, 0, -1), others):
        smalls.append(remote(small, small_in.at[me], ssend.at[flip], srecv.at[flip], device))
        smalls[-1].start()
    for _ in range(3):
        for job in jobs:
            job.advance()
    own.wait()
    for copy in smalls:
        copy.wait_recv()
    total = small_in[0]
    for index in range(1, 8):
        total = total + small_in[index]
    small_low[...] = total.astype(BF)
    quarter = x * 2 + core
    keep = pltpu.make_async_copy(small_low, small_out.at[quarter], slocal.at[1])
    keep.start()
    lows = []
    for slot, device in enumerate(mates):
        lows.append(remote(small_low, small_out.at[quarter], bsend.at[slot], brecv.at[slot], device))
        lows[-1].start()
    for _ in range(4):
        for job in jobs:
            job.advance()
    for job in jobs:
        job.finish()
    for copy in smalls:
        copy.wait_send()
    keep.wait()
    for copy in lows:
        copy.wait()


def reduce_grads(halves, shapes, folded, small):
    views, outs, buffers, jobs = [], [], [], 0
    for grad in halves:
        rows, width = grad.shape
        views.append(grad.reshape(2, 2, 2, 2, 2, rows // 32, width))
    for index, (rows, width) in enumerate([grad.shape for grad in halves] + list(shapes)):
        span = rows // 32
        outs.append(jax.ShapeDtypeStruct((2, 2, span, width), BF))
        whole = index < len(halves)
        lead, orders = (4, FULL_ORDERS) if whole else (2, FOLDED_ORDERS)
        for cols in split_columns(width, (1,) * len(orders)):
            jobs += 1
            tail = (span, cols.size)
            for left in [lead] * (2 if whole else 1) + list(range(lead - 1, -1, -1)):
                buffers.append(pltpu.VMEM((2,) * left + tail, BF))
    anywhere = pl.BlockSpec(memory_space=pl.ANY)
    dma = pltpu.SemaphoreType.DMA
    outs.append(jax.ShapeDtypeStruct((4,) + small.shape, BF))
    results = pl.pallas_call(
        functools.partial(reduce_kernel, halves=len(halves), folds=len(shapes)),
        in_specs=[anywhere] * (len(halves) + len(folded) + 1),
        out_specs=[anywhere] * len(outs),
        out_shape=outs,
        scratch_shapes=buffers
        + [pltpu.VMEM((8,) + small.shape, F32), pltpu.VMEM(small.shape, BF)]
        + [dma((7 * jobs,))] * 3
        + [dma((8,)), dma((8,)), dma((3,)), dma((3,)), dma((2,))],
        compiler_params=pltpu.CompilerParams(
            vmem_limit_bytes=VMEM_LIMIT, collective_id=3, has_side_effects=True
        ),
        name="reduce_grads",
    )(*views, *folded, small)
    shards = [
        result.reshape(4 * result.shape[2], result.shape[3]).astype(jnp.float32)
        for result in results[:-1]
    ]
    return shards, results[-1].astype(jnp.float32)


def rotary_tables(positions):
    half_dim = HEAD_DIM // 2
    channel = jnp.arange(half_dim, dtype=jnp.float32)
    inverse = jnp.power(10000.0, -2.0 * channel / HEAD_DIM)
    angles = positions.astype(jnp.float32)[:, None] * inverse[None, :]
    angles = jnp.concatenate([angles, angles], axis=1)
    return (jnp.cos(angles), jnp.sin(angles))


def rotate_heads(field, cosine_table, sine_table):
    half_dim = field.shape[-1] // 2
    turned = jnp.concatenate([-field[..., half_dim:], field[..., :half_dim]], axis=-1)
    return field * cosine_table + turned * sine_table


def smooth_gelu(values):
    return jax.nn.gelu(values, approximate=True)


def cross(left, right):
    return lax.dot_general(
        left, right, (((0,), (0,)), ((), ())), preferred_element_type=jnp.float32
    )


def back_product(left, right):
    return lax.dot_general(
        left, right, (((1,), (1,)), ((), ())), preferred_element_type=jnp.float32
    )


def block_terms(query_block, dout_block, lse_block, delta_block, key_block, value_block, key_live):
    scores = jnp.einsum(
        "bqhd,bkhd->bhqk", query_block, key_block, preferred_element_type=jnp.float32
    )
    lse_heads = jnp.transpose(lse_block, (0, 2, 1))[..., None]
    probs = jnp.where(key_live[:, None, None, :], jnp.exp(scores - lse_heads), 0.0)
    grad_probs = jnp.einsum(
        "bqhd,bkhd->bhqk", dout_block, value_block, preferred_element_type=jnp.float32
    )
    delta_heads = jnp.transpose(delta_block, (0, 2, 1))[..., None]
    dscore = (probs * (grad_probs - delta_heads)).astype(jnp.bfloat16)
    return (probs.astype(jnp.bfloat16), dscore)


BATCH = ("x", "core")


def batch_index():
    return lax.axis_index("x") * lax.axis_size("core") + lax.axis_index("core")


def gather_weight(weight):
    parts = lax.axis_size(BATCH)
    if weight.shape[0] % parts:
        return lax.all_gather(weight, "seq", axis=0, tiled=True)
    rows = weight.shape[0] // parts
    mine = lax.dynamic_slice_in_dim(weight, batch_index() * rows, rows, 0)
    return lax.all_gather(mine, ("seq",) + BATCH, axis=0, tiled=True)


def sum_weight(grad):
    rows, width = grad.shape
    low = grad.astype(jnp.bfloat16)
    seq_count, cores = lax.axis_size("seq"), lax.axis_size("core")
    parts = seq_count * lax.axis_size(BATCH)
    if rows % parts or cores != 2:
        shard = lax.psum_scatter(low, "seq", scatter_dimension=0, tiled=True)
        return lax.psum(shard, BATCH).astype(jnp.float32)
    core = lax.axis_index("core")
    held = low.reshape(parts // 2, 2, rows // parts, width)
    send = lax.dynamic_index_in_dim(held, 1 - core, 1, keepdims=False)
    keep = lax.dynamic_index_in_dim(held, core, 1, keepdims=False)
    got = lax.ppermute(send, "core", [(0, 1), (1, 0)])
    half = (keep.astype(jnp.float32) + got.astype(jnp.float32)).astype(jnp.bfloat16)
    half = half.reshape(rows // 2, width)
    shard = lax.psum_scatter(half, ("seq", "x"), scatter_dimension=0, tiled=True)
    return lax.all_gather(shard, BATCH, axis=0, tiled=True).astype(jnp.float32)


def gather_kernel(*refs, count, ahead, block):
    weights, laters = refs[:count], refs[count : count + ahead]
    refs = refs[count + ahead :]
    seq_small, batch_small, first, second, cos_ref, sin_ref = refs[:6]
    outs = refs[6:]
    fulls, helds = outs[:count], outs[count : count + ahead]
    batch_out, mod_out, res_out, proj_out = outs[count + ahead : count + ahead + 4]
    (
        seq_out, mods, skip_w, qkv_w, res, proj,
        send, recv, asend, arecv, small_send, small_recv, local, lift, put,
    ) = outs[count + ahead + 4 :]
    me, x, core = lax.axis_index("seq"), lax.axis_index("x"), lax.axis_index("core")
    bits = (me // 4, (me // 2) % 2, me % 2, x, core)

    def peer(dim):
        if dim < 3:
            return (me ^ (4 >> dim), x, core)
        return (me, 1 - x, core) if dim == 3 else (me, x, 1 - core)

    others = [((me + d) % 8, x, core) for d in range(1, 8)]
    mates = [(me, (x + dx) % 2, (core + dc) % 2) for dx, dc in ((0, 1), (1, 0), (1, 1))]
    barrier = pltpu.get_barrier_semaphore()
    for device in others + mates:
        pl.semaphore_signal(barrier, inc=1, device_id=device, device_id_type=pl.DeviceIdType.MESH)
    pl.semaphore_wait(barrier, len(others) + len(mates))

    small = []
    quarter = x * 2 + core
    own_seq = pltpu.make_async_copy(seq_small, seq_out.at[me], local.at[0])
    own_batch = pltpu.make_async_copy(batch_small, batch_out.at[quarter], local.at[1])
    own_seq.start()
    own_batch.start()
    for slot, device in enumerate(others):
        small.append(
            pltpu.make_async_remote_copy(
                seq_small, seq_out.at[me], small_send.at[slot], small_recv.at[slot],
                device_id=device, device_id_type=pl.DeviceIdType.MESH,
            )
        )
    for slot, device in enumerate(mates):
        small.append(
            pltpu.make_async_remote_copy(
                batch_small, batch_out.at[quarter], small_send.at[7 + slot], small_recv.at[7 + slot],
                device_id=device, device_id_type=pl.DeviceIdType.MESH,
            )
        )
    for copy in small:
        copy.start()

    jobs = early_jobs(weights, fulls)
    chain = WeightGather(jobs, send, recv, local.at[pl.ds(2, len(jobs))])
    later = WeightGather(
        ahead_jobs(laters, helds), asend, arecv, local.at[pl.ds(2 + len(jobs), ahead)]
    )
    chain.stage()
    chain.stage()
    later.stage()
    for copy in small:
        copy.wait()
    own_seq.wait()
    own_batch.wait()
    total = seq_out[0]
    for index in range(1, 8):
        total = total + seq_out[index]
    mod_out[...] = total
    utts = mods.shape[0]
    for utt in range(utts):
        mods[utt, 0:6, :] = total[utt * 6 : utt * 6 + 6]
    chain.stage()
    later.stage()
    chain.stage()
    chain.stage()
    chain.finish()
    for index, (full, flat) in enumerate(zip(fulls, (skip_w, qkv_w))):
        span = full.shape[5]

        def carry_in(p, carry):
            bits = (p // 16, (p // 8) % 2, (p // 4) % 2, (p // 2) % 2, p % 2)
            rows = pl.ds(pl.multiple_of(p * span, span), span)
            pltpu.make_async_copy(full.at[bits], flat.at[rows, :], lift.at[index]).start()
            return carry

        lax.fori_loop(0, 32, carry_in, 0)
    for index, flat in enumerate((skip_w, qkv_w)):
        pltpu.make_async_copy(flat, flat, lift.at[index]).wait()
    rows, width = first.shape
    steps = rows // utts // block

    def enter(i, carry):
        here = pl.ds(pl.multiple_of(i * block, block), block)
        table = pl.ds(pl.multiple_of((i % steps) * block, block), block)
        mod = mods[i // steps]
        residual = nn(first[here, :], skip_w[:width, :]) + nn(second[here, :], skip_w[width:, :])
        res[here, :] = residual
        hat, _ = layer_norm(residual)
        normed = (hat * (1.0 + mod[1:2]) + mod[0:1]).astype(BF)
        lane = lanes_of(block)
        cos, sin = cos_ref[table, :], sin_ref[table, :]
        for part in range(3):
            projected = nn(normed, qkv_w[:, part * width : (part + 1) * width])
            for group in range(width // 128):
                cols = slice(group * 128, group * 128 + 128)
                piece = projected[:, cols]
                if part < 2:
                    turned = jnp.where(
                        (lane & 63) < 32, pltpu.roll(piece, 96, 1), pltpu.roll(piece, 32, 1)
                    )
                    piece = piece * cos + turned * sin
                if part == 0:
                    piece = piece * (0.125 * LOG2E)
                proj[part, here, cols] = piece.astype(BF)
        pltpu.make_async_copy(res.at[here, :], res_out.at[here, :], put.at[0]).start()
        pltpu.make_async_copy(proj.at[:, here, :], proj_out.at[:, here, :], put.at[1]).start()
        return carry

    lax.fori_loop(0, rows // block, enter, 0)
    later.finish()
    pltpu.make_async_copy(res, res_out, put.at[0]).wait()
    pltpu.make_async_copy(proj, proj_out, put.at[1]).wait()


def gather_early(weights, laters, seq_small, batch_small, first, second, cos, sin, block=256):
    anywhere = pl.BlockSpec(memory_space=pl.ANY)
    vmem = pl.BlockSpec(memory_space=pltpu.VMEM)
    jobs, ahead = 3 * len(weights), len(laters)
    rows, width = first.shape
    dma = pltpu.SemaphoreType.DMA
    quarter = lambda lead, w: jax.ShapeDtypeStruct((2,) * lead + (w.shape[0] // 4, w.shape[1]), BF)
    outs = pl.pallas_call(
        functools.partial(gather_kernel, count=len(weights), ahead=ahead, block=block),
        in_specs=[anywhere] * (len(weights) + ahead + 2) + [vmem] * 4,
        out_specs=[anywhere] * (len(weights) + ahead + 1) + [vmem] + [anywhere] * 2,
        out_shape=[quarter(5, w) for w in weights]
        + [quarter(2, w) for w in laters]
        + [
            jax.ShapeDtypeStruct((4,) + batch_small.shape, F32),
            jax.ShapeDtypeStruct(seq_small.shape, F32),
            jax.ShapeDtypeStruct((rows, width), F32),
            jax.ShapeDtypeStruct((3, rows, width), BF),
        ],
        scratch_shapes=[
            pltpu.VMEM((8,) + seq_small.shape, F32),
            pltpu.VMEM((seq_small.shape[0] // 6, 8, width), F32),
        ]
        + [pltpu.VMEM((8 * w.shape[0], w.shape[1]), BF) for w in weights]
        + [
            pltpu.VMEM((rows, width), F32),
            pltpu.VMEM((3, rows, width), BF),
            dma((5 * jobs,)),
            dma((5 * jobs,)),
            dma((5 * ahead,)),
            dma((5 * ahead,)),
            dma((10,)),
            dma((10,)),
            dma((2 + jobs + ahead,)),
            dma((2,)),
            dma((2,)),
        ],
        compiler_params=pltpu.CompilerParams(
            vmem_limit_bytes=VMEM_LIMIT, collective_id=0, has_side_effects=True
        ),
        name="gather_early",
    )(*weights, *laters, seq_small, batch_small, first, second, cos, sin)
    fulls = [full.reshape(8 * w.shape[0], w.shape[1]) for full, w in zip(outs, weights)]
    return fulls, outs[len(weights) : len(weights) + ahead], *outs[-4:]


def paired_tables(count):
    half = HEAD_DIM // 2
    inverse = np.power(10000.0, -2.0 * np.arange(half) / HEAD_DIM)
    angles = np.arange(count)[:, None] * inverse[None, :]
    cos, sin = np.cos(angles), np.sin(angles)
    tables = (np.tile(cos, (1, 4)), np.tile(np.concatenate([-sin, sin], axis=1), (1, 2)))
    return tuple(jnp.asarray(table, jnp.float32) for table in tables)


def on_device(
    layer_input,
    skip_input,
    time_embed,
    lengths,
    cond_drop,
    cotangent,
    skip_weight,
    adaln_weight,
    adaln_bias,
    qkv_weight,
    out_weight,
    up_weight,
    down_weight,
):
    utt_count, frame_span, model_width = layer_input.shape
    head_count = model_width // HEAD_DIM
    row_count = utt_count * frame_span
    seq_here = lax.axis_index("seq")
    seq_count = lax.axis_size("seq")
    frame_count = frame_span * seq_count
    by_heads = (
        seq_count == 8
        and head_count == 16
        and utt_count == 2
        and lax.axis_size(BATCH) == 4
        and frame_span == 512
    )
    local_pos = seq_here * frame_span + jnp.arange(frame_span, dtype=jnp.int32)
    local_live = local_pos[None, :] < lengths[:, None]
    valid_mask = local_live.astype(jnp.float32)
    drop = cond_drop.astype(jnp.float32)
    dropped = drop[:, None] * valid_mask
    frames_live = jnp.minimum(lengths, frame_count).astype(jnp.float32)
    counts = jnp.stack([jnp.sum((1.0 - drop) * frames_live), jnp.sum(drop * frames_live)])
    silu_time = jax.nn.silu(time_embed.astype(jnp.float32)).astype(jnp.bfloat16)
    row_span = adaln_weight.shape[0]
    silu_mine = lax.dynamic_slice_in_dim(silu_time, seq_here * row_span, row_span, 1)
    mod_part = jnp.dot(silu_mine, adaln_weight, preferred_element_type=jnp.float32)
    bias_span = adaln_bias.shape[0]
    bias_here = lax.dynamic_update_slice_in_dim(
        jnp.zeros((mod_part.shape[1],), jnp.float32),
        adaln_bias.astype(jnp.float32),
        seq_here * bias_span,
        0,
    )
    mod_part = mod_part + bias_here
    if by_heads:
        small = jnp.concatenate(
            [
                silu_time.astype(jnp.float32),
                jnp.pad(counts[None, :], ((0, 5), (0, model_width - 2))),
            ],
            axis=0,
        )
        cos_all, sin_all = paired_tables(frame_count)
        first_rows = layer_input.reshape(row_count, model_width)
        second_rows = skip_input.reshape(row_count, model_width)
        gathered = gather_early(
            (skip_weight, qkv_weight),
            (out_weight, up_weight, down_weight),
            mod_part.reshape(-1, model_width),
            small,
            first_rows,
            second_rows,
            lax.dynamic_slice_in_dim(cos_all, seq_here * frame_span, frame_span, 0),
            lax.dynamic_slice_in_dim(sin_all, seq_here * frame_span, frame_span, 0),
        )
        (skip_full, qkv_full), late_held, small_every, modulation, residual_rows, proj = gathered
        totals = jnp.sum(small_every[:, utt_count, :2], axis=0)
        silu_every = small_every[:, :utt_count].reshape(-1, model_width)
    else:
        modulation = lax.psum(mod_part, "seq")
        totals = lax.psum(counts, BATCH)
        skip_full = gather_weight(skip_weight)
        qkv_full = gather_weight(qkv_weight)
        silu_every = lax.all_gather(silu_time, BATCH, axis=0, tiled=True).astype(jnp.float32)
    modulation = modulation.reshape(utt_count, 6, model_width)
    kept_total = jnp.maximum(totals[0], 1.0)
    drop_total = jnp.maximum(totals[1], 1.0)
    every_count = kept_total + drop_total
    loss_weight = (valid_mask - dropped) * (every_count / (2.0 * kept_total)) + dropped * (
        every_count / (2.0 * drop_total)
    )
    if by_heads:
        (qkv_all, out_all, lse_all, attended_low), (out_full, up_full, down_full) = attend_forward(
            lengths, proj, *late_held, frame_span
        )
    else:
        joined = jnp.concatenate([layer_input, skip_input], axis=-1).reshape(row_count, 2 * model_width)
        residual_in = jnp.dot(joined, skip_full, preferred_element_type=jnp.float32).reshape(
            utt_count, frame_span, model_width
        )
        shift_attn = modulation[:, 0][:, None, :]
        scale_attn = modulation[:, 1][:, None, :]
        hat_attn, inv_attn = layer_norm(residual_in)
        normed_attn = (
            (hat_attn * (1.0 + scale_attn) + shift_attn)
            .astype(jnp.bfloat16)
            .reshape(row_count, model_width)
        )
        residual_rows = residual_in.reshape(row_count, model_width)
        out_full, up_full, down_full = [
            gather_weight(weight) for weight in (out_weight, up_weight, down_weight)
        ]
        projected = jnp.dot(normed_attn, qkv_full, preferred_element_type=jnp.float32).reshape(
            utt_count, frame_span, 3, head_count, HEAD_DIM
        )
        cosine_table, sine_table = rotary_tables(local_pos)
        cosine_table = cosine_table[None, :, None, :]
        sine_table = sine_table[None, :, None, :]
        queries = (rotate_heads(projected[:, :, 0], cosine_table, sine_table) * 0.125).astype(
            jnp.bfloat16
        )
        keys_rot = rotate_heads(projected[:, :, 1], cosine_table, sine_table).astype(jnp.bfloat16)
        values = projected[:, :, 2].astype(jnp.bfloat16)
        start_top = jnp.full((utt_count, head_count, frame_span), MASKED, jnp.float32)
        top_score = start_top
        key_piece = lax.all_gather(keys_rot, "seq", axis=1, tiled=True)
        value_piece = lax.all_gather(values, "seq", axis=1, tiled=True)
        piece_len = key_piece.shape[1]
        piece_live = jnp.arange(piece_len, dtype=jnp.int32)[None, :] < lengths[:, None]
        scores = jnp.einsum("bqhd,bkhd->bhqk", queries, key_piece, preferred_element_type=jnp.float32)
        scores = jnp.where(piece_live[:, None, None, :], scores, MASKED)
        new_top = jnp.maximum(top_score, jnp.max(scores, axis=-1))
        expo = jnp.where(piece_live[:, None, None, :], jnp.exp(scores - new_top[..., None]), 0.0)
        denom = jnp.sum(expo, axis=-1)
        partial_out = jnp.einsum(
            "bhqk,bkhd->bqhd",
            expo.astype(jnp.bfloat16),
            value_piece,
            preferred_element_type=jnp.float32,
        )
        accum = partial_out
        accum, top_score, denom = (accum, new_top, denom)
        attended_full = accum / jnp.transpose(denom, (0, 2, 1))[..., None]
        lse_rows = jnp.transpose(top_score + jnp.log(denom), (0, 2, 1))
        attended_low = attended_full.astype(jnp.bfloat16).reshape(row_count, model_width)
    cot_rows = cotangent.reshape(row_count, model_width)
    weight_rows = loss_weight.reshape(row_count, 1)
    branch_attn, hidden_act, hidden_slope, grad_branch_ffn, layer_output, grad_gate_ffn = ffn_forward(
        attended_low,
        out_full,
        residual_rows,
        modulation,
        cot_rows,
        weight_rows,
        up_full,
        down_full,
    )
    layer_output = layer_output.reshape(utt_count, frame_span, model_width)
    grad_up, grad_down, grad_mid, grad_attended_flat, grad_out, ffn_sums = ffn_backward(
        attended_low,
        out_full,
        residual_rows,
        branch_attn,
        modulation,
        cot_rows,
        weight_rows,
        grad_branch_ffn,
        hidden_act,
        hidden_slope,
        up_full,
        down_full,
    )
    grad_shift_ffn, grad_scale_ffn, grad_gate_attn = ffn_sums[:, 0], ffn_sums[:, 1], ffn_sums[:, 2]
    if by_heads:
        grad_projected, *arrived = attend_backward(
            lengths,
            grad_attended_flat,
            qkv_all,
            out_all,
            lse_all,
            cos_all,
            sin_all,
            (grad_down, grad_up, grad_out),
            frame_span,
        )
    else:
        grad_attended = grad_attended_flat.reshape(
            utt_count, frame_span, head_count, HEAD_DIM
        )
        delta_rows = jnp.sum(grad_attended.astype(jnp.float32) * attended_full, axis=-1)
        lse_all, delta_all = (
            lax.all_gather(lse_rows, "seq", axis=1, tiled=True),
            lax.all_gather(delta_rows, "seq", axis=1, tiled=True),
        )
        key_piece = lax.all_gather(keys_rot, "seq", axis=1, tiled=True)
        value_piece = lax.all_gather(values, "seq", axis=1, tiled=True)
        piece_len = key_piece.shape[1]
        piece_live = jnp.arange(piece_len, dtype=jnp.int32)[None, :] < lengths[:, None]
        probs_low, dscore = block_terms(
            queries, grad_attended, lse_rows, delta_rows, key_piece, value_piece, piece_live
        )
        grad_queries = jnp.einsum(
            "bhqk,bkhd->bqhd", dscore, key_piece, preferred_element_type=jnp.float32
        )
        query_piece = lax.all_gather(queries, "seq", axis=1, tiled=True)
        dout_piece = lax.all_gather(grad_attended, "seq", axis=1, tiled=True)
        probs_low, dscore = block_terms(
            query_piece, dout_piece, lse_all, delta_all, keys_rot, values, local_live
        )
        grad_k = jnp.einsum("bhqk,bqhd->bkhd", dscore, query_piece, preferred_element_type=jnp.float32)
        grad_v = jnp.einsum(
            "bhqk,bqhd->bkhd", probs_low, dout_piece, preferred_element_type=jnp.float32
        )
        grad_q_pre = rotate_heads(grad_queries * 0.125, cosine_table, -sine_table)
        grad_k_pre = rotate_heads(grad_k, cosine_table, -sine_table)
        grad_projected = (
            jnp.stack([grad_q_pre, grad_k_pre, grad_v], axis=2)
            .reshape(row_count, 3 * model_width)
            .astype(jnp.bfloat16)
        )
    if by_heads:
        grad_input, grad_skip, attn_sums, grad_qkv, grad_skip_w, folded = leave_layer(
            grad_projected,
            qkv_full,
            skip_full,
            residual_rows,
            grad_mid,
            modulation,
            first_rows,
            second_rows,
            (grad_down, grad_up, grad_out),
            arrived,
        )
        grad_input = grad_input.reshape(layer_input.shape)
        grad_skip = grad_skip.reshape(skip_input.shape)
        grad_shift_attn, grad_scale_attn = attn_sums[:, 0], attn_sums[:, 1]
    else:
        grad_mid = grad_mid.reshape(utt_count, frame_span, model_width)
        grad_qkv = cross(normed_attn, grad_projected)
        grad_normed_attn = back_product(grad_projected, qkv_full).reshape(
            utt_count, frame_span, model_width
        )
        grad_shift_attn = jnp.sum(grad_normed_attn, axis=1)
        grad_scale_attn = jnp.sum(grad_normed_attn * hat_attn, axis=1)
        grad_stream = grad_mid + norm_back(grad_normed_attn * (1.0 + scale_attn), hat_attn, inv_attn)
        grad_stream_low = grad_stream.astype(jnp.bfloat16).reshape(row_count, model_width)
        grad_skip_w = cross(joined, grad_stream_low)
        grad_joined = back_product(grad_stream_low, skip_full)
        grad_input = (
            grad_joined[:, :model_width]
            .reshape(utt_count, frame_span, model_width)
            .astype(jnp.bfloat16)
        )
        grad_skip = (
            grad_joined[:, model_width:]
            .reshape(utt_count, frame_span, model_width)
            .astype(jnp.bfloat16)
        )
    grad_modulation = jnp.stack(
        [
            grad_shift_attn,
            grad_scale_attn,
            grad_gate_attn,
            grad_shift_ffn,
            grad_scale_ffn,
            grad_gate_ffn,
        ],
        axis=1,
    ).reshape(utt_count, 6 * model_width)
    weight_grads = (grad_skip_w, grad_qkv, grad_out, grad_up, grad_down)
    if by_heads:
        shards, mod_every = reduce_grads(
            (grad_qkv, grad_skip_w),
            [grad.shape for grad in (grad_down, grad_up, grad_out)],
            folded,
            grad_modulation.reshape(-1, model_width),
        )
        summed = [shards[i] for i in (1, 0, 4, 3, 2)]
        mod_every = mod_every.reshape(-1, 6 * model_width)
    else:
        mod_total = lax.psum(grad_modulation, "seq")
        mod_every = lax.all_gather(
            mod_total.astype(jnp.bfloat16), BATCH, axis=0, tiled=True
        ).astype(jnp.float32)
        summed = [sum_weight(grad) for grad in weight_grads]
    silu_rows = lax.dynamic_slice_in_dim(silu_every, seq_here * row_span, row_span, 1)
    adaln_rows = jnp.dot(silu_rows.T, mod_every, precision=lax.Precision.HIGHEST)
    bias_rows = lax.dynamic_slice_in_dim(
        jnp.sum(mod_every, axis=0), seq_here * bias_span, bias_span, 0
    )
    results = (summed[0], adaln_rows, bias_rows, summed[1], summed[2], summed[3], summed[4])
    return (
        layer_output,
        grad_input,
        grad_skip,
        results[0],
        results[1],
        results[2],
        results[3],
        results[4],
        results[5],
        results[6],
    )


def solution(mesh):
    count, batch = mesh.shape["seq"], mesh.shape["batch"]
    cores = 2 if batch % 2 == 0 else 1
    split = Mesh(mesh.devices.reshape(count, batch // cores, cores), ("seq",) + BATCH)
    placed = (
        P(BATCH, "seq", None),
        P(BATCH, "seq", None),
        P(BATCH, None),
        P(BATCH),
        P(BATCH),
        P(BATCH, "seq", None),
        P("seq", None),
        P("seq", None),
        P("seq"),
        P("seq", None),
        P("seq", None),
        P("seq", None),
        P("seq", None),
    )
    return jax.shard_map(
        on_device,
        mesh=split,
        in_specs=placed,
        out_specs=(
            P(BATCH, "seq", None),
            P(BATCH, "seq", None),
            P(BATCH, "seq", None),
            P("seq", None),
            P("seq", None),
            P("seq"),
            P("seq", None),
            P("seq", None),
            P("seq", None),
            P("seq", None),
        ),
        check_vma=False,
    )
```

```python
import functools
import jax
import jax.numpy as jnp
import numpy as np
from jax import lax
from jax.sharding import Mesh, PartitionSpec as P
from jax.experimental import pallas as pl
from jax.experimental.pallas import tpu as pltpu
HEAD_DIM = 64
EPS = 1e-06
LOG2E = 1.4426950408889634
LN2 = 0.6931471805599453
MASKED = -1e30
BF = jnp.bfloat16
F32 = jnp.float32
VMEM_LIMIT = 60 * 2**20


def nt(left, right):
    return lax.dot_general(left, right, (((1,), (1,)), ((), ())), preferred_element_type=F32)


def nn(left, right):
    return lax.dot_general(left, right, (((1,), (0,)), ((), ())), preferred_element_type=F32)


def head_sums(product, lane):
    first = jnp.sum(jnp.where(lane < 64, product, 0.0), axis=1, keepdims=True)
    second = jnp.sum(jnp.where(lane >= 64, product, 0.0), axis=1, keepdims=True)
    return (first, second)


def lanes_of(rows):
    return lax.broadcasted_iota(jnp.int32, (rows, 128), 1)


def attention_cost(frames, products):
    return pl.CostEstimate(
        flops=2 * products * 2 * frames * frames * 128,
        bytes_accessed=frames * 128 * 2 * 8,
        transcendentals=2 * frames * frames,
    )


def turn_back(grad, cos, sin):
    lane = lanes_of(grad.shape[0])
    turned = jnp.where((lane & 63) < 32, pltpu.roll(grad, 96, 1), pltpu.roll(grad, 32, 1))
    return grad * cos - turned * sin


def three(column, lane, at):
    high = column.astype(BF).astype(F32)
    rest = column - high
    mid = rest.astype(BF).astype(F32)
    low = rest - mid
    return jnp.where(lane == at, -high, jnp.where(lane == at + 1, -mid, jnp.where(lane == at + 2, -low, 0.0)))


MESH_IDS = pl.DeviceIdType.MESH


def seq_flip(flip):
    return (lax.axis_index("seq") ^ flip, lax.axis_index("x"), lax.axis_index("core"))


def greet(devices):
    barrier = pltpu.get_barrier_semaphore()
    for device in devices:
        pl.semaphore_signal(barrier, inc=1, device_id=device, device_id_type=MESH_IDS)
    pl.semaphore_wait(barrier, len(devices))


def far_first(at, count):
    near = lax.axis_index("seq") // 4
    return (at + (count // 2) * (1 - near)) % count


def remote(source, target, send, recv, device):
    return pltpu.make_async_remote_copy(
        source, target, send, recv, device_id=device, device_id_type=MESH_IDS
    )


class WeightGather:
    def __init__(self, jobs, send, recv, local):
        self.jobs, self.send, self.recv, self.local = jobs, send, recv, local
        me, x, core = lax.axis_index("seq"), lax.axis_index("x"), lax.axis_index("core")
        self.bits = (me // 4, (me // 2) % 2, me % 2, x, core)
        self.copies = [[] for _ in jobs]
        self.owns = []

    def peer(self, dim):
        me, x, core = lax.axis_index("seq"), lax.axis_index("x"), lax.axis_index("core")
        if dim < 3:
            return (me ^ (4 >> dim), x, core)
        return (me, 1 - x, core) if dim == 3 else (me, x, 1 - core)

    def stage(self):
        for index, (full, cols, source, ready, order) in enumerate(self.jobs):
            at = len(self.copies[index])
            where = tuple(
                slice(None) if d in ready + order[:at] else self.bits[d]
                for d in range(len(full.shape) - 2)
            ) + (slice(None), cols)
            if at == 0:
                own = pltpu.make_async_copy(source, full.at[where], self.local.at[index])
                own.start()
                self.owns.append(own)
            else:
                if at == 1:
                    self.owns[index].wait()
                self.copies[index][at - 1].wait_recv()
            copy = remote(
                source if at == 0 else full.at[where],
                full.at[where],
                self.send.at[index * 5 + at],
                self.recv.at[index * 5 + at],
                self.peer(order[at]),
            )
            copy.start()
            self.copies[index].append(copy)

    def finish(self):
        for chain in self.copies:
            chain[-1].wait_recv()
        for chain in self.copies:
            for copy in chain:
                copy.wait_send()


def split_columns(width, shares):
    total, start, out = sum(shares), 0, []
    for n in range(len(shares)):
        stop = width * sum(shares[: n + 1]) // total // 128 * 128
        out.append(pl.ds(start, stop - start))
        start = stop
    return out


def quarter_of(weight, cols):
    quarter = lax.axis_index("x") * 2 + lax.axis_index("core")
    span = weight.shape[0] // 4
    return weight.at[pl.ds(quarter * span, span), cols]


def early_jobs(weights, fulls):
    orders = ((0, 1, 2, 3, 4), (0, 1, 3, 2, 4)) * 2
    return [
        (full, cols, quarter_of(weight, cols), (), order)
        for weight, full in zip(weights, fulls)
        for cols, order in zip(split_columns(weight.shape[1], (1,) * 4), orders)
    ]


def late_jobs(helds, fulls):
    return [
        (full, cols, held.at[:, :, :, cols], (0, 1), order)
        for held, full in zip(helds, fulls)
        for cols, order in zip(split_columns(held.shape[3], (3, 1)), ((2, 3, 4), (3, 2, 4)))
    ]


def attend_forward_kernel(
    len_ref, proj, out_w, up_w, down_w,
    qkv_all, o_all, lse_ref, att, out_full, up_full, down_full,
    qkv, outs, ka, kb, vta, vtb,
    wsend, wrecv, wlocal, qsend, qrecv, qlocal, osend, orecv, olocal, slocal,
    *, span, bq, bk,
):
    me, x, core = lax.axis_index("seq"), lax.axis_index("x"), lax.axis_index("core")
    frames = qkv.shape[2]
    mine = pl.ds(pl.multiple_of(me * span, span), span)
    my_cols = pl.ds(pl.multiple_of(me * 128, 128), 128)
    flips = (7, 6, 5, 4, 3, 2, 1)
    greet([seq_flip(flip) for flip in flips] + [(me, 1 - x, core), (me, x, 1 - core)])
    weights = WeightGather(
        late_jobs((out_w, up_w, down_w), (out_full, up_full, down_full)), wsend, wrecv, wlocal
    )

    def send_heads(utt):
        rows = pl.ds(utt * span, span)
        own = pltpu.make_async_copy(
            proj.at[:, rows, my_cols], qkv.at[utt, :, mine, :], qlocal.at[utt]
        )
        own.start()
        copies = []
        for flip in flips:
            there = me ^ flip
            cols = pl.ds(pl.multiple_of(there * 128, 128), 128)
            copy = remote(
                proj.at[:, rows, cols],
                qkv.at[utt, :, mine, :],
                qsend.at[utt * 8 + flip],
                qrecv.at[utt * 8 + flip],
                seq_flip(flip),
            )
            copy.start()
            copies.append(copy)
        return own, copies

    def arrive(sent):
        own, copies = sent
        own.wait()
        for copy in copies:
            copy.wait_recv()

    def send_out(utt, there):
        rows = pl.ds(pl.multiple_of(there * span, span), span)
        target = att.at[pl.ds(utt * span, span), my_cols]

        @pl.when(there != me)
        def _():
            remote(
                outs.at[utt, rows, :],
                target,
                osend.at[utt * 8 + (there ^ me)],
                orecv.at[utt * 8 + (there ^ me)],
                (there, x, core),
            ).start()

        @pl.when(there == me)
        def _():
            pltpu.make_async_copy(outs.at[utt, rows, :], target, olocal.at[utt]).start()

    def attend(utt, between):
        length = len_ref[utt]
        save = pltpu.make_async_copy(qkv.at[utt], qkv_all.at[utt], slocal.at[utt])
        save.start()

        def build(j, carry):
            rows = pl.ds(pl.multiple_of(j * bk, bk), bk)
            lane = lanes_of(bk)
            pos = j * bk + lax.broadcasted_iota(jnp.int32, (bk, 128), 0)
            bias = jnp.where(pos < length, 0.0, MASKED)
            keys = qkv[utt, 1, rows, :].astype(F32)
            ka[rows, :] = jnp.where(lane < 64, keys, jnp.where(lane == 64, bias, 0.0)).astype(BF)
            kb[rows, :] = jnp.where(lane >= 64, keys, jnp.where(lane == 0, bias, 0.0)).astype(BF)
            vals = qkv[utt, 2, rows, :].astype(F32)
            vta[:, rows] = jnp.where(lane < 64, vals, 1.0).T.astype(BF)
            vtb[:, rows] = jnp.where(lane >= 64, vals, 1.0).T.astype(BF)
            return carry

        lax.fori_loop(0, frames // bk, build, 0)

        def block(i_at, carry):
            i = far_first(i_at, frames // bq)
            here = pl.ds(pl.multiple_of(i * bq, bq), bq)
            lane = lanes_of(bq)
            queries = qkv[utt, 0, here, :].astype(F32)
            qa = jnp.where(lane < 64, queries, jnp.where(lane == 64, 1.0, 0.0)).astype(BF)
            qb = jnp.where(lane >= 64, queries, jnp.where(lane == 0, 1.0, 0.0)).astype(BF)

            def body(j, inner):
                rows = pl.ds(pl.multiple_of(j * bk, bk), bk)
                result = []
                scores = [nt(ka[rows, :], qa), nt(kb[rows, :], qb)]
                for score, vt, (top, acc) in zip(scores, (vta, vtb), inner):
                    new = jnp.maximum(top, jnp.max(score, axis=0, keepdims=True))
                    probs = jnp.exp2(score - new).astype(BF)
                    acc = acc * jnp.exp2(top - new) + nn(vt[:, rows], probs)
                    result.append((new, acc))
                return tuple(result)

            start = (jnp.full((1, bq), MASKED, F32), jnp.zeros((128, bq), F32))
            (top_a, acc_a), (top_b, acc_b) = lax.fori_loop(0, frames // bk, body, (start, start))
            sum_a, sum_b = acc_a[64:65], acc_b[0:1]
            both = jnp.concatenate([acc_a[:64] / sum_a, acc_b[64:] / sum_b], axis=0)
            outs[utt, here, :] = both.T.astype(BF)
            lse_ref[utt, :, here] = jnp.concatenate(
                [top_a + jnp.log2(sum_a), top_b + jnp.log2(sum_b), jnp.zeros((6, bq), F32)],
                axis=0,
            )
            if utt == 1:
                for part in range(bq // span):
                    send_out(utt, i * (bq // span) + part)
            return carry

        most = frames // bq - 1
        lax.fori_loop(0, most, block, 0)
        between()
        lax.fori_loop(most, most + 1, block, 0)
        keep = pltpu.make_async_copy(outs.at[utt], o_all.at[utt], slocal.at[2 + utt])
        keep.start()
        return [save, keep]

    first = send_heads(0)
    weights.stage()
    arrive(first)
    second = send_heads(1)
    weights.stage()
    saves = attend(0, lambda: None)
    arrive(second)

    def send_first(i, carry):
        send_out(0, i)
        return carry

    lax.fori_loop(0, 8, send_first, 0)
    saves += attend(1, weights.stage)
    for sent in (first, second):
        for copy in sent[1]:
            copy.wait_send()
    weights.finish()
    for save in saves:
        save.wait()
    for utt in range(2):
        target = att.at[pl.ds(utt * span, span), my_cols]
        pltpu.make_async_copy(outs.at[utt, mine, :], target, olocal.at[utt]).wait()
        for flip in flips:
            copy = remote(
                outs.at[utt, mine, :],
                target,
                osend.at[utt * 8 + flip],
                orecv.at[utt * 8 + flip],
                seq_flip(flip),
            )
            copy.wait_send()
            copy.wait_recv()


def attend_forward(lengths, proj, out_w, up_w, down_w, span, bq=1024, bk=512):
    rows, width = proj.shape[1:]
    frames = 8 * span
    anywhere = pl.BlockSpec(memory_space=pl.ANY)
    vmem = pl.BlockSpec(memory_space=pltpu.VMEM)
    full = lambda w: jax.ShapeDtypeStruct((2, 2, 2, 2, 2) + w.shape[2:], BF)
    dma = pltpu.SemaphoreType.DMA
    outs = pl.pallas_call(
        functools.partial(attend_forward_kernel, span=span, bq=bq, bk=bk),
        in_specs=[pl.BlockSpec(memory_space=pltpu.SMEM)] + [anywhere] * 4,
        out_specs=[anywhere, anywhere, vmem] + [anywhere] * 4,
        out_shape=[
            jax.ShapeDtypeStruct((2, 3, frames, 128), BF),
            jax.ShapeDtypeStruct((2, frames, 128), BF),
            jax.ShapeDtypeStruct((2, 8, frames), F32),
            jax.ShapeDtypeStruct((rows, width), BF),
            full(out_w),
            full(up_w),
            full(down_w),
        ],
        scratch_shapes=[
            pltpu.VMEM((2, 3, frames, 128), BF),
            pltpu.VMEM((2, frames, 128), BF),
            pltpu.VMEM((frames, 128), BF),
            pltpu.VMEM((frames, 128), BF),
            pltpu.VMEM((128, frames), BF),
            pltpu.VMEM((128, frames), BF),
            dma((30,)),
            dma((30,)),
            dma((6,)),
            dma((16,)),
            dma((16,)),
            dma((2,)),
            dma((16,)),
            dma((16,)),
            dma((2,)),
            dma((4,)),
        ],
        compiler_params=pltpu.CompilerParams(
            vmem_limit_bytes=VMEM_LIMIT, collective_id=1, has_side_effects=True
        ),
        cost_estimate=attention_cost(frames, 4),
        name="attend_forward",
    )(lengths, proj, out_w, up_w, down_w)
    fulls = [
        outs[4 + i].reshape(32 * w.shape[2], w.shape[3]) for i, w in enumerate((out_w, up_w, down_w))
    ]
    return outs[:4], fulls


def attend_backward_kernel(
    len_ref, dout, qkv_all, o_all, lse_ref, cos_ref, sin_ref, raw_a, raw_b, raw_c,
    grads, got_a, got_b, got_c,
    qkv, outs, douts, qa, qb, da, db, qt, dt, dqa, dqb,
    dsend, drecv, dlocal, gsend, grecv, glocal, load, rsend, rrecv,
    *, span, block,
):
    me, x, core = lax.axis_index("seq"), lax.axis_index("x"), lax.axis_index("core")
    frames = qkv.shape[2]
    width = grads.shape[1] // 3
    count = frames // block
    mine = pl.ds(pl.multiple_of(me * span, span), span)
    flips = (7, 6, 5, 4, 3, 2, 1)
    mates = [(me, x ^ dx, core ^ dc) for dx, dc in ((0, 1), (1, 0), (1, 1))]
    greet([seq_flip(flip) for flip in flips] + mates)
    loads = []
    for utt in range(2):
        loads.append(
            [
                pltpu.make_async_copy(qkv_all.at[utt], qkv.at[utt], load.at[utt]),
                pltpu.make_async_copy(o_all.at[utt], outs.at[utt], load.at[2 + utt]),
            ]
        )
        for copy in loads[-1]:
            copy.start()

    def send_heads(utt):
        rows = pl.ds(utt * span, span)
        my_cols = pl.ds(pl.multiple_of(me * 128, 128), 128)
        own = pltpu.make_async_copy(dout.at[rows, my_cols], douts.at[utt, mine, :], dlocal.at[utt])
        own.start()
        copies = []
        for flip in flips:
            cols = pl.ds(pl.multiple_of((me ^ flip) * 128, 128), 128)
            copy = remote(
                dout.at[rows, cols],
                douts.at[utt, mine, :],
                dsend.at[utt * 8 + flip],
                drecv.at[utt * 8 + flip],
                seq_flip(flip),
            )
            copy.start()
            copies.append(copy)
        return own, copies

    def arrive(sent):
        own, copies = sent
        own.wait()
        for copy in copies:
            copy.wait_recv()

    def slot(utt, part, flip):
        return (utt * 3 + part) * 8 + flip

    def target(utt, part):
        cols = pl.ds(pl.multiple_of(part * width + me * 128, 128), 128)
        return grads.at[pl.ds(utt * span, span), cols]

    def send_grads(utt, part, there):
        rows = pl.ds(pl.multiple_of(there * span, span), span)

        @pl.when(there != me)
        def _():
            at = slot(utt, part, there ^ me)
            remote(
                qkv.at[utt, part, rows, :],
                target(utt, part),
                gsend.at[at],
                grecv.at[at],
                (there, x, core),
            ).start()

        @pl.when(there == me)
        def _():
            pltpu.make_async_copy(
                qkv.at[utt, part, rows, :], target(utt, part), glocal.at[utt * 3 + part]
            ).start()

    def differentiate(utt):
        length = len_ref[utt]

        def build(j, carry):
            rows = pl.ds(pl.multiple_of(j * block, block), block)
            lane = lanes_of(block)
            queries = qkv[utt, 0, rows, :].astype(F32)
            grad = douts[utt, rows, :].astype(F32)
            delta_a, delta_b = head_sums(grad * outs[utt, rows, :].astype(F32), lane)
            lse = lse_ref[utt, :, rows].T
            one_a, one_b = lse[:, 0:1], lse[:, 1:2]
            qa[rows, :] = jnp.where(
                lane < 64, queries, jnp.where(lane == 67, 1.0, three(one_a, lane, 64))
            ).astype(BF)
            qb[rows, :] = jnp.where(
                lane >= 64, queries, jnp.where(lane == 3, 1.0, three(one_b, lane, 0))
            ).astype(BF)
            da[rows, :] = jnp.where(lane < 64, grad, three(delta_a, lane, 64)).astype(BF)
            db[rows, :] = jnp.where(lane >= 64, grad, three(delta_b, lane, 0)).astype(BF)
            qt[:, rows] = queries.T.astype(BF)
            dt[:, rows] = grad.T.astype(BF)
            dqa[rows, :] = jnp.zeros((block, 128), F32)
            dqb[rows, :] = jnp.zeros((block, 128), F32)
            return carry

        lax.fori_loop(0, count, build, 0)

        def keys_block(step_at, carry):
            i = far_first(step_at, count)
            here = pl.ds(pl.multiple_of(i * block, block), block)
            lane = lanes_of(block)
            pos = i * block + lax.broadcasted_iota(jnp.int32, (block, 128), 0)
            bias = jnp.where(pos < length, 0.0, MASKED)
            keys = qkv[utt, 1, here, :].astype(F32)
            vals = qkv[utt, 2, here, :].astype(F32)
            ones_a = jnp.where(lane < 67, 1.0, 0.0)
            ones_b = jnp.where(lane < 3, 1.0, 0.0)
            ka = jnp.where(lane < 64, keys, jnp.where(lane == 67, bias, ones_a)).astype(BF)
            kb = jnp.where(lane >= 64, keys, jnp.where(lane == 3, bias, ones_b)).astype(BF)
            va = jnp.where(lane < 64, vals, ones_a).astype(BF)
            vb = jnp.where(lane >= 64, vals, ones_b).astype(BF)

            def body(j_at, inner):
                j = far_first(j_at, count)
                rows = pl.ds(pl.multiple_of(j * block, block), block)
                result = []
                for head, (qh, dh, kh, vh, dq) in enumerate(
                    ((qa, da, ka, va, dqa), (qb, db, kb, vb, dqb))
                ):
                    part = slice(head * 64, head * 64 + 64)
                    probs = jnp.exp2(nt(qh[rows, :], kh))
                    grad = (probs * nt(dh[rows, :], vh)).astype(BF)
                    dv = inner[2 * head + 1] + nn(dt[:, rows], probs.astype(BF))[part]
                    dk = inner[2 * head] + nn(qt[:, rows], grad)[part]
                    dq[rows, :] += nn(grad, kh)
                    result += [dk, dv]

                @pl.when(step_at == count - 1)
                def _():
                    low = jnp.where(lanes_of(block) < 64, dqa[rows, :], dqb[rows, :]) * 0.125
                    low = turn_back(low, cos_ref[rows, :], sin_ref[rows, :])
                    qkv[utt, 0, rows, :] = low.astype(BF)
                    for step in range(block // span):
                        send_grads(utt, 0, j * (block // span) + step)

                return tuple(result)

            zero = jnp.zeros((64, block), F32)
            dk_a, dv_a, dk_b, dv_b = lax.fori_loop(0, count, body, (zero,) * 4)
            dk = jnp.concatenate([dk_a, dk_b], axis=0).T * LN2
            dv = jnp.concatenate([dv_a, dv_b], axis=0).T
            qkv[utt, 1, here, :] = turn_back(dk, cos_ref[here, :], sin_ref[here, :]).astype(BF)
            qkv[utt, 2, here, :] = dv.astype(BF)
            for step in range(block // span):
                there = i * (block // span) + step
                send_grads(utt, 1, there)
                send_grads(utt, 2, there)
            return carry

        lax.fori_loop(0, count, keys_block, 0)

    first = send_heads(0)
    raws = []
    for index, (raw, got) in enumerate(((raw_a, got_a), (raw_b, got_b), (raw_c, got_c))):
        for slot_at, device in enumerate(mates):
            at = index * 3 + slot_at
            copy = remote(
                raw.at[:, :, :, device[1], device[2]],
                got.at[slot_at],
                rsend.at[at],
                rrecv.at[at],
                device,
            )
            copy.start()
            raws.append(copy)
    for copy in loads[0]:
        copy.wait()
    arrive(first)
    second = send_heads(1)
    differentiate(0)
    for copy in loads[1]:
        copy.wait()
    arrive(second)
    differentiate(1)
    for sent in (first, second):
        for copy in sent[1]:
            copy.wait_send()
    for copy in raws:
        copy.wait()
    for utt in range(2):
        for part in range(3):
            own = qkv.at[utt, part, mine, :]
            pltpu.make_async_copy(own, target(utt, part), glocal.at[utt * 3 + part]).wait()
            for flip in flips:
                at = slot(utt, part, flip)
                copy = remote(own, target(utt, part), gsend.at[at], grecv.at[at], seq_flip(flip))
                copy.wait_send()
                copy.wait_recv()


def attend_backward(lengths, dout, qkv_all, o_all, lse, cos, sin, raws, span, block=1024):
    raws = [raw.reshape(2, 2, 2, 2, 2, raw.shape[0] // 32, raw.shape[1]) for raw in raws]
    frames = 8 * span
    rows, width = dout.shape
    anywhere = pl.BlockSpec(memory_space=pl.ANY)
    vmem = pl.BlockSpec(memory_space=pltpu.VMEM)
    dma = pltpu.SemaphoreType.DMA
    return pl.pallas_call(
        functools.partial(attend_backward_kernel, span=span, block=block),
        in_specs=[pl.BlockSpec(memory_space=pltpu.SMEM)]
        + [anywhere] * 3
        + [vmem] * 3
        + [anywhere] * 3,
        out_specs=[anywhere] * 4,
        out_shape=[jax.ShapeDtypeStruct((rows, 3 * width), BF)]
        + [jax.ShapeDtypeStruct((3, 2, 2, 2) + raw.shape[5:], BF) for raw in raws],
        scratch_shapes=[
            pltpu.VMEM((2, 3, frames, 128), BF),
            pltpu.VMEM((2, frames, 128), BF),
            pltpu.VMEM((2, frames, 128), BF),
        ]
        + [pltpu.VMEM((frames, 128), BF)] * 4
        + [pltpu.VMEM((128, frames), BF)] * 2
        + [pltpu.VMEM((frames, 128), F32)] * 2
        + [dma((16,)), dma((16,)), dma((2,)), dma((48,)), dma((48,)), dma((6,)), dma((4,)), dma((9,)), dma((9,))],
        compiler_params=pltpu.CompilerParams(
            vmem_limit_bytes=VMEM_LIMIT, collective_id=2, has_side_effects=True
        ),
        cost_estimate=attention_cost(frames, 10),
        name="attend_backward",
    )(lengths, dout, qkv_all, o_all, lse, cos, sin, *raws)


def layer_norm(stream):
    centre = stream - jnp.mean(stream, axis=-1, keepdims=True)
    spread = jnp.mean(centre * centre, axis=-1, keepdims=True)
    inverse = lax.rsqrt(spread + EPS)
    return (centre * inverse, inverse)


def norm_back(grad_normed, normed, inverse):
    first_mean = jnp.mean(grad_normed, axis=-1, keepdims=True)
    second_mean = jnp.mean(grad_normed * normed, axis=-1, keepdims=True)
    return inverse * (grad_normed - first_mean - normed * second_mean)


def tn(left, right):
    return lax.dot_general(left, right, (((0,), (0,)), ((), ())), preferred_element_type=F32)


GELU_C = 0.7978845608028654
GELU_A = 0.044715


def gelu_and_slope(z):
    square = z * z
    turn = jnp.tanh(GELU_C * z * (1.0 + GELU_A * square))
    half = 0.5 * (1.0 + turn)
    slope = half + 0.5 * z * (1.0 - turn * turn) * (GELU_C * (1.0 + 3.0 * GELU_A * square))
    return z * half, slope


def row_blocks(rows):
    block = min(rows, 512)
    return [(at, slice(at, at + block)) for at in range(0, rows, block)]


def ffn_forward_kernel(
    att_ref, outw_ref, res_ref, mod_ref, cot_ref, weight_ref, up_ref, down_ref,
    branch_ref, act_ref, slope_ref, gb_ref, out_ref, gate_ref, normed, acc,
):
    step = pl.program_id(0)
    rows = att_ref.shape[0]
    span = rows // mod_ref.shape[0]

    @pl.when(step == 0)
    def _():
        for at, part in row_blocks(span):
            for utt in range(mod_ref.shape[0]):
                here = slice(utt * span + part.start, utt * span + part.stop)
                mod = mod_ref[utt]
                branch = nn(att_ref[here, :], outw_ref[...])
                branch_ref[here, :] = branch
                hat, _ = layer_norm(res_ref[here, :] + mod[2:3] * branch)
                normed[here, :] = (hat * (1.0 + mod[4:5]) + mod[3:4]).astype(BF)
        acc[...] = jnp.zeros_like(acc)

    parts = [part for _, part in row_blocks(rows)]
    ahead = nn(normed[parts[0], :], up_ref[...])
    for index, part in enumerate(parts):
        hidden = ahead
        if index + 1 < len(parts):
            ahead = nn(normed[parts[index + 1], :], up_ref[...])
        act, slope = gelu_and_slope(hidden)
        act = act.astype(BF)
        act_ref[part, :] = act
        slope_ref[part, :] = slope.astype(BF)
        acc[part, :] += nn(act, down_ref[...])

    @pl.when(step == pl.num_programs(0) - 1)
    def _():
        for utt in range(mod_ref.shape[0]):
            mod = mod_ref[utt]
            total = jnp.zeros((1, acc.shape[1]), F32)
            for _, part in row_blocks(span):
                here = slice(utt * span + part.start, utt * span + part.stop)
                branch = acc[here, :]
                mid = res_ref[here, :] + mod[2:3] * branch_ref[here, :]
                out_ref[here, :] = (mid + mod[5:6] * branch).astype(BF)
                upstream = cot_ref[here, :].astype(F32) * weight_ref[here, :]
                gb_ref[here, :] = (upstream * mod[5:6]).astype(BF)
                total += jnp.sum(upstream * branch, axis=0, keepdims=True)
            gate_ref[utt : utt + 1, :] = total


def ffn_backward_kernel(
    att_ref, outw_ref, res_ref, branch_ref, mod_ref, cot_ref, weight_ref, gb_ref,
    act_ref, slope_ref, up_ref, down_ref,
    gup_ref, gdown_ref, gmid_ref, gatt_ref, gout_ref, sums_ref, normed, acc, gba,
):
    step = pl.program_id(0)
    rows = att_ref.shape[0]
    utts = mod_ref.shape[0]
    span = rows // utts

    def hat_of(here, mod):
        return layer_norm(res_ref[here, :] + mod[2:3] * branch_ref[here, :])

    @pl.when(step == 0)
    def _():
        for utt in range(utts):
            mod = mod_ref[utt]
            for _, part in row_blocks(span):
                here = slice(utt * span + part.start, utt * span + part.stop)
                hat, _ = hat_of(here, mod)
                normed[here, :] = (hat * (1.0 + mod[4:5]) + mod[3:4]).astype(BF)
        acc[...] = jnp.zeros_like(acc)

    pieces = []
    for _, part in row_blocks(rows):
        grad = nt(gb_ref[part, :], down_ref[...]) * slope_ref[part, :].astype(F32)
        grad = grad.astype(BF)
        acc[part, :] += nt(grad, up_ref[...])
        pieces.append(grad)
    gdown_ref[...] = tn(act_ref[...], gb_ref[...]).astype(BF)
    gup_ref[...] = tn(normed[...], jnp.concatenate(pieces, axis=0)).astype(BF)

    @pl.when(step == pl.num_programs(0) - 1)
    def _():
        for utt in range(utts):
            mod = mod_ref[utt]
            width = acc.shape[1]
            shift = jnp.zeros((1, width), F32)
            scale = jnp.zeros((1, width), F32)
            gate = jnp.zeros((1, width), F32)
            for _, part in row_blocks(span):
                here = slice(utt * span + part.start, utt * span + part.stop)
                hat, inverse = hat_of(here, mod)
                grad = acc[here, :]
                shift += jnp.sum(grad, axis=0, keepdims=True)
                scale += jnp.sum(grad * hat, axis=0, keepdims=True)
                upstream = cot_ref[here, :].astype(F32) * weight_ref[here, :]
                mid = upstream + norm_back(grad * (1.0 + mod[4:5]), hat, inverse)
                gmid_ref[here, :] = mid
                gate += jnp.sum(mid * branch_ref[here, :], axis=0, keepdims=True)
                low = (mid * mod[2:3]).astype(BF)
                gba[here, :] = low
                gatt_ref[here, :] = nt(low, outw_ref[...]).astype(BF)
            sums_ref[utt, 0:1, :] = shift
            sums_ref[utt, 1:2, :] = scale
            sums_ref[utt, 2:3, :] = gate
        gout_ref[...] = tn(att_ref[...], gba[...]).astype(BF)


def whole_spec(shape):
    zeros = (0,) * len(shape)
    return pl.BlockSpec(shape, lambda i: zeros, pipeline_mode=pl.Buffered(1))


def ffn_forward(att, outw, res, mods, cot, weight, up, down, chunk=1024):
    rows, width = res.shape
    hidden = up.shape[1]
    whole = [whole_spec(a.shape) for a in (att, outw, res, mods, cot, weight)]
    col = pl.BlockSpec((rows, chunk), lambda i: (0, i))
    utts = mods.shape[0]
    return pl.pallas_call(
        ffn_forward_kernel,
        grid=(hidden // chunk,),
        in_specs=whole
        + [
            pl.BlockSpec((width, chunk), lambda i: (0, i)),
            pl.BlockSpec((chunk, width), lambda i: (i, 0)),
        ],
        out_specs=[
            whole_spec((rows, width)),
            col,
            col,
            whole_spec((rows, width)),
            whole_spec((rows, width)),
            whole_spec((utts, width)),
        ],
        out_shape=[
            jax.ShapeDtypeStruct((rows, width), F32),
            jax.ShapeDtypeStruct((rows, hidden), BF),
            jax.ShapeDtypeStruct((rows, hidden), BF),
            jax.ShapeDtypeStruct((rows, width), BF),
            jax.ShapeDtypeStruct((rows, width), BF),
            jax.ShapeDtypeStruct((utts, width), F32),
        ],
        scratch_shapes=[pltpu.VMEM((rows, width), BF), pltpu.VMEM((rows, width), F32)],
        compiler_params=pltpu.CompilerParams(vmem_limit_bytes=VMEM_LIMIT),
        cost_estimate=pl.CostEstimate(
            flops=2 * rows * width * (width + 2 * hidden),
            bytes_accessed=60 * 2**20,
            transcendentals=rows * hidden,
        ),
        name="ffn_forward",
    )(att, outw, res, mods, cot, weight, up, down)


def ffn_backward(att, outw, res, branch, mods, cot, weight, gb, act, slope, up, down, chunk=512):
    rows, width = res.shape
    hidden = up.shape[1]
    utts = mods.shape[0]
    whole = [whole_spec(a.shape) for a in (att, outw, res, branch, mods, cot, weight, gb)]
    col = pl.BlockSpec((rows, chunk), lambda i: (0, i))
    upspec = pl.BlockSpec((width, chunk), lambda i: (0, i))
    downspec = pl.BlockSpec((chunk, width), lambda i: (i, 0))
    return pl.pallas_call(
        ffn_backward_kernel,
        grid=(hidden // chunk,),
        in_specs=whole + [col, col, upspec, downspec],
        out_specs=[
            upspec,
            downspec,
            whole_spec((rows, width)),
            whole_spec((rows, width)),
            whole_spec((width, width)),
            whole_spec((utts, 8, width)),
        ],
        out_shape=[
            jax.ShapeDtypeStruct((width, hidden), BF),
            jax.ShapeDtypeStruct((hidden, width), BF),
            jax.ShapeDtypeStruct((rows, width), F32),
            jax.ShapeDtypeStruct((rows, width), BF),
            jax.ShapeDtypeStruct((width, width), BF),
            jax.ShapeDtypeStruct((utts, 8, width), F32),
        ],
        scratch_shapes=[
            pltpu.VMEM((rows, width), BF),
            pltpu.VMEM((rows, width), F32),
            pltpu.VMEM((rows, width), BF),
        ],
        compiler_params=pltpu.CompilerParams(vmem_limit_bytes=VMEM_LIMIT),
        cost_estimate=pl.CostEstimate(
            flops=2 * rows * width * (2 * width + 4 * hidden),
            bytes_accessed=90 * 2**20,
            transcendentals=0,
        ),
        name="ffn_backward",
    )(att, outw, res, branch, mods, cot, weight, gb, act, slope, up, down)


FOLD_DIMS = (2, 1)


def fold_jobs(raws, arrived, folded, keeps, buffers):
    jobs = []
    for index, (raw, got) in enumerate(zip(raws, arrived)):
        for side, cols in enumerate(split_columns(raw.shape[-1], (1, 1))):
            at = 2 * index + side
            jobs.append((raw, got, cols, FOLD_DIMS[side], folded[at], keeps[at], buffers[at]))
    return jobs


def fold_pair(index, job, send, recv):
    _, _, _, dim, _, keep, buffer = job
    me, x, core = lax.axis_index("seq"), lax.axis_index("x"), lax.axis_index("core")
    bit = ((me // 4) % 2, (me // 2) % 2, me % 2)[dim]
    lead = (slice(None),) * dim
    copy = remote(
        keep.at[lead + (1 - bit,)],
        buffer,
        send.at[index],
        recv.at[index],
        (me ^ (4 >> dim), x, core),
    )
    return copy, lead + (bit,), bit


def fold_start(jobs, temps, send, recv, own, tsem, store):
    x, core = lax.axis_index("x"), lax.axis_index("core")
    greet([seq_flip(1), seq_flip(2)])
    owns, pieces = [], []
    for index, (raw, got, cols, dim, folded, keep, buffer) in enumerate(jobs):
        owns.append(
            pltpu.make_async_copy(raw.at[:, :, :, x, core, :, cols], keep, own.at[index])
        )
        owns[-1].start()
        for row in range(0, keep.shape[3], 32):
            for col in range(0, keep.shape[4], 512):
                pieces.append((index, row, col))
    depth = temps.shape[0]

    def loads(at):
        index, row, col = pieces[at]
        _, got, cols, *_ = jobs[index]
        slot = at % depth
        return [
            pltpu.make_async_copy(
                got.at[n, :, :, :, pl.ds(row, 32), pl.ds(cols.start + col, 512)],
                temps.at[slot, n],
                tsem.at[3 * slot + n],
            )
            for n in range(3)
        ]

    for at in range(depth):
        for copy in loads(at):
            copy.start()
    for at, (index, row, col) in enumerate(pieces):
        keep = jobs[index][5]
        if at == 0 or pieces[at - 1][0] != index:
            owns[index].wait()
        for copy in loads(at):
            copy.wait()
        slot = at % depth
        rows, cols = pl.ds(row, 32), pl.ds(col, 512)

        def body(i, carry):
            a, b, c = i // 4, (i // 2) % 2, i % 2
            total = keep[a, b, c, rows, cols].astype(F32)
            for n in range(3):
                total = total + temps[slot, n, a, b, c].astype(F32)
            keep[a, b, c, rows, cols] = total.astype(BF)
            return carry

        lax.fori_loop(0, 8, body, 0)
        if at + depth < len(pieces):
            for copy in loads(at + depth):
                copy.start()
        if at + 1 == len(pieces) or pieces[at + 1][0] != index:
            fold_pair(index, jobs[index], send, recv)[0].start()


def fold_finish(jobs, send, recv, own, tsem, store):
    stores = []
    for index, job in enumerate(jobs):
        _, _, _, dim, folded, keep, buffer = job
        copy, where, bit = fold_pair(index, job, send, recv)
        copy.wait_recv()

        def body(i, carry):
            place = [i // 2, i % 2]
            at = list(place)
            at.insert(dim, bit)
            total = keep[tuple(at)].astype(F32) + buffer[tuple(place)].astype(F32)
            keep[tuple(at)] = total.astype(BF)
            return carry

        lax.fori_loop(0, 4, body, 0)
        stores.append(pltpu.make_async_copy(keep.at[where], folded, store.at[index]))
        stores[-1].start()
    for index, job in enumerate(jobs):
        fold_pair(index, job, send, recv)[0].wait_send()
        stores[index].wait()


def leave_kernel(
    grad_ref, qkv_w, skip_w, res_ref, mid_ref, mod_ref, in_ref, skip_ref, *refs
):
    raws, arrived = refs[:3], refs[3:6]
    gin_ref, gskip_ref, sums_ref, gqkv_ref, gw_ref = refs[6:11]
    folded, normed, stream = refs[11:17], refs[17], refs[18]
    jobs = fold_jobs(raws, arrived, folded, refs[19:25], refs[25:31])
    temps, sems = refs[31], refs[32:]
    step = pl.program_id(0)

    @pl.when(step == 0)
    def _():
        fold_start(jobs, temps, *sems)

    leave_compute(
        step, grad_ref, qkv_w, skip_w, res_ref, mid_ref, mod_ref, in_ref, skip_ref,
        gin_ref, gskip_ref, sums_ref, gqkv_ref, gw_ref, normed, stream,
    )

    @pl.when(step == pl.num_programs(0) - 1)
    def _():
        fold_finish(jobs, *sems)


def leave_compute(
    step, grad_ref, qkv_w, skip_w, res_ref, mid_ref, mod_ref, in_ref, skip_ref,
    gin_ref, gskip_ref, sums_ref, gqkv_ref, gw_ref, normed, stream,
):
    rows, width = res_ref.shape
    utts = mod_ref.shape[0]
    span = rows // utts

    @pl.when(step == 0)
    def _():
        for utt in range(utts):
            mod = mod_ref[utt]
            shift = jnp.zeros((1, width), F32)
            scale = jnp.zeros((1, width), F32)
            for _, part in row_blocks(span):
                here = slice(utt * span + part.start, utt * span + part.stop)
                hat, inverse = layer_norm(res_ref[here, :])
                normed[here, :] = (hat * (1.0 + mod[1:2]) + mod[0:1]).astype(BF)
                grad = nt(grad_ref[here, :], qkv_w[...])
                shift += jnp.sum(grad, axis=0, keepdims=True)
                scale += jnp.sum(grad * hat, axis=0, keepdims=True)
                total = mid_ref[here, :] + norm_back(grad * (1.0 + mod[1:2]), hat, inverse)
                low = total.astype(BF)
                stream[here, :] = low
                gin_ref[here, :] = nt(low, skip_w[:width, :]).astype(BF)
                gskip_ref[here, :] = nt(low, skip_w[width:, :]).astype(BF)
            sums_ref[utt, 0:1, :] = shift
            sums_ref[utt, 1:2, :] = scale

    chunk = gqkv_ref.shape[1]
    cols = pl.ds(pl.multiple_of(step * chunk, chunk), chunk)
    gqkv_ref[...] = tn(normed[...], grad_ref[:, cols]).astype(BF)
    part = gw_ref.shape[2]
    here = pl.ds(pl.multiple_of(step * part, part), part)
    gw_ref[0] = tn(in_ref[...], stream[:, here]).astype(BF)
    gw_ref[1] = tn(skip_ref[...], stream[:, here]).astype(BF)


def leave_layer(grads, qkv_w, skip_w, res, mid, mods, first, second, raws, arrived, steps=4):
    rows, width = res.shape
    utts = mods.shape[0]
    ins = (grads, qkv_w, skip_w, res, mid, mods, first, second)
    views = [raw.reshape(2, 2, 2, 2, 2, raw.shape[0] // 32, raw.shape[1]) for raw in raws]
    tails = [
        (view.shape[5], cols.size)
        for view in views
        for cols in split_columns(view.shape[-1], (1, 1))
    ]
    anywhere = pl.BlockSpec(memory_space=pl.ANY)
    dma = pltpu.SemaphoreType.DMA
    outs = pl.pallas_call(
        leave_kernel,
        grid=(steps,),
        in_specs=[whole_spec(a.shape) for a in ins] + [anywhere] * 6,
        out_specs=[
            whole_spec((rows, width)),
            whole_spec((rows, width)),
            whole_spec((utts, 8, width)),
            pl.BlockSpec((width, 3 * width // steps), lambda i: (0, i)),
            pl.BlockSpec((2, width, width // steps), lambda i: (0, 0, i)),
        ]
        + [anywhere] * 6,
        out_shape=[
            jax.ShapeDtypeStruct((rows, width), BF),
            jax.ShapeDtypeStruct((rows, width), BF),
            jax.ShapeDtypeStruct((utts, 8, width), F32),
            jax.ShapeDtypeStruct((width, 3 * width), BF),
            jax.ShapeDtypeStruct((2, width, width), BF),
        ]
        + [jax.ShapeDtypeStruct((2, 2) + tail, BF) for tail in tails],
        scratch_shapes=[pltpu.VMEM((rows, width), BF), pltpu.VMEM((rows, width), BF)]
        + [pltpu.VMEM((2, 2, 2) + tail, BF) for tail in tails]
        + [pltpu.VMEM((2, 2) + tail, BF) for tail in tails]
        + [pltpu.VMEM((4, 3, 2, 2, 2, 32, 512), BF)]
        + [dma((6,)), dma((6,)), dma((6,)), dma((12,)), dma((6,))],
        compiler_params=pltpu.CompilerParams(
            vmem_limit_bytes=VMEM_LIMIT, collective_id=4, has_side_effects=True
        ),
        cost_estimate=pl.CostEstimate(
            flops=4 * rows * (skip_w.size + qkv_w.size),
            bytes_accessed=60 * 2**20,
            transcendentals=0,
        ),
        name="leave_layer",
    )(*ins, *views, *arrived)
    return tuple(outs[:4]) + (outs[4].reshape(2 * width, width), outs[5:])


class GradJob:
    def __init__(self, grad, out, cols, dims, order, keep, buffers, loads, sems, base):
        self.grad, self.out, self.cols, self.dims, self.order = grad, out, cols, dims, order
        self.keep, self.buffers, self.loads = keep, buffers, loads
        self.send, self.recv, self.local, self.base = *sems, base
        me, x, core = lax.axis_index("seq"), lax.axis_index("x"), lax.axis_index("core")
        self.bits = (me // 4, (me // 2) % 2, me % 2, x, core)
        self.copies, self.locals, self.round = [], [], 0

    def peer(self, dim):
        me, x, core = lax.axis_index("seq"), lax.axis_index("x"), lax.axis_index("core")
        if dim < 3:
            return (me ^ (4 >> dim), x, core)
        return (me, 1 - x, core) if dim == 3 else (me, x, 1 - core)

    def launch(self, source, target, dim):
        at = self.base + len(self.copies)
        copy = remote(source, target, self.send.at[at], self.recv.at[at], self.peer(dim))
        copy.start()
        self.copies.append(copy)

    def load(self, source, target):
        copy = pltpu.make_async_copy(source, target, self.local.at[self.base + len(self.locals)])
        copy.start()
        self.locals.append(copy)

    def add(self, done, others):
        left = [dim for dim in self.dims if dim not in done]

        def body(i, carry):
            at, place = [self.bits[dim] for dim in self.dims], []
            for n, dim in enumerate(left):
                bit = (i >> (len(left) - 1 - n)) & 1
                at[self.dims.index(dim)] = bit
                place.append(bit)
            total = self.keep[tuple(at)].astype(F32)
            for other in others:
                total = total + (other[tuple(place)] if place else other[...]).astype(F32)
            self.keep[tuple(at)] = total.astype(BF)
            return carry

        lax.fori_loop(0, 2 ** len(left), body, 0)

    def exchange(self, step):
        dim, done = self.order[step], self.order[:step]
        where = tuple(
            1 - self.bits[d] if d == dim else self.bits[d] if d in done else slice(None)
            for d in self.dims
        )
        self.launch(self.keep.at[where], self.buffers[step], dim)

    def advance(self):
        number, self.round = self.round, self.round + 1
        tail, bits = (slice(None), self.cols), self.bits
        steps = len(self.order)
        every = (slice(None),) * len(self.dims)
        if number == 0:
            if self.loads:
                self.load(self.grad.at[every + (bits[4],) + tail], self.keep)
                self.launch(self.grad.at[every + (1 - bits[4],) + tail], self.loads[0], 4)
            else:
                self.load(self.grad, self.keep)
        elif number == 1:
            self.locals[0].wait()
            if self.loads:
                self.copies[0].wait_recv()
                self.add((), self.loads)
            self.exchange(0)
        elif number <= steps + 1:
            self.copies[-1].wait_recv()
            self.add(self.order[: number - 1], [self.buffers[number - 2]])
            if number <= steps:
                self.exchange(number - 1)
            else:
                mine = self.keep.at[tuple(bits[dim] for dim in self.dims)]
                spot = self.out.at[bits[3:5] + tail]
                self.load(mine, spot)
                self.launch(mine, spot, 3)
        elif number == steps + 2:
            self.locals[-1].wait()
            self.copies[-1].wait_recv()
            both = self.out.at[(slice(None), bits[4]) + tail]
            self.launch(both, both, 4)

    def finish(self):
        self.copies[-1].wait_recv()
        for copy in self.copies:
            copy.wait_send()


FULL_ORDERS = ((3, 2, 1, 0), (2, 1, 3, 0), (1, 3, 2, 0))
FOLDED_DIMS = ((0, 1), (0, 2))
FOLDED_ORDERS = ((1, 0), (2, 0))


def reduce_kernel(*refs, halves, folds):
    grads, folded, small = refs[:halves], refs[halves : halves + 2 * folds], refs[halves + 2 * folds]
    refs = refs[halves + 2 * folds + 1 :]
    outs, small_out = refs[: halves + folds], refs[halves + folds]
    rest = list(refs[halves + folds + 1 :])
    small_in, small_low, send, recv, local, ssend, srecv, bsend, brecv, slocal = rest[-10:]
    me, x, core = lax.axis_index("seq"), lax.axis_index("x"), lax.axis_index("core")
    others = [seq_flip(flip) for flip in range(7, 0, -1)]
    mates = [(me, (x + dx) % 2, (core + dc) % 2) for dx, dc in ((0, 1), (1, 0), (1, 1))]
    greet(others + mates)
    jobs = []
    for index, out in enumerate(outs):
        whole = index < halves
        orders = FULL_ORDERS if whole else FOLDED_ORDERS
        for side, cols in enumerate(split_columns(out.shape[-1], (1,) * len(orders))):
            keep = rest.pop(0)
            loads = [rest.pop(0)] if whole else []
            buffers = [rest.pop(0) for _ in orders[side]]
            jobs.append(
                GradJob(
                    grads[index] if whole else folded[2 * (index - halves) + side],
                    out,
                    cols,
                    (0, 1, 2, 3) if whole else FOLDED_DIMS[side],
                    orders[side],
                    keep,
                    buffers,
                    loads,
                    (send, recv, local),
                    7 * len(jobs),
                )
            )
    own = pltpu.make_async_copy(small, small_in.at[me], slocal.at[0])
    own.start()
    smalls = []
    for flip, device in zip(range(7, 0, -1), others):
        smalls.append(remote(small, small_in.at[me], ssend.at[flip], srecv.at[flip], device))
        smalls[-1].start()
    for _ in range(3):
        for job in jobs:
            job.advance()
    own.wait()
    for copy in smalls:
        copy.wait_recv()
    total = small_in[0]
    for index in range(1, 8):
        total = total + small_in[index]
    small_low[...] = total.astype(BF)
    quarter = x * 2 + core
    keep = pltpu.make_async_copy(small_low, small_out.at[quarter], slocal.at[1])
    keep.start()
    lows = []
    for slot, device in enumerate(mates):
        lows.append(remote(small_low, small_out.at[quarter], bsend.at[slot], brecv.at[slot], device))
        lows[-1].start()
    for _ in range(4):
        for job in jobs:
            job.advance()
    for job in jobs:
        job.finish()
    for copy in smalls:
        copy.wait_send()
    keep.wait()
    for copy in lows:
        copy.wait()


def reduce_grads(halves, shapes, folded, small):
    views, outs, buffers, jobs = [], [], [], 0
    for grad in halves:
        rows, width = grad.shape
        views.append(grad.reshape(2, 2, 2, 2, 2, rows // 32, width))
    for index, (rows, width) in enumerate([grad.shape for grad in halves] + list(shapes)):
        span = rows // 32
        outs.append(jax.ShapeDtypeStruct((2, 2, span, width), BF))
        whole = index < len(halves)
        lead, orders = (4, FULL_ORDERS) if whole else (2, FOLDED_ORDERS)
        for cols in split_columns(width, (1,) * len(orders)):
            jobs += 1
            tail = (span, cols.size)
            for left in [lead] * (2 if whole else 1) + list(range(lead - 1, -1, -1)):
                buffers.append(pltpu.VMEM((2,) * left + tail, BF))
    anywhere = pl.BlockSpec(memory_space=pl.ANY)
    dma = pltpu.SemaphoreType.DMA
    outs.append(jax.ShapeDtypeStruct((4,) + small.shape, BF))
    results = pl.pallas_call(
        functools.partial(reduce_kernel, halves=len(halves), folds=len(shapes)),
        in_specs=[anywhere] * (len(halves) + len(folded) + 1),
        out_specs=[anywhere] * len(outs),
        out_shape=outs,
        scratch_shapes=buffers
        + [pltpu.VMEM((8,) + small.shape, F32), pltpu.VMEM(small.shape, BF)]
        + [dma((7 * jobs,))] * 3
        + [dma((8,)), dma((8,)), dma((3,)), dma((3,)), dma((2,))],
        compiler_params=pltpu.CompilerParams(
            vmem_limit_bytes=VMEM_LIMIT, collective_id=3, has_side_effects=True
        ),
        name="reduce_grads",
    )(*views, *folded, small)
    shards = [
        result.reshape(4 * result.shape[2], result.shape[3]).astype(jnp.float32)
        for result in results[:-1]
    ]
    return shards, results[-1].astype(jnp.float32)


def rotary_tables(positions):
    half_dim = HEAD_DIM // 2
    channel = jnp.arange(half_dim, dtype=jnp.float32)
    inverse = jnp.power(10000.0, -2.0 * channel / HEAD_DIM)
    angles = positions.astype(jnp.float32)[:, None] * inverse[None, :]
    angles = jnp.concatenate([angles, angles], axis=1)
    return (jnp.cos(angles), jnp.sin(angles))


def rotate_heads(field, cosine_table, sine_table):
    half_dim = field.shape[-1] // 2
    turned = jnp.concatenate([-field[..., half_dim:], field[..., :half_dim]], axis=-1)
    return field * cosine_table + turned * sine_table


def smooth_gelu(values):
    return jax.nn.gelu(values, approximate=True)


def cross(left, right):
    return lax.dot_general(
        left, right, (((0,), (0,)), ((), ())), preferred_element_type=jnp.float32
    )


def back_product(left, right):
    return lax.dot_general(
        left, right, (((1,), (1,)), ((), ())), preferred_element_type=jnp.float32
    )


def block_terms(query_block, dout_block, lse_block, delta_block, key_block, value_block, key_live):
    scores = jnp.einsum(
        "bqhd,bkhd->bhqk", query_block, key_block, preferred_element_type=jnp.float32
    )
    lse_heads = jnp.transpose(lse_block, (0, 2, 1))[..., None]
    probs = jnp.where(key_live[:, None, None, :], jnp.exp(scores - lse_heads), 0.0)
    grad_probs = jnp.einsum(
        "bqhd,bkhd->bhqk", dout_block, value_block, preferred_element_type=jnp.float32
    )
    delta_heads = jnp.transpose(delta_block, (0, 2, 1))[..., None]
    dscore = (probs * (grad_probs - delta_heads)).astype(jnp.bfloat16)
    return (probs.astype(jnp.bfloat16), dscore)


BATCH = ("x", "core")


def batch_index():
    return lax.axis_index("x") * lax.axis_size("core") + lax.axis_index("core")


def gather_weight(weight):
    parts = lax.axis_size(BATCH)
    if weight.shape[0] % parts:
        return lax.all_gather(weight, "seq", axis=0, tiled=True)
    rows = weight.shape[0] // parts
    mine = lax.dynamic_slice_in_dim(weight, batch_index() * rows, rows, 0)
    return lax.all_gather(mine, ("seq",) + BATCH, axis=0, tiled=True)


def sum_weight(grad):
    rows, width = grad.shape
    low = grad.astype(jnp.bfloat16)
    seq_count, cores = lax.axis_size("seq"), lax.axis_size("core")
    parts = seq_count * lax.axis_size(BATCH)
    if rows % parts or cores != 2:
        shard = lax.psum_scatter(low, "seq", scatter_dimension=0, tiled=True)
        return lax.psum(shard, BATCH).astype(jnp.float32)
    core = lax.axis_index("core")
    held = low.reshape(parts // 2, 2, rows // parts, width)
    send = lax.dynamic_index_in_dim(held, 1 - core, 1, keepdims=False)
    keep = lax.dynamic_index_in_dim(held, core, 1, keepdims=False)
    got = lax.ppermute(send, "core", [(0, 1), (1, 0)])
    half = (keep.astype(jnp.float32) + got.astype(jnp.float32)).astype(jnp.bfloat16)
    half = half.reshape(rows // 2, width)
    shard = lax.psum_scatter(half, ("seq", "x"), scatter_dimension=0, tiled=True)
    return lax.all_gather(shard, BATCH, axis=0, tiled=True).astype(jnp.float32)


def gather_kernel(*refs, count, ahead, block):
    weights, laters = refs[:count], refs[count : count + ahead]
    refs = refs[count + ahead :]
    seq_small, batch_small, first, second, cos_ref, sin_ref = refs[:6]
    outs = refs[6:]
    fulls, helds = outs[:count], outs[count : count + ahead]
    batch_out, mod_out, res_out, proj_out = outs[count + ahead : count + ahead + 4]
    (
        seq_out, mods, skip_w, qkv_w, res, proj,
        send, recv, asend, arecv, small_send, small_recv, local, lift, put,
    ) = outs[count + ahead + 4 :]
    me, x, core = lax.axis_index("seq"), lax.axis_index("x"), lax.axis_index("core")
    bits = (me // 4, (me // 2) % 2, me % 2, x, core)

    def peer(dim):
        if dim < 3:
            return (me ^ (4 >> dim), x, core)
        return (me, 1 - x, core) if dim == 3 else (me, x, 1 - core)

    others = [((me + d) % 8, x, core) for d in range(1, 8)]
    mates = [(me, (x + dx) % 2, (core + dc) % 2) for dx, dc in ((0, 1), (1, 0), (1, 1))]
    barrier = pltpu.get_barrier_semaphore()
    for device in others + mates:
        pl.semaphore_signal(barrier, inc=1, device_id=device, device_id_type=pl.DeviceIdType.MESH)
    pl.semaphore_wait(barrier, len(others) + len(mates))

    small = []
    quarter = x * 2 + core
    own_seq = pltpu.make_async_copy(seq_small, seq_out.at[me], local.at[0])
    own_batch = pltpu.make_async_copy(batch_small, batch_out.at[quarter], local.at[1])
    own_seq.start()
    own_batch.start()
    for slot, device in enumerate(others):
        small.append(
            pltpu.make_async_remote_copy(
                seq_small, seq_out.at[me], small_send.at[slot], small_recv.at[slot],
                device_id=device, device_id_type=pl.DeviceIdType.MESH,
            )
        )
    for slot, device in enumerate(mates):
        small.append(
            pltpu.make_async_remote_copy(
                batch_small, batch_out.at[quarter], small_send.at[7 + slot], small_recv.at[7 + slot],
                device_id=device, device_id_type=pl.DeviceIdType.MESH,
            )
        )
    for copy in small:
        copy.start()

    jobs = early_jobs(weights, fulls)
    chain = WeightGather(jobs, send, recv, local.at[pl.ds(2, len(jobs))])
    chain.stage()
    chain.stage()
    late = []
    for index, (weight, held) in enumerate(zip(laters, helds)):
        source = quarter_of(weight, pl.ds(0, weight.shape[1]))
        spot = held.at[me // 4, (me // 2) % 2]
        own = pltpu.make_async_copy(source, spot, local.at[2 + len(jobs) + index])
        own.start()
        late.append(own)
        for flip in (2, 3, 1):
            at = 3 * index + flip - 1
            copy = remote(source, spot, asend.at[at], arecv.at[at], seq_flip(2 * flip))
            copy.start()
            late.append(copy)
    for copy in small:
        copy.wait()
    own_seq.wait()
    own_batch.wait()
    total = seq_out[0]
    for index in range(1, 8):
        total = total + seq_out[index]
    mod_out[...] = total
    utts = mods.shape[0]
    for utt in range(utts):
        mods[utt, 0:6, :] = total[utt * 6 : utt * 6 + 6]
    chain.stage()
    chain.stage()
    chain.stage()
    chain.finish()
    for index, (full, flat) in enumerate(zip(fulls, (skip_w, qkv_w))):
        span = full.shape[5]

        def carry_in(p, carry):
            bits = (p // 16, (p // 8) % 2, (p // 4) % 2, (p // 2) % 2, p % 2)
            rows = pl.ds(pl.multiple_of(p * span, span), span)
            pltpu.make_async_copy(full.at[bits], flat.at[rows, :], lift.at[index]).start()
            return carry

        lax.fori_loop(0, 32, carry_in, 0)
    for index, flat in enumerate((skip_w, qkv_w)):
        pltpu.make_async_copy(flat, flat, lift.at[index]).wait()
    rows, width = first.shape
    steps = rows // utts // block

    def enter(i, carry):
        here = pl.ds(pl.multiple_of(i * block, block), block)
        table = pl.ds(pl.multiple_of((i % steps) * block, block), block)
        mod = mods[i // steps]
        residual = nn(first[here, :], skip_w[:width, :]) + nn(second[here, :], skip_w[width:, :])
        res[here, :] = residual
        hat, _ = layer_norm(residual)
        normed = (hat * (1.0 + mod[1:2]) + mod[0:1]).astype(BF)
        lane = lanes_of(block)
        cos, sin = cos_ref[table, :], sin_ref[table, :]
        for part in range(3):
            projected = nn(normed, qkv_w[:, part * width : (part + 1) * width])
            for group in range(width // 128):
                cols = slice(group * 128, group * 128 + 128)
                piece = projected[:, cols]
                if part < 2:
                    turned = jnp.where(
                        (lane & 63) < 32, pltpu.roll(piece, 96, 1), pltpu.roll(piece, 32, 1)
                    )
                    piece = piece * cos + turned * sin
                if part == 0:
                    piece = piece * (0.125 * LOG2E)
                proj[part, here, cols] = piece.astype(BF)
        pltpu.make_async_copy(res.at[here, :], res_out.at[here, :], put.at[0]).start()
        pltpu.make_async_copy(proj.at[:, here, :], proj_out.at[:, here, :], put.at[1]).start()
        return carry

    lax.fori_loop(0, rows // block, enter, 0)
    for copy in late:
        copy.wait()
    pltpu.make_async_copy(res, res_out, put.at[0]).wait()
    pltpu.make_async_copy(proj, proj_out, put.at[1]).wait()


def gather_early(weights, laters, seq_small, batch_small, first, second, cos, sin, block=256):
    anywhere = pl.BlockSpec(memory_space=pl.ANY)
    vmem = pl.BlockSpec(memory_space=pltpu.VMEM)
    jobs, ahead = 4 * len(weights), len(laters)
    rows, width = first.shape
    dma = pltpu.SemaphoreType.DMA
    quarter = lambda lead, w: jax.ShapeDtypeStruct((2,) * lead + (w.shape[0] // 4, w.shape[1]), BF)
    outs = pl.pallas_call(
        functools.partial(gather_kernel, count=len(weights), ahead=ahead, block=block),
        in_specs=[anywhere] * (len(weights) + ahead + 2) + [vmem] * 4,
        out_specs=[anywhere] * (len(weights) + ahead + 1) + [vmem] + [anywhere] * 2,
        out_shape=[quarter(5, w) for w in weights]
        + [quarter(2, w) for w in laters]
        + [
            jax.ShapeDtypeStruct((4,) + batch_small.shape, F32),
            jax.ShapeDtypeStruct(seq_small.shape, F32),
            jax.ShapeDtypeStruct((rows, width), F32),
            jax.ShapeDtypeStruct((3, rows, width), BF),
        ],
        scratch_shapes=[
            pltpu.VMEM((8,) + seq_small.shape, F32),
            pltpu.VMEM((seq_small.shape[0] // 6, 8, width), F32),
        ]
        + [pltpu.VMEM((8 * w.shape[0], w.shape[1]), BF) for w in weights]
        + [
            pltpu.VMEM((rows, width), F32),
            pltpu.VMEM((3, rows, width), BF),
            dma((5 * jobs,)),
            dma((5 * jobs,)),
            dma((5 * ahead,)),
            dma((5 * ahead,)),
            dma((10,)),
            dma((10,)),
            dma((2 + jobs + ahead,)),
            dma((2,)),
            dma((2,)),
        ],
        compiler_params=pltpu.CompilerParams(
            vmem_limit_bytes=VMEM_LIMIT, collective_id=0, has_side_effects=True
        ),
        name="gather_early",
    )(*weights, *laters, seq_small, batch_small, first, second, cos, sin)
    fulls = [full.reshape(8 * w.shape[0], w.shape[1]) for full, w in zip(outs, weights)]
    return fulls, outs[len(weights) : len(weights) + ahead], *outs[-4:]


def paired_tables(count):
    half = HEAD_DIM // 2
    inverse = np.power(10000.0, -2.0 * np.arange(half) / HEAD_DIM)
    angles = np.arange(count)[:, None] * inverse[None, :]
    cos, sin = np.cos(angles), np.sin(angles)
    tables = (np.tile(cos, (1, 4)), np.tile(np.concatenate([-sin, sin], axis=1), (1, 2)))
    return tuple(jnp.asarray(table, jnp.float32) for table in tables)


def on_device(
    layer_input,
    skip_input,
    time_embed,
    lengths,
    cond_drop,
    cotangent,
    skip_weight,
    adaln_weight,
    adaln_bias,
    qkv_weight,
    out_weight,
    up_weight,
    down_weight,
):
    utt_count, frame_span, model_width = layer_input.shape
    head_count = model_width // HEAD_DIM
    row_count = utt_count * frame_span
    seq_here = lax.axis_index("seq")
    seq_count = lax.axis_size("seq")
    frame_count = frame_span * seq_count
    by_heads = (
        seq_count == 8
        and head_count == 16
        and utt_count == 2
        and lax.axis_size(BATCH) == 4
        and frame_span == 512
    )
    local_pos = seq_here * frame_span + jnp.arange(frame_span, dtype=jnp.int32)
    local_live = local_pos[None, :] < lengths[:, None]
    valid_mask = local_live.astype(jnp.float32)
    drop = cond_drop.astype(jnp.float32)
    dropped = drop[:, None] * valid_mask
    frames_live = jnp.minimum(lengths, frame_count).astype(jnp.float32)
    counts = jnp.stack([jnp.sum((1.0 - drop) * frames_live), jnp.sum(drop * frames_live)])
    silu_time = jax.nn.silu(time_embed.astype(jnp.float32)).astype(jnp.bfloat16)
    row_span = adaln_weight.shape[0]
    silu_mine = lax.dynamic_slice_in_dim(silu_time, seq_here * row_span, row_span, 1)
    mod_part = jnp.dot(silu_mine, adaln_weight, preferred_element_type=jnp.float32)
    bias_span = adaln_bias.shape[0]
    bias_here = lax.dynamic_update_slice_in_dim(
        jnp.zeros((mod_part.shape[1],), jnp.float32),
        adaln_bias.astype(jnp.float32),
        seq_here * bias_span,
        0,
    )
    mod_part = mod_part + bias_here
    if by_heads:
        small = jnp.concatenate(
            [
                silu_time.astype(jnp.float32),
                jnp.pad(counts[None, :], ((0, 5), (0, model_width - 2))),
            ],
            axis=0,
        )
        cos_all, sin_all = paired_tables(frame_count)
        first_rows = layer_input.reshape(row_count, model_width)
        second_rows = skip_input.reshape(row_count, model_width)
        gathered = gather_early(
            (skip_weight, qkv_weight),
            (out_weight, up_weight, down_weight),
            mod_part.reshape(-1, model_width),
            small,
            first_rows,
            second_rows,
            lax.dynamic_slice_in_dim(cos_all, seq_here * frame_span, frame_span, 0),
            lax.dynamic_slice_in_dim(sin_all, seq_here * frame_span, frame_span, 0),
        )
        (skip_full, qkv_full), late_held, small_every, modulation, residual_rows, proj = gathered
        totals = jnp.sum(small_every[:, utt_count, :2], axis=0)
        silu_every = small_every[:, :utt_count].reshape(-1, model_width)
    else:
        modulation = lax.psum(mod_part, "seq")
        totals = lax.psum(counts, BATCH)
        skip_full = gather_weight(skip_weight)
        qkv_full = gather_weight(qkv_weight)
        silu_every = lax.all_gather(silu_time, BATCH, axis=0, tiled=True).astype(jnp.float32)
    modulation = modulation.reshape(utt_count, 6, model_width)
    kept_total = jnp.maximum(totals[0], 1.0)
    drop_total = jnp.maximum(totals[1], 1.0)
    every_count = kept_total + drop_total
    loss_weight = (valid_mask - dropped) * (every_count / (2.0 * kept_total)) + dropped * (
        every_count / (2.0 * drop_total)
    )
    if by_heads:
        (qkv_all, out_all, lse_all, attended_low), (out_full, up_full, down_full) = attend_forward(
            lengths, proj, *late_held, frame_span
        )
    else:
        joined = jnp.concatenate([layer_input, skip_input], axis=-1).reshape(row_count, 2 * model_width)
        residual_in = jnp.dot(joined, skip_full, preferred_element_type=jnp.float32).reshape(
            utt_count, frame_span, model_width
        )
        shift_attn = modulation[:, 0][:, None, :]
        scale_attn = modulation[:, 1][:, None, :]
        hat_attn, inv_attn = layer_norm(residual_in)
        normed_attn = (
            (hat_attn * (1.0 + scale_attn) + shift_attn)
            .astype(jnp.bfloat16)
            .reshape(row_count, model_width)
        )
        residual_rows = residual_in.reshape(row_count, model_width)
        out_full, up_full, down_full = [
            gather_weight(weight) for weight in (out_weight, up_weight, down_weight)
        ]
        projected = jnp.dot(normed_attn, qkv_full, preferred_element_type=jnp.float32).reshape(
            utt_count, frame_span, 3, head_count, HEAD_DIM
        )
        cosine_table, sine_table = rotary_tables(local_pos)
        cosine_table = cosine_table[None, :, None, :]
        sine_table = sine_table[None, :, None, :]
        queries = (rotate_heads(projected[:, :, 0], cosine_table, sine_table) * 0.125).astype(
            jnp.bfloat16
        )
        keys_rot = rotate_heads(projected[:, :, 1], cosine_table, sine_table).astype(jnp.bfloat16)
        values = projected[:, :, 2].astype(jnp.bfloat16)
        start_top = jnp.full((utt_count, head_count, frame_span), MASKED, jnp.float32)
        top_score = start_top
        key_piece = lax.all_gather(keys_rot, "seq", axis=1, tiled=True)
        value_piece = lax.all_gather(values, "seq", axis=1, tiled=True)
        piece_len = key_piece.shape[1]
        piece_live = jnp.arange(piece_len, dtype=jnp.int32)[None, :] < lengths[:, None]
        scores = jnp.einsum("bqhd,bkhd->bhqk", queries, key_piece, preferred_element_type=jnp.float32)
        scores = jnp.where(piece_live[:, None, None, :], scores, MASKED)
        new_top = jnp.maximum(top_score, jnp.max(scores, axis=-1))
        expo = jnp.where(piece_live[:, None, None, :], jnp.exp(scores - new_top[..., None]), 0.0)
        denom = jnp.sum(expo, axis=-1)
        partial_out = jnp.einsum(
            "bhqk,bkhd->bqhd",
            expo.astype(jnp.bfloat16),
            value_piece,
            preferred_element_type=jnp.float32,
        )
        accum = partial_out
        accum, top_score, denom = (accum, new_top, denom)
        attended_full = accum / jnp.transpose(denom, (0, 2, 1))[..., None]
        lse_rows = jnp.transpose(top_score + jnp.log(denom), (0, 2, 1))
        attended_low = attended_full.astype(jnp.bfloat16).reshape(row_count, model_width)
    cot_rows = cotangent.reshape(row_count, model_width)
    weight_rows = loss_weight.reshape(row_count, 1)
    branch_attn, hidden_act, hidden_slope, grad_branch_ffn, layer_output, grad_gate_ffn = ffn_forward(
        attended_low,
        out_full,
        residual_rows,
        modulation,
        cot_rows,
        weight_rows,
        up_full,
        down_full,
    )
    layer_output = layer_output.reshape(utt_count, frame_span, model_width)
    grad_up, grad_down, grad_mid, grad_attended_flat, grad_out, ffn_sums = ffn_backward(
        attended_low,
        out_full,
        residual_rows,
        branch_attn,
        modulation,
        cot_rows,
        weight_rows,
        grad_branch_ffn,
        hidden_act,
        hidden_slope,
        up_full,
        down_full,
    )
    grad_shift_ffn, grad_scale_ffn, grad_gate_attn = ffn_sums[:, 0], ffn_sums[:, 1], ffn_sums[:, 2]
    if by_heads:
        grad_projected, *arrived = attend_backward(
            lengths,
            grad_attended_flat,
            qkv_all,
            out_all,
            lse_all,
            cos_all,
            sin_all,
            (grad_down, grad_up, grad_out),
            frame_span,
        )
    else:
        grad_attended = grad_attended_flat.reshape(
            utt_count, frame_span, head_count, HEAD_DIM
        )
        delta_rows = jnp.sum(grad_attended.astype(jnp.float32) * attended_full, axis=-1)
        lse_all, delta_all = (
            lax.all_gather(lse_rows, "seq", axis=1, tiled=True),
            lax.all_gather(delta_rows, "seq", axis=1, tiled=True),
        )
        key_piece = lax.all_gather(keys_rot, "seq", axis=1, tiled=True)
        value_piece = lax.all_gather(values, "seq", axis=1, tiled=True)
        piece_len = key_piece.shape[1]
        piece_live = jnp.arange(piece_len, dtype=jnp.int32)[None, :] < lengths[:, None]
        probs_low, dscore = block_terms(
            queries, grad_attended, lse_rows, delta_rows, key_piece, value_piece, piece_live
        )
        grad_queries = jnp.einsum(
            "bhqk,bkhd->bqhd", dscore, key_piece, preferred_element_type=jnp.float32
        )
        query_piece = lax.all_gather(queries, "seq", axis=1, tiled=True)
        dout_piece = lax.all_gather(grad_attended, "seq", axis=1, tiled=True)
        probs_low, dscore = block_terms(
            query_piece, dout_piece, lse_all, delta_all, keys_rot, values, local_live
        )
        grad_k = jnp.einsum("bhqk,bqhd->bkhd", dscore, query_piece, preferred_element_type=jnp.float32)
        grad_v = jnp.einsum(
            "bhqk,bqhd->bkhd", probs_low, dout_piece, preferred_element_type=jnp.float32
        )
        grad_q_pre = rotate_heads(grad_queries * 0.125, cosine_table, -sine_table)
        grad_k_pre = rotate_heads(grad_k, cosine_table, -sine_table)
        grad_projected = (
            jnp.stack([grad_q_pre, grad_k_pre, grad_v], axis=2)
            .reshape(row_count, 3 * model_width)
            .astype(jnp.bfloat16)
        )
    if by_heads:
        grad_input, grad_skip, attn_sums, grad_qkv, grad_skip_w, folded = leave_layer(
            grad_projected,
            qkv_full,
            skip_full,
            residual_rows,
            grad_mid,
            modulation,
            first_rows,
            second_rows,
            (grad_down, grad_up, grad_out),
            arrived,
        )
        grad_input = grad_input.reshape(layer_input.shape)
        grad_skip = grad_skip.reshape(skip_input.shape)
        grad_shift_attn, grad_scale_attn = attn_sums[:, 0], attn_sums[:, 1]
    else:
        grad_mid = grad_mid.reshape(utt_count, frame_span, model_width)
        grad_qkv = cross(normed_attn, grad_projected)
        grad_normed_attn = back_product(grad_projected, qkv_full).reshape(
            utt_count, frame_span, model_width
        )
        grad_shift_attn = jnp.sum(grad_normed_attn, axis=1)
        grad_scale_attn = jnp.sum(grad_normed_attn * hat_attn, axis=1)
        grad_stream = grad_mid + norm_back(grad_normed_attn * (1.0 + scale_attn), hat_attn, inv_attn)
        grad_stream_low = grad_stream.astype(jnp.bfloat16).reshape(row_count, model_width)
        grad_skip_w = cross(joined, grad_stream_low)
        grad_joined = back_product(grad_stream_low, skip_full)
        grad_input = (
            grad_joined[:, :model_width]
            .reshape(utt_count, frame_span, model_width)
            .astype(jnp.bfloat16)
        )
        grad_skip = (
            grad_joined[:, model_width:]
            .reshape(utt_count, frame_span, model_width)
            .astype(jnp.bfloat16)
        )
    grad_modulation = jnp.stack(
        [
            grad_shift_attn,
            grad_scale_attn,
            grad_gate_attn,
            grad_shift_ffn,
            grad_scale_ffn,
            grad_gate_ffn,
        ],
        axis=1,
    ).reshape(utt_count, 6 * model_width)
    weight_grads = (grad_skip_w, grad_qkv, grad_out, grad_up, grad_down)
    if by_heads:
        shards, mod_every = reduce_grads(
            (grad_qkv, grad_skip_w),
            [grad.shape for grad in (grad_down, grad_up, grad_out)],
            folded,
            grad_modulation.reshape(-1, model_width),
        )
        summed = [shards[i] for i in (1, 0, 4, 3, 2)]
        mod_every = mod_every.reshape(-1, 6 * model_width)
    else:
        mod_total = lax.psum(grad_modulation, "seq")
        mod_every = lax.all_gather(
            mod_total.astype(jnp.bfloat16), BATCH, axis=0, tiled=True
        ).astype(jnp.float32)
        summed = [sum_weight(grad) for grad in weight_grads]
    silu_rows = lax.dynamic_slice_in_dim(silu_every, seq_here * row_span, row_span, 1)
    adaln_rows = jnp.dot(silu_rows.T, mod_every, precision=lax.Precision.HIGHEST)
    bias_rows = lax.dynamic_slice_in_dim(
        jnp.sum(mod_every, axis=0), seq_here * bias_span, bias_span, 0
    )
    results = (summed[0], adaln_rows, bias_rows, summed[1], summed[2], summed[3], summed[4])
    return (
        layer_output,
        grad_input,
        grad_skip,
        results[0],
        results[1],
        results[2],
        results[3],
        results[4],
        results[5],
        results[6],
    )


def solution(mesh):
    count, batch = mesh.shape["seq"], mesh.shape["batch"]
    cores = 2 if batch % 2 == 0 else 1
    split = Mesh(mesh.devices.reshape(count, batch // cores, cores), ("seq",) + BATCH)
    placed = (
        P(BATCH, "seq", None),
        P(BATCH, "seq", None),
        P(BATCH, None),
        P(BATCH),
        P(BATCH),
        P(BATCH, "seq", None),
        P("seq", None),
        P("seq", None),
        P("seq"),
        P("seq", None),
        P("seq", None),
        P("seq", None),
        P("seq", None),
    )
    return jax.shard_map(
        on_device,
        mesh=split,
        in_specs=placed,
        out_specs=(
            P(BATCH, "seq", None),
            P(BATCH, "seq", None),
            P(BATCH, "seq", None),
            P("seq", None),
            P("seq", None),
            P("seq"),
            P("seq", None),
            P("seq", None),
            P("seq", None),
            P("seq", None),
        ),
        check_vma=False,
    )
```

```python
import functools
import jax
import jax.numpy as jnp
import numpy as np
from jax import lax
from jax.sharding import Mesh, PartitionSpec as P
from jax.experimental import pallas as pl
from jax.experimental.pallas import tpu as pltpu
HEAD_DIM = 64
EPS = 1e-06
LOG2E = 1.4426950408889634
LN2 = 0.6931471805599453
MASKED = -1e30
BF = jnp.bfloat16
F32 = jnp.float32
VMEM_LIMIT = 60 * 2**20


def nt(left, right):
    return lax.dot_general(left, right, (((1,), (1,)), ((), ())), preferred_element_type=F32)


def nn(left, right):
    return lax.dot_general(left, right, (((1,), (0,)), ((), ())), preferred_element_type=F32)


def head_sums(product, lane):
    first = jnp.sum(jnp.where(lane < 64, product, 0.0), axis=1, keepdims=True)
    second = jnp.sum(jnp.where(lane >= 64, product, 0.0), axis=1, keepdims=True)
    return (first, second)


def lanes_of(rows):
    return lax.broadcasted_iota(jnp.int32, (rows, 128), 1)


def attention_cost(frames, products):
    return pl.CostEstimate(
        flops=2 * products * 2 * frames * frames * 128,
        bytes_accessed=frames * 128 * 2 * 8,
        transcendentals=2 * frames * frames,
    )


def turn_back(grad, cos, sin):
    lane = lanes_of(grad.shape[0])
    turned = jnp.where((lane & 63) < 32, pltpu.roll(grad, 96, 1), pltpu.roll(grad, 32, 1))
    return grad * cos - turned * sin


def three(column, lane, at):
    high = column.astype(BF).astype(F32)
    rest = column - high
    mid = rest.astype(BF).astype(F32)
    low = rest - mid
    return jnp.where(lane == at, -high, jnp.where(lane == at + 1, -mid, jnp.where(lane == at + 2, -low, 0.0)))


MESH_IDS = pl.DeviceIdType.MESH


def seq_flip(flip):
    return (lax.axis_index("seq") ^ flip, lax.axis_index("x"), lax.axis_index("core"))


def greet(devices):
    barrier = pltpu.get_barrier_semaphore()
    for device in devices:
        pl.semaphore_signal(barrier, inc=1, device_id=device, device_id_type=MESH_IDS)
    pl.semaphore_wait(barrier, len(devices))


def far_first(at, count):
    near = lax.axis_index("seq") // 4
    return (at + (count // 2) * (1 - near)) % count


def remote(source, target, send, recv, device):
    return pltpu.make_async_remote_copy(
        source, target, send, recv, device_id=device, device_id_type=MESH_IDS
    )


class WeightGather:
    def __init__(self, jobs, send, recv, local):
        self.jobs, self.send, self.recv, self.local = jobs, send, recv, local
        me, x, core = lax.axis_index("seq"), lax.axis_index("x"), lax.axis_index("core")
        self.bits = (me // 4, (me // 2) % 2, me % 2, x, core)
        self.copies = [[] for _ in jobs]
        self.owns = []

    def peer(self, dim):
        me, x, core = lax.axis_index("seq"), lax.axis_index("x"), lax.axis_index("core")
        if dim < 3:
            return (me ^ (4 >> dim), x, core)
        return (me, 1 - x, core) if dim == 3 else (me, x, 1 - core)

    def stage(self):
        for index, (full, cols, source, ready, order) in enumerate(self.jobs):
            at = len(self.copies[index])
            where = tuple(
                slice(None) if d in ready + order[:at] else self.bits[d]
                for d in range(len(full.shape) - 2)
            ) + (slice(None), cols)
            if at == 0:
                own = pltpu.make_async_copy(source, full.at[where], self.local.at[index])
                own.start()
                self.owns.append(own)
            else:
                if at == 1:
                    self.owns[index].wait()
                self.copies[index][at - 1].wait_recv()
            copy = remote(
                source if at == 0 else full.at[where],
                full.at[where],
                self.send.at[index * 5 + at],
                self.recv.at[index * 5 + at],
                self.peer(order[at]),
            )
            copy.start()
            self.copies[index].append(copy)

    def finish(self):
        for chain in self.copies:
            chain[-1].wait_recv()
        for chain in self.copies:
            for copy in chain:
                copy.wait_send()


def split_columns(width, shares):
    total, start, out = sum(shares), 0, []
    for n in range(len(shares)):
        stop = width * sum(shares[: n + 1]) // total // 128 * 128
        out.append(pl.ds(start, stop - start))
        start = stop
    return out


def quarter_of(weight, cols):
    quarter = lax.axis_index("x") * 2 + lax.axis_index("core")
    span = weight.shape[0] // 4
    return weight.at[pl.ds(quarter * span, span), cols]


def early_jobs(weights, fulls):
    orders = ((0, 1, 2, 3, 4), (0, 1, 3, 2, 4)) * 2
    return [
        (full, cols, quarter_of(weight, cols), (), order)
        for weight, full in zip(weights, fulls)
        for cols, order in zip(split_columns(weight.shape[1], (1,) * 4), orders)
    ]


def late_jobs(helds, fulls):
    return [
        (full, cols, held.at[:, :, :, cols], (0, 1), order)
        for held, full in zip(helds, fulls)
        for cols, order in zip(split_columns(held.shape[3], (2, 1)), ((2, 3, 4), (3, 2, 4)))
    ]


def attend_forward_kernel(
    len_ref, proj, out_w, up_w, down_w,
    qkv_all, o_all, lse_ref, att, out_full, up_full, down_full,
    qkv, outs, ka, kb, vta, vtb,
    wsend, wrecv, wlocal, qsend, qrecv, qlocal, osend, orecv, olocal, slocal,
    *, span, bq, bk,
):
    me, x, core = lax.axis_index("seq"), lax.axis_index("x"), lax.axis_index("core")
    frames = qkv.shape[2]
    mine = pl.ds(pl.multiple_of(me * span, span), span)
    my_cols = pl.ds(pl.multiple_of(me * 128, 128), 128)
    flips = (7, 6, 5, 4, 3, 2, 1)
    greet([seq_flip(flip) for flip in flips] + [(me, 1 - x, core), (me, x, 1 - core)])
    weights = WeightGather(
        late_jobs((out_w, up_w, down_w), (out_full, up_full, down_full)), wsend, wrecv, wlocal
    )

    def send_heads(utt):
        rows = pl.ds(utt * span, span)
        own = pltpu.make_async_copy(
            proj.at[:, rows, my_cols], qkv.at[utt, :, mine, :], qlocal.at[utt]
        )
        own.start()
        copies = []
        for flip in flips:
            there = me ^ flip
            cols = pl.ds(pl.multiple_of(there * 128, 128), 128)
            copy = remote(
                proj.at[:, rows, cols],
                qkv.at[utt, :, mine, :],
                qsend.at[utt * 8 + flip],
                qrecv.at[utt * 8 + flip],
                seq_flip(flip),
            )
            copy.start()
            copies.append(copy)
        return own, copies

    def arrive(sent):
        own, copies = sent
        own.wait()
        for copy in copies:
            copy.wait_recv()

    def send_out(utt, there):
        rows = pl.ds(pl.multiple_of(there * span, span), span)
        target = att.at[pl.ds(utt * span, span), my_cols]

        @pl.when(there != me)
        def _():
            remote(
                outs.at[utt, rows, :],
                target,
                osend.at[utt * 8 + (there ^ me)],
                orecv.at[utt * 8 + (there ^ me)],
                (there, x, core),
            ).start()

        @pl.when(there == me)
        def _():
            pltpu.make_async_copy(outs.at[utt, rows, :], target, olocal.at[utt]).start()

    def attend(utt, between):
        length = len_ref[utt]
        save = pltpu.make_async_copy(qkv.at[utt], qkv_all.at[utt], slocal.at[utt])
        save.start()

        def build(j, carry):
            rows = pl.ds(pl.multiple_of(j * bk, bk), bk)
            lane = lanes_of(bk)
            pos = j * bk + lax.broadcasted_iota(jnp.int32, (bk, 128), 0)
            bias = jnp.where(pos < length, 0.0, MASKED)
            keys = qkv[utt, 1, rows, :].astype(F32)
            ka[rows, :] = jnp.where(lane < 64, keys, jnp.where(lane == 64, bias, 0.0)).astype(BF)
            kb[rows, :] = jnp.where(lane >= 64, keys, jnp.where(lane == 0, bias, 0.0)).astype(BF)
            vals = qkv[utt, 2, rows, :].astype(F32)
            vta[:, rows] = jnp.where(lane < 64, vals, 1.0).T.astype(BF)
            vtb[:, rows] = jnp.where(lane >= 64, vals, 1.0).T.astype(BF)
            return carry

        lax.fori_loop(0, frames // bk, build, 0)

        def block(i_at, carry):
            i = far_first(i_at, frames // bq)
            here = pl.ds(pl.multiple_of(i * bq, bq), bq)
            lane = lanes_of(bq)
            queries = qkv[utt, 0, here, :].astype(F32)
            qa = jnp.where(lane < 64, queries, jnp.where(lane == 64, 1.0, 0.0)).astype(BF)
            qb = jnp.where(lane >= 64, queries, jnp.where(lane == 0, 1.0, 0.0)).astype(BF)

            def body(j, inner):
                rows = pl.ds(pl.multiple_of(j * bk, bk), bk)
                result = []
                scores = [nt(ka[rows, :], qa), nt(kb[rows, :], qb)]
                for score, vt, (top, acc) in zip(scores, (vta, vtb), inner):
                    new = jnp.maximum(top, jnp.max(score, axis=0, keepdims=True))
                    probs = jnp.exp2(score - new).astype(BF)
                    acc = acc * jnp.exp2(top - new) + nn(vt[:, rows], probs)
                    result.append((new, acc))
                return tuple(result)

            start = (jnp.full((1, bq), MASKED, F32), jnp.zeros((128, bq), F32))
            (top_a, acc_a), (top_b, acc_b) = lax.fori_loop(0, frames // bk, body, (start, start))
            sum_a, sum_b = acc_a[64:65], acc_b[0:1]
            both = jnp.concatenate([acc_a[:64] / sum_a, acc_b[64:] / sum_b], axis=0)
            outs[utt, here, :] = both.T.astype(BF)
            lse_ref[utt, :, here] = jnp.concatenate(
                [top_a + jnp.log2(sum_a), top_b + jnp.log2(sum_b), jnp.zeros((6, bq), F32)],
                axis=0,
            )
            if utt == 1:
                for part in range(bq // span):
                    send_out(utt, i * (bq // span) + part)
            return carry

        most = frames // bq - 1
        lax.fori_loop(0, most, block, 0)
        between()
        lax.fori_loop(most, most + 1, block, 0)
        keep = pltpu.make_async_copy(outs.at[utt], o_all.at[utt], slocal.at[2 + utt])
        keep.start()
        return [save, keep]

    first = send_heads(0)
    weights.stage()
    arrive(first)
    second = send_heads(1)
    weights.stage()
    saves = attend(0, lambda: None)
    arrive(second)

    def send_first(i, carry):
        send_out(0, i)
        return carry

    lax.fori_loop(0, 8, send_first, 0)
    saves += attend(1, weights.stage)
    for sent in (first, second):
        for copy in sent[1]:
            copy.wait_send()
    weights.finish()
    for save in saves:
        save.wait()
    for utt in range(2):
        target = att.at[pl.ds(utt * span, span), my_cols]
        pltpu.make_async_copy(outs.at[utt, mine, :], target, olocal.at[utt]).wait()
        for flip in flips:
            copy = remote(
                outs.at[utt, mine, :],
                target,
                osend.at[utt * 8 + flip],
                orecv.at[utt * 8 + flip],
                seq_flip(flip),
            )
            copy.wait_send()
            copy.wait_recv()


def attend_forward(lengths, proj, out_w, up_w, down_w, span, bq=1024, bk=512):
    rows, width = proj.shape[1:]
    frames = 8 * span
    anywhere = pl.BlockSpec(memory_space=pl.ANY)
    vmem = pl.BlockSpec(memory_space=pltpu.VMEM)
    full = lambda w: jax.ShapeDtypeStruct((2, 2, 2, 2, 2) + w.shape[2:], BF)
    dma = pltpu.SemaphoreType.DMA
    outs = pl.pallas_call(
        functools.partial(attend_forward_kernel, span=span, bq=bq, bk=bk),
        in_specs=[pl.BlockSpec(memory_space=pltpu.SMEM)] + [anywhere] * 4,
        out_specs=[anywhere, anywhere, vmem] + [anywhere] * 4,
        out_shape=[
            jax.ShapeDtypeStruct((2, 3, frames, 128), BF),
            jax.ShapeDtypeStruct((2, frames, 128), BF),
            jax.ShapeDtypeStruct((2, 8, frames), F32),
            jax.ShapeDtypeStruct((rows, width), BF),
            full(out_w),
            full(up_w),
            full(down_w),
        ],
        scratch_shapes=[
            pltpu.VMEM((2, 3, frames, 128), BF),
            pltpu.VMEM((2, frames, 128), BF),
            pltpu.VMEM((frames, 128), BF),
            pltpu.VMEM((frames, 128), BF),
            pltpu.VMEM((128, frames), BF),
            pltpu.VMEM((128, frames), BF),
            dma((30,)),
            dma((30,)),
            dma((6,)),
            dma((16,)),
            dma((16,)),
            dma((2,)),
            dma((16,)),
            dma((16,)),
            dma((2,)),
            dma((4,)),
        ],
        compiler_params=pltpu.CompilerParams(
            vmem_limit_bytes=VMEM_LIMIT, collective_id=1, has_side_effects=True
        ),
        cost_estimate=attention_cost(frames, 4),
        name="attend_forward",
    )(lengths, proj, out_w, up_w, down_w)
    fulls = [
        outs[4 + i].reshape(32 * w.shape[2], w.shape[3]) for i, w in enumerate((out_w, up_w, down_w))
    ]
    return outs[:4], fulls


def attend_backward_kernel(
    len_ref, dout, qkv_all, o_all, lse_ref, cos_ref, sin_ref, raw_a, raw_b, raw_c,
    grads, got_a, got_b, got_c,
    qkv, outs, douts, qa, qb, da, db, qt, dt, dqa, dqb,
    dsend, drecv, dlocal, gsend, grecv, glocal, load, rsend, rrecv,
    *, span, block,
):
    me, x, core = lax.axis_index("seq"), lax.axis_index("x"), lax.axis_index("core")
    frames = qkv.shape[2]
    width = grads.shape[1] // 3
    count = frames // block
    mine = pl.ds(pl.multiple_of(me * span, span), span)
    flips = (7, 6, 5, 4, 3, 2, 1)
    mates = [(me, x ^ dx, core ^ dc) for dx, dc in ((0, 1), (1, 0), (1, 1))]
    greet([seq_flip(flip) for flip in flips] + mates)
    loads = []
    for utt in range(2):
        loads.append(
            [
                pltpu.make_async_copy(qkv_all.at[utt], qkv.at[utt], load.at[utt]),
                pltpu.make_async_copy(o_all.at[utt], outs.at[utt], load.at[2 + utt]),
            ]
        )
        for copy in loads[-1]:
            copy.start()

    def send_heads(utt):
        rows = pl.ds(utt * span, span)
        my_cols = pl.ds(pl.multiple_of(me * 128, 128), 128)
        own = pltpu.make_async_copy(dout.at[rows, my_cols], douts.at[utt, mine, :], dlocal.at[utt])
        own.start()
        copies = []
        for flip in flips:
            cols = pl.ds(pl.multiple_of((me ^ flip) * 128, 128), 128)
            copy = remote(
                dout.at[rows, cols],
                douts.at[utt, mine, :],
                dsend.at[utt * 8 + flip],
                drecv.at[utt * 8 + flip],
                seq_flip(flip),
            )
            copy.start()
            copies.append(copy)
        return own, copies

    def arrive(sent):
        own, copies = sent
        own.wait()
        for copy in copies:
            copy.wait_recv()

    def slot(utt, part, flip):
        return (utt * 3 + part) * 8 + flip

    def target(utt, part):
        cols = pl.ds(pl.multiple_of(part * width + me * 128, 128), 128)
        return grads.at[pl.ds(utt * span, span), cols]

    def send_grads(utt, part, there):
        rows = pl.ds(pl.multiple_of(there * span, span), span)

        @pl.when(there != me)
        def _():
            at = slot(utt, part, there ^ me)
            remote(
                qkv.at[utt, part, rows, :],
                target(utt, part),
                gsend.at[at],
                grecv.at[at],
                (there, x, core),
            ).start()

        @pl.when(there == me)
        def _():
            pltpu.make_async_copy(
                qkv.at[utt, part, rows, :], target(utt, part), glocal.at[utt * 3 + part]
            ).start()

    def differentiate(utt):
        length = len_ref[utt]

        def build(j, carry):
            rows = pl.ds(pl.multiple_of(j * block, block), block)
            lane = lanes_of(block)
            queries = qkv[utt, 0, rows, :].astype(F32)
            grad = douts[utt, rows, :].astype(F32)
            delta_a, delta_b = head_sums(grad * outs[utt, rows, :].astype(F32), lane)
            lse = lse_ref[utt, :, rows].T
            one_a, one_b = lse[:, 0:1], lse[:, 1:2]
            qa[rows, :] = jnp.where(
                lane < 64, queries, jnp.where(lane == 67, 1.0, three(one_a, lane, 64))
            ).astype(BF)
            qb[rows, :] = jnp.where(
                lane >= 64, queries, jnp.where(lane == 3, 1.0, three(one_b, lane, 0))
            ).astype(BF)
            da[rows, :] = jnp.where(lane < 64, grad, three(delta_a, lane, 64)).astype(BF)
            db[rows, :] = jnp.where(lane >= 64, grad, three(delta_b, lane, 0)).astype(BF)
            qt[:, rows] = queries.T.astype(BF)
            dt[:, rows] = grad.T.astype(BF)
            dqa[rows, :] = jnp.zeros((block, 128), F32)
            dqb[rows, :] = jnp.zeros((block, 128), F32)
            return carry

        lax.fori_loop(0, count, build, 0)

        def keys_block(step_at, carry):
            i = far_first(step_at, count)
            here = pl.ds(pl.multiple_of(i * block, block), block)
            lane = lanes_of(block)
            pos = i * block + lax.broadcasted_iota(jnp.int32, (block, 128), 0)
            bias = jnp.where(pos < length, 0.0, MASKED)
            keys = qkv[utt, 1, here, :].astype(F32)
            vals = qkv[utt, 2, here, :].astype(F32)
            ones_a = jnp.where(lane < 67, 1.0, 0.0)
            ones_b = jnp.where(lane < 3, 1.0, 0.0)
            ka = jnp.where(lane < 64, keys, jnp.where(lane == 67, bias, ones_a)).astype(BF)
            kb = jnp.where(lane >= 64, keys, jnp.where(lane == 3, bias, ones_b)).astype(BF)
            va = jnp.where(lane < 64, vals, ones_a).astype(BF)
            vb = jnp.where(lane >= 64, vals, ones_b).astype(BF)

            def body(j_at, inner):
                j = far_first(j_at, count)
                rows = pl.ds(pl.multiple_of(j * block, block), block)
                result = []
                for head, (qh, dh, kh, vh, dq) in enumerate(
                    ((qa, da, ka, va, dqa), (qb, db, kb, vb, dqb))
                ):
                    part = slice(head * 64, head * 64 + 64)
                    probs = jnp.exp2(nt(qh[rows, :], kh))
                    grad = (probs * nt(dh[rows, :], vh)).astype(BF)
                    dv = inner[2 * head + 1] + nn(dt[:, rows], probs.astype(BF))[part]
                    dk = inner[2 * head] + nn(qt[:, rows], grad)[part]
                    dq[rows, :] += nn(grad, kh)
                    result += [dk, dv]

                @pl.when(step_at == count - 1)
                def _():
                    low = jnp.where(lanes_of(block) < 64, dqa[rows, :], dqb[rows, :]) * 0.125
                    low = turn_back(low, cos_ref[rows, :], sin_ref[rows, :])
                    qkv[utt, 0, rows, :] = low.astype(BF)
                    for step in range(block // span):
                        send_grads(utt, 0, j * (block // span) + step)

                return tuple(result)

            zero = jnp.zeros((64, block), F32)
            dk_a, dv_a, dk_b, dv_b = lax.fori_loop(0, count, body, (zero,) * 4)
            dk = jnp.concatenate([dk_a, dk_b], axis=0).T * LN2
            dv = jnp.concatenate([dv_a, dv_b], axis=0).T
            qkv[utt, 1, here, :] = turn_back(dk, cos_ref[here, :], sin_ref[here, :]).astype(BF)
            qkv[utt, 2, here, :] = dv.astype(BF)
            for step in range(block // span):
                there = i * (block // span) + step
                send_grads(utt, 1, there)
                send_grads(utt, 2, there)
            return carry

        lax.fori_loop(0, count, keys_block, 0)

    first = send_heads(0)
    raws = []
    for index, (raw, got) in enumerate(((raw_a, got_a), (raw_b, got_b), (raw_c, got_c))):
        for slot_at, device in enumerate(mates):
            at = index * 3 + slot_at
            copy = remote(
                raw.at[:, :, :, device[1], device[2]],
                got.at[slot_at],
                rsend.at[at],
                rrecv.at[at],
                device,
            )
            copy.start()
            raws.append(copy)
    for copy in loads[0]:
        copy.wait()
    arrive(first)
    second = send_heads(1)
    differentiate(0)
    for copy in loads[1]:
        copy.wait()
    arrive(second)
    differentiate(1)
    for sent in (first, second):
        for copy in sent[1]:
            copy.wait_send()
    for copy in raws:
        copy.wait()
    for utt in range(2):
        for part in range(3):
            own = qkv.at[utt, part, mine, :]
            pltpu.make_async_copy(own, target(utt, part), glocal.at[utt * 3 + part]).wait()
            for flip in flips:
                at = slot(utt, part, flip)
                copy = remote(own, target(utt, part), gsend.at[at], grecv.at[at], seq_flip(flip))
                copy.wait_send()
                copy.wait_recv()


def attend_backward(lengths, dout, qkv_all, o_all, lse, cos, sin, raws, span, block=1024):
    raws = [raw.reshape(2, 2, 2, 2, 2, raw.shape[0] // 32, raw.shape[1]) for raw in raws]
    frames = 8 * span
    rows, width = dout.shape
    anywhere = pl.BlockSpec(memory_space=pl.ANY)
    vmem = pl.BlockSpec(memory_space=pltpu.VMEM)
    dma = pltpu.SemaphoreType.DMA
    return pl.pallas_call(
        functools.partial(attend_backward_kernel, span=span, block=block),
        in_specs=[pl.BlockSpec(memory_space=pltpu.SMEM)]
        + [anywhere] * 3
        + [vmem] * 3
        + [anywhere] * 3,
        out_specs=[anywhere] * 4,
        out_shape=[jax.ShapeDtypeStruct((rows, 3 * width), BF)]
        + [jax.ShapeDtypeStruct((3, 2, 2, 2) + raw.shape[5:], BF) for raw in raws],
        scratch_shapes=[
            pltpu.VMEM((2, 3, frames, 128), BF),
            pltpu.VMEM((2, frames, 128), BF),
            pltpu.VMEM((2, frames, 128), BF),
        ]
        + [pltpu.VMEM((frames, 128), BF)] * 4
        + [pltpu.VMEM((128, frames), BF)] * 2
        + [pltpu.VMEM((frames, 128), F32)] * 2
        + [dma((16,)), dma((16,)), dma((2,)), dma((48,)), dma((48,)), dma((6,)), dma((4,)), dma((9,)), dma((9,))],
        compiler_params=pltpu.CompilerParams(
            vmem_limit_bytes=VMEM_LIMIT, collective_id=2, has_side_effects=True
        ),
        cost_estimate=attention_cost(frames, 10),
        name="attend_backward",
    )(lengths, dout, qkv_all, o_all, lse, cos, sin, *raws)


def layer_norm(stream):
    centre = stream - jnp.mean(stream, axis=-1, keepdims=True)
    spread = jnp.mean(centre * centre, axis=-1, keepdims=True)
    inverse = lax.rsqrt(spread + EPS)
    return (centre * inverse, inverse)


def norm_back(grad_normed, normed, inverse):
    first_mean = jnp.mean(grad_normed, axis=-1, keepdims=True)
    second_mean = jnp.mean(grad_normed * normed, axis=-1, keepdims=True)
    return inverse * (grad_normed - first_mean - normed * second_mean)


def tn(left, right):
    return lax.dot_general(left, right, (((0,), (0,)), ((), ())), preferred_element_type=F32)


GELU_C = 0.7978845608028654
GELU_A = 0.044715


def gelu_and_slope(z):
    square = z * z
    turn = jnp.tanh(GELU_C * z * (1.0 + GELU_A * square))
    half = 0.5 * (1.0 + turn)
    slope = half + 0.5 * z * (1.0 - turn * turn) * (GELU_C * (1.0 + 3.0 * GELU_A * square))
    return z * half, slope


def row_blocks(rows):
    block = min(rows, 512)
    return [(at, slice(at, at + block)) for at in range(0, rows, block)]


def ffn_forward_kernel(
    att_ref, outw_ref, res_ref, mod_ref, cot_ref, weight_ref, up_ref, down_ref,
    branch_ref, act_ref, slope_ref, gb_ref, out_ref, gate_ref, normed, acc,
):
    step = pl.program_id(0)
    rows = att_ref.shape[0]
    span = rows // mod_ref.shape[0]

    @pl.when(step == 0)
    def _():
        for at, part in row_blocks(span):
            for utt in range(mod_ref.shape[0]):
                here = slice(utt * span + part.start, utt * span + part.stop)
                mod = mod_ref[utt]
                branch = nn(att_ref[here, :], outw_ref[...])
                branch_ref[here, :] = branch
                hat, _ = layer_norm(res_ref[here, :] + mod[2:3] * branch)
                normed[here, :] = (hat * (1.0 + mod[4:5]) + mod[3:4]).astype(BF)
        acc[...] = jnp.zeros_like(acc)

    parts = [part for _, part in row_blocks(rows)]
    ahead = nn(normed[parts[0], :], up_ref[...])
    for index, part in enumerate(parts):
        hidden = ahead
        if index + 1 < len(parts):
            ahead = nn(normed[parts[index + 1], :], up_ref[...])
        act, slope = gelu_and_slope(hidden)
        act = act.astype(BF)
        act_ref[part, :] = act
        slope_ref[part, :] = slope.astype(BF)
        acc[part, :] += nn(act, down_ref[...])

    @pl.when(step == pl.num_programs(0) - 1)
    def _():
        for utt in range(mod_ref.shape[0]):
            mod = mod_ref[utt]
            total = jnp.zeros((1, acc.shape[1]), F32)
            for _, part in row_blocks(span):
                here = slice(utt * span + part.start, utt * span + part.stop)
                branch = acc[here, :]
                mid = res_ref[here, :] + mod[2:3] * branch_ref[here, :]
                out_ref[here, :] = (mid + mod[5:6] * branch).astype(BF)
                upstream = cot_ref[here, :].astype(F32) * weight_ref[here, :]
                gb_ref[here, :] = (upstream * mod[5:6]).astype(BF)
                total += jnp.sum(upstream * branch, axis=0, keepdims=True)
            gate_ref[utt : utt + 1, :] = total


def ffn_backward_kernel(
    att_ref, outw_ref, res_ref, branch_ref, mod_ref, cot_ref, weight_ref, gb_ref,
    act_ref, slope_ref, up_ref, down_ref,
    gup_ref, gdown_ref, gmid_ref, gatt_ref, gout_ref, sums_ref, normed, acc, gba,
):
    step = pl.program_id(0)
    rows = att_ref.shape[0]
    utts = mod_ref.shape[0]
    span = rows // utts

    def hat_of(here, mod):
        return layer_norm(res_ref[here, :] + mod[2:3] * branch_ref[here, :])

    @pl.when(step == 0)
    def _():
        for utt in range(utts):
            mod = mod_ref[utt]
            for _, part in row_blocks(span):
                here = slice(utt * span + part.start, utt * span + part.stop)
                hat, _ = hat_of(here, mod)
                normed[here, :] = (hat * (1.0 + mod[4:5]) + mod[3:4]).astype(BF)
        acc[...] = jnp.zeros_like(acc)

    pieces = []
    for _, part in row_blocks(rows):
        grad = nt(gb_ref[part, :], down_ref[...]) * slope_ref[part, :].astype(F32)
        grad = grad.astype(BF)
        acc[part, :] += nt(grad, up_ref[...])
        pieces.append(grad)
    gdown_ref[...] = tn(act_ref[...], gb_ref[...]).astype(BF)
    gup_ref[...] = tn(normed[...], jnp.concatenate(pieces, axis=0)).astype(BF)

    @pl.when(step == pl.num_programs(0) - 1)
    def _():
        for utt in range(utts):
            mod = mod_ref[utt]
            width = acc.shape[1]
            shift = jnp.zeros((1, width), F32)
            scale = jnp.zeros((1, width), F32)
            gate = jnp.zeros((1, width), F32)
            for _, part in row_blocks(span):
                here = slice(utt * span + part.start, utt * span + part.stop)
                hat, inverse = hat_of(here, mod)
                grad = acc[here, :]
                shift += jnp.sum(grad, axis=0, keepdims=True)
                scale += jnp.sum(grad * hat, axis=0, keepdims=True)
                upstream = cot_ref[here, :].astype(F32) * weight_ref[here, :]
                mid = upstream + norm_back(grad * (1.0 + mod[4:5]), hat, inverse)
                gmid_ref[here, :] = mid
                gate += jnp.sum(mid * branch_ref[here, :], axis=0, keepdims=True)
                low = (mid * mod[2:3]).astype(BF)
                gba[here, :] = low
                gatt_ref[here, :] = nt(low, outw_ref[...]).astype(BF)
            sums_ref[utt, 0:1, :] = shift
            sums_ref[utt, 1:2, :] = scale
            sums_ref[utt, 2:3, :] = gate
        gout_ref[...] = tn(att_ref[...], gba[...]).astype(BF)


def whole_spec(shape):
    zeros = (0,) * len(shape)
    return pl.BlockSpec(shape, lambda i: zeros, pipeline_mode=pl.Buffered(1))


def ffn_forward(att, outw, res, mods, cot, weight, up, down, chunk=1024):
    rows, width = res.shape
    hidden = up.shape[1]
    whole = [whole_spec(a.shape) for a in (att, outw, res, mods, cot, weight)]
    col = pl.BlockSpec((rows, chunk), lambda i: (0, i))
    utts = mods.shape[0]
    return pl.pallas_call(
        ffn_forward_kernel,
        grid=(hidden // chunk,),
        in_specs=whole
        + [
            pl.BlockSpec((width, chunk), lambda i: (0, i)),
            pl.BlockSpec((chunk, width), lambda i: (i, 0)),
        ],
        out_specs=[
            whole_spec((rows, width)),
            col,
            col,
            whole_spec((rows, width)),
            whole_spec((rows, width)),
            whole_spec((utts, width)),
        ],
        out_shape=[
            jax.ShapeDtypeStruct((rows, width), F32),
            jax.ShapeDtypeStruct((rows, hidden), BF),
            jax.ShapeDtypeStruct((rows, hidden), BF),
            jax.ShapeDtypeStruct((rows, width), BF),
            jax.ShapeDtypeStruct((rows, width), BF),
            jax.ShapeDtypeStruct((utts, width), F32),
        ],
        scratch_shapes=[pltpu.VMEM((rows, width), BF), pltpu.VMEM((rows, width), F32)],
        compiler_params=pltpu.CompilerParams(vmem_limit_bytes=VMEM_LIMIT),
        cost_estimate=pl.CostEstimate(
            flops=2 * rows * width * (width + 2 * hidden),
            bytes_accessed=60 * 2**20,
            transcendentals=rows * hidden,
        ),
        name="ffn_forward",
    )(att, outw, res, mods, cot, weight, up, down)


def ffn_backward(att, outw, res, branch, mods, cot, weight, gb, act, slope, up, down, chunk=512):
    rows, width = res.shape
    hidden = up.shape[1]
    utts = mods.shape[0]
    whole = [whole_spec(a.shape) for a in (att, outw, res, branch, mods, cot, weight, gb)]
    col = pl.BlockSpec((rows, chunk), lambda i: (0, i))
    upspec = pl.BlockSpec((width, chunk), lambda i: (0, i))
    downspec = pl.BlockSpec((chunk, width), lambda i: (i, 0))
    return pl.pallas_call(
        ffn_backward_kernel,
        grid=(hidden // chunk,),
        in_specs=whole + [col, col, upspec, downspec],
        out_specs=[
            upspec,
            downspec,
            whole_spec((rows, width)),
            whole_spec((rows, width)),
            whole_spec((width, width)),
            whole_spec((utts, 8, width)),
        ],
        out_shape=[
            jax.ShapeDtypeStruct((width, hidden), BF),
            jax.ShapeDtypeStruct((hidden, width), BF),
            jax.ShapeDtypeStruct((rows, width), F32),
            jax.ShapeDtypeStruct((rows, width), BF),
            jax.ShapeDtypeStruct((width, width), BF),
            jax.ShapeDtypeStruct((utts, 8, width), F32),
        ],
        scratch_shapes=[
            pltpu.VMEM((rows, width), BF),
            pltpu.VMEM((rows, width), F32),
            pltpu.VMEM((rows, width), BF),
        ],
        compiler_params=pltpu.CompilerParams(vmem_limit_bytes=VMEM_LIMIT),
        cost_estimate=pl.CostEstimate(
            flops=2 * rows * width * (2 * width + 4 * hidden),
            bytes_accessed=90 * 2**20,
            transcendentals=0,
        ),
        name="ffn_backward",
    )(att, outw, res, branch, mods, cot, weight, gb, act, slope, up, down)


FOLD_DIMS = (2, 1)


def fold_jobs(raws, arrived, folded, keeps, buffers):
    jobs = []
    for index, (raw, got) in enumerate(zip(raws, arrived)):
        for side, cols in enumerate(split_columns(raw.shape[-1], (1, 1))):
            at = 2 * index + side
            jobs.append((raw, got, cols, FOLD_DIMS[side], folded[at], keeps[at], buffers[at]))
    return jobs


def fold_pair(index, job, send, recv):
    _, _, _, dim, _, keep, buffer = job
    me, x, core = lax.axis_index("seq"), lax.axis_index("x"), lax.axis_index("core")
    bit = ((me // 4) % 2, (me // 2) % 2, me % 2)[dim]
    lead = (slice(None),) * dim
    copy = remote(
        keep.at[lead + (1 - bit,)],
        buffer,
        send.at[index],
        recv.at[index],
        (me ^ (4 >> dim), x, core),
    )
    return copy, lead + (bit,), bit


def fold_start(jobs, temps, send, recv, own, tsem, store):
    x, core = lax.axis_index("x"), lax.axis_index("core")
    greet([seq_flip(1), seq_flip(2)])
    owns, pieces = [], []
    for index, (raw, got, cols, dim, folded, keep, buffer) in enumerate(jobs):
        owns.append(
            pltpu.make_async_copy(raw.at[:, :, :, x, core, :, cols], keep, own.at[index])
        )
        owns[-1].start()
        for row in range(0, keep.shape[3], 32):
            for col in range(0, keep.shape[4], 512):
                pieces.append((index, row, col))
    depth = temps.shape[0]

    def loads(at):
        index, row, col = pieces[at]
        _, got, cols, *_ = jobs[index]
        slot = at % depth
        return [
            pltpu.make_async_copy(
                got.at[n, :, :, :, pl.ds(row, 32), pl.ds(cols.start + col, 512)],
                temps.at[slot, n],
                tsem.at[3 * slot + n],
            )
            for n in range(3)
        ]

    for at in range(depth):
        for copy in loads(at):
            copy.start()
    for at, (index, row, col) in enumerate(pieces):
        keep = jobs[index][5]
        if at == 0 or pieces[at - 1][0] != index:
            owns[index].wait()
        for copy in loads(at):
            copy.wait()
        slot = at % depth
        rows, cols = pl.ds(row, 32), pl.ds(col, 512)

        def body(i, carry):
            a, b, c = i // 4, (i // 2) % 2, i % 2
            total = keep[a, b, c, rows, cols].astype(F32)
            for n in range(3):
                total = total + temps[slot, n, a, b, c].astype(F32)
            keep[a, b, c, rows, cols] = total.astype(BF)
            return carry

        lax.fori_loop(0, 8, body, 0)
        if at + depth < len(pieces):
            for copy in loads(at + depth):
                copy.start()
        if at + 1 == len(pieces) or pieces[at + 1][0] != index:
            fold_pair(index, jobs[index], send, recv)[0].start()


def fold_finish(jobs, send, recv, own, tsem, store):
    stores = []
    for index, job in enumerate(jobs):
        _, _, _, dim, folded, keep, buffer = job
        copy, where, bit = fold_pair(index, job, send, recv)
        copy.wait_recv()

        def body(i, carry):
            place = [i // 2, i % 2]
            at = list(place)
            at.insert(dim, bit)
            total = keep[tuple(at)].astype(F32) + buffer[tuple(place)].astype(F32)
            keep[tuple(at)] = total.astype(BF)
            return carry

        lax.fori_loop(0, 4, body, 0)
        stores.append(pltpu.make_async_copy(keep.at[where], folded, store.at[index]))
        stores[-1].start()
    for index, job in enumerate(jobs):
        fold_pair(index, job, send, recv)[0].wait_send()
        stores[index].wait()


def leave_kernel(
    grad_ref, qkv_w, skip_w, res_ref, mid_ref, mod_ref, in_ref, skip_ref, *refs
):
    raws, arrived = refs[:3], refs[3:6]
    gin_ref, gskip_ref, sums_ref, gqkv_ref, gw_ref = refs[6:11]
    folded, normed, stream = refs[11:17], refs[17], refs[18]
    jobs = fold_jobs(raws, arrived, folded, refs[19:25], refs[25:31])
    temps, sems = refs[31], refs[32:]
    step = pl.program_id(0)

    @pl.when(step == 0)
    def _():
        fold_start(jobs, temps, *sems)

    leave_compute(
        step, grad_ref, qkv_w, skip_w, res_ref, mid_ref, mod_ref, in_ref, skip_ref,
        gin_ref, gskip_ref, sums_ref, gqkv_ref, gw_ref, normed, stream,
    )

    @pl.when(step == pl.num_programs(0) - 1)
    def _():
        fold_finish(jobs, *sems)


def leave_compute(
    step, grad_ref, qkv_w, skip_w, res_ref, mid_ref, mod_ref, in_ref, skip_ref,
    gin_ref, gskip_ref, sums_ref, gqkv_ref, gw_ref, normed, stream,
):
    rows, width = res_ref.shape
    utts = mod_ref.shape[0]
    span = rows // utts

    @pl.when(step == 0)
    def _():
        for utt in range(utts):
            mod = mod_ref[utt]
            shift = jnp.zeros((1, width), F32)
            scale = jnp.zeros((1, width), F32)
            for _, part in row_blocks(span):
                here = slice(utt * span + part.start, utt * span + part.stop)
                hat, inverse = layer_norm(res_ref[here, :])
                normed[here, :] = (hat * (1.0 + mod[1:2]) + mod[0:1]).astype(BF)
                grad = nt(grad_ref[here, :], qkv_w[...])
                shift += jnp.sum(grad, axis=0, keepdims=True)
                scale += jnp.sum(grad * hat, axis=0, keepdims=True)
                total = mid_ref[here, :] + norm_back(grad * (1.0 + mod[1:2]), hat, inverse)
                low = total.astype(BF)
                stream[here, :] = low
                gin_ref[here, :] = nt(low, skip_w[:width, :]).astype(BF)
                gskip_ref[here, :] = nt(low, skip_w[width:, :]).astype(BF)
            sums_ref[utt, 0:1, :] = shift
            sums_ref[utt, 1:2, :] = scale

    chunk = gqkv_ref.shape[1]
    cols = pl.ds(pl.multiple_of(step * chunk, chunk), chunk)
    gqkv_ref[...] = tn(normed[...], grad_ref[:, cols]).astype(BF)
    part = gw_ref.shape[2]
    here = pl.ds(pl.multiple_of(step * part, part), part)
    gw_ref[0] = tn(in_ref[...], stream[:, here]).astype(BF)
    gw_ref[1] = tn(skip_ref[...], stream[:, here]).astype(BF)


def leave_layer(grads, qkv_w, skip_w, res, mid, mods, first, second, raws, arrived, steps=4):
    rows, width = res.shape
    utts = mods.shape[0]
    ins = (grads, qkv_w, skip_w, res, mid, mods, first, second)
    views = [raw.reshape(2, 2, 2, 2, 2, raw.shape[0] // 32, raw.shape[1]) for raw in raws]
    tails = [
        (view.shape[5], cols.size)
        for view in views
        for cols in split_columns(view.shape[-1], (1, 1))
    ]
    anywhere = pl.BlockSpec(memory_space=pl.ANY)
    dma = pltpu.SemaphoreType.DMA
    outs = pl.pallas_call(
        leave_kernel,
        grid=(steps,),
        in_specs=[whole_spec(a.shape) for a in ins] + [anywhere] * 6,
        out_specs=[
            whole_spec((rows, width)),
            whole_spec((rows, width)),
            whole_spec((utts, 8, width)),
            pl.BlockSpec((width, 3 * width // steps), lambda i: (0, i)),
            pl.BlockSpec((2, width, width // steps), lambda i: (0, 0, i)),
        ]
        + [anywhere] * 6,
        out_shape=[
            jax.ShapeDtypeStruct((rows, width), BF),
            jax.ShapeDtypeStruct((rows, width), BF),
            jax.ShapeDtypeStruct((utts, 8, width), F32),
            jax.ShapeDtypeStruct((width, 3 * width), BF),
            jax.ShapeDtypeStruct((2, width, width), BF),
        ]
        + [jax.ShapeDtypeStruct((2, 2) + tail, BF) for tail in tails],
        scratch_shapes=[pltpu.VMEM((rows, width), BF), pltpu.VMEM((rows, width), BF)]
        + [pltpu.VMEM((2, 2, 2) + tail, BF) for tail in tails]
        + [pltpu.VMEM((2, 2) + tail, BF) for tail in tails]
        + [pltpu.VMEM((4, 3, 2, 2, 2, 32, 512), BF)]
        + [dma((6,)), dma((6,)), dma((6,)), dma((12,)), dma((6,))],
        compiler_params=pltpu.CompilerParams(
            vmem_limit_bytes=VMEM_LIMIT, collective_id=4, has_side_effects=True
        ),
        cost_estimate=pl.CostEstimate(
            flops=4 * rows * (skip_w.size + qkv_w.size),
            bytes_accessed=60 * 2**20,
            transcendentals=0,
        ),
        name="leave_layer",
    )(*ins, *views, *arrived)
    return tuple(outs[:4]) + (outs[4].reshape(2 * width, width), outs[5:])


class GradJob:
    def __init__(self, grad, out, cols, dims, order, keep, buffers, loads, sems, base):
        self.grad, self.out, self.cols, self.dims, self.order = grad, out, cols, dims, order
        self.keep, self.buffers, self.loads = keep, buffers, loads
        self.send, self.recv, self.local, self.base = *sems, base
        me, x, core = lax.axis_index("seq"), lax.axis_index("x"), lax.axis_index("core")
        self.bits = (me // 4, (me // 2) % 2, me % 2, x, core)
        self.copies, self.locals, self.round = [], [], 0

    def peer(self, dim):
        me, x, core = lax.axis_index("seq"), lax.axis_index("x"), lax.axis_index("core")
        if dim < 3:
            return (me ^ (4 >> dim), x, core)
        return (me, 1 - x, core) if dim == 3 else (me, x, 1 - core)

    def launch(self, source, target, dim):
        at = self.base + len(self.copies)
        copy = remote(source, target, self.send.at[at], self.recv.at[at], self.peer(dim))
        copy.start()
        self.copies.append(copy)

    def load(self, source, target):
        copy = pltpu.make_async_copy(source, target, self.local.at[self.base + len(self.locals)])
        copy.start()
        self.locals.append(copy)

    def add(self, done, others):
        left = [dim for dim in self.dims if dim not in done]

        def body(i, carry):
            at, place = [self.bits[dim] for dim in self.dims], []
            for n, dim in enumerate(left):
                bit = (i >> (len(left) - 1 - n)) & 1
                at[self.dims.index(dim)] = bit
                place.append(bit)
            total = self.keep[tuple(at)].astype(F32)
            for other in others:
                total = total + (other[tuple(place)] if place else other[...]).astype(F32)
            self.keep[tuple(at)] = total.astype(BF)
            return carry

        lax.fori_loop(0, 2 ** len(left), body, 0)

    def exchange(self, step):
        dim, done = self.order[step], self.order[:step]
        where = tuple(
            1 - self.bits[d] if d == dim else self.bits[d] if d in done else slice(None)
            for d in self.dims
        )
        self.launch(self.keep.at[where], self.buffers[step], dim)

    def advance(self):
        number, self.round = self.round, self.round + 1
        tail, bits = (slice(None), self.cols), self.bits
        steps = len(self.order)
        every = (slice(None),) * len(self.dims)
        if number == 0:
            if self.loads:
                self.load(self.grad.at[every + (bits[4],) + tail], self.keep)
                self.launch(self.grad.at[every + (1 - bits[4],) + tail], self.loads[0], 4)
            else:
                self.load(self.grad, self.keep)
        elif number == 1:
            self.locals[0].wait()
            if self.loads:
                self.copies[0].wait_recv()
                self.add((), self.loads)
            self.exchange(0)
        elif number <= steps + 1:
            self.copies[-1].wait_recv()
            self.add(self.order[: number - 1], [self.buffers[number - 2]])
            if number <= steps:
                self.exchange(number - 1)
            else:
                mine = self.keep.at[tuple(bits[dim] for dim in self.dims)]
                spot = self.out.at[bits[3:5] + tail]
                self.load(mine, spot)
                self.launch(mine, spot, 3)
        elif number == steps + 2:
            self.locals[-1].wait()
            self.copies[-1].wait_recv()
            both = self.out.at[(slice(None), bits[4]) + tail]
            self.launch(both, both, 4)

    def finish(self):
        self.copies[-1].wait_recv()
        for copy in self.copies:
            copy.wait_send()


FULL_ORDERS = ((3, 2, 1, 0), (2, 1, 3, 0), (1, 3, 2, 0))
FOLDED_DIMS = ((0, 1), (0, 2))
FOLDED_ORDERS = ((1, 0), (2, 0))


def reduce_kernel(*refs, halves, folds):
    grads, folded, small = refs[:halves], refs[halves : halves + 2 * folds], refs[halves + 2 * folds]
    refs = refs[halves + 2 * folds + 1 :]
    outs, small_out = refs[: halves + folds], refs[halves + folds]
    rest = list(refs[halves + folds + 1 :])
    small_in, small_low, send, recv, local, ssend, srecv, bsend, brecv, slocal = rest[-10:]
    me, x, core = lax.axis_index("seq"), lax.axis_index("x"), lax.axis_index("core")
    others = [seq_flip(flip) for flip in range(7, 0, -1)]
    mates = [(me, (x + dx) % 2, (core + dc) % 2) for dx, dc in ((0, 1), (1, 0), (1, 1))]
    greet(others + mates)
    jobs = []
    for index, out in enumerate(outs):
        whole = index < halves
        orders = FULL_ORDERS if whole else FOLDED_ORDERS
        for side, cols in enumerate(split_columns(out.shape[-1], (1,) * len(orders))):
            keep = rest.pop(0)
            loads = [rest.pop(0)] if whole else []
            buffers = [rest.pop(0) for _ in orders[side]]
            jobs.append(
                GradJob(
                    grads[index] if whole else folded[2 * (index - halves) + side],
                    out,
                    cols,
                    (0, 1, 2, 3) if whole else FOLDED_DIMS[side],
                    orders[side],
                    keep,
                    buffers,
                    loads,
                    (send, recv, local),
                    7 * len(jobs),
                )
            )
    own = pltpu.make_async_copy(small, small_in.at[me], slocal.at[0])
    own.start()
    smalls = []
    for flip, device in zip(range(7, 0, -1), others):
        smalls.append(remote(small, small_in.at[me], ssend.at[flip], srecv.at[flip], device))
        smalls[-1].start()
    for _ in range(3):
        for job in jobs:
            job.advance()
    own.wait()
    for copy in smalls:
        copy.wait_recv()
    total = small_in[0]
    for index in range(1, 8):
        total = total + small_in[index]
    small_low[...] = total.astype(BF)
    quarter = x * 2 + core
    keep = pltpu.make_async_copy(small_low, small_out.at[quarter], slocal.at[1])
    keep.start()
    lows = []
    for slot, device in enumerate(mates):
        lows.append(remote(small_low, small_out.at[quarter], bsend.at[slot], brecv.at[slot], device))
        lows[-1].start()
    for _ in range(4):
        for job in jobs:
            job.advance()
    for job in jobs:
        job.finish()
    for copy in smalls:
        copy.wait_send()
    keep.wait()
    for copy in lows:
        copy.wait()


def reduce_grads(halves, shapes, folded, small):
    views, outs, buffers, jobs = [], [], [], 0
    for grad in halves:
        rows, width = grad.shape
        views.append(grad.reshape(2, 2, 2, 2, 2, rows // 32, width))
    for index, (rows, width) in enumerate([grad.shape for grad in halves] + list(shapes)):
        span = rows // 32
        outs.append(jax.ShapeDtypeStruct((2, 2, span, width), BF))
        whole = index < len(halves)
        lead, orders = (4, FULL_ORDERS) if whole else (2, FOLDED_ORDERS)
        for cols in split_columns(width, (1,) * len(orders)):
            jobs += 1
            tail = (span, cols.size)
            for left in [lead] * (2 if whole else 1) + list(range(lead - 1, -1, -1)):
                buffers.append(pltpu.VMEM((2,) * left + tail, BF))
    anywhere = pl.BlockSpec(memory_space=pl.ANY)
    dma = pltpu.SemaphoreType.DMA
    outs.append(jax.ShapeDtypeStruct((4,) + small.shape, BF))
    results = pl.pallas_call(
        functools.partial(reduce_kernel, halves=len(halves), folds=len(shapes)),
        in_specs=[anywhere] * (len(halves) + len(folded) + 1),
        out_specs=[anywhere] * len(outs),
        out_shape=outs,
        scratch_shapes=buffers
        + [pltpu.VMEM((8,) + small.shape, F32), pltpu.VMEM(small.shape, BF)]
        + [dma((7 * jobs,))] * 3
        + [dma((8,)), dma((8,)), dma((3,)), dma((3,)), dma((2,))],
        compiler_params=pltpu.CompilerParams(
            vmem_limit_bytes=VMEM_LIMIT, collective_id=3, has_side_effects=True
        ),
        name="reduce_grads",
    )(*views, *folded, small)
    shards = [
        result.reshape(4 * result.shape[2], result.shape[3]).astype(jnp.float32)
        for result in results[:-1]
    ]
    return shards, results[-1].astype(jnp.float32)


def rotary_tables(positions):
    half_dim = HEAD_DIM // 2
    channel = jnp.arange(half_dim, dtype=jnp.float32)
    inverse = jnp.power(10000.0, -2.0 * channel / HEAD_DIM)
    angles = positions.astype(jnp.float32)[:, None] * inverse[None, :]
    angles = jnp.concatenate([angles, angles], axis=1)
    return (jnp.cos(angles), jnp.sin(angles))


def rotate_heads(field, cosine_table, sine_table):
    half_dim = field.shape[-1] // 2
    turned = jnp.concatenate([-field[..., half_dim:], field[..., :half_dim]], axis=-1)
    return field * cosine_table + turned * sine_table


def smooth_gelu(values):
    return jax.nn.gelu(values, approximate=True)


def cross(left, right):
    return lax.dot_general(
        left, right, (((0,), (0,)), ((), ())), preferred_element_type=jnp.float32
    )


def back_product(left, right):
    return lax.dot_general(
        left, right, (((1,), (1,)), ((), ())), preferred_element_type=jnp.float32
    )


def block_terms(query_block, dout_block, lse_block, delta_block, key_block, value_block, key_live):
    scores = jnp.einsum(
        "bqhd,bkhd->bhqk", query_block, key_block, preferred_element_type=jnp.float32
    )
    lse_heads = jnp.transpose(lse_block, (0, 2, 1))[..., None]
    probs = jnp.where(key_live[:, None, None, :], jnp.exp(scores - lse_heads), 0.0)
    grad_probs = jnp.einsum(
        "bqhd,bkhd->bhqk", dout_block, value_block, preferred_element_type=jnp.float32
    )
    delta_heads = jnp.transpose(delta_block, (0, 2, 1))[..., None]
    dscore = (probs * (grad_probs - delta_heads)).astype(jnp.bfloat16)
    return (probs.astype(jnp.bfloat16), dscore)


BATCH = ("x", "core")


def batch_index():
    return lax.axis_index("x") * lax.axis_size("core") + lax.axis_index("core")


def gather_weight(weight):
    parts = lax.axis_size(BATCH)
    if weight.shape[0] % parts:
        return lax.all_gather(weight, "seq", axis=0, tiled=True)
    rows = weight.shape[0] // parts
    mine = lax.dynamic_slice_in_dim(weight, batch_index() * rows, rows, 0)
    return lax.all_gather(mine, ("seq",) + BATCH, axis=0, tiled=True)


def sum_weight(grad):
    rows, width = grad.shape
    low = grad.astype(jnp.bfloat16)
    seq_count, cores = lax.axis_size("seq"), lax.axis_size("core")
    parts = seq_count * lax.axis_size(BATCH)
    if rows % parts or cores != 2:
        shard = lax.psum_scatter(low, "seq", scatter_dimension=0, tiled=True)
        return lax.psum(shard, BATCH).astype(jnp.float32)
    core = lax.axis_index("core")
    held = low.reshape(parts // 2, 2, rows // parts, width)
    send = lax.dynamic_index_in_dim(held, 1 - core, 1, keepdims=False)
    keep = lax.dynamic_index_in_dim(held, core, 1, keepdims=False)
    got = lax.ppermute(send, "core", [(0, 1), (1, 0)])
    half = (keep.astype(jnp.float32) + got.astype(jnp.float32)).astype(jnp.bfloat16)
    half = half.reshape(rows // 2, width)
    shard = lax.psum_scatter(half, ("seq", "x"), scatter_dimension=0, tiled=True)
    return lax.all_gather(shard, BATCH, axis=0, tiled=True).astype(jnp.float32)


def gather_kernel(*refs, count, ahead, block):
    weights, laters = refs[:count], refs[count : count + ahead]
    refs = refs[count + ahead :]
    seq_small, batch_small, first, second, cos_ref, sin_ref = refs[:6]
    outs = refs[6:]
    fulls, helds = outs[:count], outs[count : count + ahead]
    batch_out, mod_out, res_out, proj_out = outs[count + ahead : count + ahead + 4]
    (
        seq_out, mods, skip_w, qkv_w, res, proj,
        send, recv, asend, arecv, small_send, small_recv, local, lift, put,
    ) = outs[count + ahead + 4 :]
    me, x, core = lax.axis_index("seq"), lax.axis_index("x"), lax.axis_index("core")
    bits = (me // 4, (me // 2) % 2, me % 2, x, core)

    def peer(dim):
        if dim < 3:
            return (me ^ (4 >> dim), x, core)
        return (me, 1 - x, core) if dim == 3 else (me, x, 1 - core)

    others = [((me + d) % 8, x, core) for d in range(1, 8)]
    mates = [(me, (x + dx) % 2, (core + dc) % 2) for dx, dc in ((0, 1), (1, 0), (1, 1))]
    barrier = pltpu.get_barrier_semaphore()
    for device in others + mates:
        pl.semaphore_signal(barrier, inc=1, device_id=device, device_id_type=pl.DeviceIdType.MESH)
    pl.semaphore_wait(barrier, len(others) + len(mates))

    small = []
    quarter = x * 2 + core
    own_seq = pltpu.make_async_copy(seq_small, seq_out.at[me], local.at[0])
    own_batch = pltpu.make_async_copy(batch_small, batch_out.at[quarter], local.at[1])
    own_seq.start()
    own_batch.start()
    for slot, device in enumerate(others):
        small.append(
            pltpu.make_async_remote_copy(
                seq_small, seq_out.at[me], small_send.at[slot], small_recv.at[slot],
                device_id=device, device_id_type=pl.DeviceIdType.MESH,
            )
        )
    for slot, device in enumerate(mates):
        small.append(
            pltpu.make_async_remote_copy(
                batch_small, batch_out.at[quarter], small_send.at[7 + slot], small_recv.at[7 + slot],
                device_id=device, device_id_type=pl.DeviceIdType.MESH,
            )
        )
    for copy in small:
        copy.start()

    jobs = early_jobs(weights, fulls)
    chain = WeightGather(jobs, send, recv, local.at[pl.ds(2, len(jobs))])
    chain.stage()
    chain.stage()
    late = []
    for index, (weight, held) in enumerate(zip(laters, helds)):
        source = quarter_of(weight, pl.ds(0, weight.shape[1]))
        spot = held.at[me // 4, (me // 2) % 2]
        own = pltpu.make_async_copy(source, spot, local.at[2 + len(jobs) + index])
        own.start()
        late.append(own)
        for flip in (2, 3, 1):
            at = 3 * index + flip - 1
            copy = remote(source, spot, asend.at[at], arecv.at[at], seq_flip(2 * flip))
            copy.start()
            late.append(copy)
    for copy in small:
        copy.wait()
    own_seq.wait()
    own_batch.wait()
    total = seq_out[0]
    for index in range(1, 8):
        total = total + seq_out[index]
    mod_out[...] = total
    utts = mods.shape[0]
    for utt in range(utts):
        mods[utt, 0:6, :] = total[utt * 6 : utt * 6 + 6]
    chain.stage()
    chain.stage()
    chain.stage()
    chain.finish()
    for index, (full, flat) in enumerate(zip(fulls, (skip_w, qkv_w))):
        span = full.shape[5]

        def carry_in(p, carry):
            bits = (p // 16, (p // 8) % 2, (p // 4) % 2, (p // 2) % 2, p % 2)
            rows = pl.ds(pl.multiple_of(p * span, span), span)
            pltpu.make_async_copy(full.at[bits], flat.at[rows, :], lift.at[index]).start()
            return carry

        lax.fori_loop(0, 32, carry_in, 0)
    for index, flat in enumerate((skip_w, qkv_w)):
        pltpu.make_async_copy(flat, flat, lift.at[index]).wait()
    rows, width = first.shape
    steps = rows // utts // block

    def enter(i, carry):
        here = pl.ds(pl.multiple_of(i * block, block), block)
        table = pl.ds(pl.multiple_of((i % steps) * block, block), block)
        mod = mods[i // steps]
        residual = nn(first[here, :], skip_w[:width, :]) + nn(second[here, :], skip_w[width:, :])
        res[here, :] = residual
        hat, _ = layer_norm(residual)
        normed = (hat * (1.0 + mod[1:2]) + mod[0:1]).astype(BF)
        lane = lanes_of(block)
        cos, sin = cos_ref[table, :], sin_ref[table, :]
        for part in range(3):
            projected = nn(normed, qkv_w[:, part * width : (part + 1) * width])
            for group in range(width // 128):
                cols = slice(group * 128, group * 128 + 128)
                piece = projected[:, cols]
                if part < 2:
                    turned = jnp.where(
                        (lane & 63) < 32, pltpu.roll(piece, 96, 1), pltpu.roll(piece, 32, 1)
                    )
                    piece = piece * cos + turned * sin
                if part == 0:
                    piece = piece * (0.125 * LOG2E)
                proj[part, here, cols] = piece.astype(BF)
        pltpu.make_async_copy(res.at[here, :], res_out.at[here, :], put.at[0]).start()
        pltpu.make_async_copy(proj.at[:, here, :], proj_out.at[:, here, :], put.at[1]).start()
        return carry

    lax.fori_loop(0, rows // block, enter, 0)
    for copy in late:
        copy.wait()
    pltpu.make_async_copy(res, res_out, put.at[0]).wait()
    pltpu.make_async_copy(proj, proj_out, put.at[1]).wait()


def gather_early(weights, laters, seq_small, batch_small, first, second, cos, sin, block=256):
    anywhere = pl.BlockSpec(memory_space=pl.ANY)
    vmem = pl.BlockSpec(memory_space=pltpu.VMEM)
    jobs, ahead = 4 * len(weights), len(laters)
    rows, width = first.shape
    dma = pltpu.SemaphoreType.DMA
    quarter = lambda lead, w: jax.ShapeDtypeStruct((2,) * lead + (w.shape[0] // 4, w.shape[1]), BF)
    outs = pl.pallas_call(
        functools.partial(gather_kernel, count=len(weights), ahead=ahead, block=block),
        in_specs=[anywhere] * (len(weights) + ahead + 2) + [vmem] * 4,
        out_specs=[anywhere] * (len(weights) + ahead + 1) + [vmem] + [anywhere] * 2,
        out_shape=[quarter(5, w) for w in weights]
        + [quarter(2, w) for w in laters]
        + [
            jax.ShapeDtypeStruct((4,) + batch_small.shape, F32),
            jax.ShapeDtypeStruct(seq_small.shape, F32),
            jax.ShapeDtypeStruct((rows, width), F32),
            jax.ShapeDtypeStruct((3, rows, width), BF),
        ],
        scratch_shapes=[
            pltpu.VMEM((8,) + seq_small.shape, F32),
            pltpu.VMEM((seq_small.shape[0] // 6, 8, width), F32),
        ]
        + [pltpu.VMEM((8 * w.shape[0], w.shape[1]), BF) for w in weights]
        + [
            pltpu.VMEM((rows, width), F32),
            pltpu.VMEM((3, rows, width), BF),
            dma((5 * jobs,)),
            dma((5 * jobs,)),
            dma((5 * ahead,)),
            dma((5 * ahead,)),
            dma((10,)),
            dma((10,)),
            dma((2 + jobs + ahead,)),
            dma((2,)),
            dma((2,)),
        ],
        compiler_params=pltpu.CompilerParams(
            vmem_limit_bytes=VMEM_LIMIT, collective_id=0, has_side_effects=True
        ),
        name="gather_early",
    )(*weights, *laters, seq_small, batch_small, first, second, cos, sin)
    fulls = [full.reshape(8 * w.shape[0], w.shape[1]) for full, w in zip(outs, weights)]
    return fulls, outs[len(weights) : len(weights) + ahead], *outs[-4:]


def paired_tables(count):
    half = HEAD_DIM // 2
    inverse = np.power(10000.0, -2.0 * np.arange(half) / HEAD_DIM)
    angles = np.arange(count)[:, None] * inverse[None, :]
    cos, sin = np.cos(angles), np.sin(angles)
    tables = (np.tile(cos, (1, 4)), np.tile(np.concatenate([-sin, sin], axis=1), (1, 2)))
    return tuple(jnp.asarray(table, jnp.float32) for table in tables)


def on_device(
    layer_input,
    skip_input,
    time_embed,
    lengths,
    cond_drop,
    cotangent,
    skip_weight,
    adaln_weight,
    adaln_bias,
    qkv_weight,
    out_weight,
    up_weight,
    down_weight,
):
    utt_count, frame_span, model_width = layer_input.shape
    head_count = model_width // HEAD_DIM
    row_count = utt_count * frame_span
    seq_here = lax.axis_index("seq")
    seq_count = lax.axis_size("seq")
    frame_count = frame_span * seq_count
    by_heads = (
        seq_count == 8
        and head_count == 16
        and utt_count == 2
        and lax.axis_size(BATCH) == 4
        and frame_span == 512
    )
    local_pos = seq_here * frame_span + jnp.arange(frame_span, dtype=jnp.int32)
    local_live = local_pos[None, :] < lengths[:, None]
    valid_mask = local_live.astype(jnp.float32)
    drop = cond_drop.astype(jnp.float32)
    dropped = drop[:, None] * valid_mask
    frames_live = jnp.minimum(lengths, frame_count).astype(jnp.float32)
    counts = jnp.stack([jnp.sum((1.0 - drop) * frames_live), jnp.sum(drop * frames_live)])
    silu_time = jax.nn.silu(time_embed.astype(jnp.float32)).astype(jnp.bfloat16)
    row_span = adaln_weight.shape[0]
    silu_mine = lax.dynamic_slice_in_dim(silu_time, seq_here * row_span, row_span, 1)
    mod_part = jnp.dot(silu_mine, adaln_weight, preferred_element_type=jnp.float32)
    bias_span = adaln_bias.shape[0]
    bias_here = lax.dynamic_update_slice_in_dim(
        jnp.zeros((mod_part.shape[1],), jnp.float32),
        adaln_bias.astype(jnp.float32),
        seq_here * bias_span,
        0,
    )
    mod_part = mod_part + bias_here
    if by_heads:
        small = jnp.concatenate(
            [
                silu_time.astype(jnp.float32),
                jnp.pad(counts[None, :], ((0, 5), (0, model_width - 2))),
            ],
            axis=0,
        )
        cos_all, sin_all = paired_tables(frame_count)
        first_rows = layer_input.reshape(row_count, model_width)
        second_rows = skip_input.reshape(row_count, model_width)
        gathered = gather_early(
            (skip_weight, qkv_weight),
            (out_weight, up_weight, down_weight),
            mod_part.reshape(-1, model_width),
            small,
            first_rows,
            second_rows,
            lax.dynamic_slice_in_dim(cos_all, seq_here * frame_span, frame_span, 0),
            lax.dynamic_slice_in_dim(sin_all, seq_here * frame_span, frame_span, 0),
        )
        (skip_full, qkv_full), late_held, small_every, modulation, residual_rows, proj = gathered
        totals = jnp.sum(small_every[:, utt_count, :2], axis=0)
        silu_every = small_every[:, :utt_count].reshape(-1, model_width)
    else:
        modulation = lax.psum(mod_part, "seq")
        totals = lax.psum(counts, BATCH)
        skip_full = gather_weight(skip_weight)
        qkv_full = gather_weight(qkv_weight)
        silu_every = lax.all_gather(silu_time, BATCH, axis=0, tiled=True).astype(jnp.float32)
    modulation = modulation.reshape(utt_count, 6, model_width)
    kept_total = jnp.maximum(totals[0], 1.0)
    drop_total = jnp.maximum(totals[1], 1.0)
    every_count = kept_total + drop_total
    loss_weight = (valid_mask - dropped) * (every_count / (2.0 * kept_total)) + dropped * (
        every_count / (2.0 * drop_total)
    )
    if by_heads:
        (qkv_all, out_all, lse_all, attended_low), (out_full, up_full, down_full) = attend_forward(
            lengths, proj, *late_held, frame_span
        )
    else:
        joined = jnp.concatenate([layer_input, skip_input], axis=-1).reshape(row_count, 2 * model_width)
        residual_in = jnp.dot(joined, skip_full, preferred_element_type=jnp.float32).reshape(
            utt_count, frame_span, model_width
        )
        shift_attn = modulation[:, 0][:, None, :]
        scale_attn = modulation[:, 1][:, None, :]
        hat_attn, inv_attn = layer_norm(residual_in)
        normed_attn = (
            (hat_attn * (1.0 + scale_attn) + shift_attn)
            .astype(jnp.bfloat16)
            .reshape(row_count, model_width)
        )
        residual_rows = residual_in.reshape(row_count, model_width)
        out_full, up_full, down_full = [
            gather_weight(weight) for weight in (out_weight, up_weight, down_weight)
        ]
        projected = jnp.dot(normed_attn, qkv_full, preferred_element_type=jnp.float32).reshape(
            utt_count, frame_span, 3, head_count, HEAD_DIM
        )
        cosine_table, sine_table = rotary_tables(local_pos)
        cosine_table = cosine_table[None, :, None, :]
        sine_table = sine_table[None, :, None, :]
        queries = (rotate_heads(projected[:, :, 0], cosine_table, sine_table) * 0.125).astype(
            jnp.bfloat16
        )
        keys_rot = rotate_heads(projected[:, :, 1], cosine_table, sine_table).astype(jnp.bfloat16)
        values = projected[:, :, 2].astype(jnp.bfloat16)
        start_top = jnp.full((utt_count, head_count, frame_span), MASKED, jnp.float32)
        top_score = start_top
        key_piece = lax.all_gather(keys_rot, "seq", axis=1, tiled=True)
        value_piece = lax.all_gather(values, "seq", axis=1, tiled=True)
        piece_len = key_piece.shape[1]
        piece_live = jnp.arange(piece_len, dtype=jnp.int32)[None, :] < lengths[:, None]
        scores = jnp.einsum("bqhd,bkhd->bhqk", queries, key_piece, preferred_element_type=jnp.float32)
        scores = jnp.where(piece_live[:, None, None, :], scores, MASKED)
        new_top = jnp.maximum(top_score, jnp.max(scores, axis=-1))
        expo = jnp.where(piece_live[:, None, None, :], jnp.exp(scores - new_top[..., None]), 0.0)
        denom = jnp.sum(expo, axis=-1)
        partial_out = jnp.einsum(
            "bhqk,bkhd->bqhd",
            expo.astype(jnp.bfloat16),
            value_piece,
            preferred_element_type=jnp.float32,
        )
        accum = partial_out
        accum, top_score, denom = (accum, new_top, denom)
        attended_full = accum / jnp.transpose(denom, (0, 2, 1))[..., None]
        lse_rows = jnp.transpose(top_score + jnp.log(denom), (0, 2, 1))
        attended_low = attended_full.astype(jnp.bfloat16).reshape(row_count, model_width)
    cot_rows = cotangent.reshape(row_count, model_width)
    weight_rows = loss_weight.reshape(row_count, 1)
    branch_attn, hidden_act, hidden_slope, grad_branch_ffn, layer_output, grad_gate_ffn = ffn_forward(
        attended_low,
        out_full,
        residual_rows,
        modulation,
        cot_rows,
        weight_rows,
        up_full,
        down_full,
    )
    layer_output = layer_output.reshape(utt_count, frame_span, model_width)
    grad_up, grad_down, grad_mid, grad_attended_flat, grad_out, ffn_sums = ffn_backward(
        attended_low,
        out_full,
        residual_rows,
        branch_attn,
        modulation,
        cot_rows,
        weight_rows,
        grad_branch_ffn,
        hidden_act,
        hidden_slope,
        up_full,
        down_full,
    )
    grad_shift_ffn, grad_scale_ffn, grad_gate_attn = ffn_sums[:, 0], ffn_sums[:, 1], ffn_sums[:, 2]
    if by_heads:
        grad_projected, *arrived = attend_backward(
            lengths,
            grad_attended_flat,
            qkv_all,
            out_all,
            lse_all,
            cos_all,
            sin_all,
            (grad_down, grad_up, grad_out),
            frame_span,
        )
    else:
        grad_attended = grad_attended_flat.reshape(
            utt_count, frame_span, head_count, HEAD_DIM
        )
        delta_rows = jnp.sum(grad_attended.astype(jnp.float32) * attended_full, axis=-1)
        lse_all, delta_all = (
            lax.all_gather(lse_rows, "seq", axis=1, tiled=True),
            lax.all_gather(delta_rows, "seq", axis=1, tiled=True),
        )
        key_piece = lax.all_gather(keys_rot, "seq", axis=1, tiled=True)
        value_piece = lax.all_gather(values, "seq", axis=1, tiled=True)
        piece_len = key_piece.shape[1]
        piece_live = jnp.arange(piece_len, dtype=jnp.int32)[None, :] < lengths[:, None]
        probs_low, dscore = block_terms(
            queries, grad_attended, lse_rows, delta_rows, key_piece, value_piece, piece_live
        )
        grad_queries = jnp.einsum(
            "bhqk,bkhd->bqhd", dscore, key_piece, preferred_element_type=jnp.float32
        )
        query_piece = lax.all_gather(queries, "seq", axis=1, tiled=True)
        dout_piece = lax.all_gather(grad_attended, "seq", axis=1, tiled=True)
        probs_low, dscore = block_terms(
            query_piece, dout_piece, lse_all, delta_all, keys_rot, values, local_live
        )
        grad_k = jnp.einsum("bhqk,bqhd->bkhd", dscore, query_piece, preferred_element_type=jnp.float32)
        grad_v = jnp.einsum(
            "bhqk,bqhd->bkhd", probs_low, dout_piece, preferred_element_type=jnp.float32
        )
        grad_q_pre = rotate_heads(grad_queries * 0.125, cosine_table, -sine_table)
        grad_k_pre = rotate_heads(grad_k, cosine_table, -sine_table)
        grad_projected = (
            jnp.stack([grad_q_pre, grad_k_pre, grad_v], axis=2)
            .reshape(row_count, 3 * model_width)
            .astype(jnp.bfloat16)
        )
    if by_heads:
        grad_input, grad_skip, attn_sums, grad_qkv, grad_skip_w, folded = leave_layer(
            grad_projected,
            qkv_full,
            skip_full,
            residual_rows,
            grad_mid,
            modulation,
            first_rows,
            second_rows,
            (grad_down, grad_up, grad_out),
            arrived,
        )
        grad_input = grad_input.reshape(layer_input.shape)
        grad_skip = grad_skip.reshape(skip_input.shape)
        grad_shift_attn, grad_scale_attn = attn_sums[:, 0], attn_sums[:, 1]
    else:
        grad_mid = grad_mid.reshape(utt_count, frame_span, model_width)
        grad_qkv = cross(normed_attn, grad_projected)
        grad_normed_attn = back_product(grad_projected, qkv_full).reshape(
            utt_count, frame_span, model_width
        )
        grad_shift_attn = jnp.sum(grad_normed_attn, axis=1)
        grad_scale_attn = jnp.sum(grad_normed_attn * hat_attn, axis=1)
        grad_stream = grad_mid + norm_back(grad_normed_attn * (1.0 + scale_attn), hat_attn, inv_attn)
        grad_stream_low = grad_stream.astype(jnp.bfloat16).reshape(row_count, model_width)
        grad_skip_w = cross(joined, grad_stream_low)
        grad_joined = back_product(grad_stream_low, skip_full)
        grad_input = (
            grad_joined[:, :model_width]
            .reshape(utt_count, frame_span, model_width)
            .astype(jnp.bfloat16)
        )
        grad_skip = (
            grad_joined[:, model_width:]
            .reshape(utt_count, frame_span, model_width)
            .astype(jnp.bfloat16)
        )
    grad_modulation = jnp.stack(
        [
            grad_shift_attn,
            grad_scale_attn,
            grad_gate_attn,
            grad_shift_ffn,
            grad_scale_ffn,
            grad_gate_ffn,
        ],
        axis=1,
    ).reshape(utt_count, 6 * model_width)
    weight_grads = (grad_skip_w, grad_qkv, grad_out, grad_up, grad_down)
    if by_heads:
        shards, mod_every = reduce_grads(
            (grad_qkv, grad_skip_w),
            [grad.shape for grad in (grad_down, grad_up, grad_out)],
            folded,
            grad_modulation.reshape(-1, model_width),
        )
        summed = [shards[i] for i in (1, 0, 4, 3, 2)]
        mod_every = mod_every.reshape(-1, 6 * model_width)
    else:
        mod_total = lax.psum(grad_modulation, "seq")
        mod_every = lax.all_gather(
            mod_total.astype(jnp.bfloat16), BATCH, axis=0, tiled=True
        ).astype(jnp.float32)
        summed = [sum_weight(grad) for grad in weight_grads]
    silu_rows = lax.dynamic_slice_in_dim(silu_every, seq_here * row_span, row_span, 1)
    adaln_rows = jnp.dot(silu_rows.T, mod_every, precision=lax.Precision.HIGHEST)
    bias_rows = lax.dynamic_slice_in_dim(
        jnp.sum(mod_every, axis=0), seq_here * bias_span, bias_span, 0
    )
    results = (summed[0], adaln_rows, bias_rows, summed[1], summed[2], summed[3], summed[4])
    return (
        layer_output,
        grad_input,
        grad_skip,
        results[0],
        results[1],
        results[2],
        results[3],
        results[4],
        results[5],
        results[6],
    )


def solution(mesh):
    count, batch = mesh.shape["seq"], mesh.shape["batch"]
    cores = 2 if batch % 2 == 0 else 1
    split = Mesh(mesh.devices.reshape(count, batch // cores, cores), ("seq",) + BATCH)
    placed = (
        P(BATCH, "seq", None),
        P(BATCH, "seq", None),
        P(BATCH, None),
        P(BATCH),
        P(BATCH),
        P(BATCH, "seq", None),
        P("seq", None),
        P("seq", None),
        P("seq"),
        P("seq", None),
        P("seq", None),
        P("seq", None),
        P("seq", None),
    )
    return jax.shard_map(
        on_device,
        mesh=split,
        in_specs=placed,
        out_specs=(
            P(BATCH, "seq", None),
            P(BATCH, "seq", None),
            P(BATCH, "seq", None),
            P("seq", None),
            P("seq", None),
            P("seq"),
            P("seq", None),
            P("seq", None),
            P("seq", None),
            P("seq", None),
        ),
        check_vma=False,
    )
```
